32 devices in a mesh: blk: 8 (over z, y), rows: 4 (over x, core).
Axes of the slice: x: 2, y: 2, z: 4, core: 2. Of those that a mesh axis runs over, the one named last changes fastest.
Arguments:
- fine_blocks: bfloat16 [4, 8, 8, 8, 128, 128], P('rows', 'blk'), may hold values from -0.5 to 0.5
- block_rows: int32 [4, 8, 8, 8], P('rows', 'blk'), may hold values from 0 to 15
- block_cols: int32 [4, 8, 8, 8], P('rows', 'blk'), may hold values from 0 to 15
- block_counts: int32 [4, 8, 8], P('rows', 'blk'), may hold values from 1 to 8, 36 in all within a row
- prolong_blocks: bfloat16 [4, 128, 128, 384], P('rows', 'blk'), may hold values from -1.1953125 to 1.1953125
- prolong_mask: int32 [4, 128, 3], P('rows', 'blk'), may hold values 0 or 1
Outputs:
- coarse_blocks: float32 [4, 8, 128, 8, 5, 128], P('rows', 'blk')
The draws below stay inside these ranges and needn't reach their ends.
Inputs may be any that keep to these rules, and one draw needn't show every extreme that they name: `block_counts`: the 8 counts of one device sum to 36, and one of them is 8.
All inputs are finite; a program needn't handle non-finite values. No bound on the sum of `prolong_mask` on one device may be relied on, other than what follows from the above.
Results may differ from the reference program's by a relative error of at most 0.004.
Values may be sent and summed in bfloat16 or wider, within the bound.
No kernel may reach another device: no remote copies, remote signals or barrier semaphores. Data moves between devices by JAX's collectives and lax.ppermute only.
A program may use at most 128 MiB of HBM per device.

```python
import math
import jax
import jax.numpy as jnp
import numpy as np
from jax import lax

PORES = 128
CDOF = 128
ROWS_DEV = 16
CAP = 8
LIVE = 36
GROUP_ROWS = 128
N_BLK = 8
N_ROWS = 4


def touch_ends(values, own_key, smallest, largest):
    shape = values.shape
    place = [jax.random.randint(jax.random.fold_in(own_key, axis), (), 0, shape[axis]) for axis in range(len(shape))]
    values = values.at[tuple(place)].set(smallest)
    longest = shape.index(max(shape))
    place[longest] = (place[longest] + 1) % shape[longest]
    return values.at[tuple(place)].set(largest)


def shard_levels(stream_key, shape, pieces, smallest, largest):
    def one(axis_at, parts):
        heights = jax.random.uniform(jax.random.fold_in(jax.random.fold_in(stream_key, 6), axis_at), (parts,), jnp.float32, smallest / len(pieces), largest / len(pieces))
        return jnp.repeat(jnp.exp(heights), shape[axis_at] // parts).reshape((-1,) + (1,) * (len(shape) - axis_at - 1))

    gain = one(*pieces[0])
    for cut in pieces[1:]:
        gain = gain * one(*cut)
    return gain


def split_up(amount, total, bound, slope):
    loads = [(1 << 20) // math.isqrt(grade ** slope) + 1 for grade in range(2, amount + 1)]
    spare, counts = total - bound - (amount - 1), [1] * (amount - 1)
    while spare > 0:
        free = [i for i in range(amount - 1) if counts[i] < bound]
        whole, remaining = sum([loads[i] for i in free]), spare
        for i in free:
            extra = min(bound - counts[i], max(1, remaining * loads[i] // whole), spare)
            counts[i] = counts[i] + extra
            spare = spare - extra
    return np.array([bound] + counts)


def uneven(rng, number_of, total, bound, skew):
    if number_of == 2:
        one = jax.random.randint(rng, (), max(1, total - bound), min(bound, total - 1) + 1)
        return jnp.stack([one, total - one])
    sizes = jnp.asarray(split_up(number_of, total, bound, skew), jnp.int32)
    twos = (number_of - 1) // 2
    giver, receiver = sizes[1:1 + 2 * twos:2], sizes[2:2 + 2 * twos:2]
    margin = jnp.minimum(giver - 1, bound - receiver)
    shifted = jax.random.randint(jax.random.fold_in(rng, 1), (twos,), 0, 1 << 20) % (margin + 1)
    sizes = sizes.at[1:1 + 2 * twos:2].set(giver - shifted).at[2:2 + 2 * twos:2].set(receiver + shifted)
    return sizes[jax.random.permutation(jax.random.fold_in(rng, 2), number_of)]


def normal_values(own_key, extent, deviation, limit, split=(), held_as=jnp.bfloat16):
    gain = shard_levels(own_key, extent, split, -0.22, 0.18) if split else 1.0
    result = jax.random.normal(own_key, extent, jnp.float32) * deviation * gain
    return jnp.minimum(jnp.maximum(result, -limit), limit).astype(held_as)


def setup_inputs(seed: int = 0) -> dict:
    streams_of = jax.random.split(jax.random.key(seed), 7)
    fine_blocks = normal_values(streams_of[0], (N_ROWS, N_BLK, N_BLK, CAP, PORES, PORES), PORES ** -0.5, 0.5, ((0, 4), (1, 8)))
    block_rows = touch_ends(jax.random.randint(streams_of[1], (N_ROWS, N_BLK, N_BLK, CAP), 0, ROWS_DEV), jax.random.fold_in(streams_of[1], 1), 0, ROWS_DEV - 1).astype(jnp.int32)
    block_cols = touch_ends(jax.random.randint(streams_of[2], (N_ROWS, N_BLK, N_BLK, CAP), 0, ROWS_DEV), jax.random.fold_in(streams_of[2], 1), 0, ROWS_DEV - 1).astype(jnp.int32)
    block_counts = jax.vmap(lambda own: uneven(own, N_BLK, LIVE, CAP, 2))(jax.random.split(streams_of[3], N_ROWS * N_BLK)).reshape((N_ROWS, N_BLK, N_BLK)).astype(jnp.int32)
    prolong_blocks = normal_values(streams_of[4], (N_ROWS, GROUP_ROWS, PORES, 3 * CDOF), 0.2, 1.1953125, ((0, 4), (1, 8)))
    prolong_mask = touch_ends((jax.random.randint(streams_of[5], (N_ROWS, GROUP_ROWS, 3), 0, 3) < 2).astype(jnp.int32), jax.random.fold_in(streams_of[5], 1), 0, 1)
    return dict(fine_blocks=fine_blocks, block_rows=block_rows, block_cols=block_cols, block_counts=block_counts, prolong_blocks=prolong_blocks, prolong_mask=prolong_mask)


def masked_prolong(prolong_blocks, prolong_mask):
    groups = jnp.arange(N_ROWS, dtype=jnp.int32)[:, None, None]
    target = groups + jnp.arange(3, dtype=jnp.int32)[None, None, :] - 1
    keeper = (prolong_mask == 1) & (target >= 0) & (target < N_ROWS)
    reshaped_blocks = prolong_blocks.reshape(N_ROWS, GROUP_ROWS, PORES, 3, CDOF)
    kept_blocks = reshaped_blocks * keeper[:, :, None, :, None].astype(prolong_blocks.dtype)
    return kept_blocks.reshape(N_ROWS, GROUP_ROWS, PORES, 3 * CDOF)


def reference(fine_blocks, block_rows, block_cols, block_counts, prolong_blocks, prolong_mask):
    valid_rows = masked_prolong(prolong_blocks, prolong_mask)

    def one_device(device_index):
        group_index = (device_index // N_BLK).astype(jnp.int32)
        panel_index = (device_index % N_BLK).astype(jnp.int32)
        group_rows = lax.dynamic_index_in_dim(valid_rows, group_index, 0, keepdims=False)
        slot_blocks = lax.dynamic_index_in_dim(lax.dynamic_index_in_dim(fine_blocks, group_index, 0, keepdims=False), panel_index, 0, keepdims=False)
        slot_rows = lax.dynamic_index_in_dim(lax.dynamic_index_in_dim(block_rows, group_index, 0, keepdims=False), panel_index, 0, keepdims=False)
        slot_cols = lax.dynamic_index_in_dim(lax.dynamic_index_in_dim(block_cols, group_index, 0, keepdims=False), panel_index, 0, keepdims=False)
        slot_counts = lax.dynamic_index_in_dim(lax.dynamic_index_in_dim(block_counts, group_index, 0, keepdims=False), panel_index, 0, keepdims=False)
        global_rows = (jnp.arange(N_BLK, dtype=jnp.int32)[:, None] * ROWS_DEV + slot_cols).astype(jnp.int32)
        chosen_entries = jnp.take(group_rows, global_rows, axis=0)
        block_products = jnp.einsum("ptab,ptbc->ptac", slot_blocks.astype(jnp.float32), chosen_entries.astype(jnp.float32))
        is_live = jnp.arange(CAP, dtype=jnp.int32)[None, :] < slot_counts[:, None]
        selector_mask = ((slot_rows[:, :, None] == jnp.arange(ROWS_DEV, dtype=jnp.int32)[None, None, :]) & is_live[:, :, None]).astype(jnp.float32)
        operator_prolong_blocks = jnp.einsum("pti,ptac->iapc", selector_mask, block_products, precision=lax.Precision.HIGHEST).astype(jnp.bfloat16)
        own_rows = lax.dynamic_slice_in_dim(group_rows, (panel_index * ROWS_DEV).astype(jnp.int32), ROWS_DEV, 0)
        partial_value = jnp.dot(own_rows.reshape(ROWS_DEV * PORES, 3 * CDOF).T, operator_prolong_blocks.reshape(ROWS_DEV * PORES, N_BLK * 3 * CDOF), preferred_element_type=jnp.float32)
        return partial_value.astype(jnp.bfloat16).reshape(3, CDOF, N_BLK, 3, CDOF)

    partial_all = lax.map(one_device, jnp.arange(N_ROWS * N_BLK, dtype=jnp.int32))
    partial_all = partial_all.reshape(N_ROWS, N_BLK, 3, CDOF, N_BLK, 3, CDOF)
    own_part = partial_all[:, :, 1].astype(jnp.float32)
    empty_rim = jnp.zeros((1, N_BLK, CDOF, N_BLK, 3, CDOF), jnp.float32)
    from_lower = jnp.concatenate([empty_rim, partial_all[:-1, :, 2].astype(jnp.float32)], axis=0)
    from_upper = jnp.concatenate([partial_all[1:, :, 0].astype(jnp.float32), empty_rim], axis=0)
    widths_own = ((0, 0), (0, 0), (0, 0), (0, 0), (1, 1), (0, 0))
    widths_low = ((0, 0), (0, 0), (0, 0), (0, 0), (0, 2), (0, 0))
    widths_up = ((0, 0), (0, 0), (0, 0), (0, 0), (2, 0), (0, 0))
    return jnp.pad(own_part, widths_own) + jnp.pad(from_lower, widths_low) + jnp.pad(from_upper, widths_up)
```

```python
import functools
import jax
import jax.numpy as jnp
from jax import lax
from jax.experimental import pallas as pl
from jax.experimental.pallas import tpu as pltpu
from jax.sharding import PartitionSpec as P

VMEM_LIMIT = 28 * 1024 * 1024


def grid_of(panels):
    columns = max(d for d in range(1, panels + 1) if panels % d == 0 and d * d <= panels)
    return panels // columns, columns


def pack_kernel(info, mask, prolong, head, tail, turned):
    step = pl.program_id(0)
    group, groups, turn = info[0], info[1], info[2]
    rows = prolong.shape[0]
    width = head.shape[-1]
    for i in range(rows):
        row = step * rows + i
        blocks = []
        for e in range(3):
            candidate = group + e - 1
            keep = (mask[3 * row + e] == 1) & (candidate >= 0) & (candidate < groups)
            block = prolong[i, :, e * width:(e + 1) * width]
            blocks.append(block * jnp.where(keep, 1.0, 0.0).astype(block.dtype))
        packed = [jnp.where(turn == 1, blocks[(k + 1) % 3], blocks[k]) for k in range(3)]
        head[i, 0] = packed[0]
        head[i, 1] = packed[1]
        tail[i] = packed[2]
        for k in range(3):
            turned[i, k * width:(k + 1) * width, :] = packed[k].T


def pack(info, mask, prolong):
    rows, pores, width3 = prolong.shape
    width = width3 // 3
    step = 4 if rows % 4 == 0 else rows
    kind = prolong.dtype
    return pl.pallas_call(
        pack_kernel,
        grid_spec=pltpu.PrefetchScalarGridSpec(
            num_scalar_prefetch=2,
            grid=(rows // step,),
            in_specs=[pl.BlockSpec((step, pores, width3), lambda i, *_: (i, 0, 0))],
            out_specs=[
                pl.BlockSpec((step, 2, pores, width), lambda i, *_: (i, 0, 0, 0)),
                pl.BlockSpec((step, pores, width), lambda i, *_: (i, 0, 0)),
                pl.BlockSpec((step, width3, pores), lambda i, *_: (i, 0, 0)),
            ],
        ),
        out_shape=[
            jax.ShapeDtypeStruct((rows, 2, pores, width), kind),
            jax.ShapeDtypeStruct((rows, pores, width), kind),
            jax.ShapeDtypeStruct((rows, width3, pores), kind),
        ],
        compiler_params=pltpu.CompilerParams(vmem_limit_bytes=VMEM_LIMIT),
        cost_estimate=pl.CostEstimate(flops=0, bytes_accessed=8 * 2 ** 20, transcendentals=0),
        name="pack_rows",
    )(info, mask, prolong)


def stage_kernel(layout, scalars, slot_rows, slot_cols, turned, *refs):
    slots = len(layout)
    sources = sum(len(s) for s in layout)
    matrix = refs[:slots]
    heads = refs[slots:slots + sources]
    tails = refs[slots + sources:slots + 2 * sources]
    own, up, down, total = refs[slots + 2 * sources:]
    cap = matrix[0].shape[1]
    pores = matrix[0].shape[2]
    width = tails[0].shape[-1]
    turn = scalars[0]
    at = 0
    for slot, kinds in enumerate(layout):
        panel = scalars[1 + slot]
        total[...] = jnp.zeros_like(total)
        for whole in kinds:
            live = scalars[1 + slots + at]
            head, tail = heads[at], tails[at]

            def product(entry, whole=whole, head=head, tail=tail, slot=slot, panel=panel):
                pick = slot_cols[panel * cap + entry] if whole else entry
                right = jnp.concatenate([head[pick, 0], head[pick, 1], tail[pick]], axis=1)
                return jnp.dot(matrix[slot][0, entry], right, preferred_element_type=jnp.float32)

            def add(left, value):
                result = jnp.dot(left, value, preferred_element_type=jnp.float32)
                for k in range(3):
                    total[k] += result[:, k * width:(k + 1) * width]

            def two(u, carry, product=product, panel=panel):
                first, second = 2 * u, 2 * u + 1
                left = jnp.concatenate(
                    [turned[slot_rows[panel * cap + first]], turned[slot_rows[panel * cap + second]]], axis=1)
                value = jnp.concatenate([product(first), product(second)], axis=0).astype(jnp.bfloat16)
                add(left, value)
                return carry

            lax.fori_loop(0, live // 2, two, 0)

            @pl.when(live % 2 == 1)
            def _(live=live, product=product, panel=panel):
                entry = live - 1
                add(turned[slot_rows[panel * cap + entry]], product(entry).astype(jnp.bfloat16))

            at += 1
        for f in range(3):
            k = jnp.where(turn == 1, (f + 2) % 3, f)
            own[slot, f] = total[k, pl.ds(pl.multiple_of((1 - turn) * width, width), width), :].astype(own.dtype)
            up[slot, f] = total[k, pl.ds(pl.multiple_of((2 - turn) * width, width), width), :].astype(up.dtype)
            down[slot, f] = total[k, 0:width, :].astype(down.dtype)


def stage(layout, scalars, slot_rows, slot_cols, turned, matrix, heads, tails):
    slots = len(layout)
    panels, cap, pores, _ = matrix.shape
    width3 = turned.shape[1]
    width = width3 // 3

    def whole_spec(x):
        return pl.BlockSpec(x.shape, lambda i, *_, n=x.ndim: (0,) * n)

    matrix_specs = [
        pl.BlockSpec((1, cap, pores, pores), lambda i, s, *_, j=j: (s[1 + j], 0, 0, 0)) for j in range(slots)]
    out = jax.ShapeDtypeStruct((slots, 3, width, width), jnp.bfloat16)
    flops = 2 * slots * 5 * (pores * pores * width3 + width3 * width3 * pores)
    size = sum(2 * x.size for x in (*heads, *tails)) + 2 * turned.size + 2 * slots * cap * pores * pores
    return pl.pallas_call(
        functools.partial(stage_kernel, layout),
        grid_spec=pltpu.PrefetchScalarGridSpec(
            num_scalar_prefetch=3,
            grid=(1,),
            in_specs=[whole_spec(turned), *matrix_specs, *map(whole_spec, heads), *map(whole_spec, tails)],
            out_specs=[pl.BlockSpec(out.shape, lambda i, *_: (0, 0, 0, 0))] * 3,
            scratch_shapes=[pltpu.VMEM((3, width3, width), jnp.float32)],
        ),
        out_shape=[out] * 3,
        compiler_params=pltpu.CompilerParams(vmem_limit_bytes=VMEM_LIMIT),
        cost_estimate=pl.CostEstimate(flops=flops, bytes_accessed=size, transcendentals=0),
        name="stage_products",
    )(scalars, slot_rows, slot_cols, turned, *([matrix] * slots), *heads, *tails)


def assemble_kernel(counts, panels, info, *refs):
    out = refs[-1]
    total = sum(counts)
    rows = refs[0].shape[2]
    pitch = 5 * panels
    at = 0
    for index, slots in enumerate(counts):
        own, lower, upper = refs[3 * index:3 * index + 3]
        for slot in range(slots):
            @pl.when(info[total + at] == 1)
            def _(slot=slot, own=own, lower=lower, upper=upper, at=at):
                panel = info[at]
                for d in range(5):
                    terms = []
                    if 0 <= d - 1 < 3:
                        terms.append(own[slot, d - 1].astype(jnp.float32))
                    if d < 3:
                        terms.append(lower[slot, d].astype(jnp.float32))
                    if 0 <= d - 2 < 3:
                        terms.append(upper[slot, d - 2].astype(jnp.float32))
                    out[pl.ds(d * panels + panel, rows, stride=pitch), :] = functools.reduce(jnp.add, terms)
            at += 1


def assemble(info, pieces, panels):
    counts = tuple(own.shape[0] for own, _, _ in pieces)
    width = pieces[0][0].shape[-1]
    rows = width // 4
    specs = [
        pl.BlockSpec((x.shape[0], 3, rows, width), lambda i, *_: (0, 0, i, 0)) for piece in pieces for x in piece]
    flat = [x for piece in pieces for x in piece]
    result = pl.pallas_call(
        functools.partial(assemble_kernel, counts, panels),
        grid_spec=pltpu.PrefetchScalarGridSpec(
            num_scalar_prefetch=1,
            grid=(width // rows,),
            in_specs=specs,
            out_specs=pl.BlockSpec((rows * 5 * panels, width), lambda i, *_: (i, 0)),
        ),
        out_shape=jax.ShapeDtypeStruct((width * 5 * panels, width), jnp.float32),
        compiler_params=pltpu.CompilerParams(vmem_limit_bytes=VMEM_LIMIT),
        cost_estimate=pl.CostEstimate(flops=0, bytes_accessed=8 * 2 ** 20, transcendentals=0),
        name="assemble_coarse",
    )(info, *flat)
    return result.reshape(width, 5, panels, width).transpose(0, 2, 1, 3)


def per_device(fine_blocks, block_rows, block_cols, block_counts, prolong_blocks, prolong_mask):
    matrix = fine_blocks[0, 0]
    rows_list = block_rows[0, 0]
    cols_list = block_cols[0, 0]
    count_list = block_counts[0, 0]
    prolong = prolong_blocks[0]
    panels = lax.axis_size("blk")
    groups = lax.axis_size("rows")
    lines, columns = grid_of(panels)
    group = lax.axis_index("rows")
    place = lax.axis_index("blk")
    z, y = place // columns, place % columns
    turn = (group == 0).astype(jnp.int32)
    flat_rows, flat_cols = rows_list.reshape(-1), cols_list.reshape(-1)

    every = range(groups)
    inner = range(1, groups - 1)

    def move(x, pairs, members):
        perm = [(a * groups + g, b * groups + g) for g in members for a, b in pairs]
        if not perm:
            return jnp.zeros_like(x)
        return lax.ppermute(x, ("blk", "rows"), perm)

    def move_both(pair, pairs):
        return move(pair[0], pairs, every), move(pair[1], pairs, inner)

    def line_pairs(s, sign):
        return [(h * columns + c, (h + sign) * columns + c)
                for h in range(lines) for c in range(columns)
                if 0 <= h + sign < lines and 0 <= h + sign - sign * s < lines]

    def across_pairs(shift, present):
        return [(h * columns + c, h * columns + (c + shift) % columns)
                for h in range(lines) if present(h) for c in range(columns)]

    served = [move(cols_list, [(b, a) for a, b in across_pairs(shift, lambda h: True)], every)
              for shift in range(1, columns)]

    info = jnp.stack([group, jnp.int32(groups), turn]).astype(jnp.int32)
    head, tail, turned = pack(info, prolong_mask[0].reshape(-1), prolong)
    own = (head, tail)

    def has(s, sign):
        source = z + sign * s
        return (source >= 0) & (source < lines)

    def picked(pair, line, shift):
        wanted = lax.dynamic_index_in_dim(served[shift - 1], jnp.clip(line, 0, lines - 1) * columns + y, 0, False)
        return tuple(x.at[wanted].get(mode="promise_in_bounds") for x in pair)

    def entry(line, shift):
        return jnp.clip(line, 0, lines - 1) * columns + (y - shift) % columns

    merged = [2 * s > lines - 1 for s in range(lines)]
    received = [[(z, jnp.bool_(True), [(own, jnp.bool_(True))])]]
    below, above = own, own
    crossing = []
    pieces, slot_panels, slot_present = [], [], []
    for s in range(lines + 1):
        if 0 < s < lines:
            below = move_both(below, line_pairs(s, 1))
            above = move_both(above, line_pairs(s, -1))
            has_below, has_above = has(s, -1), has(s, 1)
            if merged[s]:
                line = jnp.where(has_below, z - s, z + s)
                received.append([(line, has_below | has_above, [(below, has_below), (above, has_above)])])
            else:
                received.append([(z - s, has_below, [(below, has_below)]), (z + s, has_above, [(above, has_above)])])
        work = []
        if s < lines:
            work += [(entry(line, 0), there, [(p, ok, True) for p, ok in sources])
                     for line, there, sources in received[s]]
        if s > 0:
            work += crossing
        crossing = []
        if s < lines:
            for shift in range(1, columns):
                for index, (line, there, sources) in enumerate(received[s]):
                    pair = picked(sources[0][0], line, shift)
                    if len(sources) == 2:
                        other = picked(sources[1][0], line, shift)
                        pair = tuple(jnp.where(sources[0][1], a, b) for a, b in zip(pair, other))
                    if s == 0:
                        present = lambda h: True
                    elif merged[s]:
                        present = lambda h: 0 <= h - s or h + s < lines
                    else:
                        present = (lambda h: 0 <= h - s) if index == 0 else (lambda h: h + s < lines)
                    crossing.append((entry(line, shift), there,
                                     [(move_both(pair, across_pairs(shift, present)), there, False)]))
        if not work:
            continue
        layout = tuple(tuple(whole for _, _, whole in sources) for _, _, sources in work)
        panel_of = [panel for panel, _, _ in work]
        lives = [jnp.where(ok, count_list[panel], 0) for panel, _, sources in work for _, ok, _ in sources]
        scalars = jnp.stack([turn, *panel_of, *lives]).astype(jnp.int32)
        heads = [pair[0] for _, _, sources in work for pair, _, _ in sources]
        tails = [pair[1] for _, _, sources in work for pair, _, _ in sources]
        mine, up, down = stage(layout, scalars, flat_rows, flat_cols, turned, matrix, heads, tails)
        lower = lax.ppermute(up, "rows", [(g, g + 1) for g in range(groups - 1)])
        upper = lax.ppermute(down, "rows", [(g + 1, g) for g in range(groups - 1)])
        pieces.append((mine, lower, upper))
        slot_panels += panel_of
        slot_present += [there.astype(jnp.int32) for _, there, _ in work]
    where = jnp.stack([*slot_panels, *slot_present]).astype(jnp.int32)
    return assemble(where, pieces, panels)[None, None]


def solution(mesh):
    in_specs = (
        P("rows", "blk", None, None, None, None),
        P("rows", "blk", None, None),
        P("rows", "blk", None, None),
        P("rows", "blk", None),
        P("rows", "blk", None, None),
        P("rows", "blk", None),
    )
    out_specs = P("rows", "blk", None, None, None, None)
    return jax.shard_map(
        per_device, mesh=mesh, in_specs=in_specs, out_specs=out_specs, check_vma=False
    )
```

```python
import functools
import jax
import jax.numpy as jnp
from jax import lax
from jax.experimental import pallas as pl
from jax.experimental.pallas import tpu as pltpu
from jax.sharding import PartitionSpec as P

VMEM_LIMIT = 28 * 1024 * 1024


def grid_of(panels):
    columns = max(d for d in range(1, panels + 1) if panels % d == 0 and d * d <= panels)
    return panels // columns, columns


def pack_kernel(info, mask, prolong, head, tail, turned):
    step = pl.program_id(0)
    group, groups, turn = info[0], info[1], info[2]
    rows = prolong.shape[0]
    width = head.shape[-1]
    for i in range(rows):
        row = step * rows + i
        blocks = []
        for e in range(3):
            candidate = group + e - 1
            keep = (mask[3 * row + e] == 1) & (candidate >= 0) & (candidate < groups)
            block = prolong[i, :, e * width:(e + 1) * width]
            blocks.append(block * jnp.where(keep, 1.0, 0.0).astype(block.dtype))
        packed = [jnp.where(turn == 1, blocks[(k + 1) % 3], blocks[k]) for k in range(3)]
        head[i, 0] = packed[0]
        head[i, 1] = packed[1]
        tail[i] = packed[2]
        for k in range(3):
            turned[i, k * width:(k + 1) * width, :] = packed[k].T


def pack(info, mask, prolong):
    rows, pores, width3 = prolong.shape
    width = width3 // 3
    step = 4 if rows % 4 == 0 else rows
    kind = prolong.dtype
    return pl.pallas_call(
        pack_kernel,
        grid_spec=pltpu.PrefetchScalarGridSpec(
            num_scalar_prefetch=2,
            grid=(rows // step,),
            in_specs=[pl.BlockSpec((step, pores, width3), lambda i, *_: (i, 0, 0))],
            out_specs=[
                pl.BlockSpec((step, 2, pores, width), lambda i, *_: (i, 0, 0, 0)),
                pl.BlockSpec((step, pores, width), lambda i, *_: (i, 0, 0)),
                pl.BlockSpec((step, width3, pores), lambda i, *_: (i, 0, 0)),
            ],
        ),
        out_shape=[
            jax.ShapeDtypeStruct((rows, 2, pores, width), kind),
            jax.ShapeDtypeStruct((rows, pores, width), kind),
            jax.ShapeDtypeStruct((rows, width3, pores), kind),
        ],
        compiler_params=pltpu.CompilerParams(vmem_limit_bytes=VMEM_LIMIT),
        cost_estimate=pl.CostEstimate(flops=0, bytes_accessed=8 * 2 ** 20, transcendentals=0),
        name="pack_rows",
    )(info, mask, prolong)


def pick_kernel(plan, outputs, wanted, choice, *refs):
    panels = len(refs) - 2 * outputs - 1
    sources = max(max(options) for _, _, options in plan) + 1
    heads, tails = refs[:sources], refs[sources:2 * sources]
    out = refs[panels:panels + 2 * outputs]
    done = refs[-1]
    cap = wanted.shape[0] // len(plan)

    def copies(request, option, entry):
        target, base, options = plan[request]
        row = wanted[request * cap + entry]
        source = options[option]
        return [
            pltpu.make_async_copy(x.at[row], out[2 * target + part].at[base + entry], done.at[request, entry, part])
            for part, x in enumerate((heads[source], tails[source]))]

    for request, (_, _, options) in enumerate(plan):
        for option in range(len(options)):
            def begin(request=request, option=option):
                for entry in range(cap):
                    for copy in copies(request, option, entry):
                        copy.start()
            if len(options) == 1:
                begin()
            else:
                pl.when(choice[request] == option)(begin)
    for request in range(len(plan)):
        for entry in range(cap):
            for copy in copies(request, 0, entry):
                copy.wait()


def pick(plan, sizes, wanted, choice, pairs, after):
    cap = wanted.shape[0] // len(plan)
    heads, tails = [p[0] for p in pairs], [p[1] for p in pairs]
    anywhere = pl.BlockSpec(memory_space=pl.ANY)
    shapes = []
    for size in sizes:
        shapes += [jax.ShapeDtypeStruct((size, *x.shape[1:]), x.dtype) for x in pairs[0]]
    moved = sum(2 * 2 * x.size for x in shapes)
    result = pl.pallas_call(
        functools.partial(pick_kernel, plan, len(sizes)),
        grid_spec=pltpu.PrefetchScalarGridSpec(
            num_scalar_prefetch=2,
            grid=(1,),
            in_specs=[anywhere] * (2 * len(pairs) + len(after)),
            out_specs=[anywhere] * len(shapes),
            scratch_shapes=[pltpu.SemaphoreType.DMA((len(plan), cap, 2))],
        ),
        out_shape=shapes,
        compiler_params=pltpu.CompilerParams(vmem_limit_bytes=VMEM_LIMIT),
        cost_estimate=pl.CostEstimate(flops=0, bytes_accessed=moved, transcendentals=0),
        name="pick_rows",
    )(wanted, choice, *heads, *tails, *after)
    return [(result[2 * i], result[2 * i + 1]) for i in range(len(sizes))]


def stage_kernel(layout, arrays, extra, scalars, slot_rows, slot_cols, turned, *refs):
    slots = len(layout)
    matrix = refs[:slots]
    heads = refs[slots:slots + arrays]
    tails = refs[slots + arrays:slots + 2 * arrays]
    own, up, down, total = refs[slots + 2 * arrays + extra:]
    cap = matrix[0].shape[1]
    width = tails[0].shape[-1]
    turn = scalars[0]
    at = 0
    for slot, sources in enumerate(layout):
        panel = scalars[1 + slot]
        total[...] = jnp.zeros_like(total)
        for array, base, whole in sources:
            live = scalars[1 + slots + at]
            head, tail = heads[array], tails[array]

            def product(entry, whole=whole, base=base, head=head, tail=tail, slot=slot, panel=panel):
                pick = slot_cols[panel * cap + entry] if whole else base + entry
                right = jnp.concatenate([head[pick, 0], head[pick, 1], tail[pick]], axis=1)
                return jnp.dot(matrix[slot][0, entry], right, preferred_element_type=jnp.float32)

            def add(left, value):
                result = jnp.dot(left, value, preferred_element_type=jnp.float32)
                for k in range(3):
                    total[k] += result[:, k * width:(k + 1) * width]

            def two(u, carry, product=product, panel=panel):
                first, second = 2 * u, 2 * u + 1
                left = jnp.concatenate(
                    [turned[slot_rows[panel * cap + first]], turned[slot_rows[panel * cap + second]]], axis=1)
                value = jnp.concatenate([product(first), product(second)], axis=0).astype(jnp.bfloat16)
                add(left, value)
                return carry

            lax.fori_loop(0, live // 2, two, 0)

            @pl.when(live % 2 == 1)
            def _(live=live, product=product, panel=panel):
                entry = live - 1
                add(turned[slot_rows[panel * cap + entry]], product(entry).astype(jnp.bfloat16))

            at += 1
        for f in range(3):
            k = jnp.where(turn == 1, (f + 2) % 3, f)
            own[slot, f] = total[k, pl.ds(pl.multiple_of((1 - turn) * width, width), width), :].astype(own.dtype)
            up[slot, f] = total[k, pl.ds(pl.multiple_of((2 - turn) * width, width), width), :].astype(up.dtype)
            down[slot, f] = total[k, 0:width, :].astype(down.dtype)


def stage(layout, scalars, slot_rows, slot_cols, turned, matrix, pairs, after):
    slots = len(layout)
    panels, cap, pores, _ = matrix.shape
    width3 = turned.shape[1]
    width = width3 // 3
    heads, tails = [p[0] for p in pairs], [p[1] for p in pairs]

    def whole_spec(x):
        return pl.BlockSpec(x.shape, lambda i, *_, n=x.ndim: (0,) * n)

    matrix_specs = [
        pl.BlockSpec((1, cap, pores, pores), lambda i, s, *_, j=j: (s[1 + j], 0, 0, 0)) for j in range(slots)]
    out = jax.ShapeDtypeStruct((slots, 3, width, width), jnp.bfloat16)
    flops = 2 * slots * 5 * (pores * pores * width3 + width3 * width3 * pores)
    size = sum(2 * x.size for x in (*heads, *tails)) + 2 * turned.size + 2 * slots * cap * pores * pores
    return pl.pallas_call(
        functools.partial(stage_kernel, layout, len(pairs), len(after)),
        grid_spec=pltpu.PrefetchScalarGridSpec(
            num_scalar_prefetch=3,
            grid=(1,),
            in_specs=[whole_spec(turned), *matrix_specs, *map(whole_spec, heads), *map(whole_spec, tails),
                      *([pl.BlockSpec(memory_space=pl.ANY)] * len(after))],
            out_specs=[pl.BlockSpec(out.shape, lambda i, *_: (0, 0, 0, 0))] * 3,
            scratch_shapes=[pltpu.VMEM((3, width3, width), jnp.float32)],
        ),
        out_shape=[out] * 3,
        compiler_params=pltpu.CompilerParams(vmem_limit_bytes=VMEM_LIMIT),
        cost_estimate=pl.CostEstimate(flops=flops, bytes_accessed=size, transcendentals=0),
        name="stage_products",
    )(scalars, slot_rows, slot_cols, turned, *([matrix] * slots), *heads, *tails, *after)


def assemble_kernel(counts, panels, info, *refs):
    out = refs[-1]
    total = sum(counts)
    rows = refs[0].shape[2]
    pitch = 5 * panels
    at = 0
    for index, slots in enumerate(counts):
        own, lower, upper = refs[3 * index:3 * index + 3]
        for slot in range(slots):
            @pl.when(info[total + at] == 1)
            def _(slot=slot, own=own, lower=lower, upper=upper, at=at):
                panel = info[at]
                for d in range(5):
                    terms = []
                    if 0 <= d - 1 < 3:
                        terms.append(own[slot, d - 1].astype(jnp.float32))
                    if d < 3:
                        terms.append(lower[slot, d].astype(jnp.float32))
                    if 0 <= d - 2 < 3:
                        terms.append(upper[slot, d - 2].astype(jnp.float32))
                    out[pl.ds(d * panels + panel, rows, stride=pitch), :] = functools.reduce(jnp.add, terms)
            at += 1


def assemble(info, pieces, panels):
    counts = tuple(own.shape[0] for own, _, _ in pieces)
    width = pieces[0][0].shape[-1]
    rows = width // 4
    specs = [
        pl.BlockSpec((x.shape[0], 3, rows, width), lambda i, *_: (0, 0, i, 0)) for piece in pieces for x in piece]
    flat = [x for piece in pieces for x in piece]
    result = pl.pallas_call(
        functools.partial(assemble_kernel, counts, panels),
        grid_spec=pltpu.PrefetchScalarGridSpec(
            num_scalar_prefetch=1,
            grid=(width // rows,),
            in_specs=specs,
            out_specs=pl.BlockSpec((rows * 5 * panels, width), lambda i, *_: (i, 0)),
        ),
        out_shape=jax.ShapeDtypeStruct((width * 5 * panels, width), jnp.float32),
        compiler_params=pltpu.CompilerParams(vmem_limit_bytes=VMEM_LIMIT),
        cost_estimate=pl.CostEstimate(flops=0, bytes_accessed=8 * 2 ** 20, transcendentals=0),
        name="assemble_coarse",
    )(info, *flat)
    return result.reshape(width, 5, panels, width).transpose(0, 2, 1, 3)


def per_device(fine_blocks, block_rows, block_cols, block_counts, prolong_blocks, prolong_mask):
    matrix = fine_blocks[0, 0]
    rows_list = block_rows[0, 0]
    cols_list = block_cols[0, 0]
    count_list = block_counts[0, 0]
    prolong = prolong_blocks[0]
    cap = cols_list.shape[1]
    panels = lax.axis_size("blk")
    groups = lax.axis_size("rows")
    lines, columns = grid_of(panels)
    group = lax.axis_index("rows")
    place = lax.axis_index("blk")
    z, y = place // columns, place % columns
    turn = (group == 0).astype(jnp.int32)
    flat_rows, flat_cols = rows_list.reshape(-1), cols_list.reshape(-1)
    every = range(groups)
    inner = range(1, groups - 1)
    sides = range(1, columns)
    relays = min(2, lines - 1)

    def move(x, pairs, members):
        perm = [(a * groups + g, b * groups + g) for g in members for a, b in pairs]
        if not perm:
            return jnp.zeros_like(x)
        return lax.ppermute(x, ("blk", "rows"), perm)

    def move_both(pair, pairs):
        return move(pair[0], pairs, every), move(pair[1], pairs, inner)

    def ways(s):
        return [(1, -1)] if 2 * s >= lines else [(1,), (-1,)]

    def far_pairs(s, signs, shift):
        return [(h * columns + c, (h + sign * s) * columns + (c + shift) % columns)
                for h in range(lines) for sign in signs if 0 <= h + sign * s < lines for c in range(columns)]

    def relay_pairs(s, sign):
        return [(h * columns + c, (h + sign) * columns + c)
                for h in range(lines) for c in range(columns)
                if 0 <= h + sign < lines and 0 <= h + sign - sign * s < lines]

    def back(pairs):
        return [(b, a) for a, b in pairs]

    def has(s, sign):
        return (z + sign * s >= 0) & (z + sign * s < lines)

    def panel_at(line, shift):
        return jnp.clip(line, 0, lines - 1) * columns + (y - shift) % columns

    def exchange(parts):
        lower = lax.ppermute(parts[1], "rows", [(g, g + 1) for g in range(groups - 1)])
        upper = lax.ppermute(parts[2], "rows", [(g + 1, g) for g in range(groups - 1)])
        return parts[0], lower, upper

    def run(work, pairs, after):
        layout = tuple(tuple(source[:3] for source in sources) for _, _, sources in work)
        lives = [jnp.where(ok, count_list[panel], 0) for panel, _, sources in work for *_, ok in sources]
        scalars = jnp.stack([turn, *[panel for panel, _, _ in work], *lives]).astype(jnp.int32)
        for panel, there, _ in work:
            slot_panels.append(panel)
            slot_present.append(there)
        return stage(layout, scalars, flat_rows, flat_cols, turned, matrix, pairs, after)

    slot_panels, slot_present, pieces = [], [], []
    yes = jnp.bool_(True)

    info = jnp.stack([group, jnp.int32(groups), turn]).astype(jnp.int32)
    head, tail, turned = pack(info, prolong_mask[0].reshape(-1), prolong)
    own = (head, tail)
    near = [move_both(own, relay_pairs(1, 1)), move_both(own, relay_pairs(1, -1))]
    beside = [move_both(own, far_pairs(0, (1,), shift)) for shift in sides]
    side_lists = [move(cols_list, back(far_pairs(0, (1,), shift)), every) for shift in sides]
    far = [(s, signs, shift) for s in range(relays + 1, lines) for signs in ways(s) for shift in range(columns)]
    far_lists = [move(cols_list, back(far_pairs(*entry)), every) for entry in far]
    parts = run([(place, yes, [(0, 0, True, yes)])], [own], [*side_lists, *far_lists])
    pieces.append(exchange(parts))

    next_up = move_both(near[0], relay_pairs(2, 1))
    next_down = move_both(near[1], relay_pairs(2, -1))
    plan, wanted = [], []
    for index, shift in enumerate(sides):
        for side, line in enumerate((z - 1, z + 1)):
            plan.append((index, side * cap, (side,)))
            wanted.append(lax.dynamic_index_in_dim(side_lists[index], panel_at(line, 0), 0, False))
    picked = pick(tuple(plan), [2 * cap] * len(sides), jnp.concatenate(wanted), jnp.zeros((len(plan),), jnp.int32),
                  near, pieces[-1][1:])
    crossed = [move_both(pair, far_pairs(0, (1,), shift)) for pair, shift in zip(picked, sides)]
    work = [(panel_at(z - 1, 0), has(1, -1), [(0, 0, True, has(1, -1))]),
            (panel_at(z + 1, 0), has(1, 1), [(1, 0, True, has(1, 1))])]
    work += [(panel_at(z, shift), yes, [(2 + i, 0, True, yes)]) for i, shift in enumerate(sides)]
    parts = run(work, [*near, *beside], [])
    pieces.append(exchange(parts))

    from_below = has(2, -1)
    second = jnp.where(from_below, z - 2, z + 2)
    second_there = from_below | has(2, 1)
    plan, wanted, choice = [], [], []
    for index, shift in enumerate(sides):
        plan.append((index, 0, (0, 1)))
        wanted.append(lax.dynamic_index_in_dim(side_lists[index], panel_at(second, 0), 0, False))
        choice.append(jnp.where(from_below, 0, 1))
    for index in range(len(far)):
        plan.append((len(sides) + index, 0, (2,)))
        wanted.append(lax.dynamic_index_in_dim(far_lists[index], place, 0, False))
        choice.append(0)
    picked = pick(tuple(plan), [cap] * len(plan), jnp.concatenate(wanted), jnp.stack(choice).astype(jnp.int32),
                  [next_up, next_down, own], pieces[-1][1:])
    second_crossed = [move_both(pair, far_pairs(0, (1,), shift)) for pair, shift in zip(picked, sides)]
    far_crossed = [move_both(pair, far_pairs(*entry)) for pair, entry in zip(picked[len(sides):], far)]
    work = [(panel_at(second, 0), second_there, [(0, 0, True, from_below), (1, 0, True, has(2, 1))])]
    for i, shift in enumerate(sides):
        work += [(panel_at(z - 1, shift), has(1, -1), [(2 + i, 0, False, has(1, -1))]),
                 (panel_at(z + 1, shift), has(1, 1), [(2 + i, cap, False, has(1, 1))])]
    parts = run(work, [next_up, next_down, *crossed], [])
    pieces.append(exchange(parts))

    work = [(panel_at(second, shift), second_there, [(i, 0, False, second_there)]) for i, shift in enumerate(sides)]
    for i, (s, signs, shift) in enumerate(far):
        present = [has(s, -sign) for sign in signs]
        line = jnp.where(present[0], z - signs[0] * s, z - signs[-1] * s)
        there = functools.reduce(jnp.logical_or, present)
        work.append((panel_at(line, shift), there, [(len(sides) + i, 0, False, there)]))
    parts = run(work, [*second_crossed, *far_crossed], pieces[-1][1:])
    pieces.append(exchange(parts))

    where = jnp.stack([*slot_panels, *slot_present]).astype(jnp.int32)
    return assemble(where, pieces, panels)[None, None]


def solution(mesh):
    in_specs = (
        P("rows", "blk", None, None, None, None),
        P("rows", "blk", None, None),
        P("rows", "blk", None, None),
        P("rows", "blk", None),
        P("rows", "blk", None, None),
        P("rows", "blk", None),
    )
    out_specs = P("rows", "blk", None, None, None, None)
    return jax.shard_map(
        per_device, mesh=mesh, in_specs=in_specs, out_specs=out_specs, check_vma=False
    )
```

```python
import functools
import jax
import jax.numpy as jnp
from jax import lax
from jax.experimental import pallas as pl
from jax.experimental.pallas import tpu as pltpu
from jax.sharding import PartitionSpec as P

VMEM_LIMIT = 56 * 1024 * 1024


def grid_of(panels):
    columns = max(d for d in range(1, panels + 1) if panels % d == 0 and d * d <= panels)
    return panels // columns, columns


def pack_kernel(info, mask, prolong, *refs):
    head, tail, full, turned = refs[-4:]
    step = pl.program_id(0)
    group, groups, turn = info[0], info[1], info[2]
    rows = prolong.shape[0]
    width = tail.shape[-1]
    for i in range(rows):
        row = step * rows + i
        blocks = []
        for e in range(3):
            candidate = group + e - 1
            keep = (mask[3 * row + e] == 1) & (candidate >= 0) & (candidate < groups)
            block = prolong[i, :, e * width:(e + 1) * width]
            blocks.append(block * jnp.where(keep, 1.0, 0.0).astype(block.dtype))
        packed = [jnp.where(turn == 1, blocks[(k + 1) % 3], blocks[k]) for k in range(3)]
        head[i, 0] = packed[0]
        head[i, 1] = packed[1]
        tail[i, 0] = packed[2]
        for k in range(3):
            full[i, k] = packed[k]
            turned[i, k * width:(k + 1) * width, :] = packed[k].T


def pack(info, mask, prolong, after):
    rows, pores, width3 = prolong.shape
    width = width3 // 3
    step = 4 if rows % 4 == 0 else rows
    kind = prolong.dtype

    def part(blocks):
        return (pl.BlockSpec((step, blocks, pores, width), lambda i, *_: (i, 0, 0, 0)),
                jax.ShapeDtypeStruct((rows, blocks, pores, width), kind))

    outs = [part(2), part(1), part(3), (pl.BlockSpec((step, width3, pores), lambda i, *_: (i, 0, 0)),
                                        jax.ShapeDtypeStruct((rows, width3, pores), kind))]
    return pl.pallas_call(
        pack_kernel,
        grid_spec=pltpu.PrefetchScalarGridSpec(
            num_scalar_prefetch=2,
            grid=(rows // step,),
            in_specs=[pl.BlockSpec((step, pores, width3), lambda i, *_: (i, 0, 0)),
                      *([pl.BlockSpec(memory_space=pl.ANY)] * len(after))],
            out_specs=[spec for spec, _ in outs],
        ),
        out_shape=[shape for _, shape in outs],
        compiler_params=pltpu.CompilerParams(vmem_limit_bytes=VMEM_LIMIT),
        cost_estimate=pl.CostEstimate(flops=0, bytes_accessed=8 * 2 ** 20, transcendentals=0),
        name="pack_rows",
    )(info, mask, prolong, *after)


def pick_kernel(plan, sources, counts, wanted, choice, *refs):
    done = refs[-1]
    cap = wanted.shape[0] // len(plan)
    arrays, at = [], 0
    for count in counts:
        arrays.append(refs[at:at + count])
        at += count
    outs = refs[-1 - sources:-1]

    def copies(request, option, entry):
        options, target = plan[request]
        row = wanted[request * cap + entry]
        result, k = [], 0
        for x in arrays[options[option]]:
            for block in range(x.shape[1]):
                output, base, place = target[k]
                result.append(pltpu.make_async_copy(
                    x.at[row, block], outs[output].at[base + entry, place], done.at[request, entry, k]))
                k += 1
        return result

    for request, (options, _) in enumerate(plan):
        for option in range(len(options)):
            def begin(request=request, option=option):
                for entry in range(cap):
                    for copy in copies(request, option, entry):
                        copy.start()
            if len(options) == 1:
                begin()
            else:
                pl.when(choice[request] == option)(begin)
    for request in range(len(plan)):
        for entry in range(cap):
            for copy in copies(request, 0, entry):
                copy.wait()


def pick(plan, sizes, wanted, choice, sources, after):
    cap = wanted.shape[0] // len(plan)
    flat = [x for source in sources for x in source]
    anywhere = pl.BlockSpec(memory_space=pl.ANY)
    shapes = [jax.ShapeDtypeStruct((*size, *flat[0].shape[2:]), flat[0].dtype) for size in sizes]
    return pl.pallas_call(
        functools.partial(pick_kernel, plan, len(sizes), tuple(len(source) for source in sources)),
        grid_spec=pltpu.PrefetchScalarGridSpec(
            num_scalar_prefetch=2,
            grid=(1,),
            in_specs=[anywhere] * (len(flat) + len(after)),
            out_specs=[pl.BlockSpec(x.shape, lambda i, *_: (0, 0, 0, 0)) for x in shapes],
            scratch_shapes=[pltpu.SemaphoreType.DMA((len(plan), cap, 3))],
        ),
        out_shape=shapes,
        compiler_params=pltpu.CompilerParams(vmem_limit_bytes=VMEM_LIMIT),
        cost_estimate=pl.CostEstimate(flops=0, bytes_accessed=sum(4 * x.size for x in shapes), transcendentals=0),
        name="pick_rows",
    )(wanted, choice, *flat, *after)


def stage_kernel(layout, counts, extra, scalars, slot_rows, slot_cols, turned, *refs):
    slots = len(layout)
    matrix = refs[:slots]
    arrays, at = [], slots
    for count in counts:
        arrays.append(refs[at:at + count])
        at += count
    own, up, down, total = refs[at + extra:]
    cap = matrix[0].shape[1]
    width = own.shape[-1]
    turn = scalars[0]
    at = 0
    for slot, sources in enumerate(layout):
        panel = scalars[1 + slot]
        total[...] = jnp.zeros_like(total)
        for array, base, whole in sources:
            live = scalars[1 + slots + at]
            parts = arrays[array]

            def product(entry, whole=whole, base=base, parts=parts, slot=slot, panel=panel):
                pick = slot_cols[panel * cap + entry] if whole else base + entry
                right = jnp.concatenate([x[pick, block] for x in parts for block in range(x.shape[1])], axis=1)
                return jnp.dot(matrix[slot][0, entry], right, preferred_element_type=jnp.float32)

            def add(left, value):
                result = jnp.dot(left, value, preferred_element_type=jnp.float32)
                for k in range(3):
                    total[k] += result[:, k * width:(k + 1) * width]

            def two(u, carry, product=product, panel=panel):
                first, second = 2 * u, 2 * u + 1
                left = jnp.concatenate(
                    [turned[slot_rows[panel * cap + first]], turned[slot_rows[panel * cap + second]]], axis=1)
                value = jnp.concatenate([product(first), product(second)], axis=0).astype(jnp.bfloat16)
                add(left, value)
                return carry

            lax.fori_loop(0, live // 2, two, 0)

            @pl.when(live % 2 == 1)
            def _(live=live, product=product, panel=panel):
                entry = live - 1
                add(turned[slot_rows[panel * cap + entry]], product(entry).astype(jnp.bfloat16))

            at += 1
        for f in range(3):
            k = jnp.where(turn == 1, (f + 2) % 3, f)
            own[slot, f] = total[k, pl.ds(pl.multiple_of((1 - turn) * width, width), width), :].astype(own.dtype)
            up[slot, f] = total[k, pl.ds(pl.multiple_of((2 - turn) * width, width), width), :].astype(up.dtype)
            down[slot, f] = total[k, 0:width, :].astype(down.dtype)


def stage(layout, scalars, slot_rows, slot_cols, turned, matrix, sources, after):
    slots = len(layout)
    panels, cap, pores, _ = matrix.shape
    width3 = turned.shape[1]
    width = width3 // 3
    flat = [x for source in sources for x in source]

    def whole_spec(x):
        return pl.BlockSpec(x.shape, lambda i, *_, n=x.ndim: (0,) * n)

    matrix_specs = [
        pl.BlockSpec((1, cap, pores, pores), lambda i, s, *_, j=j: (s[1 + j], 0, 0, 0)) for j in range(slots)]
    out = jax.ShapeDtypeStruct((slots, 3, width, width), jnp.bfloat16)
    flops = 2 * slots * 5 * (pores * pores * width3 + width3 * width3 * pores)
    size = sum(2 * x.size for x in flat) + 2 * turned.size + 2 * slots * cap * pores * pores
    return pl.pallas_call(
        functools.partial(stage_kernel, layout, tuple(len(source) for source in sources), len(after)),
        grid_spec=pltpu.PrefetchScalarGridSpec(
            num_scalar_prefetch=3,
            grid=(1,),
            in_specs=[whole_spec(turned), *matrix_specs, *map(whole_spec, flat),
                      *([pl.BlockSpec(memory_space=pl.ANY)] * len(after))],
            out_specs=[pl.BlockSpec(out.shape, lambda i, *_: (0, 0, 0, 0))] * 3,
            scratch_shapes=[pltpu.VMEM((3, width3, width), jnp.float32)],
        ),
        out_shape=[out] * 3,
        compiler_params=pltpu.CompilerParams(vmem_limit_bytes=VMEM_LIMIT),
        cost_estimate=pl.CostEstimate(flops=flops, bytes_accessed=size, transcendentals=0),
        name="stage_products",
    )(scalars, slot_rows, slot_cols, turned, *([matrix] * slots), *flat, *after)


def assemble_kernel(counts, panels, info, *refs):
    out = refs[-1]
    total = sum(counts)
    rows = refs[0].shape[2]
    pitch = 5 * panels
    at = 0
    for index, slots in enumerate(counts):
        own, lower, upper = refs[3 * index:3 * index + 3]
        for slot in range(slots):
            @pl.when(info[total + at] == 1)
            def _(slot=slot, own=own, lower=lower, upper=upper, at=at):
                panel = info[at]
                for d in range(5):
                    terms = []
                    if 0 <= d - 1 < 3:
                        terms.append(own[slot, d - 1].astype(jnp.float32))
                    if d < 3:
                        terms.append(lower[slot, d].astype(jnp.float32))
                    if 0 <= d - 2 < 3:
                        terms.append(upper[slot, d - 2].astype(jnp.float32))
                    out[pl.ds(d * panels + panel, rows, stride=pitch), :] = functools.reduce(jnp.add, terms)
            at += 1


def assemble(info, pieces, panels):
    counts = tuple(own.shape[0] for own, _, _ in pieces)
    width = pieces[0][0].shape[-1]
    rows = width // 4
    specs = [
        pl.BlockSpec((x.shape[0], 3, rows, width), lambda i, *_: (0, 0, i, 0)) for piece in pieces for x in piece]
    flat = [x for piece in pieces for x in piece]
    result = pl.pallas_call(
        functools.partial(assemble_kernel, counts, panels),
        grid_spec=pltpu.PrefetchScalarGridSpec(
            num_scalar_prefetch=1,
            grid=(width // rows,),
            in_specs=specs,
            out_specs=pl.BlockSpec((rows * 5 * panels, width), lambda i, *_: (i, 0)),
        ),
        out_shape=jax.ShapeDtypeStruct((width * 5 * panels, width), jnp.float32),
        compiler_params=pltpu.CompilerParams(vmem_limit_bytes=VMEM_LIMIT),
        cost_estimate=pl.CostEstimate(flops=0, bytes_accessed=8 * 2 ** 20, transcendentals=0),
        name="assemble_coarse",
    )(info, *flat)
    return result.reshape(width, 5, panels, width).transpose(0, 2, 1, 3)


def per_device(fine_blocks, block_rows, block_cols, block_counts, prolong_blocks, prolong_mask):
    matrix = fine_blocks[0, 0]
    rows_list = block_rows[0, 0]
    cols_list = block_cols[0, 0]
    count_list = block_counts[0, 0]
    prolong = prolong_blocks[0]
    cap = cols_list.shape[1]
    panels = lax.axis_size("blk")
    groups = lax.axis_size("rows")
    lines, columns = grid_of(panels)
    group = lax.axis_index("rows")
    place = lax.axis_index("blk")
    z, y = place // columns, place % columns
    turn = (group == 0).astype(jnp.int32)
    flat_rows, flat_cols = rows_list.reshape(-1), cols_list.reshape(-1)
    every = range(groups)
    inner = range(1, groups - 1)
    sides = range(1, columns)
    relays = min(2, lines - 1)

    def move(x, pairs, members):
        perm = [(a * groups + g, b * groups + g) for g in members for a, b in pairs]
        if not perm:
            return jnp.zeros_like(x)
        return lax.ppermute(x, ("blk", "rows"), perm)

    def move_both(pair, pairs):
        return move(pair[0], pairs, every), move(pair[1], pairs, inner)

    def ways(s):
        return [(1, -1)] if 2 * s >= lines else [(1,), (-1,)]

    def far_pairs(s, signs, shift):
        return [(h * columns + c, (h + sign * s) * columns + (c + shift) % columns)
                for h in range(lines) for sign in signs if 0 <= h + sign * s < lines for c in range(columns)]

    def relay_pairs(s, sign):
        return [(h * columns + c, (h + sign) * columns + c)
                for h in range(lines) for c in range(columns)
                if 0 <= h + sign < lines and 0 <= h + sign - sign * s < lines]

    def back(pairs):
        return [(b, a) for a, b in pairs]

    def has(s, sign):
        return (z + sign * s >= 0) & (z + sign * s < lines)

    def panel_at(line, shift):
        return jnp.clip(line, 0, lines - 1) * columns + (y - shift) % columns

    def exchange(parts):
        lower = lax.ppermute(parts[1], "rows", [(g, g + 1) for g in range(groups - 1)])
        upper = lax.ppermute(parts[2], "rows", [(g + 1, g) for g in range(groups - 1)])
        return parts[0], lower, upper

    def run(work, arrays, after):
        layout = tuple(tuple(source[:3] for source in sources) for _, _, sources in work)
        lives = [jnp.where(ok, count_list[panel], 0) for panel, _, sources in work for *_, ok in sources]
        scalars = jnp.stack([turn, *[panel for panel, _, _ in work], *lives]).astype(jnp.int32)
        for panel, there, _ in work:
            slot_panels.append(panel)
            slot_present.append(there)
        return stage(layout, scalars, flat_rows, flat_cols, turned, matrix, arrays, after)

    slot_panels, slot_present, pieces = [], [], []
    yes = jnp.bool_(True)

    side_lists = [move(cols_list, back(far_pairs(0, (1,), shift)), every) for shift in sides]
    far = [(s, signs, shift) for s in range(relays + 1, lines) for signs in ways(s) for shift in range(columns)]
    far_lists = [move(cols_list, back(far_pairs(*entry)), every) for entry in far]

    info = jnp.stack([group, jnp.int32(groups), turn]).astype(jnp.int32)
    head, tail, full, turned = pack(info, prolong_mask[0].reshape(-1), prolong, [*side_lists, *far_lists])
    own = (head, tail)
    near = [move_both(own, relay_pairs(1, 1)), move_both(own, relay_pairs(1, -1))]
    beside = [move(full, far_pairs(0, (1,), shift), every) for shift in sides]

    next_up = move_both(near[0], relay_pairs(2, 1))
    next_down = move_both(near[1], relay_pairs(2, -1))
    plan, wanted = [], []
    for index, shift in enumerate(sides):
        for side, line in enumerate((z - 1, z + 1)):
            plan.append(((side,), tuple((index, side * cap, k) for k in range(3))))
            wanted.append(lax.dynamic_index_in_dim(side_lists[index], panel_at(line, 0), 0, False))
    picked = pick(tuple(plan), [(2 * cap, 3)] * len(sides), jnp.concatenate(wanted),
                  jnp.zeros((len(plan),), jnp.int32), near, [])
    crossed = [move(x, far_pairs(0, (1,), shift), every) for x, shift in zip(picked, sides)]
    work = [(place, yes, [(2, 0, True, yes)]),
            (panel_at(z - 1, 0), has(1, -1), [(0, 0, True, has(1, -1))]),
            (panel_at(z + 1, 0), has(1, 1), [(1, 0, True, has(1, 1))])]
    work += [(panel_at(z, shift), yes, [(3 + i, 0, True, yes)]) for i, shift in enumerate(sides)]
    parts = run(work, [*near, (full,), *[(x,) for x in beside]], [])
    pieces.append(exchange(parts))

    from_below = has(2, -1)
    second = jnp.where(from_below, z - 2, z + 2)
    second_there = from_below | has(2, 1)
    plan, wanted, choice, sizes = [], [], [], []
    for index, shift in enumerate(sides):
        plan.append(((0, 1), tuple((index, 0, k) for k in range(3))))
        wanted.append(lax.dynamic_index_in_dim(side_lists[index], panel_at(second, 0), 0, False))
        choice.append(jnp.where(from_below, 0, 1))
        sizes.append((cap, 3))
    for index in range(len(far)):
        at = len(sizes)
        plan.append(((2,), ((at, 0, 0), (at, 0, 1), (at + 1, 0, 0))))
        wanted.append(lax.dynamic_index_in_dim(far_lists[index], place, 0, False))
        choice.append(0)
        sizes += [(cap, 2), (cap, 1)]
    picked = pick(tuple(plan), sizes, jnp.concatenate(wanted), jnp.stack(choice).astype(jnp.int32),
                  [next_up, next_down, (full,)], pieces[-1][1:])
    second_crossed = [move(x, far_pairs(0, (1,), shift), every) for x, shift in zip(picked, sides)]
    picked = picked[len(sides):]
    far_crossed = [move_both(picked[2 * i:2 * i + 2], far_pairs(*entry)) for i, entry in enumerate(far)]
    work = [(panel_at(second, 0), second_there, [(0, 0, True, from_below), (1, 0, True, has(2, 1))])]
    for i, shift in enumerate(sides):
        work += [(panel_at(z - 1, shift), has(1, -1), [(2 + i, 0, False, has(1, -1))]),
                 (panel_at(z + 1, shift), has(1, 1), [(2 + i, cap, False, has(1, 1))])]
    parts = run(work, [next_up, next_down, *[(x,) for x in crossed]], [])
    pieces.append(exchange(parts))
    work = [(panel_at(second, shift), second_there, [(i, 0, False, second_there)]) for i, shift in enumerate(sides)]
    parts = run(work, [(x,) for x in second_crossed], pieces[-1][1:])
    pieces.append(exchange(parts))

    work = []
    for i, (s, signs, shift) in enumerate(far):
        present = [has(s, -sign) for sign in signs]
        line = jnp.where(present[0], z - signs[0] * s, z - signs[-1] * s)
        there = functools.reduce(jnp.logical_or, present)
        work.append((panel_at(line, shift), there, [(i, 0, False, there)]))
    parts = run(work, far_crossed, pieces[-1][1:])
    pieces.append(exchange(parts))

    where = jnp.stack([*slot_panels, *slot_present]).astype(jnp.int32)
    return assemble(where, pieces, panels)[None, None]


def solution(mesh):
    in_specs = (
        P("rows", "blk", None, None, None, None),
        P("rows", "blk", None, None),
        P("rows", "blk", None, None),
        P("rows", "blk", None),
        P("rows", "blk", None, None),
        P("rows", "blk", None),
    )
    out_specs = P("rows", "blk", None, None, None, None)
    return jax.shard_map(
        per_device, mesh=mesh, in_specs=in_specs, out_specs=out_specs, check_vma=False
    )
```

```python
import functools
import jax
import jax.numpy as jnp
from jax import lax
from jax.experimental import pallas as pl
from jax.experimental.pallas import tpu as pltpu
from jax.sharding import PartitionSpec as P

VMEM_LIMIT = 24 * 1024 * 1024
PARAMS = pltpu.CompilerParams(vmem_limit_bytes=VMEM_LIMIT)
COST = pl.CostEstimate(flops=1024, bytes_accessed=1024, transcendentals=0)
PICK_COST = pl.CostEstimate(flops=2 * 10 ** 10, bytes_accessed=1024, transcendentals=0)
ANYWHERE = pl.BlockSpec(memory_space=pl.ANY)


def resident(x):
    return pl.BlockSpec(x.shape, lambda i, *_, n=len(x.shape): (0,) * n)


class Grid:
    def __init__(self, panels):
        self.columns = max(d for d in range(1, panels + 1) if panels % d == 0 and d * d <= panels)
        self.lines = panels // self.columns
        self.sides = range(1, self.columns)
        self.far = [(s, signs, shift) for s in range(3, self.lines)
                    for signs in ([(1, -1)] if 2 * s >= self.lines else [(1,), (-1,)])
                    for shift in range(self.columns)]

    def spot(self):
        place = lax.axis_index("blk")
        return place // self.columns, place % self.columns

    def has(self, z, s, sign):
        return (z + sign * s >= 0) & (z + sign * s < self.lines)

    def panel(self, line, y, shift):
        column = y - shift
        return jnp.clip(line, 0, self.lines - 1) * self.columns + jnp.where(column < 0, column + self.columns, column)

    def second(self, z):
        below = self.has(z, 2, -1)
        return jnp.where(below, z - 2, z + 2), below, self.has(z, 2, 1)

    def hops(self, s, sign):
        return [(h * self.columns + c, (h + sign) * self.columns + c)
                for h in range(self.lines) for c in range(self.columns)
                if 0 <= h + sign < self.lines and 0 <= h + sign - sign * s < self.lines]

    def jumps(self, s, signs, shift):
        return [(h * self.columns + c, (h + sign * s) * self.columns + (c + shift) % self.columns)
                for h in range(self.lines) for sign in signs if 0 <= h + sign * s < self.lines
                for c in range(self.columns)]


    def work_near(self, z, y, cap):
        below, above = self.has(z, 1, -1), self.has(z, 1, 1)
        work = [(self.panel(z, y, 0), True, [(2, 0, True, True)]),
                (self.panel(z - 1, y, 0), below, [(0, 0, True, below)]),
                (self.panel(z + 1, y, 0), above, [(1, 0, True, above)])]
        return work + [(self.panel(z, y, shift), True, [(3 + i, 0, False, True)]) for i, shift in enumerate(self.sides)]

    def work_second(self, z, y, cap):
        line, below, above = self.second(z)
        work = [(self.panel(line, y, 0), below | above, [(0, 0, True, below), (1, 0, True, above)])]
        below, above = self.has(z, 1, -1), self.has(z, 1, 1)
        for i, shift in enumerate(self.sides):
            work += [(self.panel(z - 1, y, shift), below, [(2 + i, 0, False, below)]),
                     (self.panel(z + 1, y, shift), above, [(2 + i, cap, False, above)])]
        return work

    def work_crossed(self, z, y, cap):
        line, below, above = self.second(z)
        return [(self.panel(line, y, shift), below | above, [(i, 0, False, below | above)])
                for i, shift in enumerate(self.sides)]

    def work_far(self, z, y, cap):
        work = []
        for i, (s, signs, shift) in enumerate(self.far):
            present = [self.has(z, s, -sign) for sign in signs]
            line = jnp.where(present[0], z - signs[0] * s, z - signs[-1] * s)
            there = functools.reduce(jnp.logical_or, present)
            work.append((self.panel(line, y, shift), there, [(i, 0, False, there)]))
        return work


def pack_kernel(grid, mask, *refs):
    sides = len(grid.sides)
    wanted, prolong = refs[:sides], refs[sides]
    head, tail, *listed = refs[len(refs) - 2 - sides:]
    group, groups = lax.axis_index("rows"), lax.axis_size("rows")
    width = tail.shape[-1]
    for i in range(prolong.shape[0]):
        blocks = []
        for e in range(3):
            candidate = group + e - 1
            keep = (mask[e, 0, i] == 1) & (candidate >= 0) & (candidate < groups)
            block = prolong[i, :, e * width:(e + 1) * width]
            blocks.append(block * jnp.where(keep, 1.0, 0.0).astype(block.dtype))
        head[i, 0] = jnp.where(group == 0, blocks[1], blocks[0])
        head[i, 1] = jnp.where(group == 0, blocks[2], blocks[1])
        tail[i, 0] = jnp.where(group == 0, blocks[0], blocks[2])
    z, y = grid.spot()
    for rows, out in zip(wanted, listed):
        for entry in range(rows.shape[1]):
            row = rows[grid.panel(z, y, 0), entry]
            out[entry, 0] = head[row, 0]
            out[entry, 1] = head[row, 1]
            out[entry, 2] = tail[row, 0]


def pack(grid, mask, prolong, side_lists, after):
    rows, pores, width3 = prolong.shape
    shapes = [(rows, 2), (rows, 1), *[(x.shape[1], 3) for x in side_lists]]
    outs = [jax.ShapeDtypeStruct((*shape, pores, width3 // 3), prolong.dtype) for shape in shapes]
    return pl.pallas_call(
        functools.partial(pack_kernel, grid),
        grid_spec=pltpu.PrefetchScalarGridSpec(
            num_scalar_prefetch=1 + len(side_lists),
            grid=(1,),
            in_specs=[resident(prolong), *([ANYWHERE] * len(after))],
            out_specs=[*map(resident, outs)],
        ),
        out_shape=outs,
        compiler_params=PARAMS,
        cost_estimate=COST,
        name="pack_rows",
    )(mask, *side_lists, prolong, *after)


def turn_kernel(head, tail, turned):
    width = head.shape[-1]
    for i in range(head.shape[0]):
        for k, block in enumerate((head[i, 0], head[i, 1], tail[i, 0])):
            turned[i, k * width:(k + 1) * width, :] = block.T


def turn(head, tail):
    rows, _, pores, width = head.shape
    out = jax.ShapeDtypeStruct((rows, 3 * width, pores), head.dtype)
    return pl.pallas_call(
        turn_kernel,
        grid=(1,),
        in_specs=[resident(head), resident(tail)],
        out_specs=resident(out),
        out_shape=out,
        compiler_params=PARAMS,
        cost_estimate=COST,
        name="turn_rows",
    )(head, tail)


def pick_kernel(grid, plan, lists, counts, outputs, *refs):
    wanted = refs[:lists]
    arrays, at = [], lists
    for count in counts:
        arrays.append(refs[at:at + count])
        at += count
    outs = refs[len(refs) - outputs:]
    cap = wanted[0].shape[1]
    for index, entry_row, options, target in plan(*grid.spot()):
        for present, source in options:
            def copy(index=index, entry_row=entry_row, source=source, target=target):
                for entry in range(cap):
                    row = wanted[index][entry_row, entry]
                    blocks = [(x, block) for x in arrays[source] for block in range(x.shape[1])]
                    for (x, block), (output, base, place) in zip(blocks, target):
                        outs[output][base + entry, place] = x[row, block]
            if present is True:
                copy()
            else:
                pl.when(present)(copy)


def pick(grid, plan, sizes, lists, sources, after):
    flat = [x for source in sources for x in source]
    shapes = [jax.ShapeDtypeStruct((*size, *flat[0].shape[2:]), flat[0].dtype) for size in sizes]
    return pl.pallas_call(
        functools.partial(
            pick_kernel, grid, plan, len(lists), tuple(len(source) for source in sources), len(sizes)),
        grid_spec=pltpu.PrefetchScalarGridSpec(
            num_scalar_prefetch=len(lists),
            grid=(1,),
            in_specs=[*map(resident, flat), *([ANYWHERE] * len(after))],
            out_specs=[*map(resident, shapes)],
        ),
        out_shape=shapes,
        compiler_params=PARAMS,
        cost_estimate=PICK_COST,
        name="pick_rows",
    )(*lists, *flat, *after)


def stage_kernel(grid, plan, counts, carried, slot_rows, slot_cols, slot_counts, turned, matrix, *refs):
    arrays, at = [], 0
    for count in counts:
        arrays.append(refs[at:at + count])
        at += count
    earlier = refs[at:at + 3] if carried else ()
    own, up, down, total = refs[-4:]
    cap = matrix.shape[1]
    width = own.shape[-1]
    first_group = lax.axis_index("rows") == 0
    for old, new in zip(earlier, (own, up, down)):
        for slot in range(carried):
            for f in range(3):
                new[slot, f] = old[slot, f]
    z, y = grid.spot()
    for slot, (panel, _, sources) in enumerate(plan(z, y, cap), start=carried):
        total[...] = jnp.zeros_like(total)
        for array, base, whole, present in sources:
            live = slot_counts[0, panel]
            if present is not True:
                live = jnp.where(present, live, 0)
            parts = arrays[array]

            def product(entry, whole=whole, base=base, parts=parts, panel=panel):
                pick = slot_cols[panel, entry] if whole else base + entry
                right = jnp.concatenate([x[pick, block] for x in parts for block in range(x.shape[1])], axis=1)
                return jnp.dot(matrix[panel, entry], right, preferred_element_type=jnp.float32)

            def add(left, value):
                result = jnp.dot(left, value, preferred_element_type=jnp.float32)
                for k in range(3):
                    total[k] += result[:, k * width:(k + 1) * width]

            def two(u, carry, product=product, panel=panel):
                first, second = 2 * u, 2 * u + 1
                left = jnp.concatenate(
                    [turned[slot_rows[panel, first]], turned[slot_rows[panel, second]]], axis=1)
                value = jnp.concatenate([product(first), product(second)], axis=0).astype(jnp.bfloat16)
                add(left, value)
                return carry

            lax.fori_loop(0, live // 2, two, 0)

            @pl.when(live % 2 == 1)
            def _(live=live, product=product, panel=panel):
                add(turned[slot_rows[panel, live - 1]], product(live - 1).astype(jnp.bfloat16))

        begin = jnp.where(first_group, 0, width)
        for f in range(3):
            k = jnp.where(first_group, (f + 2) % 3, f)
            own[slot, f] = total[k, pl.ds(pl.multiple_of(begin, width), width), :].astype(own.dtype)
            up[slot, f] = total[k, pl.ds(pl.multiple_of(begin + width, width), width), :].astype(up.dtype)
            down[slot, f] = total[k, 0:width, :].astype(down.dtype)


def stage(grid, plan, lists, turned, matrix, sources, earlier=(), after=()):
    cap = matrix.shape[1]
    width = turned.shape[1] // 3
    carried = earlier[0].shape[0] if earlier else 0
    slots = carried + len(plan(jnp.int32(0), jnp.int32(0), cap))
    flat = [x for source in sources for x in source]
    out = jax.ShapeDtypeStruct((slots, 3, width, width), jnp.bfloat16)
    return pl.pallas_call(
        functools.partial(stage_kernel, grid, plan, tuple(len(source) for source in sources), carried),
        grid_spec=pltpu.PrefetchScalarGridSpec(
            num_scalar_prefetch=3,
            grid=(1,),
            in_specs=[*map(resident, (turned, matrix, *flat, *earlier)), *([ANYWHERE] * len(after))],
            out_specs=[resident(out)] * 3,
            scratch_shapes=[pltpu.VMEM((3, 3 * width, width), jnp.float32)],
        ),
        out_shape=[out] * 3,
        compiler_params=PARAMS,
        cost_estimate=COST,
        name="stage_products",
    )(*lists, turned, matrix, *flat, *earlier, *after)


def assemble_kernel(grid, plans, cap, *refs):
    out = refs[-1]
    rows = refs[0].shape[2]
    panels = grid.lines * grid.columns
    z, y = grid.spot()
    for index, group in enumerate(plans):
        own, lower, upper = refs[3 * index:3 * index + 3]
        slots = [slot for plan in group for slot in plan(z, y, cap)]
        for slot, (panel, present, _) in enumerate(slots):
            def write(slot=slot, own=own, lower=lower, upper=upper, panel=panel):
                for d in range(5):
                    terms = []
                    if 0 <= d - 1 < 3:
                        terms.append(own[slot, d - 1].astype(jnp.float32))
                    if d < 3:
                        terms.append(lower[slot, d].astype(jnp.float32))
                    if 0 <= d - 2 < 3:
                        terms.append(upper[slot, d - 2].astype(jnp.float32))
                    out[pl.ds(d * panels + panel, rows, stride=5 * panels), :] = functools.reduce(jnp.add, terms)
            if present is True:
                write()
            else:
                pl.when(present)(write)


def assemble(grid, plans, cap, pieces):
    panels = grid.lines * grid.columns
    width = pieces[0][0].shape[-1]
    rows = width // 4
    flat = [x for piece in pieces for x in piece]
    result = pl.pallas_call(
        functools.partial(assemble_kernel, grid, plans, cap),
        grid=(width // rows,),
        in_specs=[pl.BlockSpec((x.shape[0], 3, rows, width), lambda i: (0, 0, i, 0)) for x in flat],
        out_specs=pl.BlockSpec((rows * 5 * panels, width), lambda i: (i, 0)),
        out_shape=jax.ShapeDtypeStruct((width * 5 * panels, width), jnp.float32),
        compiler_params=PARAMS,
        cost_estimate=COST,
        name="assemble_coarse",
    )(*flat)
    return result.reshape(width, 5, panels, width).transpose(0, 2, 1, 3)


def per_device(fine_blocks, block_rows, block_cols, block_counts, prolong_blocks, prolong_mask):
    matrix = fine_blocks[0, 0]
    cols_list = block_cols[0, 0]
    lists = (block_rows[0, 0], cols_list, block_counts[0])
    cap = cols_list.shape[1]
    panels = lax.axis_size("blk")
    groups = lax.axis_size("rows")
    grid = Grid(panels)
    sides, far = grid.sides, grid.far
    every, inner = range(groups), range(1, groups - 1)

    def move(x, pairs, members=every):
        perm = [(a * groups + g, b * groups + g) for g in members for a, b in pairs]
        return lax.ppermute(x, ("blk", "rows"), perm) if perm else jnp.zeros_like(x)

    def move_both(pair, pairs):
        return move(pair[0], pairs), move(pair[1], pairs, inner)

    def back(pairs):
        return [(b, a) for a, b in pairs]

    def exchange(parts):
        lower = lax.ppermute(parts[1], "rows", [(g, g + 1) for g in range(groups - 1)])
        upper = lax.ppermute(parts[2], "rows", [(g + 1, g) for g in range(groups - 1)])
        return parts[0], lower, upper

    side_lists = [move(cols_list, back(grid.jumps(0, (1,), shift))) for shift in sides]
    far_lists = [move(cols_list, back(grid.jumps(*entry))) for entry in far]

    head, tail, *picked = pack(grid, prolong_mask.transpose(2, 0, 1), prolong_blocks[0], side_lists, far_lists)
    own = (head, tail)
    near = [move_both(own, grid.hops(1, 1)), move_both(own, grid.hops(1, -1))]
    beside = [move(x, grid.jumps(0, (1,), shift)) for x, shift in zip(picked, sides)]
    turned = turn(head, tail)

    second = [move_both(near[0], grid.hops(2, 1)), move_both(near[1], grid.hops(2, -1))]

    def near_requests(z, y):
        return [(index, grid.panel(z + step, y, 0), [(True, side)], [(index, side * cap, k) for k in range(3)])
                for index in range(len(sides)) for side, step in enumerate((-1, 1))]

    picked = pick(grid, near_requests, [(2 * cap, 3)] * len(sides), side_lists, near, beside)
    crossed = [move(x, grid.jumps(0, (1,), shift)) for x, shift in zip(picked, sides)]
    parts = stage(grid, grid.work_near, lists, turned, matrix, [*near, own, *[(x,) for x in beside]])

    def second_requests(z, y):
        line, below, above = grid.second(z)
        requests = [(index, grid.panel(line, y, 0), [(below, 0), (above, 1)], [(index, 0, k) for k in range(3)])
                    for index in range(len(sides))]
        for index in range(len(sides), len(sides) + len(far)):
            requests.append((index, grid.panel(z, y, 0), [(True, 2)], [(index, 0, k) for k in range(3)]))
        return requests

    sizes = [(cap, 3)] * (len(sides) + len(far))
    picked = pick(grid, second_requests, sizes, [*side_lists, *far_lists], [*second, own], [parts[0]])
    second_crossed = [move(x, grid.jumps(0, (1,), shift)) for x, shift in zip(picked, sides)]
    far_crossed = [move(x, grid.jumps(*entry)) for x, entry in zip(picked[len(sides):], far)]
    parts = stage(grid, grid.work_second, lists, turned, matrix, [*second, *[(x,) for x in crossed]], parts)
    first = exchange(parts)
    parts = stage(grid, grid.work_crossed, lists, turned, matrix, [(x,) for x in second_crossed], (), [parts[0]])

    parts = stage(grid, grid.work_far, lists, turned, matrix, [(x,) for x in far_crossed], parts, first[1:])
    last = exchange(parts)
    plans = ((grid.work_near, grid.work_second), (grid.work_crossed, grid.work_far))
    return assemble(grid, plans, cap, [first, last])[None, None]


def solution(mesh):
    in_specs = (
        P("rows", "blk", None, None, None, None),
        P("rows", "blk", None, None),
        P("rows", "blk", None, None),
        P("rows", "blk", None),
        P("rows", "blk", None, None),
        P("rows", "blk", None),
    )
    out_specs = P("rows", "blk", None, None, None, None)
    return jax.shard_map(
        per_device, mesh=mesh, in_specs=in_specs, out_specs=out_specs, check_vma=False
    )
```

```python
import functools
import jax
import jax.numpy as jnp
from jax import lax
from jax.experimental import pallas as pl
from jax.experimental.pallas import tpu as pltpu
from jax.sharding import PartitionSpec as P

VMEM_LIMIT = 24 * 1024 * 1024
PARAMS = pltpu.CompilerParams(vmem_limit_bytes=VMEM_LIMIT)
COST = pl.CostEstimate(flops=1024, bytes_accessed=1024, transcendentals=0)
NEAR_COST = pl.CostEstimate(flops=6 * 10 ** 9, bytes_accessed=1024, transcendentals=0)
PICK_COST = pl.CostEstimate(flops=2 * 10 ** 10, bytes_accessed=1024, transcendentals=0)
ANYWHERE = pl.BlockSpec(memory_space=pl.ANY)


def resident(x):
    return pl.BlockSpec(x.shape, lambda i, *_, n=len(x.shape): (0,) * n)


LINES = 4


class Grid:
    def __init__(self, panels, cap, pores):
        self.panels, self.cap, self.pores = panels, cap, pores
        self.columns = panels // LINES
        self.sides = range(1, self.columns)
        self.list_rows = -(-panels // 16) * 16

    def spot(self):
        place = lax.axis_index("blk")
        return place // self.columns, place % self.columns

    def has(self, z, s, sign):
        return (z + sign * s >= 0) & (z + sign * s < LINES)

    def panel(self, line, y, shift):
        column = y - shift
        return jnp.clip(line, 0, LINES - 1) * self.columns + jnp.where(column < 0, column + self.columns, column)

    def second(self, z):
        below = self.has(z, 2, -1)
        return jnp.where(below, z - 2, z + 2), below, self.has(z, 2, 1)

    def hops(self, s, sign):
        return [(h * self.columns + c, (h + sign) * self.columns + c)
                for h in range(LINES) for c in range(self.columns)
                if 0 <= h + sign < LINES and 0 <= h + sign - sign * s < LINES]

    def across(self, shift):
        return [(h * self.columns + c, h * self.columns + (c + shift) % self.columns)
                for h in range(LINES) for c in range(self.columns)]

    def ends(self, shift):
        return [(h * self.columns + c, end * self.columns + (c + shift) % self.columns)
                for h, end in ((1, 0), (LINES - 2, LINES - 1)) for c in range(self.columns)]

    def part(self, ref, blocks, row, block):
        start = (row * blocks + block) * self.pores
        if not isinstance(start, int):
            start = pl.multiple_of(start, self.pores)
        return ref.at[pl.ds(start, self.pores), :]

    def shape(self, rows, blocks, width, lists=0):
        return jax.ShapeDtypeStruct((rows * blocks * self.pores + lists * self.list_rows, width), jnp.bfloat16)


    def work_near(self, z, y):
        below, above = self.has(z, 1, -1), self.has(z, 1, 1)
        work = [(self.panel(z, y, 0), True, [(2, 0, True, True)]),
                (self.panel(z - 1, y, 0), below, [(0, 0, True, below)]),
                (self.panel(z + 1, y, 0), above, [(1, 0, True, above)])]
        return work + [(self.panel(z, y, shift), True, [(3 + i, 0, False, True)]) for i, shift in enumerate(self.sides)]

    def work_second(self, z, y):
        line, below, above = self.second(z)
        work = [(self.panel(line, y, 0), below | above, [(0, 0, True, below), (1, 0, True, above)])]
        below, above = self.has(z, 1, -1), self.has(z, 1, 1)
        for i, shift in enumerate(self.sides):
            work += [(self.panel(z - 1, y, shift), below, [(2 + i, 0, False, below)]),
                     (self.panel(z + 1, y, shift), above, [(2 + i, self.cap, False, above)])]
        return work

    def work_crossed(self, z, y):
        line, below, above = self.second(z)
        return [(self.panel(line, y, shift), below | above, [(i, 0, False, below | above)])
                for i, shift in enumerate(self.sides)]

    def work_far(self, z, y):
        there = (z == 0) | (z == LINES - 1)
        return [(self.panel(LINES - 1 - z, y, shift), there, [(shift, 0, False, there)])
                for shift in range(self.columns)]


def pack_kernel(grid, mask, cols, prolong, head, tail):
    group, groups = lax.axis_index("rows"), lax.axis_size("rows")
    width = tail.shape[-1]
    for i in range(prolong.shape[0]):
        blocks = []
        for e in range(3):
            candidate = group + e - 1
            keep = (mask[e, 0, i] == 1) & (candidate >= 0) & (candidate < groups)
            block = prolong[i, :, e * width:(e + 1) * width]
            blocks.append(block * jnp.where(keep, 1.0, 0.0).astype(block.dtype))
        grid.part(head, 2, i, 0)[...] = jnp.where(group == 0, blocks[1], blocks[0])
        grid.part(head, 2, i, 1)[...] = jnp.where(group == 0, blocks[2], blocks[1])
        grid.part(tail, 1, i, 0)[...] = jnp.where(group == 0, blocks[0], blocks[2])
    row = lax.broadcasted_iota(jnp.int32, (grid.list_rows, width), 0)
    column = lax.broadcasted_iota(jnp.int32, (grid.list_rows, width), 1)
    numbers = jnp.zeros((grid.list_rows, width), jnp.int32)
    for panel in range(grid.panels):
        for entry in range(grid.cap):
            numbers = jnp.where((row == panel) & (column == entry), cols[panel, entry], numbers)
    start = prolong.shape[0] * 2 * grid.pores
    head[start:start + grid.list_rows, :] = numbers.astype(jnp.float32).astype(head.dtype)


def pack(grid, mask, cols, prolong):
    rows, _, width3 = prolong.shape
    outs = [grid.shape(rows, 2, width3 // 3, 1), grid.shape(rows, 1, width3 // 3)]
    return pl.pallas_call(
        functools.partial(pack_kernel, grid),
        grid_spec=pltpu.PrefetchScalarGridSpec(
            num_scalar_prefetch=2,
            grid=(1,),
            in_specs=[resident(prolong)],
            out_specs=[*map(resident, outs)],
        ),
        out_shape=outs,
        compiler_params=PARAMS,
        cost_estimate=COST,
        name="pack_rows",
    )(mask, cols, prolong)


def turn_kernel(grid, head, tail, turned):
    width = head.shape[-1]
    for i in range(turned.shape[0]):
        parts = (grid.part(head, 2, i, 0), grid.part(head, 2, i, 1), grid.part(tail, 1, i, 0))
        for k, part in enumerate(parts):
            turned[i, k * width:(k + 1) * width, :] = part[...].T


def turn(grid, head, tail):
    rows, width = tail.shape[0] // grid.pores, tail.shape[1]
    out = jax.ShapeDtypeStruct((rows, 3 * width, grid.pores), head.dtype)
    return pl.pallas_call(
        functools.partial(turn_kernel, grid),
        grid=(1,),
        in_specs=[resident(head), resident(tail)],
        out_specs=resident(out),
        out_shape=out,
        compiler_params=PARAMS,
        cost_estimate=COST,
        name="turn_rows",
    )(head, tail)


def pick_kernel(grid, plan, layout, carry, tables, lists, outputs, *refs):
    wanted = list(refs[:lists])
    sources, at = [], lists
    for blocks in layout:
        sources.append([(refs[at + i], k) for i, k in enumerate(blocks)])
        at += len(blocks)
    scratch = 2 * len(tables) + 1 if tables else 0
    outs = refs[len(refs) - outputs - scratch:len(refs) - scratch]
    z, y = grid.spot()

    def list_at(ref, place):
        start = ref.shape[0] - (place + 1) * grid.list_rows
        return ref[start:start + grid.list_rows, :]

    if tables:
        numbers, plain, done = refs[-scratch:-1 - len(tables)], refs[-1 - len(tables):-1], refs[-1]
        for table, options in enumerate(tables):
            value = None
            for present, source, place in options:
                here = list_at(sources[source][0][0], place).astype(jnp.float32)
                value = here if value is None else jnp.where(present(z), here, value)
            numbers[table][...] = value.astype(jnp.int32)
            pltpu.make_async_copy(numbers[table], plain[table], done.at[table]).start()
        for table in range(len(tables)):
            pltpu.make_async_copy(numbers[table], plain[table], done.at[table]).wait()
        wanted += plain
    for index, list_row, options, output, base in plan(z, y):
        for present, source in options:
            def copy(index=index, list_row=list_row, source=source, output=output, base=base):
                for entry in range(grid.cap):
                    row = wanted[index][list_row, entry]
                    place = 0
                    for ref, blocks in sources[source]:
                        for block in range(blocks):
                            grid.part(outs[output], 3, base + entry, place)[...] = grid.part(ref, blocks, row, block)[...]
                            place += 1
            if present is True:
                copy()
            else:
                pl.when(present)(copy)
    for source, place in carry:
        for out in outs:
            start = out.shape[0] - (place + 1) * grid.list_rows
            out[start:start + grid.list_rows, :] = list_at(sources[source][0][0], 0)


def pick(grid, plan, sizes, lists, sources, carry=(), tables=(), after=(), cost=COST):
    flat = [x for source in sources for x, _ in source]
    width = flat[0].shape[-1]
    shapes = [grid.shape(size, 3, width, len(carry)) for size in sizes]
    layout = tuple(tuple(blocks for _, blocks in source) for source in sources)
    table = (grid.list_rows, width)
    scratch = [pltpu.VMEM(table, jnp.int32)] * len(tables) + [pltpu.SMEM(table, jnp.int32)] * len(tables)
    scratch += [pltpu.SemaphoreType.DMA((len(tables),))] if tables else []
    return pl.pallas_call(
        functools.partial(pick_kernel, grid, plan, layout, carry, tables, len(lists), len(sizes)),
        grid_spec=pltpu.PrefetchScalarGridSpec(
            num_scalar_prefetch=len(lists),
            grid=(1,),
            in_specs=[*map(resident, flat), *([ANYWHERE] * len(after))],
            out_specs=[*map(resident, shapes)],
            scratch_shapes=scratch,
        ),
        out_shape=shapes,
        compiler_params=PARAMS,
        cost_estimate=cost,
        name="pick_rows",
    )(*lists, *flat, *after)


def stage_kernel(grid, plan, layout, carried, slot_rows, slot_cols, slot_counts, turned, matrix, *refs):
    arrays, at = [], 0
    for blocks in layout:
        arrays.append([(refs[at + i], k) for i, k in enumerate(blocks)])
        at += len(blocks)
    earlier = refs[at:at + 3] if carried else ()
    own, up, down, total = refs[-4:]
    width = own.shape[-1]
    first_group = lax.axis_index("rows") == 0
    for old, new in zip(earlier, (own, up, down)):
        for slot in range(carried):
            for f in range(3):
                new[slot, f] = old[slot, f]
    z, y = grid.spot()
    for slot, (panel, _, sources) in enumerate(plan(z, y), start=carried):
        total[...] = jnp.zeros_like(total)
        for array, base, whole, present in sources:
            live = slot_counts[0, panel]
            if present is not True:
                live = jnp.where(present, live, 0)
            parts = arrays[array]

            def product(entry, whole=whole, base=base, parts=parts, panel=panel):
                pick = slot_cols[panel, entry] if whole else base + entry
                right = jnp.concatenate(
                    [grid.part(x, blocks, pick, block)[...] for x, blocks in parts for block in range(blocks)], axis=1)
                return jnp.dot(matrix[panel, entry], right, preferred_element_type=jnp.float32)

            def add(left, value):
                result = jnp.dot(left, value, preferred_element_type=jnp.float32)
                for k in range(3):
                    total[k] += result[:, k * width:(k + 1) * width]

            def two(u, carry, product=product, panel=panel):
                first, second = 2 * u, 2 * u + 1
                left = jnp.concatenate(
                    [turned[slot_rows[panel, first]], turned[slot_rows[panel, second]]], axis=1)
                value = jnp.concatenate([product(first), product(second)], axis=0).astype(jnp.bfloat16)
                add(left, value)
                return carry

            lax.fori_loop(0, live // 2, two, 0)

            @pl.when(live % 2 == 1)
            def _(live=live, product=product, panel=panel):
                add(turned[slot_rows[panel, live - 1]], product(live - 1).astype(jnp.bfloat16))

        begin = jnp.where(first_group, 0, width)
        for f in range(3):
            k = jnp.where(first_group, (f + 2) % 3, f)
            own[slot, f] = total[k, pl.ds(pl.multiple_of(begin, width), width), :].astype(own.dtype)
            up[slot, f] = total[k, pl.ds(pl.multiple_of(begin + width, width), width), :].astype(up.dtype)
            down[slot, f] = total[k, 0:width, :].astype(down.dtype)


def stage(grid, plan, lists, turned, matrix, sources, earlier=(), after=()):
    width = turned.shape[1] // 3
    carried = earlier[0].shape[0] if earlier else 0
    slots = carried + len(plan(jnp.int32(0), jnp.int32(0)))
    flat = [x for source in sources for x, _ in source]
    layout = tuple(tuple(blocks for _, blocks in source) for source in sources)
    out = jax.ShapeDtypeStruct((slots, 3, width, width), jnp.bfloat16)
    return pl.pallas_call(
        functools.partial(stage_kernel, grid, plan, layout, carried),
        grid_spec=pltpu.PrefetchScalarGridSpec(
            num_scalar_prefetch=3,
            grid=(1,),
            in_specs=[*map(resident, (turned, matrix, *flat, *earlier)), *([ANYWHERE] * len(after))],
            out_specs=[resident(out)] * 3,
            scratch_shapes=[pltpu.VMEM((3, 3 * width, width), jnp.float32)],
        ),
        out_shape=[out] * 3,
        compiler_params=PARAMS,
        cost_estimate=COST,
        name="stage_products",
    )(*lists, turned, matrix, *flat, *earlier, *after)


def assemble_kernel(grid, plans, *refs):
    out = refs[-1]
    rows = refs[0].shape[2]
    panels = grid.panels
    z, y = grid.spot()
    for index, group in enumerate(plans):
        own, lower, upper = refs[3 * index:3 * index + 3]
        slots = [slot for plan in group for slot in plan(z, y)]
        for slot, (panel, present, _) in enumerate(slots):
            def write(slot=slot, own=own, lower=lower, upper=upper, panel=panel):
                for d in range(5):
                    terms = []
                    if 0 <= d - 1 < 3:
                        terms.append(own[slot, d - 1].astype(jnp.float32))
                    if d < 3:
                        terms.append(lower[slot, d].astype(jnp.float32))
                    if 0 <= d - 2 < 3:
                        terms.append(upper[slot, d - 2].astype(jnp.float32))
                    out[pl.ds(d * panels + panel, rows, stride=5 * panels), :] = functools.reduce(jnp.add, terms)
            if present is True:
                write()
            else:
                pl.when(present)(write)


def assemble(grid, plans, pieces):
    panels = grid.panels
    width = pieces[0][0].shape[-1]
    rows = width // 4
    flat = [x for piece in pieces for x in piece]
    result = pl.pallas_call(
        functools.partial(assemble_kernel, grid, plans),
        grid=(width // rows,),
        in_specs=[pl.BlockSpec((x.shape[0], 3, rows, width), lambda i: (0, 0, i, 0)) for x in flat],
        out_specs=pl.BlockSpec((rows * 5 * panels, width), lambda i: (i, 0)),
        out_shape=jax.ShapeDtypeStruct((width * 5 * panels, width), jnp.float32),
        compiler_params=PARAMS,
        cost_estimate=COST,
        name="assemble_coarse",
    )(*flat)
    return result.reshape(width, 5, panels, width).transpose(0, 2, 1, 3)


def per_device(fine_blocks, block_rows, block_cols, block_counts, prolong_blocks, prolong_mask):
    matrix = fine_blocks[0, 0]
    cols_list = block_cols[0, 0]
    lists = (block_rows[0, 0], cols_list, block_counts[0])
    groups = lax.axis_size("rows")
    grid = Grid(lax.axis_size("blk"), cols_list.shape[1], matrix.shape[2])
    cap, sides, columns = grid.cap, grid.sides, grid.columns
    every, inner = range(groups), range(1, groups - 1)

    def move(x, pairs, members=every):
        perm = [(a * groups + g, b * groups + g) for g in members for a, b in pairs]
        return lax.ppermute(x, ("blk", "rows"), perm) if perm else jnp.zeros_like(x)

    def move_both(pair, pairs):
        return (move(pair[0][0], pairs), 2), (move(pair[1][0], pairs, inner), 1)

    def move_across(arrays):
        return [((move(x, grid.across(shift)), 3),) for x, shift in zip(arrays, sides)]

    def exchange(parts):
        lower = lax.ppermute(parts[1], "rows", [(g, g + 1) for g in range(groups - 1)])
        upper = lax.ppermute(parts[2], "rows", [(g + 1, g) for g in range(groups - 1)])
        return parts[0], lower, upper

    head, tail = pack(grid, prolong_mask.transpose(2, 0, 1), cols_list, prolong_blocks[0])
    own = ((head, 2), (tail, 1))
    near = [move_both(own, grid.hops(1, 1)), move_both(own, grid.hops(1, -1))]
    side_lists = [move(cols_list, [(b, a) for a, b in grid.across(shift)]) for shift in sides]

    def own_requests(z, y):
        return [(index, grid.panel(z, y, 0), [(True, 0)], index, 0) for index in range(len(sides))]

    beside = move_across(pick(grid, own_requests, [cap] * len(sides), side_lists, [own]))
    turned = turn(grid, head, tail)

    second = [move_both(near[0], grid.hops(2, 1)), move_both(near[1], grid.hops(2, -1))]

    def near_requests(z, y):
        return [(index, grid.panel(z + step, y, 0), [(True, side)], index, side * cap)
                for index in range(len(sides)) for side, step in enumerate((-1, 1))]

    picked = pick(grid, near_requests, [2 * cap] * len(sides), side_lists, near, ((0, 1), (1, 0)),
                  after=[x for ((x, _),) in beside], cost=NEAR_COST)
    crossed = move_across(picked)
    parts = stage(grid, grid.work_near, lists, turned, matrix, [*near, own, *beside])

    def second_requests(z, y):
        line, below, above = grid.second(z)
        return [(index, grid.panel(line, y, 0), [(below, 0), (above, 1)], index, 0) for index in range(columns)]

    def far_requests(z, y):
        line, below, above = grid.second(z)
        return [(index, grid.panel(line, y, 0), [(below, 0), (above, 1)], index, 0) for index in range(len(sides))]

    def low(z):
        return z == 1

    picked = pick(grid, second_requests, [cap] * columns, side_lists, [*second, *near],
                  tables=(((None, 3, 0), (low, 2, 0)),), after=[parts[0]], cost=PICK_COST)
    second_crossed = move_across(picked[:-1])
    far = [((move(picked[-1], grid.ends(0)), 3),)]
    tables = tuple(((None, 2 + columns - 1 - shift, 0), (low, 2 + columns - 1 - shift, 1)) for shift in sides)
    picked = pick(grid, far_requests, [cap] * len(sides), [], [*second, *crossed], tables=tables)
    far += [((move(x, grid.ends(shift)), 3),) for shift, x in zip(sides, picked)]
    parts = stage(grid, grid.work_second, lists, turned, matrix, [*second, *crossed], parts)
    first = exchange(parts)
    parts = stage(grid, grid.work_crossed, lists, turned, matrix, second_crossed, (), [parts[0]])

    parts = stage(grid, grid.work_far, lists, turned, matrix, far, parts, first[1:])
    last = exchange(parts)
    plans = ((grid.work_near, grid.work_second), (grid.work_crossed, grid.work_far))
    return assemble(grid, plans, [first, last])[None, None]


def solution(mesh):
    in_specs = (
        P("rows", "blk", None, None, None, None),
        P("rows", "blk", None, None),
        P("rows", "blk", None, None),
        P("rows", "blk", None),
        P("rows", "blk", None, None),
        P("rows", "blk", None),
    )
    out_specs = P("rows", "blk", None, None, None, None)
    return jax.shard_map(
        per_device, mesh=mesh, in_specs=in_specs, out_specs=out_specs, check_vma=False
    )
```

```python
import functools
import jax
import jax.numpy as jnp
from jax import lax
from jax.experimental import pallas as pl
from jax.experimental.pallas import tpu as pltpu
from jax.sharding import PartitionSpec as P

VMEM_LIMIT = 24 * 1024 * 1024
PARAMS = pltpu.CompilerParams(vmem_limit_bytes=VMEM_LIMIT)
COST = pl.CostEstimate(flops=1024, bytes_accessed=1024, transcendentals=0)
NEAR_COST = pl.CostEstimate(flops=6 * 10 ** 9, bytes_accessed=1024, transcendentals=0)
PICK_COST = pl.CostEstimate(flops=2 * 10 ** 10, bytes_accessed=1024, transcendentals=0)
ANYWHERE = pl.BlockSpec(memory_space=pl.ANY)


def resident(x):
    return pl.BlockSpec(x.shape, lambda i, *_, n=len(x.shape): (0,) * n)


LINES = 4


class Grid:
    def __init__(self, panels, cap, pores):
        self.panels, self.cap, self.pores = panels, cap, pores
        self.columns = panels // LINES
        self.sides = range(1, self.columns)
        self.list_rows = -(-panels // 16) * 16

    def spot(self):
        place = lax.axis_index("blk")
        return place // self.columns, place % self.columns

    def has(self, z, s, sign):
        return (z + sign * s >= 0) & (z + sign * s < LINES)

    def panel(self, line, y, shift):
        column = y - shift
        return jnp.clip(line, 0, LINES - 1) * self.columns + jnp.where(column < 0, column + self.columns, column)

    def second(self, z):
        below = self.has(z, 2, -1)
        return jnp.where(below, z - 2, z + 2), below, self.has(z, 2, 1)

    def hops(self, s, sign):
        return [(h * self.columns + c, (h + sign) * self.columns + c)
                for h in range(LINES) for c in range(self.columns)
                if 0 <= h + sign < LINES and 0 <= h + sign - sign * s < LINES]

    def across(self, shift, lines=range(LINES)):
        return [(h * self.columns + c, h * self.columns + (c + shift) % self.columns)
                for h in lines for c in range(self.columns)]

    def ends(self, shift):
        return [(h * self.columns + c, end * self.columns + (c + shift) % self.columns)
                for h, end in ((1, 0), (LINES - 2, LINES - 1)) for c in range(self.columns)]

    def part(self, ref, blocks, row, block):
        start = (row * blocks + block) * self.pores
        if not isinstance(start, int):
            start = pl.multiple_of(start, self.pores)
        return ref.at[pl.ds(start, self.pores), :]

    def shape(self, rows, blocks, width, lists=0):
        return jax.ShapeDtypeStruct((rows * blocks * self.pores + lists * self.list_rows, width), jnp.bfloat16)


    def work_near(self, z, y):
        below, above = self.has(z, 1, -1), self.has(z, 1, 1)
        work = [(self.panel(z, y, 0), True, [(2, 0, True, True)]),
                (self.panel(z - 1, y, 0), below, [(0, 0, True, below)]),
                (self.panel(z + 1, y, 0), above, [(1, 0, True, above)])]
        return work + [(self.panel(z, y, shift), True, [(3 + i, 0, False, True)]) for i, shift in enumerate(self.sides)]

    def paired(self, z):
        odd = z % 2 == 1
        return jnp.where(odd, z - 1, z + 1), jnp.where(odd, z + 1, z - 1), odd

    def work_second(self, z, y):
        line, below, above = self.second(z)
        work = [(self.panel(line, y, 0), below | above, [(0, 0, True, below), (1, 0, True, above)])]
        first, other, _ = self.paired(z)
        middle = (z == 1) | (z == LINES - 2)
        for i, shift in enumerate(self.sides):
            work += [(self.panel(first, y, shift), True, [(2 + 2 * i, 0, False, True)]),
                     (self.panel(other, y, shift), middle, [(3 + 2 * i, 0, False, middle)])]
        return work

    def work_crossed(self, z, y):
        line, below, above = self.second(z)
        return [(self.panel(line, y, shift), below | above, [(i, 0, False, below | above)])
                for i, shift in enumerate(self.sides)]

    def work_far(self, z, y):
        there = (z == 0) | (z == LINES - 1)
        return [(self.panel(LINES - 1 - z, y, shift), there, [(shift, 0, False, there)])
                for shift in range(self.columns)]


def pack_kernel(grid, mask, cols, prolong, head, tail):
    group, groups = lax.axis_index("rows"), lax.axis_size("rows")
    width = tail.shape[-1]
    for i in range(prolong.shape[0]):
        blocks = []
        for e in range(3):
            candidate = group + e - 1
            keep = (mask[e, 0, i] == 1) & (candidate >= 0) & (candidate < groups)
            block = prolong[i, :, e * width:(e + 1) * width]
            blocks.append(block * jnp.where(keep, 1.0, 0.0).astype(block.dtype))
        grid.part(head, 2, i, 0)[...] = jnp.where(group == 0, blocks[1], blocks[0])
        grid.part(head, 2, i, 1)[...] = jnp.where(group == 0, blocks[2], blocks[1])
        grid.part(tail, 1, i, 0)[...] = jnp.where(group == 0, blocks[0], blocks[2])
    row = lax.broadcasted_iota(jnp.int32, (grid.list_rows, width), 0)
    column = lax.broadcasted_iota(jnp.int32, (grid.list_rows, width), 1)
    numbers = jnp.zeros((grid.list_rows, width), jnp.int32)
    for panel in range(grid.panels):
        for entry in range(grid.cap):
            numbers = jnp.where((row == panel) & (column == entry), cols[panel, entry], numbers)
    start = prolong.shape[0] * 2 * grid.pores
    head[start:start + grid.list_rows, :] = numbers.astype(jnp.float32).astype(head.dtype)


def pack(grid, mask, cols, prolong):
    rows, _, width3 = prolong.shape
    outs = [grid.shape(rows, 2, width3 // 3, 1), grid.shape(rows, 1, width3 // 3)]
    return pl.pallas_call(
        functools.partial(pack_kernel, grid),
        grid_spec=pltpu.PrefetchScalarGridSpec(
            num_scalar_prefetch=2,
            grid=(1,),
            in_specs=[resident(prolong)],
            out_specs=[*map(resident, outs)],
        ),
        out_shape=outs,
        compiler_params=PARAMS,
        cost_estimate=COST,
        name="pack_rows",
    )(mask, cols, prolong)


def turn_kernel(grid, head, tail, turned):
    width = head.shape[-1]
    for i in range(turned.shape[0]):
        parts = (grid.part(head, 2, i, 0), grid.part(head, 2, i, 1), grid.part(tail, 1, i, 0))
        for k, part in enumerate(parts):
            turned[i, k * width:(k + 1) * width, :] = part[...].T


def turn(grid, head, tail):
    rows, width = tail.shape[0] // grid.pores, tail.shape[1]
    out = jax.ShapeDtypeStruct((rows, 3 * width, grid.pores), head.dtype)
    return pl.pallas_call(
        functools.partial(turn_kernel, grid),
        grid=(1,),
        in_specs=[resident(head), resident(tail)],
        out_specs=resident(out),
        out_shape=out,
        compiler_params=PARAMS,
        cost_estimate=COST,
        name="turn_rows",
    )(head, tail)


def pick_kernel(grid, plan, layout, carry, tables, lists, outputs, *refs):
    wanted = list(refs[:lists])
    sources, at = [], lists
    for blocks in layout:
        sources.append([(refs[at + i], k) for i, k in enumerate(blocks)])
        at += len(blocks)
    scratch = 2 * len(tables) + 1 if tables else 0
    outs = refs[len(refs) - outputs - scratch:len(refs) - scratch]
    z, y = grid.spot()

    def list_at(options):
        value = None
        for present, source in options:
            ref = sources[source][0][0]
            here = ref[ref.shape[0] - grid.list_rows:, :].astype(jnp.float32)
            value = here if value is None else jnp.where(present(z), here, value)
        return value

    if tables:
        numbers, plain, done = refs[-scratch:-1 - len(tables)], refs[-1 - len(tables):-1], refs[-1]
        for table, options in enumerate(tables):
            numbers[table][...] = list_at(options).astype(jnp.int32)
            pltpu.make_async_copy(numbers[table], plain[table], done.at[table]).start()
        for table in range(len(tables)):
            pltpu.make_async_copy(numbers[table], plain[table], done.at[table]).wait()
        wanted += plain
    for index, list_row, options, output, base in plan(z, y):
        for present, source in options:
            def copy(index=index, list_row=list_row, source=source, output=output, base=base):
                for entry in range(grid.cap):
                    row = wanted[index][list_row, entry]
                    place = 0
                    for ref, blocks in sources[source]:
                        for block in range(blocks):
                            grid.part(outs[output], 3, base + entry, place)[...] = grid.part(ref, blocks, row, block)[...]
                            place += 1
            if present is True:
                copy()
            else:
                pl.when(present)(copy)
    for out, options in zip(outs, carry):
        if options:
            out[out.shape[0] - grid.list_rows:, :] = list_at(options).astype(out.dtype)


def pick(grid, plan, sizes, lists, sources, carry=(), tables=(), after=(), cost=COST):
    flat = [x for source in sources for x, _ in source]
    width = flat[0].shape[-1]
    carry = carry or ((),) * len(sizes)
    shapes = [grid.shape(size, 3, width, 1 if options else 0) for size, options in zip(sizes, carry)]
    layout = tuple(tuple(blocks for _, blocks in source) for source in sources)
    table = (grid.list_rows, width)
    scratch = [pltpu.VMEM(table, jnp.int32)] * len(tables) + [pltpu.SMEM(table, jnp.int32)] * len(tables)
    scratch += [pltpu.SemaphoreType.DMA((len(tables),))] if tables else []
    return pl.pallas_call(
        functools.partial(pick_kernel, grid, plan, layout, carry, tables, len(lists), len(sizes)),
        grid_spec=pltpu.PrefetchScalarGridSpec(
            num_scalar_prefetch=len(lists),
            grid=(1,),
            in_specs=[*map(resident, flat), *([ANYWHERE] * len(after))],
            out_specs=[*map(resident, shapes)],
            scratch_shapes=scratch,
        ),
        out_shape=shapes,
        compiler_params=PARAMS,
        cost_estimate=cost,
        name="pick_rows",
    )(*lists, *flat, *after)


def stage_kernel(grid, plan, layout, carried, slot_rows, slot_cols, slot_counts, turned, matrix, *refs):
    arrays, at = [], 0
    for blocks in layout:
        arrays.append([(refs[at + i], k) for i, k in enumerate(blocks)])
        at += len(blocks)
    earlier = refs[at:at + 3] if carried else ()
    own, up, down, total = refs[-4:]
    width = own.shape[-1]
    first_group = lax.axis_index("rows") == 0
    for old, new in zip(earlier, (own, up, down)):
        for slot in range(carried):
            for f in range(3):
                new[slot, f] = old[slot, f]
    z, y = grid.spot()
    for slot, (panel, _, sources) in enumerate(plan(z, y), start=carried):
        total[...] = jnp.zeros_like(total)
        for array, base, whole, present in sources:
            live = slot_counts[0, panel]
            if present is not True:
                live = jnp.where(present, live, 0)
            parts = arrays[array]

            def product(entry, whole=whole, base=base, parts=parts, panel=panel):
                pick = slot_cols[panel, entry] if whole else base + entry
                right = jnp.concatenate(
                    [grid.part(x, blocks, pick, block)[...] for x, blocks in parts for block in range(blocks)], axis=1)
                return jnp.dot(matrix[panel, entry], right, preferred_element_type=jnp.float32)

            def add(left, value):
                result = jnp.dot(left, value, preferred_element_type=jnp.float32)
                for k in range(3):
                    total[k] += result[:, k * width:(k + 1) * width]

            def two(u, carry, product=product, panel=panel):
                first, second = 2 * u, 2 * u + 1
                left = jnp.concatenate(
                    [turned[slot_rows[panel, first]], turned[slot_rows[panel, second]]], axis=1)
                value = jnp.concatenate([product(first), product(second)], axis=0).astype(jnp.bfloat16)
                add(left, value)
                return carry

            lax.fori_loop(0, live // 2, two, 0)

            @pl.when(live % 2 == 1)
            def _(live=live, product=product, panel=panel):
                add(turned[slot_rows[panel, live - 1]], product(live - 1).astype(jnp.bfloat16))

        begin = jnp.where(first_group, 0, width)
        for f in range(3):
            k = jnp.where(first_group, (f + 2) % 3, f)
            own[slot, f] = total[k, pl.ds(pl.multiple_of(begin, width), width), :].astype(own.dtype)
            up[slot, f] = total[k, pl.ds(pl.multiple_of(begin + width, width), width), :].astype(up.dtype)
            down[slot, f] = total[k, 0:width, :].astype(down.dtype)


def stage(grid, plan, lists, turned, matrix, sources, earlier=(), after=()):
    width = turned.shape[1] // 3
    carried = earlier[0].shape[0] if earlier else 0
    slots = carried + len(plan(jnp.int32(0), jnp.int32(0)))
    flat = [x for source in sources for x, _ in source]
    layout = tuple(tuple(blocks for _, blocks in source) for source in sources)
    out = jax.ShapeDtypeStruct((slots, 3, width, width), jnp.bfloat16)
    return pl.pallas_call(
        functools.partial(stage_kernel, grid, plan, layout, carried),
        grid_spec=pltpu.PrefetchScalarGridSpec(
            num_scalar_prefetch=3,
            grid=(1,),
            in_specs=[*map(resident, (turned, matrix, *flat, *earlier)), *([ANYWHERE] * len(after))],
            out_specs=[resident(out)] * 3,
            scratch_shapes=[pltpu.VMEM((3, 3 * width, width), jnp.float32)],
        ),
        out_shape=[out] * 3,
        compiler_params=PARAMS,
        cost_estimate=COST,
        name="stage_products",
    )(*lists, turned, matrix, *flat, *earlier, *after)


def assemble_kernel(grid, plans, *refs):
    out = refs[-1]
    rows = refs[0].shape[2]
    panels = grid.panels
    z, y = grid.spot()
    for index, group in enumerate(plans):
        own, lower, upper = refs[3 * index:3 * index + 3]
        slots = [slot for plan in group for slot in plan(z, y)]
        for slot, (panel, present, _) in enumerate(slots):
            def write(slot=slot, own=own, lower=lower, upper=upper, panel=panel):
                for d in range(5):
                    terms = []
                    if 0 <= d - 1 < 3:
                        terms.append(own[slot, d - 1].astype(jnp.float32))
                    if d < 3:
                        terms.append(lower[slot, d].astype(jnp.float32))
                    if 0 <= d - 2 < 3:
                        terms.append(upper[slot, d - 2].astype(jnp.float32))
                    out[pl.ds(d * panels + panel, rows, stride=5 * panels), :] = functools.reduce(jnp.add, terms)
            if present is True:
                write()
            else:
                pl.when(present)(write)


def assemble(grid, plans, pieces):
    panels = grid.panels
    width = pieces[0][0].shape[-1]
    rows = width // 4
    flat = [x for piece in pieces for x in piece]
    result = pl.pallas_call(
        functools.partial(assemble_kernel, grid, plans),
        grid=(width // rows,),
        in_specs=[pl.BlockSpec((x.shape[0], 3, rows, width), lambda i: (0, 0, i, 0)) for x in flat],
        out_specs=pl.BlockSpec((rows * 5 * panels, width), lambda i: (i, 0)),
        out_shape=jax.ShapeDtypeStruct((width * 5 * panels, width), jnp.float32),
        compiler_params=PARAMS,
        cost_estimate=COST,
        name="assemble_coarse",
    )(*flat)
    return result.reshape(width, 5, panels, width).transpose(0, 2, 1, 3)


def per_device(fine_blocks, block_rows, block_cols, block_counts, prolong_blocks, prolong_mask):
    matrix = fine_blocks[0, 0]
    cols_list = block_cols[0, 0]
    lists = (block_rows[0, 0], cols_list, block_counts[0])
    groups = lax.axis_size("rows")
    grid = Grid(lax.axis_size("blk"), cols_list.shape[1], matrix.shape[2])
    cap, sides, columns = grid.cap, grid.sides, grid.columns
    every, inner = range(groups), range(1, groups - 1)

    def move(x, pairs, members=every):
        perm = [(a * groups + g, b * groups + g) for g in members for a, b in pairs]
        return lax.ppermute(x, ("blk", "rows"), perm) if perm else jnp.zeros_like(x)

    def move_both(pair, pairs):
        return (move(pair[0][0], pairs), 2), (move(pair[1][0], pairs, inner), 1)

    def move_across(arrays, lines=range(LINES)):
        return [((move(x, grid.across(shift, lines)), 3),) for x, shift in zip(arrays, sides)]

    def exchange(parts):
        lower = lax.ppermute(parts[1], "rows", [(g, g + 1) for g in range(groups - 1)])
        upper = lax.ppermute(parts[2], "rows", [(g + 1, g) for g in range(groups - 1)])
        return parts[0], lower, upper

    head, tail = pack(grid, prolong_mask.transpose(2, 0, 1), cols_list, prolong_blocks[0])
    own = ((head, 2), (tail, 1))
    near = [move_both(own, grid.hops(1, 1)), move_both(own, grid.hops(1, -1))]
    side_lists = [move(cols_list, [(b, a) for a, b in grid.across(shift)]) for shift in sides]

    def own_requests(z, y):
        return [(index, grid.panel(z, y, 0), [(True, 0)], index, 0) for index in range(len(sides))]

    beside = move_across(pick(grid, own_requests, [cap] * len(sides), side_lists, [own]))
    turned = turn(grid, head, tail)

    second = [move_both(near[0], grid.hops(2, 1)), move_both(near[1], grid.hops(2, -1))]

    def near_requests(z, y):
        first, other, odd = grid.paired(z)
        requests = []
        for index in range(len(sides)):
            requests += [
                (index, grid.panel(first, y, 0), [(odd, 0), (jnp.logical_not(odd), 1)], 2 * index, 0),
                (index, grid.panel(other, y, 0), [(z == 1, 1), (z == LINES - 2, 0)], 2 * index + 1, 0)]
        return requests

    def is_odd(z):
        return z % 2 == 1

    paired = ((None, 1), (is_odd, 0))
    picked = pick(grid, near_requests, [cap] * (2 * len(sides)), side_lists, near, (paired, ()) * len(sides),
                  after=[x for ((x, _),) in beside], cost=NEAR_COST)
    crossed, middle = move_across(picked[::2]), move_across(picked[1::2], (1, LINES - 2))
    parts = stage(grid, grid.work_near, lists, turned, matrix, [*near, own, *beside])

    def second_requests(z, y):
        line, below, above = grid.second(z)
        return [(index, grid.panel(line, y, 0), [(below, 0), (above, 1)], index, 0)
                for index in range(len(sides) + columns)]

    tables = [((None, 3), (is_odd, 2))] + [((None, 4 + columns - 1 - shift),) for shift in sides]
    picked = pick(grid, second_requests, [cap] * (len(sides) + columns), side_lists, [*second, *near, *crossed],
                  tables=tuple(tables), after=[parts[0]], cost=PICK_COST)
    second_crossed = move_across(picked)
    far = [((move(x, grid.ends(shift)), 3),) for shift, x in enumerate(picked[len(sides):])]
    both = [x for pair in zip(crossed, middle) for x in pair]
    parts = stage(grid, grid.work_second, lists, turned, matrix, [*second, *both], parts)
    first = exchange(parts)
    parts = stage(grid, grid.work_crossed, lists, turned, matrix, second_crossed, (), [parts[0]])

    parts = stage(grid, grid.work_far, lists, turned, matrix, far, parts, first[1:])
    last = exchange(parts)
    plans = ((grid.work_near, grid.work_second), (grid.work_crossed, grid.work_far))
    return assemble(grid, plans, [first, last])[None, None]


def solution(mesh):
    in_specs = (
        P("rows", "blk", None, None, None, None),
        P("rows", "blk", None, None),
        P("rows", "blk", None, None),
        P("rows", "blk", None),
        P("rows", "blk", None, None),
        P("rows", "blk", None),
    )
    out_specs = P("rows", "blk", None, None, None, None)
    return jax.shard_map(
        per_device, mesh=mesh, in_specs=in_specs, out_specs=out_specs, check_vma=False
    )
```

```python
import functools
import jax
import jax.numpy as jnp
from jax import lax
from jax.experimental import pallas as pl
from jax.experimental.pallas import tpu as pltpu
from jax.sharding import PartitionSpec as P

VMEM_LIMIT = 24 * 1024 * 1024
PARAMS = pltpu.CompilerParams(vmem_limit_bytes=VMEM_LIMIT)
COST = pl.CostEstimate(flops=1024, bytes_accessed=1024, transcendentals=0)
EARLY_COST = pl.CostEstimate(flops=1024, bytes_accessed=1024, transcendentals=0)
NEAR_COST = pl.CostEstimate(flops=6 * 10 ** 9, bytes_accessed=1024, transcendentals=0)
PICK_COST = pl.CostEstimate(flops=2 * 10 ** 10, bytes_accessed=1024, transcendentals=0)
ANYWHERE = pl.BlockSpec(memory_space=pl.ANY)


def resident(x):
    return pl.BlockSpec(x.shape, lambda i, *_, n=len(x.shape): (0,) * n)


LINES = 4


class Grid:
    def __init__(self, panels, cap, pores):
        self.panels, self.cap, self.pores = panels, cap, pores
        self.columns = panels // LINES
        self.sides = range(1, self.columns)
        self.list_rows = -(-panels // 16) * 16

    def spot(self):
        place = lax.axis_index("blk")
        return place // self.columns, place % self.columns

    def has(self, z, s, sign):
        return (z + sign * s >= 0) & (z + sign * s < LINES)

    def panel(self, line, y, shift):
        column = y - shift
        return jnp.clip(line, 0, LINES - 1) * self.columns + jnp.where(column < 0, column + self.columns, column)

    def second(self, z):
        below = self.has(z, 2, -1)
        return jnp.where(below, z - 2, z + 2), below, self.has(z, 2, 1)

    def hops(self, s, sign):
        return [(h * self.columns + c, (h + sign) * self.columns + c)
                for h in range(LINES) for c in range(self.columns)
                if 0 <= h + sign < LINES and 0 <= h + sign - sign * s < LINES]

    def across(self, shift, lines=range(LINES)):
        return [(h * self.columns + c, h * self.columns + (c + shift) % self.columns)
                for h in lines for c in range(self.columns)]

    def ends(self, shift):
        return [(h * self.columns + c, end * self.columns + (c + shift) % self.columns)
                for h, end in ((1, 0), (LINES - 2, LINES - 1)) for c in range(self.columns)]

    def part(self, ref, blocks, row, block):
        start = (row * blocks + block) * self.pores
        if not isinstance(start, int):
            start = pl.multiple_of(start, self.pores)
        return ref.at[pl.ds(start, self.pores), :]

    def shape(self, rows, blocks, width, lists=0):
        return jax.ShapeDtypeStruct((rows * blocks * self.pores + lists * self.list_rows, width), jnp.bfloat16)


    def work_near(self, z, y):
        below, above = self.has(z, 1, -1), self.has(z, 1, 1)
        work = [(self.panel(z, y, 0), True, [(2, 0, True, True)]),
                (self.panel(z - 1, y, 0), below, [(0, 0, True, below)]),
                (self.panel(z + 1, y, 0), above, [(1, 0, True, above)])]
        return work + [(self.panel(z, y, shift), True, [(3 + i, 0, False, True)]) for i, shift in enumerate(self.sides)]

    def paired(self, z):
        odd = z % 2 == 1
        return jnp.where(odd, z - 1, z + 1), jnp.where(odd, z + 1, z - 1), odd

    def work_second(self, z, y):
        line, below, above = self.second(z)
        work = [(self.panel(line, y, 0), below | above, [(0, 0, True, below), (1, 0, True, above)])]
        first, other, _ = self.paired(z)
        middle = (z == 1) | (z == LINES - 2)
        for i, shift in enumerate(self.sides):
            work += [(self.panel(first, y, shift), True, [(2 + 2 * i, 0, False, True)]),
                     (self.panel(other, y, shift), middle, [(3 + 2 * i, 0, False, middle)])]
        return work

    def work_crossed(self, z, y):
        line, below, above = self.second(z)
        return [(self.panel(line, y, shift), below | above, [(i, 0, False, below | above)])
                for i, shift in enumerate(self.sides)]

    def work_far(self, z, y):
        there = (z == 0) | (z == LINES - 1)
        return [(self.panel(LINES - 1 - z, y, shift), there, [(shift, 0, False, there)])
                for shift in range(self.columns)]


def pack_kernel(grid, mask, cols, prolong, head, tail):
    group, groups = lax.axis_index("rows"), lax.axis_size("rows")
    width = tail.shape[-1]
    for i in range(prolong.shape[0]):
        blocks = []
        for e in range(3):
            candidate = group + e - 1
            keep = (mask[e, 0, i] == 1) & (candidate >= 0) & (candidate < groups)
            block = prolong[i, :, e * width:(e + 1) * width]
            blocks.append(block * jnp.where(keep, 1.0, 0.0).astype(block.dtype))
        grid.part(head, 2, i, 0)[...] = jnp.where(group == 0, blocks[1], blocks[0])
        grid.part(head, 2, i, 1)[...] = jnp.where(group == 0, blocks[2], blocks[1])
        grid.part(tail, 1, i, 0)[...] = jnp.where(group == 0, blocks[0], blocks[2])
    row = lax.broadcasted_iota(jnp.int32, (grid.list_rows, width), 0)
    column = lax.broadcasted_iota(jnp.int32, (grid.list_rows, width), 1)
    numbers = jnp.zeros((grid.list_rows, width), jnp.int32)
    for panel in range(grid.panels):
        for entry in range(grid.cap):
            numbers = jnp.where((row == panel) & (column == entry), cols[panel, entry], numbers)
    start = prolong.shape[0] * 2 * grid.pores
    head[start:start + grid.list_rows, :] = numbers.astype(jnp.float32).astype(head.dtype)


def pack(grid, mask, cols, prolong):
    rows, _, width3 = prolong.shape
    outs = [grid.shape(rows, 2, width3 // 3, 1), grid.shape(rows, 1, width3 // 3)]
    return pl.pallas_call(
        functools.partial(pack_kernel, grid),
        grid_spec=pltpu.PrefetchScalarGridSpec(
            num_scalar_prefetch=2,
            grid=(1,),
            in_specs=[resident(prolong)],
            out_specs=[*map(resident, outs)],
        ),
        out_shape=outs,
        compiler_params=PARAMS,
        cost_estimate=COST,
        name="pack_rows",
    )(mask, cols, prolong)


def turn_kernel(grid, head, tail, turned):
    width = head.shape[-1]
    for i in range(turned.shape[0]):
        parts = (grid.part(head, 2, i, 0), grid.part(head, 2, i, 1), grid.part(tail, 1, i, 0))
        for k, part in enumerate(parts):
            turned[i, k * width:(k + 1) * width, :] = part[...].T


def turn(grid, head, tail):
    rows, width = tail.shape[0] // grid.pores, tail.shape[1]
    out = jax.ShapeDtypeStruct((rows, 3 * width, grid.pores), head.dtype)
    return pl.pallas_call(
        functools.partial(turn_kernel, grid),
        grid=(1,),
        in_specs=[resident(head), resident(tail)],
        out_specs=resident(out),
        out_shape=out,
        compiler_params=PARAMS,
        cost_estimate=COST,
        name="turn_rows",
    )(head, tail)


def pick_kernel(grid, plan, layout, carry, tables, lists, filled, *refs):
    wanted = list(refs[:lists])
    sources, at = [], lists
    for blocks in layout:
        sources.append([(refs[at + i], k) for i, k in enumerate(blocks)])
        at += len(blocks)
    scratch = 2 * len(tables) + 1 if tables else 0
    outs = refs[len(refs) - len(filled) - scratch:len(refs) - scratch]
    z, y = grid.spot()

    def list_at(options):
        value = None
        for present, source in options:
            ref = sources[source][0][0]
            here = ref[ref.shape[0] - grid.list_rows:, :].astype(jnp.float32)
            value = here if value is None else jnp.where(present(z), here, value)
        return value

    if tables:
        numbers, plain, done = refs[-scratch:-1 - len(tables)], refs[-1 - len(tables):-1], refs[-1]
        for table, options in enumerate(tables):
            numbers[table][...] = list_at(options).astype(jnp.int32)
            pltpu.make_async_copy(numbers[table], plain[table], done.at[table]).start()
        for table in range(len(tables)):
            pltpu.make_async_copy(numbers[table], plain[table], done.at[table]).wait()
        wanted += plain
    for index, list_row, options, output in plan(z, y):
        for present, source in options:
            def copy(index=index, list_row=list_row, source=source, output=output):
                for entry in range(grid.cap):
                    row = wanted[index][list_row, entry]
                    place = 0
                    for ref, blocks in sources[source]:
                        for block in range(blocks):
                            target = grid.part(outs[output], filled[output], entry, place)
                            target[...] = grid.part(ref, blocks, row, block)[...]
                            place += 1
            if present is True:
                copy()
            else:
                pl.when(present)(copy)
    for out, options in zip(outs, carry):
        if options:
            out[out.shape[0] - grid.list_rows:, :] = list_at(options).astype(out.dtype)


def pick(grid, plan, filled, lists, sources, carry=(), tables=(), after=(), cost=COST):
    flat = [x for source in sources for x, _ in source]
    width = flat[0].shape[-1]
    carry = carry or ((),) * len(filled)
    shapes = [grid.shape(grid.cap, blocks, width, 1 if options else 0) for blocks, options in zip(filled, carry)]
    layout = tuple(tuple(blocks for _, blocks in source) for source in sources)
    table = (grid.list_rows, width)
    scratch = [pltpu.VMEM(table, jnp.int32)] * len(tables) + [pltpu.SMEM(table, jnp.int32)] * len(tables)
    scratch += [pltpu.SemaphoreType.DMA((len(tables),))] if tables else []
    return pl.pallas_call(
        functools.partial(pick_kernel, grid, plan, layout, carry, tables, len(lists), tuple(filled)),
        grid_spec=pltpu.PrefetchScalarGridSpec(
            num_scalar_prefetch=len(lists),
            grid=(1,),
            in_specs=[*map(resident, flat), *([ANYWHERE] * len(after))],
            out_specs=[*map(resident, shapes)],
            scratch_shapes=scratch,
        ),
        out_shape=shapes,
        compiler_params=PARAMS,
        cost_estimate=cost,
        name="pick_rows",
    )(*lists, *flat, *after)


def stage_kernel(grid, plan, layout, carried, slot_rows, slot_cols, slot_counts, turned, matrix, *refs):
    arrays, at = [], 0
    for blocks in layout:
        arrays.append([(refs[at + i], k) for i, k in enumerate(blocks)])
        at += len(blocks)
    earlier = refs[at:at + 3] if carried else ()
    own, up, down, total = refs[-4:]
    width = own.shape[-1]
    first_group = lax.axis_index("rows") == 0
    for old, new in zip(earlier, (own, up, down)):
        for slot in range(carried):
            for f in range(3):
                new[slot, f] = old[slot, f]
    z, y = grid.spot()
    for slot, (panel, _, sources) in enumerate(plan(z, y), start=carried):
        total[...] = jnp.zeros_like(total)
        for array, base, whole, present in sources:
            live = slot_counts[0, panel]
            if present is not True:
                live = jnp.where(present, live, 0)
            parts = arrays[array]

            def product(entry, whole=whole, base=base, parts=parts, panel=panel):
                pick = slot_cols[panel, entry] if whole else base + entry
                right = jnp.concatenate(
                    [grid.part(x, blocks, pick, block)[...] for x, blocks in parts for block in range(blocks)], axis=1)
                return jnp.dot(matrix[panel, entry], right, preferred_element_type=jnp.float32)

            def add(left, value):
                result = jnp.dot(left, value, preferred_element_type=jnp.float32)
                for k in range(3):
                    total[k] += result[:, k * width:(k + 1) * width]

            def two(u, carry, product=product, panel=panel):
                first, second = 2 * u, 2 * u + 1
                left = jnp.concatenate(
                    [turned[slot_rows[panel, first]], turned[slot_rows[panel, second]]], axis=1)
                value = jnp.concatenate([product(first), product(second)], axis=0).astype(jnp.bfloat16)
                add(left, value)
                return carry

            lax.fori_loop(0, live // 2, two, 0)

            @pl.when(live % 2 == 1)
            def _(live=live, product=product, panel=panel):
                add(turned[slot_rows[panel, live - 1]], product(live - 1).astype(jnp.bfloat16))

        begin = jnp.where(first_group, 0, width)
        for f in range(3):
            k = jnp.where(first_group, (f + 2) % 3, f)
            own[slot, f] = total[k, pl.ds(pl.multiple_of(begin, width), width), :].astype(own.dtype)
            up[slot, f] = total[k, pl.ds(pl.multiple_of(begin + width, width), width), :].astype(up.dtype)
            down[slot, f] = total[k, 0:width, :].astype(down.dtype)


def stage(grid, plan, lists, turned, matrix, sources, earlier=(), after=()):
    width = turned.shape[1] // 3
    carried = earlier[0].shape[0] if earlier else 0
    slots = carried + len(plan(jnp.int32(0), jnp.int32(0)))
    flat = [x for source in sources for x, _ in source]
    layout = tuple(tuple(blocks for _, blocks in source) for source in sources)
    out = jax.ShapeDtypeStruct((slots, 3, width, width), jnp.bfloat16)
    return pl.pallas_call(
        functools.partial(stage_kernel, grid, plan, layout, carried),
        grid_spec=pltpu.PrefetchScalarGridSpec(
            num_scalar_prefetch=3,
            grid=(1,),
            in_specs=[*map(resident, (turned, matrix, *flat, *earlier)), *([ANYWHERE] * len(after))],
            out_specs=[resident(out)] * 3,
            scratch_shapes=[pltpu.VMEM((3, 3 * width, width), jnp.float32)],
        ),
        out_shape=[out] * 3,
        compiler_params=PARAMS,
        cost_estimate=COST,
        name="stage_products",
    )(*lists, turned, matrix, *flat, *earlier, *after)


def assemble_kernel(grid, plans, *refs):
    out = refs[-1]
    rows = refs[0].shape[2]
    panels = grid.panels
    z, y = grid.spot()
    for index, group in enumerate(plans):
        own, lower, upper = refs[3 * index:3 * index + 3]
        slots = [slot for plan in group for slot in plan(z, y)]
        for slot, (panel, present, _) in enumerate(slots):
            def write(slot=slot, own=own, lower=lower, upper=upper, panel=panel):
                for d in range(5):
                    terms = []
                    if 0 <= d - 1 < 3:
                        terms.append(own[slot, d - 1].astype(jnp.float32))
                    if d < 3:
                        terms.append(lower[slot, d].astype(jnp.float32))
                    if 0 <= d - 2 < 3:
                        terms.append(upper[slot, d - 2].astype(jnp.float32))
                    out[pl.ds(d * panels + panel, rows, stride=5 * panels), :] = functools.reduce(jnp.add, terms)
            if present is True:
                write()
            else:
                pl.when(present)(write)


def assemble(grid, plans, pieces):
    panels = grid.panels
    width = pieces[0][0].shape[-1]
    rows = width // 4
    flat = [x for piece in pieces for x in piece]
    result = pl.pallas_call(
        functools.partial(assemble_kernel, grid, plans),
        grid=(width // rows,),
        in_specs=[pl.BlockSpec((x.shape[0], 3, rows, width), lambda i: (0, 0, i, 0)) for x in flat],
        out_specs=pl.BlockSpec((rows * 5 * panels, width), lambda i: (i, 0)),
        out_shape=jax.ShapeDtypeStruct((width * 5 * panels, width), jnp.float32),
        compiler_params=PARAMS,
        cost_estimate=COST,
        name="assemble_coarse",
    )(*flat)
    return result.reshape(width, 5, panels, width).transpose(0, 2, 1, 3)


def per_device(fine_blocks, block_rows, block_cols, block_counts, prolong_blocks, prolong_mask):
    matrix = fine_blocks[0, 0]
    cols_list = block_cols[0, 0]
    lists = (block_rows[0, 0], cols_list, block_counts[0])
    groups = lax.axis_size("rows")
    grid = Grid(lax.axis_size("blk"), cols_list.shape[1], matrix.shape[2])
    cap, sides, columns = grid.cap, grid.sides, grid.columns
    every, inner = range(groups), range(1, groups - 1)

    def move(x, pairs, members=every):
        perm = [(a * groups + g, b * groups + g) for g in members for a, b in pairs]
        return lax.ppermute(x, ("blk", "rows"), perm) if perm else jnp.zeros_like(x)

    def move_both(pair, pairs):
        return (move(pair[0][0], pairs), 2), (move(pair[1][0], pairs, inner), 1)

    def move_across(arrays, lines=range(LINES)):
        return [((move(x, grid.across(shift, lines)), 3),) for x, shift in zip(arrays, sides)]

    def exchange(parts):
        lower = lax.ppermute(parts[1], "rows", [(g, g + 1) for g in range(groups - 1)])
        upper = lax.ppermute(parts[2], "rows", [(g + 1, g) for g in range(groups - 1)])
        return parts[0], lower, upper

    head, tail = pack(grid, prolong_mask.transpose(2, 0, 1), cols_list, prolong_blocks[0])
    own = ((head, 2), (tail, 1))
    near = [move_both(own, grid.hops(1, 1)), move_both(own, grid.hops(1, -1))]
    side_lists = [move(cols_list, [(b, a) for a, b in grid.across(shift)]) for shift in sides]

    def own_requests(z, y):
        return [(index, grid.panel(z, y, 0), [(True, 0)], index) for index in range(len(sides))]

    beside = move_across(pick(grid, own_requests, [3] * len(sides), side_lists, [own]))
    turned = turn(grid, head, tail)

    second = [move_both(near[0], grid.hops(2, 1)), move_both(near[1], grid.hops(2, -1))]

    def near_requests(z, y):
        first, other, odd = grid.paired(z)
        requests = []
        for index in range(len(sides)):
            requests += [
                (index, grid.panel(first, y, 0), [(odd, 0), (jnp.logical_not(odd), 1)], 2 * index),
                (index, grid.panel(other, y, 0), [(z == 1, 1), (z == LINES - 2, 0)], 2 * index + 1)]
        return requests

    def is_odd(z):
        return z % 2 == 1

    paired = ((None, 1), (is_odd, 0))
    picked = pick(grid, near_requests, [3] * (2 * len(sides)), side_lists, near, (paired, ()) * len(sides),
                  after=[x for ((x, _),) in beside], cost=NEAR_COST)
    crossed, middle = move_across(picked[::2]), move_across(picked[1::2], (1, LINES - 2))
    parts = stage(grid, grid.work_near, lists, turned, matrix, [*near, own, *beside])

    def early_requests(z, y):
        line, below, above = grid.second(z)
        return [(0, grid.panel(line, y, 0), [(below, 0), (above, 1)], 0)]

    def late_requests(z, y):
        line, below, above = grid.second(z)
        row = grid.panel(line, y, 0)
        return ([(index, row, [(below, 0), (above, 1)], index) for index in range(2 * len(sides))] +
                [(2 * len(sides), row, [(below, 2), (above, 3)], 2 * len(sides))])

    heads, tails = [(pair[0],) for pair in second], [(pair[1],) for pair in second]
    near_heads = [(pair[0],) for pair in near]
    end_list = ((None, 3), (is_odd, 2))
    early = pick(grid, early_requests, [2], [], [*heads, *near_heads], tables=(end_list,), cost=EARLY_COST)
    far_head = move(early[0], grid.ends(0))
    tables = [((None, 6 + columns - 1 - shift),) for shift in sides] + [((None, 5), (is_odd, 4))]
    picked = pick(grid, late_requests, [3] * (2 * len(sides)) + [1], side_lists,
                  [*second, *tails, *near_heads, *crossed], tables=tuple(tables), after=[parts[0]], cost=PICK_COST)
    second_crossed = move_across(picked)
    far = [((far_head, 2), (move(picked[-1], grid.ends(0), inner), 1))]
    far += [((move(x, grid.ends(shift)), 3),) for shift, x in zip(sides, picked[len(sides):])]
    both = [x for pair in zip(crossed, middle) for x in pair]
    parts = stage(grid, grid.work_second, lists, turned, matrix, [*second, *both], parts, [far_head])
    first = exchange(parts)
    parts = stage(grid, grid.work_crossed, lists, turned, matrix, second_crossed, (), [parts[0]])

    parts = stage(grid, grid.work_far, lists, turned, matrix, far, parts, first[1:])
    last = exchange(parts)
    plans = ((grid.work_near, grid.work_second), (grid.work_crossed, grid.work_far))
    return assemble(grid, plans, [first, last])[None, None]


def solution(mesh):
    in_specs = (
        P("rows", "blk", None, None, None, None),
        P("rows", "blk", None, None),
        P("rows", "blk", None, None),
        P("rows", "blk", None),
        P("rows", "blk", None, None),
        P("rows", "blk", None),
    )
    out_specs = P("rows", "blk", None, None, None, None)
    return jax.shard_map(
        per_device, mesh=mesh, in_specs=in_specs, out_specs=out_specs, check_vma=False
    )
```

```python
import functools
import jax
import jax.numpy as jnp
from jax import lax
from jax.experimental import pallas as pl
from jax.experimental.pallas import tpu as pltpu
from jax.sharding import PartitionSpec as P

VMEM_LIMIT = 24 * 1024 * 1024
PACK_VMEM_LIMIT = 60 * 1024 * 1024
PARAMS = pltpu.CompilerParams(vmem_limit_bytes=VMEM_LIMIT)
COST = pl.CostEstimate(flops=1024, bytes_accessed=1024, transcendentals=0)
EARLY_COST = pl.CostEstimate(flops=1024, bytes_accessed=1024, transcendentals=0)
NEAR_COST = pl.CostEstimate(flops=6 * 10 ** 9, bytes_accessed=1024, transcendentals=0)
PICK_COST = pl.CostEstimate(flops=2 * 10 ** 10, bytes_accessed=1024, transcendentals=0)
ANYWHERE = pl.BlockSpec(memory_space=pl.ANY)


def resident(x):
    return pl.BlockSpec(x.shape, lambda i, *_, n=len(x.shape): (0,) * n)


LINES = 4


class Grid:
    def __init__(self, panels, cap, pores):
        self.panels, self.cap, self.pores = panels, cap, pores
        self.columns = panels // LINES
        self.sides = range(1, self.columns)
        self.list_rows = -(-panels // 16) * 16

    def spot(self):
        place = lax.axis_index("blk")
        return place // self.columns, place % self.columns

    def has(self, z, s, sign):
        return (z + sign * s >= 0) & (z + sign * s < LINES)

    def panel(self, line, y, shift):
        column = y - shift
        return jnp.clip(line, 0, LINES - 1) * self.columns + jnp.where(column < 0, column + self.columns, column)

    def second(self, z):
        below = self.has(z, 2, -1)
        return jnp.where(below, z - 2, z + 2), below, self.has(z, 2, 1)

    def hops(self, s, sign):
        return [(h * self.columns + c, (h + sign) * self.columns + c)
                for h in range(LINES) for c in range(self.columns)
                if 0 <= h + sign < LINES and 0 <= h + sign - sign * s < LINES]

    def across(self, shift, lines=range(LINES)):
        return [(h * self.columns + c, h * self.columns + (c + shift) % self.columns)
                for h in lines for c in range(self.columns)]

    def ends(self, shift):
        return [(h * self.columns + c, end * self.columns + (c + shift) % self.columns)
                for h, end in ((1, 0), (LINES - 2, LINES - 1)) for c in range(self.columns)]

    def part(self, ref, blocks, row, block):
        start = (row * blocks + block) * self.pores
        if not isinstance(start, int):
            start = pl.multiple_of(start, self.pores)
        return ref.at[pl.ds(start, self.pores), :]

    def shape(self, rows, blocks, width, lists=0):
        return jax.ShapeDtypeStruct((rows * blocks * self.pores + lists * self.list_rows, width), jnp.bfloat16)


    def work_near(self, z, y):
        below, above = self.has(z, 1, -1), self.has(z, 1, 1)
        work = [(self.panel(z, y, 0), True, [(2, 0, True, True)]),
                (self.panel(z - 1, y, 0), below, [(0, 0, True, below)]),
                (self.panel(z + 1, y, 0), above, [(1, 0, True, above)])]
        return work + [(self.panel(z, y, shift), True, [(3 + i, 0, False, True)]) for i, shift in enumerate(self.sides)]

    def paired(self, z):
        odd = z % 2 == 1
        return jnp.where(odd, z - 1, z + 1), jnp.where(odd, z + 1, z - 1), odd

    def work_second(self, z, y):
        line, below, above = self.second(z)
        work = [(self.panel(line, y, 0), below | above, [(0, 0, True, below), (1, 0, True, above)])]
        first, other, _ = self.paired(z)
        middle = (z == 1) | (z == LINES - 2)
        for i, shift in enumerate(self.sides):
            work += [(self.panel(first, y, shift), True, [(2 + 2 * i, 0, False, True)]),
                     (self.panel(other, y, shift), middle, [(3 + 2 * i, 0, False, middle)])]
        return work

    def work_crossed(self, z, y):
        line, below, above = self.second(z)
        return [(self.panel(line, y, shift), below | above, [(i, 0, False, below | above)])
                for i, shift in enumerate(self.sides)]

    def work_far(self, z, y):
        there = (z == 0) | (z == LINES - 1)
        return [(self.panel(LINES - 1 - z, y, shift), there, [(shift, 0, False, there)])
                for shift in range(self.columns)]


def pack_kernel(grid, mask_from, cols_from, prolong_from, head, tail, mask, cols, prolong, done):
    group, groups = lax.axis_index("rows"), lax.axis_size("rows")
    width = tail.shape[-1]
    rows = prolong.shape[0]
    step = rows // 4 if rows % 4 == 0 else rows
    copies = [pltpu.make_async_copy(mask_from, mask, done.at[0]), pltpu.make_async_copy(cols_from, cols, done.at[1])]
    for index in range(rows // step):
        some = pl.ds(index * step, step)
        copies.append(pltpu.make_async_copy(prolong_from.at[some], prolong.at[some], done.at[2 + index]))
    for copy in copies:
        copy.start()
    copies[0].wait()
    copies[1].wait()
    for i in range(rows):
        if i % step == 0:
            copies[2 + i // step].wait()
        blocks = []
        for e in range(3):
            candidate = group + e - 1
            keep = (mask[e, 0, i] == 1) & (candidate >= 0) & (candidate < groups)
            block = prolong[i, :, e * width:(e + 1) * width]
            blocks.append(block * jnp.where(keep, 1.0, 0.0).astype(block.dtype))
        grid.part(head, 2, i, 0)[...] = jnp.where(group == 0, blocks[1], blocks[0])
        grid.part(head, 2, i, 1)[...] = jnp.where(group == 0, blocks[2], blocks[1])
        grid.part(tail, 1, i, 0)[...] = jnp.where(group == 0, blocks[0], blocks[2])
    line = lax.broadcasted_iota(jnp.int32, (grid.list_rows, width), 0)
    column = lax.broadcasted_iota(jnp.int32, (grid.list_rows, width), 1)
    numbers = jnp.zeros((grid.list_rows, width), jnp.int32)
    for panel in range(grid.panels):
        for entry in range(grid.cap):
            numbers = jnp.where((line == panel) & (column == entry), cols[panel, entry], numbers)
    start = rows * 2 * grid.pores
    head[start:start + grid.list_rows, :] = numbers.astype(jnp.float32).astype(head.dtype)


def pack(grid, mask, cols, prolong):
    rows, _, width3 = prolong.shape
    outs = [grid.shape(rows, 2, width3 // 3, 1), grid.shape(rows, 1, width3 // 3)]
    return pl.pallas_call(
        functools.partial(pack_kernel, grid),
        grid=(1,),
        in_specs=[pl.BlockSpec(memory_space=pl.ANY)] * 3,
        out_specs=[*map(resident, outs)],
        scratch_shapes=[
            pltpu.SMEM(mask.shape, mask.dtype),
            pltpu.SMEM(cols.shape, cols.dtype),
            pltpu.VMEM(prolong.shape, prolong.dtype),
            pltpu.SemaphoreType.DMA((6,)),
        ],
        out_shape=outs,
        compiler_params=pltpu.CompilerParams(vmem_limit_bytes=PACK_VMEM_LIMIT),
        cost_estimate=COST,
        name="pack_rows",
    )(mask, cols, prolong)


def turn_kernel(grid, head, tail, turned):
    width = head.shape[-1]
    for i in range(turned.shape[0]):
        parts = (grid.part(head, 2, i, 0), grid.part(head, 2, i, 1), grid.part(tail, 1, i, 0))
        for k, part in enumerate(parts):
            turned[i, k * width:(k + 1) * width, :] = part[...].T


def turn(grid, head, tail):
    rows, width = tail.shape[0] // grid.pores, tail.shape[1]
    out = jax.ShapeDtypeStruct((rows, 3 * width, grid.pores), head.dtype)
    return pl.pallas_call(
        functools.partial(turn_kernel, grid),
        grid=(1,),
        in_specs=[resident(head), resident(tail)],
        out_specs=resident(out),
        out_shape=out,
        compiler_params=PARAMS,
        cost_estimate=COST,
        name="turn_rows",
    )(head, tail)


def pick_kernel(grid, plan, layout, carry, tables, lists, filled, *refs):
    wanted = list(refs[:lists])
    sources, at = [], lists
    for blocks in layout:
        sources.append([(refs[at + i], k) for i, k in enumerate(blocks)])
        at += len(blocks)
    scratch = 2 * len(tables) + 1 if tables else 0
    outs = refs[len(refs) - len(filled) - scratch:len(refs) - scratch]
    z, y = grid.spot()

    def list_at(options):
        value = None
        for present, source in options:
            ref = sources[source][0][0]
            here = ref[ref.shape[0] - grid.list_rows:, :].astype(jnp.float32)
            value = here if value is None else jnp.where(present(z), here, value)
        return value

    if tables:
        numbers, plain, done = refs[-scratch:-1 - len(tables)], refs[-1 - len(tables):-1], refs[-1]
        for table, options in enumerate(tables):
            numbers[table][...] = list_at(options).astype(jnp.int32)
            pltpu.make_async_copy(numbers[table], plain[table], done.at[table]).start()
        for table in range(len(tables)):
            pltpu.make_async_copy(numbers[table], plain[table], done.at[table]).wait()
        wanted += plain
    for index, list_row, options, output in plan(z, y):
        for present, source in options:
            def copy(index=index, list_row=list_row, source=source, output=output):
                for entry in range(grid.cap):
                    row = wanted[index][list_row, entry]
                    place = 0
                    for ref, blocks in sources[source]:
                        for block in range(blocks):
                            target = grid.part(outs[output], filled[output], entry, place)
                            target[...] = grid.part(ref, blocks, row, block)[...]
                            place += 1
            if present is True:
                copy()
            else:
                pl.when(present)(copy)
    for out, options in zip(outs, carry):
        if options:
            out[out.shape[0] - grid.list_rows:, :] = list_at(options).astype(out.dtype)


def pick(grid, plan, filled, lists, sources, carry=(), tables=(), after=(), cost=COST):
    flat = [x for source in sources for x, _ in source]
    width = flat[0].shape[-1]
    carry = carry or ((),) * len(filled)
    shapes = [grid.shape(grid.cap, blocks, width, 1 if options else 0) for blocks, options in zip(filled, carry)]
    layout = tuple(tuple(blocks for _, blocks in source) for source in sources)
    table = (grid.list_rows, width)
    scratch = [pltpu.VMEM(table, jnp.int32)] * len(tables) + [pltpu.SMEM(table, jnp.int32)] * len(tables)
    scratch += [pltpu.SemaphoreType.DMA((len(tables),))] if tables else []
    return pl.pallas_call(
        functools.partial(pick_kernel, grid, plan, layout, carry, tables, len(lists), tuple(filled)),
        grid_spec=pltpu.PrefetchScalarGridSpec(
            num_scalar_prefetch=len(lists),
            grid=(1,),
            in_specs=[*map(resident, flat), *([ANYWHERE] * len(after))],
            out_specs=[*map(resident, shapes)],
            scratch_shapes=scratch,
        ),
        out_shape=shapes,
        compiler_params=PARAMS,
        cost_estimate=cost,
        name="pick_rows",
    )(*lists, *flat, *after)


def stage_kernel(grid, plan, layout, carried, slot_rows, slot_cols, slot_counts, turned, matrix, *refs):
    arrays, at = [], 0
    for blocks in layout:
        arrays.append([(refs[at + i], k) for i, k in enumerate(blocks)])
        at += len(blocks)
    earlier = refs[at:at + 3] if carried else ()
    own, up, down, total = refs[-4:]
    width = own.shape[-1]
    first_group = lax.axis_index("rows") == 0
    for old, new in zip(earlier, (own, up, down)):
        for slot in range(carried):
            for f in range(3):
                new[slot, f] = old[slot, f]
    z, y = grid.spot()
    for slot, (panel, _, sources) in enumerate(plan(z, y), start=carried):
        total[...] = jnp.zeros_like(total)
        for array, base, whole, present in sources:
            live = slot_counts[0, panel]
            if present is not True:
                live = jnp.where(present, live, 0)
            parts = arrays[array]

            def product(entry, whole=whole, base=base, parts=parts, panel=panel):
                pick = slot_cols[panel, entry] if whole else base + entry
                right = jnp.concatenate(
                    [grid.part(x, blocks, pick, block)[...] for x, blocks in parts for block in range(blocks)], axis=1)
                return jnp.dot(matrix[panel, entry], right, preferred_element_type=jnp.float32)

            def add(left, value):
                result = jnp.dot(left, value, preferred_element_type=jnp.float32)
                for k in range(3):
                    total[k] += result[:, k * width:(k + 1) * width]

            def two(u, carry, product=product, panel=panel):
                first, second = 2 * u, 2 * u + 1
                left = jnp.concatenate(
                    [turned[slot_rows[panel, first]], turned[slot_rows[panel, second]]], axis=1)
                value = jnp.concatenate([product(first), product(second)], axis=0).astype(jnp.bfloat16)
                add(left, value)
                return carry

            lax.fori_loop(0, live // 2, two, 0)

            @pl.when(live % 2 == 1)
            def _(live=live, product=product, panel=panel):
                add(turned[slot_rows[panel, live - 1]], product(live - 1).astype(jnp.bfloat16))

        begin = jnp.where(first_group, 0, width)
        for f in range(3):
            k = jnp.where(first_group, (f + 2) % 3, f)
            own[slot, f] = total[k, pl.ds(pl.multiple_of(begin, width), width), :].astype(own.dtype)
            up[slot, f] = total[k, pl.ds(pl.multiple_of(begin + width, width), width), :].astype(up.dtype)
            down[slot, f] = total[k, 0:width, :].astype(down.dtype)


def stage(grid, plan, lists, turned, matrix, sources, earlier=(), after=()):
    width = turned.shape[1] // 3
    carried = earlier[0].shape[0] if earlier else 0
    slots = carried + len(plan(jnp.int32(0), jnp.int32(0)))
    flat = [x for source in sources for x, _ in source]
    layout = tuple(tuple(blocks for _, blocks in source) for source in sources)
    out = jax.ShapeDtypeStruct((slots, 3, width, width), jnp.bfloat16)
    return pl.pallas_call(
        functools.partial(stage_kernel, grid, plan, layout, carried),
        grid_spec=pltpu.PrefetchScalarGridSpec(
            num_scalar_prefetch=3,
            grid=(1,),
            in_specs=[*map(resident, (turned, matrix, *flat, *earlier)), *([ANYWHERE] * len(after))],
            out_specs=[resident(out)] * 3,
            scratch_shapes=[pltpu.VMEM((3, 3 * width, width), jnp.float32)],
        ),
        out_shape=[out] * 3,
        compiler_params=PARAMS,
        cost_estimate=COST,
        name="stage_products",
    )(*lists, turned, matrix, *flat, *earlier, *after)


def assemble_kernel(grid, plans, *refs):
    out = refs[-1]
    rows = refs[0].shape[2]
    panels = grid.panels
    z, y = grid.spot()
    for index, group in enumerate(plans):
        own, lower, upper = refs[3 * index:3 * index + 3]
        slots = [slot for plan in group for slot in plan(z, y)]
        for slot, (panel, present, _) in enumerate(slots):
            def write(slot=slot, own=own, lower=lower, upper=upper, panel=panel):
                for d in range(5):
                    terms = []
                    if 0 <= d - 1 < 3:
                        terms.append(own[slot, d - 1].astype(jnp.float32))
                    if d < 3:
                        terms.append(lower[slot, d].astype(jnp.float32))
                    if 0 <= d - 2 < 3:
                        terms.append(upper[slot, d - 2].astype(jnp.float32))
                    out[pl.ds(d * panels + panel, rows, stride=5 * panels), :] = functools.reduce(jnp.add, terms)
            if present is True:
                write()
            else:
                pl.when(present)(write)


def assemble(grid, plans, pieces):
    panels = grid.panels
    width = pieces[0][0].shape[-1]
    rows = width // 4
    flat = [x for piece in pieces for x in piece]
    result = pl.pallas_call(
        functools.partial(assemble_kernel, grid, plans),
        grid=(width // rows,),
        in_specs=[pl.BlockSpec((x.shape[0], 3, rows, width), lambda i: (0, 0, i, 0)) for x in flat],
        out_specs=pl.BlockSpec((rows * 5 * panels, width), lambda i: (i, 0)),
        out_shape=jax.ShapeDtypeStruct((width * 5 * panels, width), jnp.float32),
        compiler_params=PARAMS,
        cost_estimate=COST,
        name="assemble_coarse",
    )(*flat)
    return result.reshape(width, 5, panels, width).transpose(0, 2, 1, 3)


def per_device(fine_blocks, block_rows, block_cols, block_counts, prolong_blocks, prolong_mask):
    matrix = fine_blocks[0, 0]
    cols_list = block_cols[0, 0]
    lists = (block_rows[0, 0], cols_list, block_counts[0])
    groups = lax.axis_size("rows")
    grid = Grid(lax.axis_size("blk"), cols_list.shape[1], matrix.shape[2])
    cap, sides, columns = grid.cap, grid.sides, grid.columns
    every, inner = range(groups), range(1, groups - 1)

    def move(x, pairs, members=every):
        perm = [(a * groups + g, b * groups + g) for g in members for a, b in pairs]
        return lax.ppermute(x, ("blk", "rows"), perm) if perm else jnp.zeros_like(x)

    def move_both(pair, pairs):
        return (move(pair[0][0], pairs), 2), (move(pair[1][0], pairs, inner), 1)

    def move_across(arrays, lines=range(LINES)):
        return [((move(x, grid.across(shift, lines)), 3),) for x, shift in zip(arrays, sides)]

    def exchange(parts):
        lower = lax.ppermute(parts[1], "rows", [(g, g + 1) for g in range(groups - 1)])
        upper = lax.ppermute(parts[2], "rows", [(g + 1, g) for g in range(groups - 1)])
        return parts[0], lower, upper

    head, tail = pack(grid, prolong_mask.transpose(2, 0, 1), cols_list, prolong_blocks[0])
    own = ((head, 2), (tail, 1))
    near = [move_both(own, grid.hops(1, 1)), move_both(own, grid.hops(1, -1))]
    side_lists = [move(cols_list, [(b, a) for a, b in grid.across(shift)]) for shift in sides]

    def own_requests(z, y):
        return [(index, grid.panel(z, y, 0), [(True, 0)], index) for index in range(len(sides))]

    beside = move_across(pick(grid, own_requests, [3] * len(sides), side_lists, [own]))
    turned = turn(grid, head, tail)

    second = [move_both(near[0], grid.hops(2, 1)), move_both(near[1], grid.hops(2, -1))]

    def near_requests(z, y):
        first, other, odd = grid.paired(z)
        requests = []
        for index in range(len(sides)):
            requests += [
                (index, grid.panel(first, y, 0), [(odd, 0), (jnp.logical_not(odd), 1)], 2 * index),
                (index, grid.panel(other, y, 0), [(z == 1, 1), (z == LINES - 2, 0)], 2 * index + 1)]
        return requests

    def is_odd(z):
        return z % 2 == 1

    paired = ((None, 1), (is_odd, 0))
    picked = pick(grid, near_requests, [3] * (2 * len(sides)), side_lists, near, (paired, ()) * len(sides),
                  after=[x for ((x, _),) in beside], cost=NEAR_COST)
    crossed, middle = move_across(picked[::2]), move_across(picked[1::2], (1, LINES - 2))
    parts = stage(grid, grid.work_near, lists, turned, matrix, [*near, own, *beside])

    def early_requests(z, y):
        line, below, above = grid.second(z)
        return [(index, grid.panel(line, y, 0), [(below, 0), (above, 1)], index) for index in range(len(sides) + 1)]

    def late_requests(z, y):
        line, below, above = grid.second(z)
        row = grid.panel(line, y, 0)
        last, whole = [(below, 2), (above, 3)], [(below, 0), (above, 1)]
        return ([(index, row, last, index) for index in range(len(sides))] +
                [(index, row, whole, index) for index in range(len(sides), 2 * len(sides))] +
                [(2 * len(sides), row, last, 2 * len(sides))])

    heads, tails = [(pair[0],) for pair in second], [(pair[1],) for pair in second]
    near_heads = [(pair[0],) for pair in near]
    end_list = ((None, 3), (is_odd, 2))
    early = pick(grid, early_requests, [2] * (len(sides) + 1), side_lists, [*heads, *near_heads], tables=(end_list,),
                 cost=EARLY_COST)
    far_head = move(early[-1], grid.ends(0))
    second_heads = [move(x, grid.across(shift)) for x, shift in zip(early, sides)]
    tables = [((None, 6 + columns - 1 - shift),) for shift in sides] + [((None, 5), (is_odd, 4))]
    picked = pick(grid, late_requests, [1] * len(sides) + [3] * len(sides) + [1], side_lists,
                  [*second, *tails, *near_heads, *crossed], tables=tuple(tables), after=[parts[0]], cost=PICK_COST)
    second_crossed = [((x, 2), (move(last, grid.across(shift), inner), 1))
                      for x, last, shift in zip(second_heads, picked, sides)]
    far = [((far_head, 2), (move(picked[-1], grid.ends(0), inner), 1))]
    far += [((move(x, grid.ends(shift)), 3),) for shift, x in zip(sides, picked[len(sides):])]
    both = [x for pair in zip(crossed, middle) for x in pair]
    parts = stage(grid, grid.work_second, lists, turned, matrix, [*second, *both], parts, [far_head, *second_heads])
    first = exchange(parts)
    parts = stage(grid, grid.work_crossed, lists, turned, matrix, second_crossed, (), [parts[0]])

    parts = stage(grid, grid.work_far, lists, turned, matrix, far, parts, first[1:])
    last = exchange(parts)
    plans = ((grid.work_near, grid.work_second), (grid.work_crossed, grid.work_far))
    return assemble(grid, plans, [first, last])[None, None]


def solution(mesh):
    in_specs = (
        P("rows", "blk", None, None, None, None),
        P("rows", "blk", None, None),
        P("rows", "blk", None, None),
        P("rows", "blk", None),
        P("rows", "blk", None, None),
        P("rows", "blk", None),
    )
    out_specs = P("rows", "blk", None, None, None, None)
    return jax.shard_map(
        per_device, mesh=mesh, in_specs=in_specs, out_specs=out_specs, check_vma=False
    )
```

```python
import functools
import jax
import jax.numpy as jnp
from jax import lax
from jax.experimental import pallas as pl
from jax.experimental.pallas import tpu as pltpu
from jax.sharding import PartitionSpec as P

VMEM_LIMIT = 24 * 1024 * 1024
PACK_VMEM_LIMIT = 60 * 1024 * 1024
PARAMS = pltpu.CompilerParams(vmem_limit_bytes=VMEM_LIMIT)
COST = pl.CostEstimate(flops=1024, bytes_accessed=1024, transcendentals=0)
EARLY_COST = pl.CostEstimate(flops=1024, bytes_accessed=1024, transcendentals=0)
FAR_COST = pl.CostEstimate(flops=1024, bytes_accessed=1024, transcendentals=0)
NEAR_COST = pl.CostEstimate(flops=6 * 10 ** 9, bytes_accessed=1024, transcendentals=0)
PICK_COST = pl.CostEstimate(flops=2 * 10 ** 10, bytes_accessed=1024, transcendentals=0)
ANYWHERE = pl.BlockSpec(memory_space=pl.ANY)


def resident(x):
    return pl.BlockSpec(x.shape, lambda i, *_, n=len(x.shape): (0,) * n)


LINES = 4


class Grid:
    def __init__(self, panels, cap, pores):
        self.panels, self.cap, self.pores = panels, cap, pores
        self.columns = panels // LINES
        self.sides = range(1, self.columns)
        self.list_rows = -(-panels // 16) * 16

    def spot(self):
        place = lax.axis_index("blk")
        return place // self.columns, place % self.columns

    def lines(self, z):
        upper = z >= 2
        return jnp.where(z % 2 == 1, z - 1, z + 1), jnp.where(upper, 1, 2), jnp.where(upper, 0, 3)

    def middle(self, z):
        return (z == 1) | (z == 2)

    def panel(self, line, y, shift):
        column = y - shift
        return line * self.columns + jnp.where(column < 0, column + self.columns, column)

    def swaps(self, lines):
        return [(h * self.columns + c, k * self.columns + c)
                for h, k in (*lines, *[(k, h) for h, k in lines]) for c in range(self.columns)]

    def across(self, shift, lines=range(LINES)):
        return [(h * self.columns + c, h * self.columns + (c + shift) % self.columns)
                for h in lines for c in range(self.columns)]

    def ends(self, shift):
        return [(h * self.columns + c, end * self.columns + (c + shift) % self.columns)
                for h, end in ((1, 0), (2, 3)) for c in range(self.columns)]

    def part(self, ref, blocks, row, block):
        start = (row * blocks + block) * self.pores
        if not isinstance(start, int):
            start = pl.multiple_of(start, self.pores)
        return ref.at[pl.ds(start, self.pores), :]

    def shape(self, rows, blocks, width, lists=0):
        return jax.ShapeDtypeStruct((rows * blocks * self.pores + lists * self.list_rows, width), jnp.bfloat16)


    def work_near(self, z, y):
        half, _, _ = self.lines(z)
        return ([(self.panel(z, y, 0), [(0, True, True)]), (self.panel(half, y, 0), [(1, True, True)])] +
                [(self.panel(z, y, shift), [(1 + shift, False, True)]) for shift in self.sides])

    def work_middle(self, z, y):
        _, other, _ = self.lines(z)
        middle = self.middle(z)
        end = jnp.logical_not(middle)
        return ([(self.panel(other, y, 0), [(0, True, middle), (1, False, end)])] +
                [(self.panel(other, y, shift), [(2 * shift, False, middle), (2 * shift + 1, False, end)])
                 for shift in self.sides])

    def work_far(self, z, y):
        half, _, far = self.lines(z)
        middle = self.middle(z)
        end = jnp.logical_not(middle)
        work = [(self.panel(far, y, 0), [(0, True, middle), (1, False, end)])]
        for i, shift in enumerate(self.sides):
            work += [(self.panel(half, y, shift), [(2 + 3 * i, False, True)]),
                     (self.panel(far, y, shift), [(3 + 3 * i, False, middle), (4 + 3 * i, False, end)])]
        return work


def pack_kernel(grid, mask_from, cols_from, prolong_from, head, tail, mask, cols, prolong, done):
    group, groups = lax.axis_index("rows"), lax.axis_size("rows")
    width = tail.shape[-1]
    rows = prolong.shape[0]
    step = rows // 4 if rows % 4 == 0 else rows
    copies = [pltpu.make_async_copy(mask_from, mask, done.at[0]), pltpu.make_async_copy(cols_from, cols, done.at[1])]
    for index in range(rows // step):
        some = pl.ds(index * step, step)
        copies.append(pltpu.make_async_copy(prolong_from.at[some], prolong.at[some], done.at[2 + index]))
    for copy in copies:
        copy.start()
    copies[0].wait()
    copies[1].wait()
    for i in range(rows):
        if i % step == 0:
            copies[2 + i // step].wait()
        blocks = []
        for e in range(3):
            candidate = group + e - 1
            keep = (mask[e, 0, i] == 1) & (candidate >= 0) & (candidate < groups)
            block = prolong[i, :, e * width:(e + 1) * width]
            blocks.append(block * jnp.where(keep, 1.0, 0.0).astype(block.dtype))
        grid.part(head, 2, i, 0)[...] = jnp.where(group == 0, blocks[1], blocks[0])
        grid.part(head, 2, i, 1)[...] = jnp.where(group == 0, blocks[2], blocks[1])
        grid.part(tail, 1, i, 0)[...] = jnp.where(group == 0, blocks[0], blocks[2])
    line = lax.broadcasted_iota(jnp.int32, (grid.list_rows, width), 0)
    column = lax.broadcasted_iota(jnp.int32, (grid.list_rows, width), 1)
    numbers = jnp.zeros((grid.list_rows, width), jnp.int32)
    for panel in range(grid.panels):
        for entry in range(grid.cap):
            numbers = jnp.where((line == panel) & (column == entry), cols[panel, entry], numbers)
    start = rows * 2 * grid.pores
    head[start:start + grid.list_rows, :] = numbers.astype(jnp.float32).astype(head.dtype)


def pack(grid, mask, cols, prolong):
    rows, _, width3 = prolong.shape
    outs = [grid.shape(rows, 2, width3 // 3, 1), grid.shape(rows, 1, width3 // 3)]
    return pl.pallas_call(
        functools.partial(pack_kernel, grid),
        grid=(1,),
        in_specs=[pl.BlockSpec(memory_space=pl.ANY)] * 3,
        out_specs=[*map(resident, outs)],
        scratch_shapes=[
            pltpu.SMEM(mask.shape, mask.dtype),
            pltpu.SMEM(cols.shape, cols.dtype),
            pltpu.VMEM(prolong.shape, prolong.dtype),
            pltpu.SemaphoreType.DMA((6,)),
        ],
        out_shape=outs,
        compiler_params=pltpu.CompilerParams(vmem_limit_bytes=PACK_VMEM_LIMIT),
        cost_estimate=COST,
        name="pack_rows",
    )(mask, cols, prolong)


def turn_kernel(grid, head, tail, turned):
    width = head.shape[-1]
    for i in range(turned.shape[0]):
        parts = (grid.part(head, 2, i, 0), grid.part(head, 2, i, 1), grid.part(tail, 1, i, 0))
        for k, part in enumerate(parts):
            turned[i, k * width:(k + 1) * width, :] = part[...].T


def turn(grid, head, tail):
    rows, width = tail.shape[0] // grid.pores, tail.shape[1]
    out = jax.ShapeDtypeStruct((rows, 3 * width, grid.pores), head.dtype)
    return pl.pallas_call(
        functools.partial(turn_kernel, grid),
        grid=(1,),
        in_specs=[resident(head), resident(tail)],
        out_specs=resident(out),
        out_shape=out,
        compiler_params=PARAMS,
        cost_estimate=COST,
        name="turn_rows",
    )(head, tail)


def pick_kernel(grid, plan, layout, carry, tables, lists, filled, passed, *refs):
    wanted = list(refs[:lists])
    sources, at = [], lists
    for blocks in layout:
        sources.append([(refs[at + i], k) for i, k in enumerate(blocks)])
        at += len(blocks)
    scratch = 2 * len(tables) + 1 if tables else 0
    outs = refs[len(refs) - len(filled) - scratch:len(refs) - scratch]
    z, y = grid.spot()

    def list_at(source):
        ref = sources[source][0][0]
        return ref[ref.shape[0] - grid.list_rows:, :]

    if tables:
        numbers, plain, done = refs[-scratch:-1 - len(tables)], refs[-1 - len(tables):-1], refs[-1]
        for table, source in enumerate(tables):
            numbers[table][...] = list_at(source).astype(jnp.float32).astype(jnp.int32)
            pltpu.make_async_copy(numbers[table], plain[table], done.at[table]).start()
        for table in range(len(tables)):
            pltpu.make_async_copy(numbers[table], plain[table], done.at[table]).wait()
        wanted += plain
    for index, list_row, source, output, base in plan(z, y):
        for entry in range(grid.cap):
            row = wanted[index][list_row, entry]
            place = 0
            for ref, blocks in sources[source]:
                for block in range(blocks):
                    target = grid.part(outs[output], filled[output][0], base + entry, place)
                    target[...] = grid.part(ref, blocks, row, block)[...]
                    place += 1
    if passed is not None:
        outs[-1][...] = sources[passed][0][0][...]
    for out, source in zip(outs, carry):
        if source is not None:
            out[out.shape[0] - grid.list_rows:, :] = list_at(source)


def pick(grid, plan, filled, lists, sources, carry=(), tables=(), passed=None, after=(), cost=COST):
    flat = [x for source in sources for x, _ in source]
    width = flat[0].shape[-1]
    carry = carry or (None,) * len(filled)
    shapes = [grid.shape(rows, blocks, width, 0 if source is None else 1)
              for (blocks, rows), source in zip(filled, carry)]
    if passed is not None:
        filled = [*filled, (0, 0)]
        shapes.append(jax.ShapeDtypeStruct(sources[passed][0][0].shape, flat[0].dtype))
    layout = tuple(tuple(blocks for _, blocks in source) for source in sources)
    table = (grid.list_rows, width)
    scratch = [pltpu.VMEM(table, jnp.int32)] * len(tables) + [pltpu.SMEM(table, jnp.int32)] * len(tables)
    scratch += [pltpu.SemaphoreType.DMA((len(tables),))] if tables else []
    return pl.pallas_call(
        functools.partial(pick_kernel, grid, plan, layout, carry, tables, len(lists), tuple(filled), passed),
        grid_spec=pltpu.PrefetchScalarGridSpec(
            num_scalar_prefetch=len(lists),
            grid=(1,),
            in_specs=[*map(resident, flat), *([ANYWHERE] * len(after))],
            out_specs=[*map(resident, shapes)],
            scratch_shapes=scratch,
        ),
        out_shape=shapes,
        compiler_params=PARAMS,
        cost_estimate=cost,
        name="pick_rows",
    )(*lists, *flat, *after)


def stage_kernel(grid, plan, layout, carried, slot_rows, slot_cols, slot_counts, turned, matrix, *refs):
    arrays, at = [], 0
    for blocks in layout:
        arrays.append([(refs[at + i], k, base) for i, (k, base) in enumerate(blocks)])
        at += len(blocks)
    earlier = refs[at:at + 3] if carried else ()
    own, up, down, total = refs[-4:]
    width = own.shape[-1]
    first_group = lax.axis_index("rows") == 0
    for old, new in zip(earlier, (own, up, down)):
        for slot in range(carried):
            for f in range(3):
                new[slot, f] = old[slot, f]
    z, y = grid.spot()
    for slot, (panel, sources) in enumerate(plan(z, y), start=carried):
        total[...] = jnp.zeros_like(total)
        for array, whole, present in sources:
            live = slot_counts[0, panel]
            if present is not True:
                live = jnp.where(present, live, 0)
            parts = arrays[array]

            def product(entry, whole=whole, parts=parts, panel=panel):
                pick = slot_cols[panel, entry] if whole else entry
                right = jnp.concatenate(
                    [grid.part(x, blocks, base + pick, block)[...] for x, blocks, base in parts for block in range(blocks)],
                    axis=1)
                return jnp.dot(matrix[panel, entry], right, preferred_element_type=jnp.float32)

            def add(left, value):
                result = jnp.dot(left, value, preferred_element_type=jnp.float32)
                for k in range(3):
                    total[k] += result[:, k * width:(k + 1) * width]

            def two(u, carry, product=product, panel=panel):
                first, second = 2 * u, 2 * u + 1
                left = jnp.concatenate(
                    [turned[slot_rows[panel, first]], turned[slot_rows[panel, second]]], axis=1)
                value = jnp.concatenate([product(first), product(second)], axis=0).astype(jnp.bfloat16)
                add(left, value)
                return carry

            lax.fori_loop(0, live // 2, two, 0)

            @pl.when(live % 2 == 1)
            def _(live=live, product=product, panel=panel):
                add(turned[slot_rows[panel, live - 1]], product(live - 1).astype(jnp.bfloat16))

        begin = jnp.where(first_group, 0, width)
        for f in range(3):
            k = jnp.where(first_group, (f + 2) % 3, f)
            own[slot, f] = total[k, pl.ds(pl.multiple_of(begin, width), width), :].astype(own.dtype)
            up[slot, f] = total[k, pl.ds(pl.multiple_of(begin + width, width), width), :].astype(up.dtype)
            down[slot, f] = total[k, 0:width, :].astype(down.dtype)


def stage(grid, plan, lists, turned, matrix, sources, earlier=(), after=()):
    width = turned.shape[1] // 3
    carried = earlier[0].shape[0] if earlier else 0
    slots = carried + len(plan(jnp.int32(0), jnp.int32(0)))
    flat = [x for source in sources for x, *_ in source]
    layout = tuple(tuple((blocks, base[0] if base else 0) for _, blocks, *base in source) for source in sources)
    out = jax.ShapeDtypeStruct((slots, 3, width, width), jnp.bfloat16)
    return pl.pallas_call(
        functools.partial(stage_kernel, grid, plan, layout, carried),
        grid_spec=pltpu.PrefetchScalarGridSpec(
            num_scalar_prefetch=3,
            grid=(1,),
            in_specs=[*map(resident, (turned, matrix, *flat, *earlier)), *([ANYWHERE] * len(after))],
            out_specs=[resident(out)] * 3,
            scratch_shapes=[pltpu.VMEM((3, 3 * width, width), jnp.float32)],
        ),
        out_shape=[out] * 3,
        compiler_params=PARAMS,
        cost_estimate=COST,
        name="stage_products",
    )(*lists, turned, matrix, *flat, *earlier, *after)


def assemble_kernel(grid, plans, *refs):
    out = refs[-1]
    rows = refs[0].shape[2]
    panels = grid.panels
    z, y = grid.spot()
    for index, group in enumerate(plans):
        own, lower, upper = refs[3 * index:3 * index + 3]
        slots = [slot for plan in group for slot in plan(z, y)]
        for slot, (panel, _) in enumerate(slots):
            for d in range(5):
                terms = []
                if 0 <= d - 1 < 3:
                    terms.append(own[slot, d - 1].astype(jnp.float32))
                if d < 3:
                    terms.append(lower[slot, d].astype(jnp.float32))
                if 0 <= d - 2 < 3:
                    terms.append(upper[slot, d - 2].astype(jnp.float32))
                out[pl.ds(d * panels + panel, rows, stride=5 * panels), :] = functools.reduce(jnp.add, terms)


def assemble(grid, plans, pieces):
    panels = grid.panels
    width = pieces[0][0].shape[-1]
    rows = width // 4
    flat = [x for piece in pieces for x in piece]
    result = pl.pallas_call(
        functools.partial(assemble_kernel, grid, plans),
        grid=(width // rows,),
        in_specs=[pl.BlockSpec((x.shape[0], 3, rows, width), lambda i: (0, 0, i, 0)) for x in flat],
        out_specs=pl.BlockSpec((rows * 5 * panels, width), lambda i: (i, 0)),
        out_shape=jax.ShapeDtypeStruct((width * 5 * panels, width), jnp.float32),
        compiler_params=PARAMS,
        cost_estimate=COST,
        name="assemble_coarse",
    )(*flat)
    return result.reshape(width, 5, panels, width).transpose(0, 2, 1, 3)


def per_device(fine_blocks, block_rows, block_cols, block_counts, prolong_blocks, prolong_mask):
    matrix = fine_blocks[0, 0]
    cols_list = block_cols[0, 0]
    lists = (block_rows[0, 0], cols_list, block_counts[0])
    groups = lax.axis_size("rows")
    grid = Grid(lax.axis_size("blk"), cols_list.shape[1], matrix.shape[2])
    cap, sides, columns = grid.cap, grid.sides, grid.columns
    every, inner = range(groups), range(1, groups - 1)

    def move(x, pairs, members=every):
        perm = [(a * groups + g, b * groups + g) for g in members for a, b in pairs]
        return lax.ppermute(x, ("blk", "rows"), perm) if perm else jnp.zeros_like(x)

    def move_both(pair, pairs):
        return (move(pair[0][0], pairs), 2), (move(pair[1][0], pairs, inner), 1)

    def move_across(arrays, lines=range(LINES)):
        return [((move(x, grid.across(shift, lines)), 3),) for x, shift in zip(arrays, sides)]

    def exchange(parts):
        lower = lax.ppermute(parts[1], "rows", [(g, g + 1) for g in range(groups - 1)])
        upper = lax.ppermute(parts[2], "rows", [(g + 1, g) for g in range(groups - 1)])
        return parts[0], lower, upper

    count = len(sides)
    mids = (1, 2)

    head, tail = pack(grid, prolong_mask.transpose(2, 0, 1), cols_list, prolong_blocks[0])
    own = ((head, 2), (tail, 1))
    half = move_both(own, grid.swaps([(0, 1), (2, 3)]))
    other = move_both(own, grid.swaps([(1, 2)]))
    side_lists = [move(cols_list, [(b, a) for a, b in grid.across(shift)]) for shift in sides]

    def own_requests(z, y):
        return [(index, grid.panel(z, y, 0), 0, index, 0) for index in range(count)]

    beside = move_across(pick(grid, own_requests, [(3, cap)] * count, side_lists, [own]))
    turned = turn(grid, head, tail)

    far_head = move(half[0][0], grid.swaps([(1, 2)]))

    def early_requests(z, y):
        return [(0, grid.panel(grid.lines(z)[1], y, 0), 0, 0, 0)]

    early, end_list = pick(grid, early_requests, [(2, cap), (0, 0)], [], [other[:1], half[:1]], (None, 1), (1,),
                           cost=EARLY_COST)
    end_lists = [move(end_list, [(b, a) for a, b in grid.across(shift, mids)]) for shift in sides]
    tables = [(half[0],), *[((x, 0),) for x in end_lists]]
    end_heads = [move(early, grid.ends(0))]

    def near_requests(z, y):
        line_half, line_other, _ = grid.lines(z)
        requests = []
        for index in range(count):
            requests += [(index, grid.panel(line_half, y, 0), 0, index, 0),
                         (index, grid.panel(line_other, y, 0), 1, count + index, 0),
                         (count + 1 + index, grid.panel(line_other, y, 0), 2, 2 * count + index, 0)]
        return requests

    picked = pick(grid, near_requests, [(3, cap)] * (2 * count) + [(2, cap)] * count, side_lists,
                  [half, other, other[:1], *tables], tables=tuple(range(3, 4 + count)),
                  after=[x for ((x, _),) in beside], cost=NEAR_COST)
    half_crossed = move_across(picked)
    other_crossed = move_across(picked[count:], mids)
    end_heads += [move(x, grid.ends(shift)) for x, shift in zip(picked[2 * count:], sides)]
    far_tail = move(half[1][0], grid.swaps([(1, 2)]), inner)
    far = ((far_head, 2), (far_tail, 1))
    parts = stage(grid, grid.work_near, lists, turned, matrix, [own, half, *beside])

    def far_requests(z, y):
        return [(index, grid.panel(grid.lines(z)[2], y, 0), 0, index, 0) for index in range(columns)]

    picked = pick(grid, far_requests, [(2, cap)] * columns, [], [far[:1], *tables], tables=tuple(range(1, 2 + count)),
                  cost=FAR_COST)
    far_heads = [move(x, grid.ends(shift)) for shift, x in enumerate(picked)]

    def last_requests(z, y):
        _, line_other, line_far = grid.lines(z)
        requests = [(index, grid.panel(line_far, y, 0), 0, index, 0) for index in range(count)]
        for index in range(columns):
            requests += [(count + index, grid.panel(line_other, y, 0), 1, count + index, 0),
                         (count + index, grid.panel(line_far, y, 0), 2, count + index, cap)]
        return requests

    picked = pick(grid, last_requests, [(3, cap)] * count + [(1, 2 * cap)] * columns, side_lists,
                  [far, other[1:], far[1:], *tables], tables=tuple(range(3, 4 + count)), after=[parts[0]],
                  cost=PICK_COST)
    far_crossed = move_across(picked, mids)
    end_tails = [move(x, grid.ends(shift), inner) for shift, x in enumerate(picked[count:])]
    end = [((x, 2), (last, 1, 0)) for x, last in zip(end_heads, end_tails)]
    far_end = [((x, 2), (last, 1, cap)) for x, last in zip(far_heads, end_tails)]
    sources = [other, end[0]]
    for i in range(count):
        sources += [other_crossed[i], end[1 + i]]
    parts = stage(grid, grid.work_middle, lists, turned, matrix, sources, parts)
    first = exchange(parts)

    sources = [far, far_end[0]]
    for i in range(count):
        sources += [half_crossed[i], far_crossed[i], far_end[1 + i]]
    last = exchange(stage(grid, grid.work_far, lists, turned, matrix, sources, (), first[1:]))
    return assemble(grid, ((grid.work_near, grid.work_middle), (grid.work_far,)), [first, last])[None, None]


def solution(mesh):
    in_specs = (
        P("rows", "blk", None, None, None, None),
        P("rows", "blk", None, None),
        P("rows", "blk", None, None),
        P("rows", "blk", None),
        P("rows", "blk", None, None),
        P("rows", "blk", None),
    )
    out_specs = P("rows", "blk", None, None, None, None)
    return jax.shard_map(
        per_device, mesh=mesh, in_specs=in_specs, out_specs=out_specs, check_vma=False
    )
```

```python
import functools
import jax
import jax.numpy as jnp
from jax import lax
from jax.experimental import pallas as pl
from jax.experimental.pallas import tpu as pltpu
from jax.sharding import PartitionSpec as P

VMEM_LIMIT = 24 * 1024 * 1024
PACK_VMEM_LIMIT = 60 * 1024 * 1024
PARAMS = pltpu.CompilerParams(vmem_limit_bytes=VMEM_LIMIT)
COST = pl.CostEstimate(flops=1024, bytes_accessed=1024, transcendentals=0)
ANYWHERE = pl.BlockSpec(memory_space=pl.ANY)


def resident(x):
    return pl.BlockSpec(x.shape, lambda i, *_, n=len(x.shape): (0,) * n)


LINES = 4


class Grid:
    def __init__(self, panels, cap, pores):
        self.panels, self.cap, self.pores = panels, cap, pores
        self.columns = panels // LINES
        self.sides = range(1, self.columns)
        self.list_rows = -(-panels // 16) * 16

    def spot(self):
        place = lax.axis_index("blk")
        return place // self.columns, place % self.columns

    def lines(self, z):
        upper = z >= 2
        return jnp.where(z % 2 == 1, z - 1, z + 1), jnp.where(upper, 1, 2), jnp.where(upper, 0, 3)

    def middle(self, z):
        return (z == 1) | (z == 2)

    def panel(self, line, y, shift):
        column = y - shift
        return line * self.columns + jnp.where(column < 0, column + self.columns, column)

    def swaps(self, lines):
        return [(h * self.columns + c, k * self.columns + c)
                for h, k in (*lines, *[(k, h) for h, k in lines]) for c in range(self.columns)]

    def across(self, shift, lines=range(LINES)):
        return [(h * self.columns + c, h * self.columns + (c + shift) % self.columns)
                for h in lines for c in range(self.columns)]

    def ends(self, shift):
        return [(h * self.columns + c, end * self.columns + (c + shift) % self.columns)
                for h, end in ((1, 0), (2, 3)) for c in range(self.columns)]

    def part(self, ref, blocks, row, block):
        start = (row * blocks + block) * self.pores
        if not isinstance(start, int):
            start = pl.multiple_of(start, self.pores)
        return ref.at[pl.ds(start, self.pores), :]

    def shape(self, rows, blocks, width, lists=0):
        return jax.ShapeDtypeStruct((rows * blocks * self.pores + lists * self.list_rows, width), jnp.bfloat16)


    def work_near(self, z, y):
        half, _, _ = self.lines(z)
        return ([(self.panel(z, y, 0), [(0, True, True)]), (self.panel(half, y, 0), [(1, True, True)])] +
                [(self.panel(z, y, shift), [(1 + shift, False, True)]) for shift in self.sides])

    def work_middle(self, z, y):
        _, other, _ = self.lines(z)
        middle = self.middle(z)
        end = jnp.logical_not(middle)
        return ([(self.panel(other, y, 0), [(0, True, middle), (1, False, end)])] +
                [(self.panel(other, y, shift), [(2 * shift, False, middle), (2 * shift + 1, False, end)])
                 for shift in self.sides])

    def work_far(self, z, y):
        half, _, far = self.lines(z)
        middle = self.middle(z)
        end = jnp.logical_not(middle)
        work = [(self.panel(far, y, 0), [(0, True, middle), (1, False, end)])]
        for i, shift in enumerate(self.sides):
            work += [(self.panel(half, y, shift), [(2 + 3 * i, False, True)]),
                     (self.panel(far, y, shift), [(3 + 3 * i, False, middle), (4 + 3 * i, False, end)])]
        return work


def keep(grid, mask, block, row, k):
    group, groups = lax.axis_index("rows"), lax.axis_size("rows")
    first, other = k, (k + 1) % 3

    def masked(e):
        candidate = group + e - 1
        present = (mask[e, 0, row] == 1) & (candidate >= 0) & (candidate < groups)
        value = block(e)
        return value * jnp.where(present, 1.0, 0.0).astype(value.dtype)

    return jnp.where(group == 0, masked(other), masked(first))


def pack_kernel(grid, blocks, passed, mask_from, cols_from, prolong_from, *refs):
    out, mask, cols, prolong, done = refs[-5:]
    width = out.shape[-1]
    rows = prolong.shape[0]
    step = rows // 4 if rows % 4 == 0 else rows
    copies = [pltpu.make_async_copy(mask_from, mask, done.at[0]), pltpu.make_async_copy(cols_from, cols, done.at[1])]
    for index in range(rows // step):
        some = pl.ds(index * step, step)
        copies.append(pltpu.make_async_copy(prolong_from.at[some], prolong.at[some], done.at[2 + index]))
    for copy in copies:
        copy.start()
    copies[0].wait()
    copies[1].wait()
    for i in range(rows):
        if i % step == 0:
            copies[2 + i // step].wait()
        for place, k in enumerate(blocks):
            grid.part(out, len(blocks), i, place)[...] = keep(
                grid, mask, lambda e, i=i: prolong[i, :, e * width:(e + 1) * width], i, k)
    if passed:
        refs[-6][...] = refs[0][...]
        line = lax.broadcasted_iota(jnp.int32, (grid.list_rows, width), 0)
        column = lax.broadcasted_iota(jnp.int32, (grid.list_rows, width), 1)
        numbers = jnp.zeros((grid.list_rows, width), jnp.int32)
        for panel in range(grid.panels):
            for entry in range(grid.cap):
                numbers = jnp.where((line == panel) & (column == entry), cols[panel, entry], numbers)
        out[out.shape[0] - grid.list_rows:, :] = numbers.astype(jnp.float32).astype(out.dtype)


def pack(grid, blocks, mask, cols, prolong, passed=None, after=()):
    rows, _, width3 = prolong.shape
    out = grid.shape(rows, len(blocks), width3 // 3, 0 if passed is None else 1)
    extra = [] if passed is None else [passed]
    return pl.pallas_call(
        functools.partial(pack_kernel, grid, blocks, bool(extra)),
        grid=(1,),
        in_specs=[ANYWHERE] * 3 + [*map(resident, extra)] + [ANYWHERE] * len(after),
        out_specs=[*map(resident, extra), resident(out)],
        scratch_shapes=[
            pltpu.SMEM(mask.shape, mask.dtype),
            pltpu.SMEM(cols.shape, cols.dtype),
            pltpu.VMEM(prolong.shape, prolong.dtype),
            pltpu.SemaphoreType.DMA((6,)),
        ],
        out_shape=[*[jax.ShapeDtypeStruct(x.shape, x.dtype) for x in extra], out],
        compiler_params=pltpu.CompilerParams(vmem_limit_bytes=PACK_VMEM_LIMIT),
        cost_estimate=COST,
        name="pack_rows",
    )(mask, cols, prolong, *extra, *after)


def turn_kernel(grid, head, tail, turned):
    width = head.shape[-1]
    for i in range(turned.shape[0]):
        parts = (grid.part(head, 2, i, 0), grid.part(head, 2, i, 1), grid.part(tail, 1, i, 0))
        for k, part in enumerate(parts):
            turned[i, k * width:(k + 1) * width, :] = part[...].T


def turn(grid, head, tail):
    rows, width = tail.shape[0] // grid.pores, tail.shape[1]
    out = jax.ShapeDtypeStruct((rows, 3 * width, grid.pores), head.dtype)
    return pl.pallas_call(
        functools.partial(turn_kernel, grid),
        grid=(1,),
        in_specs=[resident(head), resident(tail)],
        out_specs=resident(out),
        out_shape=out,
        compiler_params=PARAMS,
        cost_estimate=COST,
        name="turn_rows",
    )(head, tail)


def pick_kernel(grid, plan, layout, carry, tables, lists, filled, passed, *refs):
    wanted = list(refs[:lists])
    sources, at = [], lists
    for blocks in layout:
        sources.append([(refs[at + i], k) for i, k in enumerate(blocks)])
        at += len(blocks)
    scratch = 2 * len(tables) + 1 if tables else 0
    outs = refs[len(refs) - len(filled) - scratch:len(refs) - scratch]
    z, y = grid.spot()

    def list_at(source):
        ref = sources[source][0][0]
        return ref[ref.shape[0] - grid.list_rows:, :]

    if tables:
        numbers, plain, done = refs[-scratch:-1 - len(tables)], refs[-1 - len(tables):-1], refs[-1]
        for table, source in enumerate(tables):
            numbers[table][...] = list_at(source).astype(jnp.float32).astype(jnp.int32)
            pltpu.make_async_copy(numbers[table], plain[table], done.at[table]).start()
        for table in range(len(tables)):
            pltpu.make_async_copy(numbers[table], plain[table], done.at[table]).wait()
        wanted += plain
    for index, list_row, source, output, base in plan(z, y):
        for entry in range(grid.cap):
            row = wanted[index][list_row, entry]
            place = 0
            for ref, blocks in sources[source]:
                for block in range(blocks):
                    target = grid.part(outs[output], filled[output][0], base + entry, place)
                    target[...] = grid.part(ref, blocks, row, block)[...]
                    place += 1
    if passed is not None:
        outs[-1][...] = sources[passed][0][0][...]
    for out, source in zip(outs, carry):
        if source is not None:
            out[out.shape[0] - grid.list_rows:, :] = list_at(source)


def pick(grid, plan, filled, lists, sources, carry=(), tables=(), passed=None, after=()):
    flat = [x for source in sources for x, _ in source]
    width = flat[0].shape[-1]
    carry = carry or (None,) * len(filled)
    shapes = [grid.shape(rows, blocks, width, 0 if source is None else 1)
              for (blocks, rows), source in zip(filled, carry)]
    if passed is not None:
        filled = [*filled, (0, 0)]
        shapes.append(jax.ShapeDtypeStruct(sources[passed][0][0].shape, flat[0].dtype))
    layout = tuple(tuple(blocks for _, blocks in source) for source in sources)
    table = (grid.list_rows, width)
    scratch = [pltpu.VMEM(table, jnp.int32)] * len(tables) + [pltpu.SMEM(table, jnp.int32)] * len(tables)
    scratch += [pltpu.SemaphoreType.DMA((len(tables),))] if tables else []
    return pl.pallas_call(
        functools.partial(pick_kernel, grid, plan, layout, carry, tables, len(lists), tuple(filled), passed),
        grid_spec=pltpu.PrefetchScalarGridSpec(
            num_scalar_prefetch=len(lists),
            grid=(1,),
            in_specs=[*map(resident, flat), *([ANYWHERE] * len(after))],
            out_specs=[*map(resident, shapes)],
            scratch_shapes=scratch,
        ),
        out_shape=shapes,
        compiler_params=PARAMS,
        cost_estimate=COST,
        name="pick_rows",
    )(*lists, *flat, *after)


def stage_kernel(grid, plan, layout, carried, slot_rows, slot_cols, slot_counts, turned, matrix, *refs):
    arrays, at = [], 0
    for blocks in layout:
        arrays.append([(refs[at + i], k, base) for i, (k, base) in enumerate(blocks)])
        at += len(blocks)
    earlier = refs[at:at + 3] if carried else ()
    own, up, down, total = refs[-4:]
    width = own.shape[-1]
    first_group = lax.axis_index("rows") == 0
    for old, new in zip(earlier, (own, up, down)):
        for slot in range(carried):
            for f in range(3):
                new[slot, f] = old[slot, f]
    z, y = grid.spot()
    for slot, (panel, sources) in enumerate(plan(z, y), start=carried):
        total[...] = jnp.zeros_like(total)
        for array, whole, present in sources:
            live = slot_counts[0, panel]
            if present is not True:
                live = jnp.where(present, live, 0)
            parts = arrays[array]

            def product(entry, whole=whole, parts=parts, panel=panel):
                pick = slot_cols[panel, entry] if whole else entry
                right = jnp.concatenate(
                    [grid.part(x, blocks, base + pick, block)[...] for x, blocks, base in parts for block in range(blocks)],
                    axis=1)
                return jnp.dot(matrix[panel, entry], right, preferred_element_type=jnp.float32)

            def add(left, value):
                result = jnp.dot(left, value, preferred_element_type=jnp.float32)
                for k in range(3):
                    total[k] += result[:, k * width:(k + 1) * width]

            def two(u, carry, product=product, panel=panel):
                first, second = 2 * u, 2 * u + 1
                left = jnp.concatenate(
                    [turned[slot_rows[panel, first]], turned[slot_rows[panel, second]]], axis=1)
                value = jnp.concatenate([product(first), product(second)], axis=0).astype(jnp.bfloat16)
                add(left, value)
                return carry

            lax.fori_loop(0, live // 2, two, 0)

            @pl.when(live % 2 == 1)
            def _(live=live, product=product, panel=panel):
                add(turned[slot_rows[panel, live - 1]], product(live - 1).astype(jnp.bfloat16))

        begin = jnp.where(first_group, 0, width)
        for f in range(3):
            k = jnp.where(first_group, (f + 2) % 3, f)
            own[slot, f] = total[k, pl.ds(pl.multiple_of(begin, width), width), :].astype(own.dtype)
            up[slot, f] = total[k, pl.ds(pl.multiple_of(begin + width, width), width), :].astype(up.dtype)
            down[slot, f] = total[k, 0:width, :].astype(down.dtype)


def stage(grid, plan, lists, turned, matrix, sources, earlier=(), after=()):
    width = turned.shape[1] // 3
    carried = earlier[0].shape[0] if earlier else 0
    slots = carried + len(plan(jnp.int32(0), jnp.int32(0)))
    flat = [x for source in sources for x, *_ in source]
    layout = tuple(tuple((blocks, base[0] if base else 0) for _, blocks, *base in source) for source in sources)
    out = jax.ShapeDtypeStruct((slots, 3, width, width), jnp.bfloat16)
    return pl.pallas_call(
        functools.partial(stage_kernel, grid, plan, layout, carried),
        grid_spec=pltpu.PrefetchScalarGridSpec(
            num_scalar_prefetch=3,
            grid=(1,),
            in_specs=[*map(resident, (turned, matrix, *flat, *earlier)), *([ANYWHERE] * len(after))],
            out_specs=[resident(out)] * 3,
            scratch_shapes=[pltpu.VMEM((3, 3 * width, width), jnp.float32)],
        ),
        out_shape=[out] * 3,
        compiler_params=PARAMS,
        cost_estimate=COST,
        name="stage_products",
    )(*lists, turned, matrix, *flat, *earlier, *after)


def assemble_kernel(grid, plans, *refs):
    out = refs[-1]
    rows = refs[0].shape[2]
    panels = grid.panels
    z, y = grid.spot()
    for index, group in enumerate(plans):
        own, lower, upper = refs[3 * index:3 * index + 3]
        slots = [slot for plan in group for slot in plan(z, y)]
        for slot, (panel, _) in enumerate(slots):
            for d in range(5):
                terms = []
                if 0 <= d - 1 < 3:
                    terms.append(own[slot, d - 1].astype(jnp.float32))
                if d < 3:
                    terms.append(lower[slot, d].astype(jnp.float32))
                if 0 <= d - 2 < 3:
                    terms.append(upper[slot, d - 2].astype(jnp.float32))
                out[pl.ds(d * panels + panel, rows, stride=5 * panels), :] = functools.reduce(jnp.add, terms)


def assemble(grid, plans, pieces):
    panels = grid.panels
    width = pieces[0][0].shape[-1]
    rows = width // 4
    flat = [x for piece in pieces for x in piece]
    result = pl.pallas_call(
        functools.partial(assemble_kernel, grid, plans),
        grid=(width // rows,),
        in_specs=[pl.BlockSpec((x.shape[0], 3, rows, width), lambda i: (0, 0, i, 0)) for x in flat],
        out_specs=pl.BlockSpec((rows * 5 * panels, width), lambda i: (i, 0)),
        out_shape=jax.ShapeDtypeStruct((width * 5 * panels, width), jnp.float32),
        compiler_params=PARAMS,
        cost_estimate=COST,
        name="assemble_coarse",
    )(*flat)
    return result.reshape(width, 5, panels, width).transpose(0, 2, 1, 3)


def per_device(fine_blocks, block_rows, block_cols, block_counts, prolong_blocks, prolong_mask):
    matrix = fine_blocks[0, 0]
    cols_list = block_cols[0, 0]
    lists = (block_rows[0, 0], cols_list, block_counts[0])
    groups = lax.axis_size("rows")
    grid = Grid(lax.axis_size("blk"), cols_list.shape[1], matrix.shape[2])
    cap, sides, columns = grid.cap, grid.sides, grid.columns
    every, inner = range(groups), range(1, groups - 1)

    def move(x, pairs, members=every):
        perm = [(a * groups + g, b * groups + g) for g in members for a, b in pairs]
        return lax.ppermute(x, ("blk", "rows"), perm) if perm else jnp.zeros_like(x)

    def move_both(pair, pairs):
        return (move(pair[0][0], pairs), 2), (move(pair[1][0], pairs, inner), 1)

    def move_across(arrays, lines=range(LINES)):
        return [((move(x, grid.across(shift, lines)), 3),) for x, shift in zip(arrays, sides)]

    def exchange(parts):
        lower = lax.ppermute(parts[1], "rows", [(g, g + 1) for g in range(groups - 1)])
        upper = lax.ppermute(parts[2], "rows", [(g + 1, g) for g in range(groups - 1)])
        return parts[0], lower, upper

    count = len(sides)
    mids = (1, 2)

    inputs = (prolong_mask.transpose(2, 0, 1), cols_list, prolong_blocks[0])
    within, across = grid.swaps([(0, 1), (2, 3)]), grid.swaps([(1, 2)])
    (tail,) = pack(grid, (2,), *inputs)
    half_tail, other_tail = move(tail, within, inner), move(tail, across, inner)
    passed_tail, head = pack(grid, (0, 1), *inputs, half_tail, [other_tail])
    own = ((head, 2), (tail, 1))
    half = ((move(head, within), 2), (half_tail, 1))
    other = ((move(head, across), 2), (other_tail, 1))
    far_tail = move(passed_tail, across, inner)
    side_lists = [move(cols_list, [(b, a) for a, b in grid.across(shift)]) for shift in sides]

    def own_requests(z, y):
        return [(index, grid.panel(z, y, 0), 0, index, 0) for index in range(count)]

    beside = move_across(pick(grid, own_requests, [(3, cap)] * count, side_lists, [own]))
    turned = turn(grid, head, tail)

    def early_requests(z, y):
        return [(0, grid.panel(grid.lines(z)[1], y, 0), 0, 0, 0)]

    early, end_list, head = pick(grid, early_requests, [(2, cap), (0, 0)], [], [other[:1], half[:1]], (None, 1), (1,), 1,
                                 [x for ((x, _),) in beside])
    far_head = move(head, across)
    far = ((far_head, 2), (far_tail, 1))
    end_lists = [move(end_list, [(b, a) for a, b in grid.across(shift, mids)]) for shift in sides]
    tables = [(half[0],), *[((x, 0),) for x in end_lists]]
    end_heads = [move(early, grid.ends(0))]

    def near_requests(z, y):
        line_half, line_other, _ = grid.lines(z)
        requests = []
        for index in range(count):
            requests += [(index, grid.panel(line_half, y, 0), 0, index, 0),
                         (index, grid.panel(line_other, y, 0), 1, count + index, 0),
                         (count + 1 + index, grid.panel(line_other, y, 0), 2, 2 * count + index, 0)]
        return requests

    picked = pick(grid, near_requests, [(3, cap)] * (2 * count) + [(2, cap)] * count, side_lists,
                  [half, other, other[:1], *tables], tables=tuple(range(3, 4 + count)))
    half_crossed = move_across(picked)
    other_crossed = move_across(picked[count:], mids)
    end_heads += [move(x, grid.ends(shift)) for x, shift in zip(picked[2 * count:], sides)]

    def last_requests(z, y):
        _, line_other, line_far = grid.lines(z)
        requests = []
        for index in range(columns):
            requests += [(index, grid.panel(line_other, y, 0), 0, index, 0),
                         (index, grid.panel(line_far, y, 0), 1, index, cap)]
        return requests

    picked = pick(grid, last_requests, [(1, 2 * cap)] * columns, [], [other[1:], far[1:], *tables],
                  tables=tuple(range(2, 3 + count)), after=picked[:1])
    end_tails = [move(x, grid.ends(shift), inner) for shift, x in enumerate(picked)]
    parts = stage(grid, grid.work_near, lists, turned, matrix, [own, half, *beside], (), picked[:1])

    def far_requests(z, y):
        row = grid.panel(grid.lines(z)[2], y, 0)
        return ([(index, row, 0, index, 0) for index in range(count)] +
                [(count + index, row, 1, count + index, 0) for index in range(columns)])

    picked = pick(grid, far_requests, [(3, cap)] * count + [(2, cap)] * columns, side_lists, [far, far[:1], *tables],
                  tables=tuple(range(2, 3 + count)), after=[parts[0]])
    far_crossed = move_across(picked, mids)
    far_heads = [move(x, grid.ends(shift)) for shift, x in enumerate(picked[count:])]
    end = [((x, 2), (last, 1, 0)) for x, last in zip(end_heads, end_tails)]
    far_end = [((x, 2), (last, 1, cap)) for x, last in zip(far_heads, end_tails)]
    sources = [other, end[0]]
    for i in range(count):
        sources += [other_crossed[i], end[1 + i]]
    parts = stage(grid, grid.work_middle, lists, turned, matrix, sources, parts)
    first = exchange(parts)

    sources = [far, far_end[0]]
    for i in range(count):
        sources += [half_crossed[i], far_crossed[i], far_end[1 + i]]
    last = exchange(stage(grid, grid.work_far, lists, turned, matrix, sources, (), first[1:]))
    return assemble(grid, ((grid.work_near, grid.work_middle), (grid.work_far,)), [first, last])[None, None]


def solution(mesh):
    in_specs = (
        P("rows", "blk", None, None, None, None),
        P("rows", "blk", None, None),
        P("rows", "blk", None, None),
        P("rows", "blk", None),
        P("rows", "blk", None, None),
        P("rows", "blk", None),
    )
    out_specs = P("rows", "blk", None, None, None, None)
    return jax.shard_map(
        per_device, mesh=mesh, in_specs=in_specs, out_specs=out_specs, check_vma=False
    )
```

```python
import functools
import jax
import jax.numpy as jnp
from jax import lax
from jax.experimental import pallas as pl
from jax.experimental.pallas import tpu as pltpu
from jax.sharding import PartitionSpec as P

VMEM_LIMIT = 24 * 1024 * 1024
PACK_VMEM_LIMIT = 60 * 1024 * 1024
PARAMS = pltpu.CompilerParams(vmem_limit_bytes=VMEM_LIMIT)
COST = pl.CostEstimate(flops=1024, bytes_accessed=1024, transcendentals=0)
PICK_COST = pl.CostEstimate(flops=20000000000, bytes_accessed=1024, transcendentals=0)
ANYWHERE = pl.BlockSpec(memory_space=pl.ANY)


def resident(x):
    return pl.BlockSpec(x.shape, lambda i, *_, n=len(x.shape): (0,) * n)


LINES = 4


class Grid:
    def __init__(self, panels, cap, pores):
        self.panels, self.cap, self.pores = panels, cap, pores
        self.columns = panels // LINES
        self.sides = range(1, self.columns)
        self.list_rows = -(-panels // 16) * 16

    def spot(self):
        place = lax.axis_index("blk")
        return place // self.columns, place % self.columns

    def lines(self, z):
        upper = z >= 2
        return jnp.where(z % 2 == 1, z - 1, z + 1), jnp.where(upper, 1, 2), jnp.where(upper, 0, 3)

    def middle(self, z):
        return (z == 1) | (z == 2)

    def panel(self, line, y, shift):
        column = y - shift
        return line * self.columns + jnp.where(column < 0, column + self.columns, column)

    def swaps(self, lines):
        return [(h * self.columns + c, k * self.columns + c)
                for h, k in (*lines, *[(k, h) for h, k in lines]) for c in range(self.columns)]

    def across(self, shift, lines=range(LINES)):
        return [(h * self.columns + c, h * self.columns + (c + shift) % self.columns)
                for h in lines for c in range(self.columns)]

    def ends(self, shift):
        return [(h * self.columns + c, end * self.columns + (c + shift) % self.columns)
                for h, end in ((1, 0), (2, 3)) for c in range(self.columns)]

    def part(self, ref, blocks, row, block):
        start = (row * blocks + block) * self.pores
        if not isinstance(start, int):
            start = pl.multiple_of(start, self.pores)
        return ref.at[pl.ds(start, self.pores), :]

    def shape(self, rows, blocks, width, lists=0):
        return jax.ShapeDtypeStruct((rows * blocks * self.pores + lists * self.list_rows, width), jnp.bfloat16)


    def work_near(self, z, y):
        half, _, _ = self.lines(z)
        return ([(self.panel(z, y, 0), [(0, True, True)]), (self.panel(half, y, 0), [(1, True, True)])] +
                [(self.panel(z, y, shift), [(1 + shift, False, True)]) for shift in self.sides])

    def work_middle(self, z, y):
        half, other, _ = self.lines(z)
        middle = self.middle(z)
        end = jnp.logical_not(middle)
        work = []
        for i, shift in enumerate(self.sides):
            work += [(self.panel(half, y, shift), [(3 * i, False, True)]),
                     (self.panel(other, y, shift), [(3 * i + 1, False, middle), (3 * i + 2, False, end)])]
        return work

    def work_far(self, z, y):
        _, other, far = self.lines(z)
        middle = self.middle(z)
        end = jnp.logical_not(middle)
        return ([(self.panel(other, y, 0), [(0, True, middle), (1, False, end)]),
                 (self.panel(far, y, 0), [(2, True, middle), (3, False, end)])] +
                [(self.panel(far, y, shift), [(2 + 2 * shift, False, middle), (3 + 2 * shift, False, end)])
                 for shift in self.sides])


def pack_kernel(grid, mask_from, cols_from, prolong_from, head, tail, mask, cols, prolong, done):
    group, groups = lax.axis_index("rows"), lax.axis_size("rows")
    width = tail.shape[-1]
    rows = prolong.shape[0]
    step = rows // 4 if rows % 4 == 0 else rows
    copies = [pltpu.make_async_copy(mask_from, mask, done.at[0]), pltpu.make_async_copy(cols_from, cols, done.at[1])]
    for index in range(rows // step):
        some = pl.ds(index * step, step)
        copies.append(pltpu.make_async_copy(prolong_from.at[some], prolong.at[some], done.at[2 + index]))
    for copy in copies:
        copy.start()
    copies[0].wait()
    copies[1].wait()
    for i in range(rows):
        if i % step == 0:
            copies[2 + i // step].wait()
        blocks = []
        for e in range(3):
            candidate = group + e - 1
            keep = (mask[e, 0, i] == 1) & (candidate >= 0) & (candidate < groups)
            block = prolong[i, :, e * width:(e + 1) * width]
            blocks.append(block * jnp.where(keep, 1.0, 0.0).astype(block.dtype))
        grid.part(head, 2, i, 0)[...] = jnp.where(group == 0, blocks[1], blocks[0])
        grid.part(head, 2, i, 1)[...] = jnp.where(group == 0, blocks[2], blocks[1])
        grid.part(tail, 1, i, 0)[...] = jnp.where(group == 0, blocks[0], blocks[2])
    line = lax.broadcasted_iota(jnp.int32, (grid.list_rows, width), 0)
    column = lax.broadcasted_iota(jnp.int32, (grid.list_rows, width), 1)
    numbers = jnp.zeros((grid.list_rows, width), jnp.int32)
    for panel in range(grid.panels):
        for entry in range(grid.cap):
            numbers = jnp.where((line == panel) & (column == entry), cols[panel, entry], numbers)
    start = rows * 2 * grid.pores
    head[start:start + grid.list_rows, :] = numbers.astype(jnp.float32).astype(head.dtype)


def pack(grid, mask, cols, prolong):
    rows, _, width3 = prolong.shape
    outs = [grid.shape(rows, 2, width3 // 3, 1), grid.shape(rows, 1, width3 // 3)]
    return pl.pallas_call(
        functools.partial(pack_kernel, grid),
        grid=(1,),
        in_specs=[pl.BlockSpec(memory_space=pl.ANY)] * 3,
        out_specs=[*map(resident, outs)],
        scratch_shapes=[
            pltpu.SMEM(mask.shape, mask.dtype),
            pltpu.SMEM(cols.shape, cols.dtype),
            pltpu.VMEM(prolong.shape, prolong.dtype),
            pltpu.SemaphoreType.DMA((6,)),
        ],
        out_shape=outs,
        compiler_params=pltpu.CompilerParams(vmem_limit_bytes=PACK_VMEM_LIMIT),
        cost_estimate=COST,
        name="pack_rows",
    )(mask, cols, prolong)


def turn_kernel(grid, head, tail, turned):
    width = head.shape[-1]
    for i in range(turned.shape[0]):
        parts = (grid.part(head, 2, i, 0), grid.part(head, 2, i, 1), grid.part(tail, 1, i, 0))
        for k, part in enumerate(parts):
            turned[i, k * width:(k + 1) * width, :] = part[...].T


def turn(grid, head, tail):
    rows, width = tail.shape[0] // grid.pores, tail.shape[1]
    out = jax.ShapeDtypeStruct((rows, 3 * width, grid.pores), head.dtype)
    return pl.pallas_call(
        functools.partial(turn_kernel, grid),
        grid=(1,),
        in_specs=[resident(head), resident(tail)],
        out_specs=resident(out),
        out_shape=out,
        compiler_params=PARAMS,
        cost_estimate=COST,
        name="turn_rows",
    )(head, tail)


def pick_kernel(grid, plan, layout, carry, tables, lists, filled, passed, *refs):
    wanted = list(refs[:lists])
    sources, at = [], lists
    for blocks in layout:
        sources.append([(refs[at + i], k) for i, k in enumerate(blocks)])
        at += len(blocks)
    scratch = 2 * len(tables) + 1 if tables else 0
    outs = refs[len(refs) - len(filled) - scratch:len(refs) - scratch]
    z, y = grid.spot()

    def list_at(source):
        ref = sources[source][0][0]
        return ref[ref.shape[0] - grid.list_rows:, :]

    if tables:
        numbers, plain, done = refs[-scratch:-1 - len(tables)], refs[-1 - len(tables):-1], refs[-1]
        for table, source in enumerate(tables):
            numbers[table][...] = list_at(source).astype(jnp.float32).astype(jnp.int32)
            pltpu.make_async_copy(numbers[table], plain[table], done.at[table]).start()
        for table in range(len(tables)):
            pltpu.make_async_copy(numbers[table], plain[table], done.at[table]).wait()
        wanted += plain
    for index, list_row, source, output, base in plan(z, y):
        for entry in range(grid.cap):
            row = wanted[index][list_row, entry]
            place = 0
            for ref, blocks in sources[source]:
                for block in range(blocks):
                    target = grid.part(outs[output], filled[output][0], base + entry, place)
                    target[...] = grid.part(ref, blocks, row, block)[...]
                    place += 1
    if passed is not None:
        outs[-1][...] = sources[passed][0][0][...]
    for out, source in zip(outs, carry):
        if source is not None:
            out[out.shape[0] - grid.list_rows:, :] = list_at(source)


def pick(grid, plan, filled, lists, sources, carry=(), tables=(), passed=None, after=(), cost=COST):
    flat = [x for source in sources for x, _ in source]
    width = flat[0].shape[-1]
    carry = carry or (None,) * len(filled)
    shapes = [grid.shape(rows, blocks, width, 0 if source is None else 1)
              for (blocks, rows), source in zip(filled, carry)]
    if passed is not None:
        filled = [*filled, (0, 0)]
        shapes.append(jax.ShapeDtypeStruct(sources[passed][0][0].shape, flat[0].dtype))
    layout = tuple(tuple(blocks for _, blocks in source) for source in sources)
    table = (grid.list_rows, width)
    scratch = [pltpu.VMEM(table, jnp.int32)] * len(tables) + [pltpu.SMEM(table, jnp.int32)] * len(tables)
    scratch += [pltpu.SemaphoreType.DMA((len(tables),))] if tables else []
    return pl.pallas_call(
        functools.partial(pick_kernel, grid, plan, layout, carry, tables, len(lists), tuple(filled), passed),
        grid_spec=pltpu.PrefetchScalarGridSpec(
            num_scalar_prefetch=len(lists),
            grid=(1,),
            in_specs=[*map(resident, flat), *([ANYWHERE] * len(after))],
            out_specs=[*map(resident, shapes)],
            scratch_shapes=scratch,
        ),
        out_shape=shapes,
        compiler_params=PARAMS,
        cost_estimate=cost,
        name="pick_rows",
    )(*lists, *flat, *after)


def stage_kernel(grid, plan, layout, carried, slot_rows, slot_cols, slot_counts, turned, matrix, *refs):
    arrays, at = [], 0
    for blocks in layout:
        arrays.append([(refs[at + i], k, base) for i, (k, base) in enumerate(blocks)])
        at += len(blocks)
    earlier = refs[at:at + 3] if carried else ()
    own, up, down, total = refs[-4:]
    width = own.shape[-1]
    first_group = lax.axis_index("rows") == 0
    for old, new in zip(earlier, (own, up, down)):
        for slot in range(carried):
            for f in range(3):
                new[slot, f] = old[slot, f]
    z, y = grid.spot()
    for slot, (panel, sources) in enumerate(plan(z, y), start=carried):
        total[...] = jnp.zeros_like(total)
        for array, whole, present in sources:
            live = slot_counts[0, panel]
            if present is not True:
                live = jnp.where(present, live, 0)
            parts = arrays[array]

            def product(entry, whole=whole, parts=parts, panel=panel):
                pick = slot_cols[panel, entry] if whole else entry
                right = jnp.concatenate(
                    [grid.part(x, blocks, base + pick, block)[...] for x, blocks, base in parts for block in range(blocks)],
                    axis=1)
                return jnp.dot(matrix[panel, entry], right, preferred_element_type=jnp.float32)

            def add(left, value):
                result = jnp.dot(left, value, preferred_element_type=jnp.float32)
                for k in range(3):
                    total[k] += result[:, k * width:(k + 1) * width]

            def two(u, carry, product=product, panel=panel):
                first, second = 2 * u, 2 * u + 1
                left = jnp.concatenate(
                    [turned[slot_rows[panel, first]], turned[slot_rows[panel, second]]], axis=1)
                value = jnp.concatenate([product(first), product(second)], axis=0).astype(jnp.bfloat16)
                add(left, value)
                return carry

            lax.fori_loop(0, live // 2, two, 0)

            @pl.when(live % 2 == 1)
            def _(live=live, product=product, panel=panel):
                add(turned[slot_rows[panel, live - 1]], product(live - 1).astype(jnp.bfloat16))

        begin = jnp.where(first_group, 0, width)
        for f in range(3):
            k = jnp.where(first_group, (f + 2) % 3, f)
            own[slot, f] = total[k, pl.ds(pl.multiple_of(begin, width), width), :].astype(own.dtype)
            up[slot, f] = total[k, pl.ds(pl.multiple_of(begin + width, width), width), :].astype(up.dtype)
            down[slot, f] = total[k, 0:width, :].astype(down.dtype)


def stage(grid, plan, lists, turned, matrix, sources, earlier=(), after=()):
    width = turned.shape[1] // 3
    carried = earlier[0].shape[0] if earlier else 0
    slots = carried + len(plan(jnp.int32(0), jnp.int32(0)))
    flat = [x for source in sources for x, *_ in source]
    layout = tuple(tuple((blocks, base[0] if base else 0) for _, blocks, *base in source) for source in sources)
    out = jax.ShapeDtypeStruct((slots, 3, width, width), jnp.bfloat16)
    return pl.pallas_call(
        functools.partial(stage_kernel, grid, plan, layout, carried),
        grid_spec=pltpu.PrefetchScalarGridSpec(
            num_scalar_prefetch=3,
            grid=(1,),
            in_specs=[*map(resident, (turned, matrix, *flat, *earlier)), *([ANYWHERE] * len(after))],
            out_specs=[resident(out)] * 3,
            scratch_shapes=[pltpu.VMEM((3, 3 * width, width), jnp.float32)],
        ),
        out_shape=[out] * 3,
        compiler_params=PARAMS,
        cost_estimate=COST,
        name="stage_products",
    )(*lists, turned, matrix, *flat, *earlier, *after)


def assemble_kernel(grid, plans, *refs):
    out = refs[-1]
    rows = refs[0].shape[2]
    panels = grid.panels
    z, y = grid.spot()
    for index, group in enumerate(plans):
        own, lower, upper = refs[3 * index:3 * index + 3]
        slots = [slot for plan in group for slot in plan(z, y)]
        for slot, (panel, _) in enumerate(slots):
            for d in range(5):
                terms = []
                if 0 <= d - 1 < 3:
                    terms.append(own[slot, d - 1].astype(jnp.float32))
                if d < 3:
                    terms.append(lower[slot, d].astype(jnp.float32))
                if 0 <= d - 2 < 3:
                    terms.append(upper[slot, d - 2].astype(jnp.float32))
                out[pl.ds(d * panels + panel, rows, stride=5 * panels), :] = functools.reduce(jnp.add, terms)


def assemble(grid, plans, pieces):
    panels = grid.panels
    width = pieces[0][0].shape[-1]
    rows = width // 4
    flat = [x for piece in pieces for x in piece]
    result = pl.pallas_call(
        functools.partial(assemble_kernel, grid, plans),
        grid=(width // rows,),
        in_specs=[pl.BlockSpec((x.shape[0], 3, rows, width), lambda i: (0, 0, i, 0)) for x in flat],
        out_specs=pl.BlockSpec((rows * 5 * panels, width), lambda i: (i, 0)),
        out_shape=jax.ShapeDtypeStruct((width * 5 * panels, width), jnp.float32),
        compiler_params=PARAMS,
        cost_estimate=COST,
        name="assemble_coarse",
    )(*flat)
    return result.reshape(width, 5, panels, width).transpose(0, 2, 1, 3)


def per_device(fine_blocks, block_rows, block_cols, block_counts, prolong_blocks, prolong_mask):
    matrix = fine_blocks[0, 0]
    cols_list = block_cols[0, 0]
    lists = (block_rows[0, 0], cols_list, block_counts[0])
    groups = lax.axis_size("rows")
    grid = Grid(lax.axis_size("blk"), cols_list.shape[1], matrix.shape[2])
    cap, sides, columns = grid.cap, grid.sides, grid.columns
    every, inner = range(groups), range(1, groups - 1)

    def move(x, pairs, members=every):
        perm = [(a * groups + g, b * groups + g) for g in members for a, b in pairs]
        return lax.ppermute(x, ("blk", "rows"), perm) if perm else jnp.zeros_like(x)

    def move_both(pair, pairs):
        return (move(pair[0][0], pairs), 2), (move(pair[1][0], pairs, inner), 1)

    def move_across(arrays, lines=range(LINES)):
        return [((move(x, grid.across(shift, lines)), 3),) for x, shift in zip(arrays, sides)]

    def exchange(parts):
        lower = lax.ppermute(parts[1], "rows", [(g, g + 1) for g in range(groups - 1)])
        upper = lax.ppermute(parts[2], "rows", [(g + 1, g) for g in range(groups - 1)])
        return parts[0], lower, upper

    count = len(sides)
    mids = (1, 2)

    head, tail = pack(grid, prolong_mask.transpose(2, 0, 1), cols_list, prolong_blocks[0])
    own = ((head, 2), (tail, 1))
    half = move_both(own, grid.swaps([(0, 1), (2, 3)]))
    other = move_both(own, grid.swaps([(1, 2)]))
    side_lists = [move(cols_list, [(b, a) for a, b in grid.across(shift)]) for shift in sides]

    def own_requests(z, y):
        return [(index, grid.panel(z, y, 0), 0, index, 0) for index in range(count)]

    beside = move_across(pick(grid, own_requests, [(3, cap)] * count, side_lists, [own]))
    turned = turn(grid, head, tail)

    far_head = move(half[0][0], grid.swaps([(1, 2)]))

    def early_requests(z, y):
        return [(0, grid.panel(grid.lines(z)[1], y, 0), 0, 0, 0)]

    early, end_list = pick(grid, early_requests, [(2, cap), (0, 0)], [], [other[:1], half[:1]], (None, 1), (1,),
                           cost=COST)
    end_lists = [move(end_list, [(b, a) for a, b in grid.across(shift, mids)]) for shift in sides]
    tables = [(half[0],), *[((x, 0),) for x in end_lists]]
    end_heads = [move(early, grid.ends(0))]

    def near_requests(z, y):
        _, line_other, _ = grid.lines(z)
        requests = []
        for index in range(count):
            requests += [(index, grid.panel(line_other, y, 0), 0, index, 0),
                         (count + 1 + index, grid.panel(line_other, y, 0), 0, count + index, 0)]
        return requests

    picked = pick(grid, near_requests, [(3, cap)] * (2 * count), side_lists, [other, *tables],
                  tables=tuple(range(1, 2 + count)), after=[x for ((x, _),) in beside], cost=COST)
    other_crossed = move_across(picked, mids)
    end_crossed = [((move(x, grid.ends(shift)), 3),) for x, shift in zip(picked[count:], sides)]

    def half_requests(z, y):
        return [(index, grid.panel(grid.lines(z)[0], y, 0), 0, index, 0) for index in range(count)]

    picked = pick(grid, half_requests, [(3, cap)] * count, side_lists, [half], after=[x for ((x, _),) in other_crossed], cost=COST)
    half_crossed = move_across(picked)
    far_tail = move(half[1][0], grid.swaps([(1, 2)]), inner)
    far = ((far_head, 2), (far_tail, 1))
    parts = stage(grid, grid.work_near, lists, turned, matrix, [own, half, *beside])

    def far_requests(z, y):
        return [(index, grid.panel(grid.lines(z)[2], y, 0), 0, index, 0) for index in range(columns)]

    far_picked = pick(grid, far_requests, [(2, cap)] * columns, [], [far[:1], *tables], tables=tuple(range(1, 2 + count)),
                      after=[parts[0]], cost=COST)
    far_heads = [move(x, grid.ends(shift)) for shift, x in enumerate(far_picked)]

    def last_requests(z, y):
        _, line_other, line_far = grid.lines(z)
        row = grid.panel(line_far, y, 0)
        return ([(index, row, 0, index, 0) for index in range(count)] +
                [(count, grid.panel(line_other, y, 0), 1, count, 0), (count, row, 2, count, cap)] +
                [(count + 1 + index, row, 2, count + 1 + index, 0) for index in range(count)])

    picked = pick(grid, last_requests, [(3, cap)] * count + [(1, 2 * cap)] + [(1, cap)] * count, side_lists,
                  [far, other[1:], far[1:], *tables], tables=tuple(range(3, 4 + count)), after=[*far_picked, end_heads[0], *[x for ((x, _),) in end_crossed], *[x for ((x, _),) in other_crossed]],
                  cost=PICK_COST)
    far_crossed = move_across(picked, mids)
    end_tail = move(picked[count], grid.ends(0), inner)
    far_tails = [move(x, grid.ends(shift), inner) for x, shift in zip(picked[count + 1:], sides)]
    sources = []
    for i in range(count):
        sources += [half_crossed[i], other_crossed[i], end_crossed[i]]
    parts = stage(grid, grid.work_middle, lists, turned, matrix, sources, parts, far_heads[:1])
    first = exchange(parts)

    sources = [other, ((end_heads[0], 2), (end_tail, 1, 0)), far, ((far_heads[0], 2), (end_tail, 1, cap))]
    for i in range(count):
        sources += [far_crossed[i], ((far_heads[1 + i], 2), (far_tails[i], 1))]
    last = exchange(stage(grid, grid.work_far, lists, turned, matrix, sources, (), first[1:]))
    return assemble(grid, ((grid.work_near, grid.work_middle), (grid.work_far,)), [first, last])[None, None]


def solution(mesh):
    in_specs = (
        P("rows", "blk", None, None, None, None),
        P("rows", "blk", None, None),
        P("rows", "blk", None, None),
        P("rows", "blk", None),
        P("rows", "blk", None, None),
        P("rows", "blk", None),
    )
    out_specs = P("rows", "blk", None, None, None, None)
    return jax.shard_map(
        per_device, mesh=mesh, in_specs=in_specs, out_specs=out_specs, check_vma=False
    )
```

```python
import functools
import jax
import jax.numpy as jnp
from jax import lax
from jax.experimental import pallas as pl
from jax.experimental.pallas import tpu as pltpu
from jax.sharding import PartitionSpec as P

VMEM_LIMIT = 24 * 1024 * 1024
PACK_VMEM_LIMIT = 60 * 1024 * 1024
PARAMS = pltpu.CompilerParams(vmem_limit_bytes=VMEM_LIMIT)
COST = pl.CostEstimate(flops=1024, bytes_accessed=1024, transcendentals=0)
PICK_COST = pl.CostEstimate(flops=20000000000, bytes_accessed=1024, transcendentals=0)
ANYWHERE = pl.BlockSpec(memory_space=pl.ANY)


def resident(x):
    return pl.BlockSpec(x.shape, lambda i, *_, n=len(x.shape): (0,) * n)


LINES = 4


class Grid:
    def __init__(self, panels, cap, pores):
        self.panels, self.cap, self.pores = panels, cap, pores
        self.columns = panels // LINES
        self.sides = range(1, self.columns)
        self.list_rows = -(-panels // 16) * 16

    def spot(self):
        place = lax.axis_index("blk")
        return place // self.columns, place % self.columns

    def lines(self, z):
        upper = z >= 2
        return jnp.where(z % 2 == 1, z - 1, z + 1), jnp.where(upper, 1, 2), jnp.where(upper, 0, 3)

    def middle(self, z):
        return (z == 1) | (z == 2)

    def panel(self, line, y, shift):
        column = y - shift
        return line * self.columns + jnp.where(column < 0, column + self.columns, column)

    def swaps(self, lines):
        return [(h * self.columns + c, k * self.columns + c)
                for h, k in (*lines, *[(k, h) for h, k in lines]) for c in range(self.columns)]

    def across(self, shift, lines=range(LINES)):
        return [(h * self.columns + c, h * self.columns + (c + shift) % self.columns)
                for h in lines for c in range(self.columns)]

    def ends(self, shift):
        return [(h * self.columns + c, end * self.columns + (c + shift) % self.columns)
                for h, end in ((1, 0), (2, 3)) for c in range(self.columns)]

    def part(self, ref, blocks, row, block):
        start = (row * blocks + block) * self.pores
        if not isinstance(start, int):
            start = pl.multiple_of(start, self.pores)
        return ref.at[pl.ds(start, self.pores), :]

    def shape(self, rows, blocks, width, lists=0):
        return jax.ShapeDtypeStruct((rows * blocks * self.pores + lists * self.list_rows, width), jnp.bfloat16)


    def work_near(self, z, y):
        half, _, _ = self.lines(z)
        return ([(self.panel(z, y, 0), [(0, True, True)]), (self.panel(half, y, 0), [(1, True, True)])] +
                [(self.panel(z, y, shift), [(1 + shift, False, True)]) for shift in self.sides])

    def work_middle(self, z, y):
        half, other, _ = self.lines(z)
        middle = self.middle(z)
        end = jnp.logical_not(middle)
        work = []
        for i, shift in enumerate(self.sides):
            work += [(self.panel(half, y, shift), [(3 * i, False, True)]),
                     (self.panel(other, y, shift), [(3 * i + 1, False, middle), (3 * i + 2, False, end)])]
        return work

    def work_far(self, z, y):
        _, other, far = self.lines(z)
        middle = self.middle(z)
        end = jnp.logical_not(middle)
        return ([(self.panel(other, y, 0), [(0, True, middle), (1, False, end)]),
                 (self.panel(far, y, 0), [(2, True, middle), (3, False, end)])] +
                [(self.panel(far, y, shift), [(2 + 2 * shift, False, middle), (3 + 2 * shift, False, end)])
                 for shift in self.sides])


def pack_kernel(grid, mask_from, cols_from, prolong_from, head, tail, mask, cols, prolong, done):
    group, groups = lax.axis_index("rows"), lax.axis_size("rows")
    width = tail.shape[-1]
    rows = prolong.shape[0]
    step = rows // 4 if rows % 4 == 0 else rows
    copies = [pltpu.make_async_copy(mask_from, mask, done.at[0]), pltpu.make_async_copy(cols_from, cols, done.at[1])]
    for index in range(rows // step):
        some = pl.ds(index * step, step)
        copies.append(pltpu.make_async_copy(prolong_from.at[some], prolong.at[some], done.at[2 + index]))
    for copy in copies:
        copy.start()
    copies[0].wait()
    copies[1].wait()
    for i in range(rows):
        if i % step == 0:
            copies[2 + i // step].wait()
        blocks = []
        for e in range(3):
            candidate = group + e - 1
            keep = (mask[e, 0, i] == 1) & (candidate >= 0) & (candidate < groups)
            block = prolong[i, :, e * width:(e + 1) * width]
            blocks.append(block * jnp.where(keep, 1.0, 0.0).astype(block.dtype))
        grid.part(head, 2, i, 0)[...] = jnp.where(group == 0, blocks[1], blocks[0])
        grid.part(head, 2, i, 1)[...] = jnp.where(group == 0, blocks[2], blocks[1])
        grid.part(tail, 1, i, 0)[...] = jnp.where(group == 0, blocks[0], blocks[2])
    line = lax.broadcasted_iota(jnp.int32, (grid.list_rows, width), 0)
    column = lax.broadcasted_iota(jnp.int32, (grid.list_rows, width), 1)
    numbers = jnp.zeros((grid.list_rows, width), jnp.int32)
    for panel in range(grid.panels):
        for entry in range(grid.cap):
            numbers = jnp.where((line == panel) & (column == entry), cols[panel, entry], numbers)
    start = rows * 2 * grid.pores
    head[start:start + grid.list_rows, :] = numbers.astype(jnp.float32).astype(head.dtype)


def pack(grid, mask, cols, prolong):
    rows, _, width3 = prolong.shape
    outs = [grid.shape(rows, 2, width3 // 3, 1), grid.shape(rows, 1, width3 // 3)]
    return pl.pallas_call(
        functools.partial(pack_kernel, grid),
        grid=(1,),
        in_specs=[pl.BlockSpec(memory_space=pl.ANY)] * 3,
        out_specs=[*map(resident, outs)],
        scratch_shapes=[
            pltpu.SMEM(mask.shape, mask.dtype),
            pltpu.SMEM(cols.shape, cols.dtype),
            pltpu.VMEM(prolong.shape, prolong.dtype),
            pltpu.SemaphoreType.DMA((6,)),
        ],
        out_shape=outs,
        compiler_params=pltpu.CompilerParams(vmem_limit_bytes=PACK_VMEM_LIMIT),
        cost_estimate=COST,
        name="pack_rows",
    )(mask, cols, prolong)


def turn_kernel(grid, head, tail, turned):
    width = head.shape[-1]
    for i in range(turned.shape[0]):
        parts = (grid.part(head, 2, i, 0), grid.part(head, 2, i, 1), grid.part(tail, 1, i, 0))
        for k, part in enumerate(parts):
            turned[i, k * width:(k + 1) * width, :] = part[...].T


def turn(grid, head, tail):
    rows, width = tail.shape[0] // grid.pores, tail.shape[1]
    out = jax.ShapeDtypeStruct((rows, 3 * width, grid.pores), head.dtype)
    return pl.pallas_call(
        functools.partial(turn_kernel, grid),
        grid=(1,),
        in_specs=[resident(head), resident(tail)],
        out_specs=resident(out),
        out_shape=out,
        compiler_params=PARAMS,
        cost_estimate=COST,
        name="turn_rows",
    )(head, tail)


def pick_kernel(grid, plan, layout, carry, tables, lists, filled, passed, *refs):
    wanted = list(refs[:lists])
    sources, at = [], lists
    for blocks in layout:
        sources.append([(refs[at + i], k) for i, k in enumerate(blocks)])
        at += len(blocks)
    scratch = 2 * len(tables) + 1 if tables else 0
    outs = refs[len(refs) - len(filled) - scratch:len(refs) - scratch]
    z, y = grid.spot()

    def list_at(source):
        ref = sources[source][0][0]
        return ref[ref.shape[0] - grid.list_rows:, :]

    if tables:
        numbers, plain, done = refs[-scratch:-1 - len(tables)], refs[-1 - len(tables):-1], refs[-1]
        for table, source in enumerate(tables):
            numbers[table][...] = list_at(source).astype(jnp.float32).astype(jnp.int32)
            pltpu.make_async_copy(numbers[table], plain[table], done.at[table]).start()
        for table in range(len(tables)):
            pltpu.make_async_copy(numbers[table], plain[table], done.at[table]).wait()
        wanted += plain
    for index, list_row, source, output, base in plan(z, y):
        for entry in range(grid.cap):
            row = wanted[index][list_row, entry]
            place = 0
            for ref, blocks in sources[source]:
                for block in range(blocks):
                    target = grid.part(outs[output], filled[output][0], base + entry, place)
                    target[...] = grid.part(ref, blocks, row, block)[...]
                    place += 1
    if passed is not None:
        outs[-1][...] = sources[passed][0][0][...]
    for out, source in zip(outs, carry):
        if source is not None:
            out[out.shape[0] - grid.list_rows:, :] = list_at(source)


def pick(grid, plan, filled, lists, sources, carry=(), tables=(), passed=None, after=(), cost=COST):
    flat = [x for source in sources for x, _ in source]
    width = flat[0].shape[-1]
    carry = carry or (None,) * len(filled)
    shapes = [grid.shape(rows, blocks, width, 0 if source is None else 1)
              for (blocks, rows), source in zip(filled, carry)]
    if passed is not None:
        filled = [*filled, (0, 0)]
        shapes.append(jax.ShapeDtypeStruct(sources[passed][0][0].shape, flat[0].dtype))
    layout = tuple(tuple(blocks for _, blocks in source) for source in sources)
    table = (grid.list_rows, width)
    scratch = [pltpu.VMEM(table, jnp.int32)] * len(tables) + [pltpu.SMEM(table, jnp.int32)] * len(tables)
    scratch += [pltpu.SemaphoreType.DMA((len(tables),))] if tables else []
    return pl.pallas_call(
        functools.partial(pick_kernel, grid, plan, layout, carry, tables, len(lists), tuple(filled), passed),
        grid_spec=pltpu.PrefetchScalarGridSpec(
            num_scalar_prefetch=len(lists),
            grid=(1,),
            in_specs=[*map(resident, flat), *([ANYWHERE] * len(after))],
            out_specs=[*map(resident, shapes)],
            scratch_shapes=scratch,
        ),
        out_shape=shapes,
        compiler_params=PARAMS,
        cost_estimate=cost,
        name="pick_rows",
    )(*lists, *flat, *after)


def stage_kernel(grid, plan, layout, carried, slot_rows, slot_cols, slot_counts, turned, matrix, *refs):
    arrays, at = [], 0
    for blocks in layout:
        arrays.append([(refs[at + i], k, base) for i, (k, base) in enumerate(blocks)])
        at += len(blocks)
    earlier = refs[at:at + 3] if carried else ()
    own, up, down, total = refs[-4:]
    width = own.shape[-1]
    first_group = lax.axis_index("rows") == 0
    for old, new in zip(earlier, (own, up, down)):
        for slot in range(carried):
            for f in range(3):
                new[slot, f] = old[slot, f]
    z, y = grid.spot()
    for slot, (panel, sources) in enumerate(plan(z, y), start=carried):
        total[...] = jnp.zeros_like(total)
        for array, whole, present in sources:
            live = slot_counts[0, panel]
            if present is not True:
                live = jnp.where(present, live, 0)
            parts = arrays[array]

            def product(entry, whole=whole, parts=parts, panel=panel):
                pick = slot_cols[panel, entry] if whole else entry
                right = jnp.concatenate(
                    [grid.part(x, blocks, base + pick, block)[...] for x, blocks, base in parts for block in range(blocks)],
                    axis=1)
                return jnp.dot(matrix[panel, entry], right, preferred_element_type=jnp.float32)

            def add(left, value):
                result = jnp.dot(left, value, preferred_element_type=jnp.float32)
                for k in range(3):
                    total[k] += result[:, k * width:(k + 1) * width]

            def two(u, carry, product=product, panel=panel):
                first, second = 2 * u, 2 * u + 1
                left = jnp.concatenate(
                    [turned[slot_rows[panel, first]], turned[slot_rows[panel, second]]], axis=1)
                value = jnp.concatenate([product(first), product(second)], axis=0).astype(jnp.bfloat16)
                add(left, value)
                return carry

            lax.fori_loop(0, live // 2, two, 0)

            @pl.when(live % 2 == 1)
            def _(live=live, product=product, panel=panel):
                add(turned[slot_rows[panel, live - 1]], product(live - 1).astype(jnp.bfloat16))

        begin = jnp.where(first_group, 0, width)
        for f in range(3):
            k = jnp.where(first_group, (f + 2) % 3, f)
            own[slot, f] = total[k, pl.ds(pl.multiple_of(begin, width), width), :].astype(own.dtype)
            up[slot, f] = total[k, pl.ds(pl.multiple_of(begin + width, width), width), :].astype(up.dtype)
            down[slot, f] = total[k, 0:width, :].astype(down.dtype)


def stage(grid, plan, lists, turned, matrix, sources, earlier=(), after=()):
    width = turned.shape[1] // 3
    carried = earlier[0].shape[0] if earlier else 0
    slots = carried + len(plan(jnp.int32(0), jnp.int32(0)))
    flat = [x for source in sources for x, *_ in source]
    layout = tuple(tuple((blocks, base[0] if base else 0) for _, blocks, *base in source) for source in sources)
    out = jax.ShapeDtypeStruct((slots, 3, width, width), jnp.bfloat16)
    return pl.pallas_call(
        functools.partial(stage_kernel, grid, plan, layout, carried),
        grid_spec=pltpu.PrefetchScalarGridSpec(
            num_scalar_prefetch=3,
            grid=(1,),
            in_specs=[*map(resident, (turned, matrix, *flat, *earlier)), *([ANYWHERE] * len(after))],
            out_specs=[resident(out)] * 3,
            scratch_shapes=[pltpu.VMEM((3, 3 * width, width), jnp.float32)],
        ),
        out_shape=[out] * 3,
        compiler_params=PARAMS,
        cost_estimate=COST,
        name="stage_products",
    )(*lists, turned, matrix, *flat, *earlier, *after)


def assemble_kernel(grid, plans, *refs):
    out = refs[-1]
    rows = refs[0].shape[2]
    panels = grid.panels
    z, y = grid.spot()
    for index, group in enumerate(plans):
        own, lower, upper = refs[3 * index:3 * index + 3]
        slots = [slot for plan in group for slot in plan(z, y)]
        for slot, (panel, _) in enumerate(slots):
            for d in range(5):
                terms = []
                if 0 <= d - 1 < 3:
                    terms.append(own[slot, d - 1].astype(jnp.float32))
                if d < 3:
                    terms.append(lower[slot, d].astype(jnp.float32))
                if 0 <= d - 2 < 3:
                    terms.append(upper[slot, d - 2].astype(jnp.float32))
                out[pl.ds(d * panels + panel, rows, stride=5 * panels), :] = functools.reduce(jnp.add, terms)


def assemble(grid, plans, pieces):
    panels = grid.panels
    width = pieces[0][0].shape[-1]
    rows = width // 4
    flat = [x for piece in pieces for x in piece]
    result = pl.pallas_call(
        functools.partial(assemble_kernel, grid, plans),
        grid=(width // rows,),
        in_specs=[pl.BlockSpec((x.shape[0], 3, rows, width), lambda i: (0, 0, i, 0)) for x in flat],
        out_specs=pl.BlockSpec((rows * 5 * panels, width), lambda i: (i, 0)),
        out_shape=jax.ShapeDtypeStruct((width * 5 * panels, width), jnp.float32),
        compiler_params=PARAMS,
        cost_estimate=COST,
        name="assemble_coarse",
    )(*flat)
    return result.reshape(width, 5, panels, width).transpose(0, 2, 1, 3)


def per_device(fine_blocks, block_rows, block_cols, block_counts, prolong_blocks, prolong_mask):
    matrix = fine_blocks[0, 0]
    cols_list = block_cols[0, 0]
    lists = (block_rows[0, 0], cols_list, block_counts[0])
    groups = lax.axis_size("rows")
    grid = Grid(lax.axis_size("blk"), cols_list.shape[1], matrix.shape[2])
    cap, sides, columns = grid.cap, grid.sides, grid.columns
    every, inner = range(groups), range(1, groups - 1)

    def move(x, pairs, members=every):
        perm = [(a * groups + g, b * groups + g) for g in members for a, b in pairs]
        return lax.ppermute(x, ("blk", "rows"), perm) if perm else jnp.zeros_like(x)

    def move_both(pair, pairs):
        return (move(pair[0][0], pairs), 2), (move(pair[1][0], pairs, inner), 1)

    def move_across(arrays, lines=range(LINES)):
        return [((move(x, grid.across(shift, lines)), 3),) for x, shift in zip(arrays, sides)]

    def exchange(parts):
        lower = lax.ppermute(parts[1], "rows", [(g, g + 1) for g in range(groups - 1)])
        upper = lax.ppermute(parts[2], "rows", [(g + 1, g) for g in range(groups - 1)])
        return parts[0], lower, upper

    count = len(sides)
    mids = (1, 2)

    head, tail = pack(grid, prolong_mask.transpose(2, 0, 1), cols_list, prolong_blocks[0])
    own = ((head, 2), (tail, 1))
    half = move_both(own, grid.swaps([(0, 1), (2, 3)]))
    other = move_both(own, grid.swaps([(1, 2)]))
    side_lists = [move(cols_list, [(b, a) for a, b in grid.across(shift)]) for shift in sides]

    def own_requests(z, y):
        return [(index, grid.panel(z, y, 0), 0, index, 0) for index in range(count)]

    beside = move_across(pick(grid, own_requests, [(3, cap)] * count, side_lists, [own]))
    turned = turn(grid, head, tail)

    far_head = move(half[0][0], grid.swaps([(1, 2)]))

    def early_requests(z, y):
        return [(0, grid.panel(grid.lines(z)[1], y, 0), 0, 0, 0)]

    early, end_list = pick(grid, early_requests, [(2, cap), (0, 0)], [], [other[:1], half[:1]], (None, 1), (1,),
                           cost=COST)
    end_lists = [move(end_list, [(b, a) for a, b in grid.across(shift, mids)]) for shift in sides]
    tables = [(half[0],), *[((x, 0),) for x in end_lists]]
    end_heads = [move(early, grid.ends(0))]

    def other_requests(z, y):
        return [(index, grid.panel(grid.lines(z)[1], y, 0), 0, index, 0) for index in range(count)]

    picked = pick(grid, other_requests, [(3, cap)] * count, side_lists, [other], after=[x for ((x, _),) in beside], cost=COST)
    other_crossed = move_across(picked, mids)
    end_picked = pick(grid, other_requests, [(3, cap)] * count, [], [other, *tables[1:]],
                      tables=tuple(range(1, 1 + count)), after=[*picked, end_heads[0]], cost=COST)
    end_crossed = [((move(x, grid.ends(shift)), 3),) for x, shift in zip(end_picked, sides)]

    def half_requests(z, y):
        return [(index, grid.panel(grid.lines(z)[0], y, 0), 0, index, 0) for index in range(count)]

    picked = pick(grid, half_requests, [(3, cap)] * count, side_lists, [half], after=[x for ((x, _),) in other_crossed], cost=COST)
    half_crossed = move_across(picked)
    far_tail = move(half[1][0], grid.swaps([(1, 2)]), inner)
    far = ((far_head, 2), (far_tail, 1))
    parts = stage(grid, grid.work_near, lists, turned, matrix, [own, half, *beside])

    def far_requests(z, y):
        return [(index, grid.panel(grid.lines(z)[2], y, 0), 0, index, 0) for index in range(columns)]

    far_picked = pick(grid, far_requests, [(2, cap)] * columns, [], [far[:1], *tables], tables=tuple(range(1, 2 + count)),
                      after=[parts[0]], cost=COST)
    far_heads = [move(x, grid.ends(shift)) for shift, x in enumerate(far_picked)]

    def last_requests(z, y):
        _, line_other, line_far = grid.lines(z)
        row = grid.panel(line_far, y, 0)
        return ([(index, row, 0, index, 0) for index in range(count)] +
                [(count, grid.panel(line_other, y, 0), 1, count, 0), (count, row, 2, count, cap)] +
                [(count + 1 + index, row, 2, count + 1 + index, 0) for index in range(count)])

    picked = pick(grid, last_requests, [(3, cap)] * count + [(1, 2 * cap)] + [(1, cap)] * count, side_lists,
                  [far, other[1:], far[1:], *tables], tables=tuple(range(3, 4 + count)), after=[*far_picked, end_heads[0], *[x for ((x, _),) in end_crossed], *[x for ((x, _),) in other_crossed]],
                  cost=PICK_COST)
    far_crossed = move_across(picked, mids)
    end_tail = move(picked[count], grid.ends(0), inner)
    far_tails = [move(x, grid.ends(shift), inner) for x, shift in zip(picked[count + 1:], sides)]
    sources = []
    for i in range(count):
        sources += [half_crossed[i], other_crossed[i], end_crossed[i]]
    parts = stage(grid, grid.work_middle, lists, turned, matrix, sources, parts, ())
    first = exchange(parts)

    sources = [other, ((end_heads[0], 2), (end_tail, 1, 0)), far, ((far_heads[0], 2), (end_tail, 1, cap))]
    for i in range(count):
        sources += [far_crossed[i], ((far_heads[1 + i], 2), (far_tails[i], 1))]
    last = exchange(stage(grid, grid.work_far, lists, turned, matrix, sources, (), first[1:]))
    return assemble(grid, ((grid.work_near, grid.work_middle), (grid.work_far,)), [first, last])[None, None]


def solution(mesh):
    in_specs = (
        P("rows", "blk", None, None, None, None),
        P("rows", "blk", None, None),
        P("rows", "blk", None, None),
        P("rows", "blk", None),
        P("rows", "blk", None, None),
        P("rows", "blk", None),
    )
    out_specs = P("rows", "blk", None, None, None, None)
    return jax.shard_map(
        per_device, mesh=mesh, in_specs=in_specs, out_specs=out_specs, check_vma=False
    )
```

```python
import functools
import jax
import jax.numpy as jnp
from jax import lax
from jax.experimental import pallas as pl
from jax.experimental.pallas import tpu as pltpu
from jax.sharding import PartitionSpec as P

VMEM_LIMIT = 24 * 1024 * 1024
PACK_VMEM_LIMIT = 60 * 1024 * 1024
PARAMS = pltpu.CompilerParams(vmem_limit_bytes=VMEM_LIMIT)
COST = pl.CostEstimate(flops=1024, bytes_accessed=1024, transcendentals=0)
PICK_COST = pl.CostEstimate(flops=20000000000, bytes_accessed=1024, transcendentals=0)
ANYWHERE = pl.BlockSpec(memory_space=pl.ANY)


def resident(x):
    return pl.BlockSpec(x.shape, lambda i, *_, n=len(x.shape): (0,) * n)


LINES = 4


class Grid:
    def __init__(self, panels, cap, pores):
        self.panels, self.cap, self.pores = panels, cap, pores
        self.columns = panels // LINES
        self.sides = range(1, self.columns)
        self.list_rows = -(-panels // 16) * 16

    def spot(self):
        place = lax.axis_index("blk")
        return place // self.columns, place % self.columns

    def lines(self, z):
        upper = z >= 2
        return jnp.where(z % 2 == 1, z - 1, z + 1), jnp.where(upper, 1, 2), jnp.where(upper, 0, 3)

    def middle(self, z):
        return (z == 1) | (z == 2)

    def panel(self, line, y, shift):
        column = y - shift
        return line * self.columns + jnp.where(column < 0, column + self.columns, column)

    def swaps(self, lines):
        return [(h * self.columns + c, k * self.columns + c)
                for h, k in (*lines, *[(k, h) for h, k in lines]) for c in range(self.columns)]

    def across(self, shift, lines=range(LINES)):
        return [(h * self.columns + c, h * self.columns + (c + shift) % self.columns)
                for h in lines for c in range(self.columns)]

    def ends(self, shift):
        return [(h * self.columns + c, end * self.columns + (c + shift) % self.columns)
                for h, end in ((1, 0), (2, 3)) for c in range(self.columns)]

    def part(self, ref, blocks, row, block):
        start = (row * blocks + block) * self.pores
        if not isinstance(start, int):
            start = pl.multiple_of(start, self.pores)
        return ref.at[pl.ds(start, self.pores), :]

    def shape(self, rows, blocks, width, lists=0):
        return jax.ShapeDtypeStruct((rows * blocks * self.pores + lists * self.list_rows, width), jnp.bfloat16)


    def work_near(self, z, y):
        half, _, _ = self.lines(z)
        return ([(self.panel(z, y, 0), [(0, True, True)]), (self.panel(half, y, 0), [(1, True, True)])] +
                [(self.panel(z, y, shift), [(1 + shift, False, True)]) for shift in self.sides])

    def work_middle(self, z, y):
        half, other, _ = self.lines(z)
        middle = self.middle(z)
        end = jnp.logical_not(middle)
        work = []
        for i, shift in enumerate(self.sides):
            work += [(self.panel(half, y, shift), [(3 * i, False, True)]),
                     (self.panel(other, y, shift), [(3 * i + 1, False, middle), (3 * i + 2, False, end)])]
        return work

    def work_far(self, z, y):
        _, other, far = self.lines(z)
        middle = self.middle(z)
        end = jnp.logical_not(middle)
        return ([(self.panel(other, y, 0), [(0, True, middle), (1, False, end)]),
                 (self.panel(far, y, 0), [(2, True, middle), (3, False, end)])] +
                [(self.panel(far, y, shift), [(2 + 2 * shift, False, middle), (3 + 2 * shift, False, end)])
                 for shift in self.sides])


def pack_kernel(grid, mask_from, cols_from, prolong_from, head, tail, mask, cols, prolong, done):
    group, groups = lax.axis_index("rows"), lax.axis_size("rows")
    width = tail.shape[-1]
    rows = prolong.shape[0]
    step = rows // 4 if rows % 4 == 0 else rows
    copies = [pltpu.make_async_copy(mask_from, mask, done.at[0]), pltpu.make_async_copy(cols_from, cols, done.at[1])]
    for index in range(rows // step):
        some = pl.ds(index * step, step)
        copies.append(pltpu.make_async_copy(prolong_from.at[some], prolong.at[some], done.at[2 + index]))
    for copy in copies:
        copy.start()
    copies[0].wait()
    copies[1].wait()
    for i in range(rows):
        if i % step == 0:
            copies[2 + i // step].wait()
        blocks = []
        for e in range(3):
            candidate = group + e - 1
            keep = (mask[e, 0, i] == 1) & (candidate >= 0) & (candidate < groups)
            block = prolong[i, :, e * width:(e + 1) * width]
            blocks.append(block * jnp.where(keep, 1.0, 0.0).astype(block.dtype))
        grid.part(head, 2, i, 0)[...] = jnp.where(group == 0, blocks[1], blocks[0])
        grid.part(head, 2, i, 1)[...] = jnp.where(group == 0, blocks[2], blocks[1])
        grid.part(tail, 1, i, 0)[...] = jnp.where(group == 0, blocks[0], blocks[2])
    line = lax.broadcasted_iota(jnp.int32, (grid.list_rows, width), 0)
    column = lax.broadcasted_iota(jnp.int32, (grid.list_rows, width), 1)
    numbers = jnp.zeros((grid.list_rows, width), jnp.int32)
    for panel in range(grid.panels):
        for entry in range(grid.cap):
            numbers = jnp.where((line == panel) & (column == entry), cols[panel, entry], numbers)
    start = rows * 2 * grid.pores
    head[start:start + grid.list_rows, :] = numbers.astype(jnp.float32).astype(head.dtype)


def pack(grid, mask, cols, prolong):
    rows, _, width3 = prolong.shape
    outs = [grid.shape(rows, 2, width3 // 3, 1), grid.shape(rows, 1, width3 // 3)]
    return pl.pallas_call(
        functools.partial(pack_kernel, grid),
        grid=(1,),
        in_specs=[pl.BlockSpec(memory_space=pl.ANY)] * 3,
        out_specs=[*map(resident, outs)],
        scratch_shapes=[
            pltpu.SMEM(mask.shape, mask.dtype),
            pltpu.SMEM(cols.shape, cols.dtype),
            pltpu.VMEM(prolong.shape, prolong.dtype),
            pltpu.SemaphoreType.DMA((6,)),
        ],
        out_shape=outs,
        compiler_params=pltpu.CompilerParams(vmem_limit_bytes=PACK_VMEM_LIMIT),
        cost_estimate=COST,
        name="pack_rows",
    )(mask, cols, prolong)


def turn_kernel(grid, head, tail, turned):
    width = head.shape[-1]
    for i in range(turned.shape[0]):
        parts = (grid.part(head, 2, i, 0), grid.part(head, 2, i, 1), grid.part(tail, 1, i, 0))
        for k, part in enumerate(parts):
            turned[i, k * width:(k + 1) * width, :] = part[...].T


def turn(grid, head, tail):
    rows, width = tail.shape[0] // grid.pores, tail.shape[1]
    out = jax.ShapeDtypeStruct((rows, 3 * width, grid.pores), head.dtype)
    return pl.pallas_call(
        functools.partial(turn_kernel, grid),
        grid=(1,),
        in_specs=[resident(head), resident(tail)],
        out_specs=resident(out),
        out_shape=out,
        compiler_params=PARAMS,
        cost_estimate=COST,
        name="turn_rows",
    )(head, tail)


def pick_kernel(grid, plan, layout, carry, tables, lists, filled, passed, *refs):
    wanted = list(refs[:lists])
    sources, at = [], lists
    for blocks in layout:
        sources.append([(refs[at + i], k) for i, k in enumerate(blocks)])
        at += len(blocks)
    scratch = 2 * len(tables) + 1 if tables else 0
    outs = refs[len(refs) - len(filled) - scratch:len(refs) - scratch]
    z, y = grid.spot()

    def list_at(source):
        ref = sources[source][0][0]
        return ref[ref.shape[0] - grid.list_rows:, :]

    if tables:
        numbers, plain, done = refs[-scratch:-1 - len(tables)], refs[-1 - len(tables):-1], refs[-1]
        for table, source in enumerate(tables):
            numbers[table][...] = list_at(source).astype(jnp.float32).astype(jnp.int32)
            pltpu.make_async_copy(numbers[table], plain[table], done.at[table]).start()
        for table in range(len(tables)):
            pltpu.make_async_copy(numbers[table], plain[table], done.at[table]).wait()
        wanted += plain
    for index, list_row, source, output, base in plan(z, y):
        for entry in range(grid.cap):
            row = wanted[index][list_row, entry]
            place = 0
            for ref, blocks in sources[source]:
                for block in range(blocks):
                    target = grid.part(outs[output], filled[output][0], base + entry, place)
                    target[...] = grid.part(ref, blocks, row, block)[...]
                    place += 1
    if passed is not None:
        outs[-1][...] = sources[passed][0][0][...]
    for out, source in zip(outs, carry):
        if source is not None:
            out[out.shape[0] - grid.list_rows:, :] = list_at(source)


def pick(grid, plan, filled, lists, sources, carry=(), tables=(), passed=None, after=(), cost=COST):
    flat = [x for source in sources for x, _ in source]
    width = flat[0].shape[-1]
    carry = carry or (None,) * len(filled)
    shapes = [grid.shape(rows, blocks, width, 0 if source is None else 1)
              for (blocks, rows), source in zip(filled, carry)]
    if passed is not None:
        filled = [*filled, (0, 0)]
        shapes.append(jax.ShapeDtypeStruct(sources[passed][0][0].shape, flat[0].dtype))
    layout = tuple(tuple(blocks for _, blocks in source) for source in sources)
    table = (grid.list_rows, width)
    scratch = [pltpu.VMEM(table, jnp.int32)] * len(tables) + [pltpu.SMEM(table, jnp.int32)] * len(tables)
    scratch += [pltpu.SemaphoreType.DMA((len(tables),))] if tables else []
    return pl.pallas_call(
        functools.partial(pick_kernel, grid, plan, layout, carry, tables, len(lists), tuple(filled), passed),
        grid_spec=pltpu.PrefetchScalarGridSpec(
            num_scalar_prefetch=len(lists),
            grid=(1,),
            in_specs=[*map(resident, flat), *([ANYWHERE] * len(after))],
            out_specs=[*map(resident, shapes)],
            scratch_shapes=scratch,
        ),
        out_shape=shapes,
        compiler_params=PARAMS,
        cost_estimate=cost,
        name="pick_rows",
    )(*lists, *flat, *after)


def stage_kernel(grid, plan, layout, carried, slot_rows, slot_cols, slot_counts, turned, matrix, *refs):
    arrays, at = [], 0
    for blocks in layout:
        arrays.append([(refs[at + i], k, base) for i, (k, base) in enumerate(blocks)])
        at += len(blocks)
    earlier = refs[at:at + 3] if carried else ()
    own, up, down, total = refs[-4:]
    width = own.shape[-1]
    first_group = lax.axis_index("rows") == 0
    for old, new in zip(earlier, (own, up, down)):
        for slot in range(carried):
            for f in range(3):
                new[slot, f] = old[slot, f]
    z, y = grid.spot()
    for slot, (panel, sources) in enumerate(plan(z, y), start=carried):
        total[...] = jnp.zeros_like(total)
        for array, whole, present in sources:
            live = slot_counts[0, panel]
            if present is not True:
                live = jnp.where(present, live, 0)
            parts = arrays[array]

            def product(entry, whole=whole, parts=parts, panel=panel):
                pick = slot_cols[panel, entry] if whole else entry
                right = jnp.concatenate(
                    [grid.part(x, blocks, base + pick, block)[...] for x, blocks, base in parts for block in range(blocks)],
                    axis=1)
                return jnp.dot(matrix[panel, entry], right, preferred_element_type=jnp.float32)

            def add(left, value):
                result = jnp.dot(left, value, preferred_element_type=jnp.float32)
                for k in range(3):
                    total[k] += result[:, k * width:(k + 1) * width]

            def two(u, carry, product=product, panel=panel):
                first, second = 2 * u, 2 * u + 1
                left = jnp.concatenate(
                    [turned[slot_rows[panel, first]], turned[slot_rows[panel, second]]], axis=1)
                value = jnp.concatenate([product(first), product(second)], axis=0).astype(jnp.bfloat16)
                add(left, value)
                return carry

            lax.fori_loop(0, live // 2, two, 0)

            @pl.when(live % 2 == 1)
            def _(live=live, product=product, panel=panel):
                add(turned[slot_rows[panel, live - 1]], product(live - 1).astype(jnp.bfloat16))

        begin = jnp.where(first_group, 0, width)
        for f in range(3):
            k = jnp.where(first_group, (f + 2) % 3, f)
            own[slot, f] = total[k, pl.ds(pl.multiple_of(begin, width), width), :].astype(own.dtype)
            up[slot, f] = total[k, pl.ds(pl.multiple_of(begin + width, width), width), :].astype(up.dtype)
            down[slot, f] = total[k, 0:width, :].astype(down.dtype)


def stage(grid, plan, lists, turned, matrix, sources, earlier=(), after=()):
    width = turned.shape[1] // 3
    carried = earlier[0].shape[0] if earlier else 0
    slots = carried + len(plan(jnp.int32(0), jnp.int32(0)))
    flat = [x for source in sources for x, *_ in source]
    layout = tuple(tuple((blocks, base[0] if base else 0) for _, blocks, *base in source) for source in sources)
    out = jax.ShapeDtypeStruct((slots, 3, width, width), jnp.bfloat16)
    return pl.pallas_call(
        functools.partial(stage_kernel, grid, plan, layout, carried),
        grid_spec=pltpu.PrefetchScalarGridSpec(
            num_scalar_prefetch=3,
            grid=(1,),
            in_specs=[*map(resident, (turned, matrix, *flat, *earlier)), *([ANYWHERE] * len(after))],
            out_specs=[resident(out)] * 3,
            scratch_shapes=[pltpu.VMEM((3, 3 * width, width), jnp.float32)],
        ),
        out_shape=[out] * 3,
        compiler_params=PARAMS,
        cost_estimate=COST,
        name="stage_products",
    )(*lists, turned, matrix, *flat, *earlier, *after)


def assemble_kernel(grid, plans, *refs):
    out = refs[-1]
    rows = refs[0].shape[2]
    panels = grid.panels
    z, y = grid.spot()
    for index, group in enumerate(plans):
        own, lower, upper = refs[3 * index:3 * index + 3]
        slots = [slot for plan in group for slot in plan(z, y)]
        for slot, (panel, _) in enumerate(slots):
            for d in range(5):
                terms = []
                if 0 <= d - 1 < 3:
                    terms.append(own[slot, d - 1].astype(jnp.float32))
                if d < 3:
                    terms.append(lower[slot, d].astype(jnp.float32))
                if 0 <= d - 2 < 3:
                    terms.append(upper[slot, d - 2].astype(jnp.float32))
                out[pl.ds(d * panels + panel, rows, stride=5 * panels), :] = functools.reduce(jnp.add, terms)


def assemble(grid, plans, pieces):
    panels = grid.panels
    width = pieces[0][0].shape[-1]
    rows = width // 4
    flat = [x for piece in pieces for x in piece]
    result = pl.pallas_call(
        functools.partial(assemble_kernel, grid, plans),
        grid=(width // rows,),
        in_specs=[pl.BlockSpec((x.shape[0], 3, rows, width), lambda i: (0, 0, i, 0)) for x in flat],
        out_specs=pl.BlockSpec((rows * 5 * panels, width), lambda i: (i, 0)),
        out_shape=jax.ShapeDtypeStruct((width * 5 * panels, width), jnp.float32),
        compiler_params=PARAMS,
        cost_estimate=COST,
        name="assemble_coarse",
    )(*flat)
    return result.reshape(width, 5, panels, width).transpose(0, 2, 1, 3)


def per_device(fine_blocks, block_rows, block_cols, block_counts, prolong_blocks, prolong_mask):
    matrix = fine_blocks[0, 0]
    cols_list = block_cols[0, 0]
    lists = (block_rows[0, 0], cols_list, block_counts[0])
    groups = lax.axis_size("rows")
    grid = Grid(lax.axis_size("blk"), cols_list.shape[1], matrix.shape[2])
    cap, sides, columns = grid.cap, grid.sides, grid.columns
    every, inner = range(groups), range(1, groups - 1)

    def move(x, pairs, members=every):
        perm = [(a * groups + g, b * groups + g) for g in members for a, b in pairs]
        return lax.ppermute(x, ("blk", "rows"), perm) if perm else jnp.zeros_like(x)

    def move_both(pair, pairs):
        return (move(pair[0][0], pairs), 2), (move(pair[1][0], pairs, inner), 1)

    def move_across(arrays, lines=range(LINES)):
        return [((move(x, grid.across(shift, lines)), 3),) for x, shift in zip(arrays, sides)]

    def exchange(parts):
        lower = lax.ppermute(parts[1], "rows", [(g, g + 1) for g in range(groups - 1)])
        upper = lax.ppermute(parts[2], "rows", [(g + 1, g) for g in range(groups - 1)])
        return parts[0], lower, upper

    count = len(sides)
    mids = (1, 2)

    head, tail = pack(grid, prolong_mask.transpose(2, 0, 1), cols_list, prolong_blocks[0])
    own = ((head, 2), (tail, 1))
    half = move_both(own, grid.swaps([(0, 1), (2, 3)]))
    other = move_both(own, grid.swaps([(1, 2)]))
    side_lists = [move(cols_list, [(b, a) for a, b in grid.across(shift)]) for shift in sides]

    def own_requests(z, y):
        return [(index, grid.panel(z, y, 0), 0, index, 0) for index in range(count)]

    beside = move_across(pick(grid, own_requests, [(3, cap)] * count, side_lists, [own]))
    turned = turn(grid, head, tail)

    far_head = move(half[0][0], grid.swaps([(1, 2)]))

    def early_requests(z, y):
        return [(0, grid.panel(grid.lines(z)[1], y, 0), 0, 0, 0)]

    early, end_list = pick(grid, early_requests, [(2, cap), (0, 0)], [], [other[:1], half[:1]], (None, 1), (1,),
                           cost=COST)
    end_lists = [move(end_list, [(b, a) for a, b in grid.across(shift, mids)]) for shift in sides]
    tables = [(half[0],), *[((x, 0),) for x in end_lists]]
    end_heads = [move(early, grid.ends(0))]

    def half_requests(z, y):
        return [(index, grid.panel(grid.lines(z)[0], y, 0), 0, index, 0) for index in range(count)]

    half_picked = pick(grid, half_requests, [(3, cap)] * count, side_lists, [half], after=[x for ((x, _),) in beside], cost=COST)
    half_crossed = move_across(half_picked)

    def other_requests(z, y):
        return [(index, grid.panel(grid.lines(z)[1], y, 0), 0, index, 0) for index in range(count)]

    end_picked = pick(grid, other_requests, [(3, cap)] * count, [], [other, *tables[1:]],
                      tables=tuple(range(1, 1 + count)), after=[*half_picked, end_heads[0]], cost=COST)
    end_crossed = [((move(x, grid.ends(shift)), 3),) for x, shift in zip(end_picked, sides)]
    picked = pick(grid, other_requests, [(3, cap)] * count, side_lists, [other],
                  after=[x for ((x, _),) in half_crossed], cost=COST)
    other_crossed = move_across(picked, mids)
    far_tail = move(half[1][0], grid.swaps([(1, 2)]), inner)
    far = ((far_head, 2), (far_tail, 1))
    parts = stage(grid, grid.work_near, lists, turned, matrix, [own, half, *beside])

    def far_requests(z, y):
        return [(index, grid.panel(grid.lines(z)[2], y, 0), 0, index, 0) for index in range(columns)]

    far_picked = pick(grid, far_requests, [(2, cap)] * columns, [], [far[:1], *tables], tables=tuple(range(1, 2 + count)),
                      after=[parts[0]], cost=COST)
    far_heads = [move(x, grid.ends(shift)) for shift, x in enumerate(far_picked)]

    def last_requests(z, y):
        _, line_other, line_far = grid.lines(z)
        row = grid.panel(line_far, y, 0)
        return ([(index, row, 0, index, 0) for index in range(count)] +
                [(count, grid.panel(line_other, y, 0), 1, count, 0), (count, row, 2, count, cap)] +
                [(count + 1 + index, row, 2, count + 1 + index, 0) for index in range(count)])

    picked = pick(grid, last_requests, [(3, cap)] * count + [(1, 2 * cap)] + [(1, cap)] * count, side_lists,
                  [far, other[1:], far[1:], *tables], tables=tuple(range(3, 4 + count)), after=[*far_picked, end_heads[0], *[x for ((x, _),) in end_crossed], *[x for ((x, _),) in half_crossed]],
                  cost=PICK_COST)
    far_crossed = move_across(picked, mids)
    end_tail = move(picked[count], grid.ends(0), inner)
    far_tails = [move(x, grid.ends(shift), inner) for x, shift in zip(picked[count + 1:], sides)]
    sources = []
    for i in range(count):
        sources += [half_crossed[i], other_crossed[i], end_crossed[i]]
    parts = stage(grid, grid.work_middle, lists, turned, matrix, sources, parts, ())
    first = exchange(parts)

    sources = [other, ((end_heads[0], 2), (end_tail, 1, 0)), far, ((far_heads[0], 2), (end_tail, 1, cap))]
    for i in range(count):
        sources += [far_crossed[i], ((far_heads[1 + i], 2), (far_tails[i], 1))]
    last = exchange(stage(grid, grid.work_far, lists, turned, matrix, sources, (), first[1:]))
    return assemble(grid, ((grid.work_near, grid.work_middle), (grid.work_far,)), [first, last])[None, None]


def solution(mesh):
    in_specs = (
        P("rows", "blk", None, None, None, None),
        P("rows", "blk", None, None),
        P("rows", "blk", None, None),
        P("rows", "blk", None),
        P("rows", "blk", None, None),
        P("rows", "blk", None),
    )
    out_specs = P("rows", "blk", None, None, None, None)
    return jax.shard_map(
        per_device, mesh=mesh, in_specs=in_specs, out_specs=out_specs, check_vma=False
    )
```

```python
import functools
import jax
import jax.numpy as jnp
from jax import lax
from jax.experimental import pallas as pl
from jax.experimental.pallas import tpu as pltpu
from jax.sharding import PartitionSpec as P

VMEM_LIMIT = 24 * 1024 * 1024
PACK_VMEM_LIMIT = 60 * 1024 * 1024
PARAMS = pltpu.CompilerParams(vmem_limit_bytes=VMEM_LIMIT)
COST = pl.CostEstimate(flops=1024, bytes_accessed=1024, transcendentals=0)
ANYWHERE = pl.BlockSpec(memory_space=pl.ANY)


def resident(x):
    return pl.BlockSpec(x.shape, lambda i, *_, n=len(x.shape): (0,) * n)


LINES = 4


class Grid:
    def __init__(self, panels, cap, pores):
        self.panels, self.cap, self.pores = panels, cap, pores
        self.columns = panels // LINES
        self.sides = range(1, self.columns)
        self.list_rows = -(-panels // 16) * 16

    def spot(self):
        place = lax.axis_index("blk")
        return place // self.columns, place % self.columns

    def lines(self, z):
        upper = z >= 2
        return jnp.where(z % 2 == 1, z - 1, z + 1), jnp.where(upper, 1, 2), jnp.where(upper, 0, 3)

    def middle(self, z):
        return (z == 1) | (z == 2)

    def panel(self, line, y, shift):
        column = y - shift
        return line * self.columns + jnp.where(column < 0, column + self.columns, column)

    def swaps(self, lines):
        return [(h * self.columns + c, k * self.columns + c)
                for h, k in (*lines, *[(k, h) for h, k in lines]) for c in range(self.columns)]

    def across(self, shift, lines=range(LINES)):
        return [(h * self.columns + c, h * self.columns + (c + shift) % self.columns)
                for h in lines for c in range(self.columns)]

    def ends(self, shift):
        return [(h * self.columns + c, end * self.columns + (c + shift) % self.columns)
                for h, end in ((1, 0), (2, 3)) for c in range(self.columns)]

    def part(self, ref, blocks, row, block):
        start = (row * blocks + block) * self.pores
        if not isinstance(start, int):
            start = pl.multiple_of(start, self.pores)
        return ref.at[pl.ds(start, self.pores), :]

    def shape(self, rows, blocks, width, lists=0):
        return jax.ShapeDtypeStruct((rows * blocks * self.pores + lists * self.list_rows, width), jnp.bfloat16)


    def work_near(self, z, y):
        half, _, _ = self.lines(z)
        return ([(self.panel(z, y, 0), [(0, True, True)]), (self.panel(half, y, 0), [(1, True, True)])] +
                [(self.panel(z, y, shift), [(1 + shift, False, True)]) for shift in self.sides])

    def work_middle(self, z, y):
        half, other, _ = self.lines(z)
        middle = self.middle(z)
        end = jnp.logical_not(middle)
        work = []
        for i, shift in enumerate(self.sides):
            work += [(self.panel(half, y, shift), [(3 * i, False, True)]),
                     (self.panel(other, y, shift), [(3 * i + 1, False, middle), (3 * i + 2, False, end)])]
        return work

    def work_far(self, z, y):
        _, other, far = self.lines(z)
        middle = self.middle(z)
        end = jnp.logical_not(middle)
        return ([(self.panel(other, y, 0), [(0, True, middle), (1, False, end)]),
                 (self.panel(far, y, 0), [(2, True, middle), (3, False, end)])] +
                [(self.panel(far, y, shift), [(2 + 2 * shift, False, middle), (3 + 2 * shift, False, end)])
                 for shift in self.sides])


def pack_kernel(grid, mask_from, cols_from, prolong_from, head, tail, mask, cols, prolong, done):
    group, groups = lax.axis_index("rows"), lax.axis_size("rows")
    width = tail.shape[-1]
    rows = prolong.shape[0]
    step = rows // 4 if rows % 4 == 0 else rows
    copies = [pltpu.make_async_copy(mask_from, mask, done.at[0]), pltpu.make_async_copy(cols_from, cols, done.at[1])]
    for index in range(rows // step):
        some = pl.ds(index * step, step)
        copies.append(pltpu.make_async_copy(prolong_from.at[some], prolong.at[some], done.at[2 + index]))
    for copy in copies:
        copy.start()
    copies[0].wait()
    copies[1].wait()
    for i in range(rows):
        if i % step == 0:
            copies[2 + i // step].wait()
        blocks = []
        for e in range(3):
            candidate = group + e - 1
            keep = (mask[e, 0, i] == 1) & (candidate >= 0) & (candidate < groups)
            block = prolong[i, :, e * width:(e + 1) * width]
            blocks.append(block * jnp.where(keep, 1.0, 0.0).astype(block.dtype))
        grid.part(head, 2, i, 0)[...] = jnp.where(group == 0, blocks[1], blocks[0])
        grid.part(head, 2, i, 1)[...] = jnp.where(group == 0, blocks[2], blocks[1])
        grid.part(tail, 1, i, 0)[...] = jnp.where(group == 0, blocks[0], blocks[2])
    line = lax.broadcasted_iota(jnp.int32, (grid.list_rows, width), 0)
    column = lax.broadcasted_iota(jnp.int32, (grid.list_rows, width), 1)
    numbers = jnp.zeros((grid.list_rows, width), jnp.int32)
    for panel in range(grid.panels):
        for entry in range(grid.cap):
            numbers = jnp.where((line == panel) & (column == entry), cols[panel, entry], numbers)
    start = rows * 2 * grid.pores
    head[start:start + grid.list_rows, :] = numbers.astype(jnp.float32).astype(head.dtype)


def pack(grid, mask, cols, prolong):
    rows, _, width3 = prolong.shape
    outs = [grid.shape(rows, 2, width3 // 3, 1), grid.shape(rows, 1, width3 // 3)]
    return pl.pallas_call(
        functools.partial(pack_kernel, grid),
        grid=(1,),
        in_specs=[pl.BlockSpec(memory_space=pl.ANY)] * 3,
        out_specs=[*map(resident, outs)],
        scratch_shapes=[
            pltpu.SMEM(mask.shape, mask.dtype),
            pltpu.SMEM(cols.shape, cols.dtype),
            pltpu.VMEM(prolong.shape, prolong.dtype),
            pltpu.SemaphoreType.DMA((6,)),
        ],
        out_shape=outs,
        compiler_params=pltpu.CompilerParams(vmem_limit_bytes=PACK_VMEM_LIMIT),
        cost_estimate=COST,
        name="pack_rows",
    )(mask, cols, prolong)


def turn_kernel(grid, head, tail, turned):
    width = head.shape[-1]
    for i in range(turned.shape[0]):
        parts = (grid.part(head, 2, i, 0), grid.part(head, 2, i, 1), grid.part(tail, 1, i, 0))
        for k, part in enumerate(parts):
            turned[i, k * width:(k + 1) * width, :] = part[...].T


def turn(grid, head, tail):
    rows, width = tail.shape[0] // grid.pores, tail.shape[1]
    out = jax.ShapeDtypeStruct((rows, 3 * width, grid.pores), head.dtype)
    return pl.pallas_call(
        functools.partial(turn_kernel, grid),
        grid=(1,),
        in_specs=[resident(head), resident(tail)],
        out_specs=resident(out),
        out_shape=out,
        compiler_params=PARAMS,
        cost_estimate=COST,
        name="turn_rows",
    )(head, tail)


def pick_kernel(grid, plan, layout, carry, tables, lists, filled, passed, *refs):
    wanted = list(refs[:lists])
    sources, at = [], lists
    for blocks in layout:
        sources.append([(refs[at + i], k) for i, k in enumerate(blocks)])
        at += len(blocks)
    scratch = 2 * len(tables) + 1 if tables else 0
    outs = refs[len(refs) - len(filled) - scratch:len(refs) - scratch]
    z, y = grid.spot()

    def list_at(source):
        ref = sources[source][0][0]
        return ref[ref.shape[0] - grid.list_rows:, :]

    if tables:
        numbers, plain, done = refs[-scratch:-1 - len(tables)], refs[-1 - len(tables):-1], refs[-1]
        for table, source in enumerate(tables):
            numbers[table][...] = list_at(source).astype(jnp.float32).astype(jnp.int32)
            pltpu.make_async_copy(numbers[table], plain[table], done.at[table]).start()
        for table in range(len(tables)):
            pltpu.make_async_copy(numbers[table], plain[table], done.at[table]).wait()
        wanted += plain
    for index, list_row, source, output, base in plan(z, y):
        for entry in range(grid.cap):
            row = wanted[index][list_row, entry]
            place = 0
            for ref, blocks in sources[source]:
                for block in range(blocks):
                    target = grid.part(outs[output], filled[output][0], base + entry, place)
                    target[...] = grid.part(ref, blocks, row, block)[...]
                    place += 1
    if passed is not None:
        outs[-1][...] = sources[passed][0][0][...]
    for out, source in zip(outs, carry):
        if source is not None:
            out[out.shape[0] - grid.list_rows:, :] = list_at(source)


def pick(grid, plan, filled, lists, sources, carry=(), tables=(), passed=None, after=(), cost=COST):
    flat = [x for source in sources for x, _ in source]
    width = flat[0].shape[-1]
    carry = carry or (None,) * len(filled)
    shapes = [grid.shape(rows, blocks, width, 0 if source is None else 1)
              for (blocks, rows), source in zip(filled, carry)]
    if passed is not None:
        filled = [*filled, (0, 0)]
        shapes.append(jax.ShapeDtypeStruct(sources[passed][0][0].shape, flat[0].dtype))
    layout = tuple(tuple(blocks for _, blocks in source) for source in sources)
    table = (grid.list_rows, width)
    scratch = [pltpu.VMEM(table, jnp.int32)] * len(tables) + [pltpu.SMEM(table, jnp.int32)] * len(tables)
    scratch += [pltpu.SemaphoreType.DMA((len(tables),))] if tables else []
    return pl.pallas_call(
        functools.partial(pick_kernel, grid, plan, layout, carry, tables, len(lists), tuple(filled), passed),
        grid_spec=pltpu.PrefetchScalarGridSpec(
            num_scalar_prefetch=len(lists),
            grid=(1,),
            in_specs=[*map(resident, flat), *([ANYWHERE] * len(after))],
            out_specs=[*map(resident, shapes)],
            scratch_shapes=scratch,
        ),
        out_shape=shapes,
        compiler_params=PARAMS,
        cost_estimate=cost,
        name="pick_rows",
    )(*lists, *flat, *after)


def stage_kernel(grid, plan, layout, carried, slot_rows, slot_cols, slot_counts, turned, matrix, *refs):
    arrays, at = [], 0
    for blocks in layout:
        arrays.append([(refs[at + i], k, base) for i, (k, base) in enumerate(blocks)])
        at += len(blocks)
    earlier = refs[at:at + 3] if carried else ()
    own, up, down, total = refs[-4:]
    width = own.shape[-1]
    first_group = lax.axis_index("rows") == 0
    for old, new in zip(earlier, (own, up, down)):
        for slot in range(carried):
            for f in range(3):
                new[slot, f] = old[slot, f]
    z, y = grid.spot()
    for slot, (panel, sources) in enumerate(plan(z, y), start=carried):
        total[...] = jnp.zeros_like(total)
        for array, whole, present in sources:
            live = slot_counts[0, panel]
            if present is not True:
                live = jnp.where(present, live, 0)
            parts = arrays[array]

            def product(entry, whole=whole, parts=parts, panel=panel):
                pick = slot_cols[panel, entry] if whole else entry
                right = jnp.concatenate(
                    [grid.part(x, blocks, base + pick, block)[...] for x, blocks, base in parts for block in range(blocks)],
                    axis=1)
                return jnp.dot(matrix[panel, entry], right, preferred_element_type=jnp.float32)

            def add(left, value):
                result = jnp.dot(left, value, preferred_element_type=jnp.float32)
                for k in range(3):
                    total[k] += result[:, k * width:(k + 1) * width]

            def two(u, carry, product=product, panel=panel):
                first, second = 2 * u, 2 * u + 1
                left = jnp.concatenate(
                    [turned[slot_rows[panel, first]], turned[slot_rows[panel, second]]], axis=1)
                value = jnp.concatenate([product(first), product(second)], axis=0).astype(jnp.bfloat16)
                add(left, value)
                return carry

            lax.fori_loop(0, live // 2, two, 0)

            @pl.when(live % 2 == 1)
            def _(live=live, product=product, panel=panel):
                add(turned[slot_rows[panel, live - 1]], product(live - 1).astype(jnp.bfloat16))

        begin = jnp.where(first_group, 0, width)
        for f in range(3):
            k = jnp.where(first_group, (f + 2) % 3, f)
            own[slot, f] = total[k, pl.ds(pl.multiple_of(begin, width), width), :].astype(own.dtype)
            up[slot, f] = total[k, pl.ds(pl.multiple_of(begin + width, width), width), :].astype(up.dtype)
            down[slot, f] = total[k, 0:width, :].astype(down.dtype)


def stage(grid, plan, lists, turned, matrix, sources, earlier=(), after=()):
    width = turned.shape[1] // 3
    carried = earlier[0].shape[0] if earlier else 0
    slots = carried + len(plan(jnp.int32(0), jnp.int32(0)))
    flat = [x for source in sources for x, *_ in source]
    layout = tuple(tuple((blocks, base[0] if base else 0) for _, blocks, *base in source) for source in sources)
    out = jax.ShapeDtypeStruct((slots, 3, width, width), jnp.bfloat16)
    return pl.pallas_call(
        functools.partial(stage_kernel, grid, plan, layout, carried),
        grid_spec=pltpu.PrefetchScalarGridSpec(
            num_scalar_prefetch=3,
            grid=(1,),
            in_specs=[*map(resident, (turned, matrix, *flat, *earlier)), *([ANYWHERE] * len(after))],
            out_specs=[resident(out)] * 3,
            scratch_shapes=[pltpu.VMEM((3, 3 * width, width), jnp.float32)],
        ),
        out_shape=[out] * 3,
        compiler_params=PARAMS,
        cost_estimate=COST,
        name="stage_products",
    )(*lists, turned, matrix, *flat, *earlier, *after)


def assemble_kernel(grid, plans, *refs):
    out = refs[-1]
    rows = refs[0].shape[2]
    panels = grid.panels
    z, y = grid.spot()
    for index, group in enumerate(plans):
        own, lower, upper = refs[3 * index:3 * index + 3]
        slots = [slot for plan in group for slot in plan(z, y)]
        for slot, (panel, _) in enumerate(slots):
            for d in range(5):
                terms = []
                if 0 <= d - 1 < 3:
                    terms.append(own[slot, d - 1].astype(jnp.float32))
                if d < 3:
                    terms.append(lower[slot, d].astype(jnp.float32))
                if 0 <= d - 2 < 3:
                    terms.append(upper[slot, d - 2].astype(jnp.float32))
                out[pl.ds(d * panels + panel, rows, stride=5 * panels), :] = functools.reduce(jnp.add, terms)


def assemble(grid, plans, pieces):
    panels = grid.panels
    width = pieces[0][0].shape[-1]
    rows = width // 4
    flat = [x for piece in pieces for x in piece]
    result = pl.pallas_call(
        functools.partial(assemble_kernel, grid, plans),
        grid=(width // rows,),
        in_specs=[pl.BlockSpec((x.shape[0], 3, rows, width), lambda i: (0, 0, i, 0)) for x in flat],
        out_specs=pl.BlockSpec((rows * 5 * panels, width), lambda i: (i, 0)),
        out_shape=jax.ShapeDtypeStruct((width * 5 * panels, width), jnp.float32),
        compiler_params=PARAMS,
        cost_estimate=COST,
        name="assemble_coarse",
    )(*flat)
    return result.reshape(width, 5, panels, width).transpose(0, 2, 1, 3)


def per_device(fine_blocks, block_rows, block_cols, block_counts, prolong_blocks, prolong_mask):
    matrix = fine_blocks[0, 0]
    cols_list = block_cols[0, 0]
    lists = (block_rows[0, 0], cols_list, block_counts[0])
    groups = lax.axis_size("rows")
    grid = Grid(lax.axis_size("blk"), cols_list.shape[1], matrix.shape[2])
    cap, sides, columns = grid.cap, grid.sides, grid.columns
    every, inner = range(groups), range(1, groups - 1)

    def move(x, pairs, members=every):
        perm = [(a * groups + g, b * groups + g) for g in members for a, b in pairs]
        return lax.ppermute(x, ("blk", "rows"), perm) if perm else jnp.zeros_like(x)

    def move_both(pair, pairs):
        return (move(pair[0][0], pairs), 2), (move(pair[1][0], pairs, inner), 1)

    def move_across(arrays, lines=range(LINES)):
        return [((move(x, grid.across(shift, lines)), 3),) for x, shift in zip(arrays, sides)]

    def exchange(parts):
        lower = lax.ppermute(parts[1], "rows", [(g, g + 1) for g in range(groups - 1)])
        upper = lax.ppermute(parts[2], "rows", [(g + 1, g) for g in range(groups - 1)])
        return parts[0], lower, upper

    count = len(sides)
    mids = (1, 2)

    head, tail = pack(grid, prolong_mask.transpose(2, 0, 1), cols_list, prolong_blocks[0])
    own = ((head, 2), (tail, 1))
    half = move_both(own, grid.swaps([(0, 1), (2, 3)]))
    other = move_both(own, grid.swaps([(1, 2)]))
    side_lists = [move(cols_list, [(b, a) for a, b in grid.across(shift)]) for shift in sides]

    def own_requests(z, y):
        return [(index, grid.panel(z, y, 0), 0, index, 0) for index in range(count)]

    beside = move_across(pick(grid, own_requests, [(3, cap)] * count, side_lists, [own]))
    turned = turn(grid, head, tail)

    far_head = move(half[0][0], grid.swaps([(1, 2)]))

    def early_requests(z, y):
        return [(0, grid.panel(grid.lines(z)[1], y, 0), 0, 0, 0)]

    early, end_list = pick(grid, early_requests, [(2, cap), (0, 0)], [], [other[:1], half[:1]], (None, 1), (1,),
                           cost=COST)
    end_lists = [move(end_list, [(b, a) for a, b in grid.across(shift, mids)]) for shift in sides]
    tables = [(half[0],), *[((x, 0),) for x in end_lists]]
    end_heads = [move(early, grid.ends(0))]

    def half_requests(z, y):
        return [(index, grid.panel(grid.lines(z)[0], y, 0), 0, index, 0) for index in range(count)]

    half_picked = pick(grid, half_requests, [(3, cap)] * count, side_lists, [half], after=[x for ((x, _),) in beside], cost=COST)
    half_crossed = move_across(half_picked)

    def other_requests(z, y):
        return [(index, grid.panel(grid.lines(z)[1], y, 0), 0, index, 0) for index in range(count)]

    end_picked = pick(grid, other_requests, [(3, cap)] * count, [], [other, *tables[1:]],
                      tables=tuple(range(1, 1 + count)), after=[*half_picked, end_heads[0]], cost=COST)
    end_crossed = [((move(x, grid.ends(shift)), 3),) for x, shift in zip(end_picked, sides)]
    picked = pick(grid, other_requests, [(3, cap)] * count, side_lists, [other],
                  after=[*end_picked], cost=COST)
    other_crossed = move_across(picked, mids)
    far_tail = move(half[1][0], grid.swaps([(1, 2)]), inner)
    far = ((far_head, 2), (far_tail, 1))
    parts = stage(grid, grid.work_near, lists, turned, matrix, [own, half, *beside])

    def far_requests(z, y):
        return [(index, grid.panel(grid.lines(z)[2], y, 0), 0, index, 0) for index in range(columns)]

    far_picked = pick(grid, far_requests, [(2, cap)] * columns, [], [far[:1], *tables], tables=tuple(range(1, 2 + count)),
                      after=[parts[0]], cost=COST)
    far_heads = [move(x, grid.ends(shift)) for shift, x in enumerate(far_picked)]

    def last_requests(z, y):
        _, line_other, line_far = grid.lines(z)
        row = grid.panel(line_far, y, 0)
        return ([(index, row, 0, index, 0) for index in range(count)] +
                [(count, grid.panel(line_other, y, 0), 1, count, 0), (count, row, 2, count, cap)] +
                [(count + 1 + index, row, 2, count + 1 + index, 0) for index in range(count)])

    picked = pick(grid, last_requests, [(3, cap)] * count + [(1, 2 * cap)] + [(1, cap)] * count, side_lists,
                  [far, other[1:], far[1:], *tables], tables=tuple(range(3, 4 + count)), after=[*far_picked, end_heads[0], *[x for ((x, _),) in end_crossed], *[x for ((x, _),) in half_crossed]],
                  cost=COST)
    far_crossed = move_across(picked, mids)
    end_tail = move(picked[count], grid.ends(0), inner)
    far_tails = [move(x, grid.ends(shift), inner) for x, shift in zip(picked[count + 1:], sides)]
    sources = []
    for i in range(count):
        sources += [half_crossed[i], other_crossed[i], end_crossed[i]]
    parts = stage(grid, grid.work_middle, lists, turned, matrix, sources, parts, ())
    first = exchange(parts)

    sources = [other, ((end_heads[0], 2), (end_tail, 1, 0)), far, ((far_heads[0], 2), (end_tail, 1, cap))]
    for i in range(count):
        sources += [far_crossed[i], ((far_heads[1 + i], 2), (far_tails[i], 1))]
    last = exchange(stage(grid, grid.work_far, lists, turned, matrix, sources, (), first[1:]))
    return assemble(grid, ((grid.work_near, grid.work_middle), (grid.work_far,)), [first, last])[None, None]


def solution(mesh):
    in_specs = (
        P("rows", "blk", None, None, None, None),
        P("rows", "blk", None, None),
        P("rows", "blk", None, None),
        P("rows", "blk", None),
        P("rows", "blk", None, None),
        P("rows", "blk", None),
    )
    out_specs = P("rows", "blk", None, None, None, None)
    return jax.shard_map(
        per_device, mesh=mesh, in_specs=in_specs, out_specs=out_specs, check_vma=False
    )
```

```python
import functools
import jax
import jax.numpy as jnp
from jax import lax
from jax.experimental import pallas as pl
from jax.experimental.pallas import tpu as pltpu
from jax.sharding import PartitionSpec as P

VMEM_LIMIT = 24 * 1024 * 1024
PACK_VMEM_LIMIT = 60 * 1024 * 1024
PARAMS = pltpu.CompilerParams(vmem_limit_bytes=VMEM_LIMIT)
COST = pl.CostEstimate(flops=1024, bytes_accessed=1024, transcendentals=0)
ANYWHERE = pl.BlockSpec(memory_space=pl.ANY)


def resident(x):
    return pl.BlockSpec(x.shape, lambda i, *_, n=len(x.shape): (0,) * n)


LINES = 4


class Grid:
    def __init__(self, panels, cap, pores):
        self.panels, self.cap, self.pores = panels, cap, pores
        self.columns = panels // LINES
        self.sides = range(1, self.columns)
        self.list_rows = -(-panels // 16) * 16

    def spot(self):
        place = lax.axis_index("blk")
        return place // self.columns, place % self.columns

    def lines(self, z):
        upper = z >= 2
        return jnp.where(z % 2 == 1, z - 1, z + 1), jnp.where(upper, 1, 2), jnp.where(upper, 0, 3)

    def middle(self, z):
        return (z == 1) | (z == 2)

    def panel(self, line, y, shift):
        column = y - shift
        return line * self.columns + jnp.where(column < 0, column + self.columns, column)

    def swaps(self, lines):
        return [(h * self.columns + c, k * self.columns + c)
                for h, k in (*lines, *[(k, h) for h, k in lines]) for c in range(self.columns)]

    def across(self, shift, lines=range(LINES)):
        return [(h * self.columns + c, h * self.columns + (c + shift) % self.columns)
                for h in lines for c in range(self.columns)]

    def ends(self, shift):
        return [(h * self.columns + c, end * self.columns + (c + shift) % self.columns)
                for h, end in ((1, 0), (2, 3)) for c in range(self.columns)]

    def part(self, ref, blocks, row, block):
        start = (row * blocks + block) * self.pores
        if not isinstance(start, int):
            start = pl.multiple_of(start, self.pores)
        return ref.at[pl.ds(start, self.pores), :]

    def shape(self, rows, blocks, width, lists=0):
        return jax.ShapeDtypeStruct((rows * blocks * self.pores + lists * self.list_rows, width), jnp.bfloat16)


    def work_near(self, z, y):
        half, _, _ = self.lines(z)
        return ([(self.panel(z, y, 0), [(0, True, True)]), (self.panel(half, y, 0), [(1, True, True)])] +
                [(self.panel(z, y, shift), [(1 + shift, False, True)]) for shift in self.sides])

    def work_middle(self, z, y):
        half, other, _ = self.lines(z)
        middle = self.middle(z)
        end = jnp.logical_not(middle)
        work = []
        for i, shift in enumerate(self.sides):
            work += [(self.panel(half, y, shift), [(3 * i, False, True)]),
                     (self.panel(other, y, shift), [(3 * i + 1, False, middle), (3 * i + 2, False, end)])]
        return work

    def work_far(self, z, y):
        _, other, far = self.lines(z)
        middle = self.middle(z)
        end = jnp.logical_not(middle)
        return ([(self.panel(other, y, 0), [(0, True, middle), (1, False, end)]),
                 (self.panel(far, y, 0), [(2, True, middle), (3, False, end)])] +
                [(self.panel(far, y, shift), [(2 + 2 * shift, False, middle), (3 + 2 * shift, False, end)])
                 for shift in self.sides])


def pack_kernel(grid, mask_from, cols_from, prolong_from, head, tail, mask, cols, prolong, done):
    group, groups = lax.axis_index("rows"), lax.axis_size("rows")
    width = tail.shape[-1]
    rows = prolong.shape[0]
    step = rows // 4 if rows % 4 == 0 else rows
    copies = [pltpu.make_async_copy(mask_from, mask, done.at[0]), pltpu.make_async_copy(cols_from, cols, done.at[1])]
    for index in range(rows // step):
        some = pl.ds(index * step, step)
        copies.append(pltpu.make_async_copy(prolong_from.at[some], prolong.at[some], done.at[2 + index]))
    for copy in copies:
        copy.start()
    copies[0].wait()
    copies[1].wait()
    for i in range(rows):
        if i % step == 0:
            copies[2 + i // step].wait()
        blocks = []
        for e in range(3):
            candidate = group + e - 1
            keep = (mask[e, 0, i] == 1) & (candidate >= 0) & (candidate < groups)
            block = prolong[i, :, e * width:(e + 1) * width]
            blocks.append(block * jnp.where(keep, 1.0, 0.0).astype(block.dtype))
        grid.part(head, 2, i, 0)[...] = jnp.where(group == 0, blocks[1], blocks[0])
        grid.part(head, 2, i, 1)[...] = jnp.where(group == 0, blocks[2], blocks[1])
        grid.part(tail, 1, i, 0)[...] = jnp.where(group == 0, blocks[0], blocks[2])
    line = lax.broadcasted_iota(jnp.int32, (grid.list_rows, width), 0)
    column = lax.broadcasted_iota(jnp.int32, (grid.list_rows, width), 1)
    numbers = jnp.zeros((grid.list_rows, width), jnp.int32)
    for panel in range(grid.panels):
        for entry in range(grid.cap):
            numbers = jnp.where((line == panel) & (column == entry), cols[panel, entry], numbers)
    start = rows * 2 * grid.pores
    head[start:start + grid.list_rows, :] = numbers.astype(jnp.float32).astype(head.dtype)


def pack(grid, mask, cols, prolong):
    rows, _, width3 = prolong.shape
    outs = [grid.shape(rows, 2, width3 // 3, 1), grid.shape(rows, 1, width3 // 3)]
    return pl.pallas_call(
        functools.partial(pack_kernel, grid),
        grid=(1,),
        in_specs=[pl.BlockSpec(memory_space=pl.ANY)] * 3,
        out_specs=[*map(resident, outs)],
        scratch_shapes=[
            pltpu.SMEM(mask.shape, mask.dtype),
            pltpu.SMEM(cols.shape, cols.dtype),
            pltpu.VMEM(prolong.shape, prolong.dtype),
            pltpu.SemaphoreType.DMA((6,)),
        ],
        out_shape=outs,
        compiler_params=pltpu.CompilerParams(vmem_limit_bytes=PACK_VMEM_LIMIT),
        cost_estimate=COST,
        name="pack_rows",
    )(mask, cols, prolong)


def turn_kernel(grid, head, tail, turned):
    width = head.shape[-1]
    for i in range(turned.shape[0]):
        parts = (grid.part(head, 2, i, 0), grid.part(head, 2, i, 1), grid.part(tail, 1, i, 0))
        for k, part in enumerate(parts):
            turned[i, k * width:(k + 1) * width, :] = part[...].T


def turn(grid, head, tail):
    rows, width = tail.shape[0] // grid.pores, tail.shape[1]
    out = jax.ShapeDtypeStruct((rows, 3 * width, grid.pores), head.dtype)
    return pl.pallas_call(
        functools.partial(turn_kernel, grid),
        grid=(1,),
        in_specs=[resident(head), resident(tail)],
        out_specs=resident(out),
        out_shape=out,
        compiler_params=PARAMS,
        cost_estimate=COST,
        name="turn_rows",
    )(head, tail)


def pick_kernel(grid, plan, layout, carry, tables, lists, filled, passed, *refs):
    wanted = list(refs[:lists])
    sources, at = [], lists
    for blocks in layout:
        sources.append([(refs[at + i], k) for i, k in enumerate(blocks)])
        at += len(blocks)
    scratch = 2 * len(tables) + 1 if tables else 0
    outs = refs[len(refs) - len(filled) - scratch:len(refs) - scratch]
    z, y = grid.spot()

    def list_at(source):
        ref = sources[source][0][0]
        return ref[ref.shape[0] - grid.list_rows:, :]

    if tables:
        numbers, plain, done = refs[-scratch:-1 - len(tables)], refs[-1 - len(tables):-1], refs[-1]
        for table, source in enumerate(tables):
            numbers[table][...] = list_at(source).astype(jnp.float32).astype(jnp.int32)
            pltpu.make_async_copy(numbers[table], plain[table], done.at[table]).start()
        for table in range(len(tables)):
            pltpu.make_async_copy(numbers[table], plain[table], done.at[table]).wait()
        wanted += plain
    for index, list_row, source, output, base in plan(z, y):
        for entry in range(grid.cap):
            row = wanted[index][list_row, entry]
            place = 0
            for ref, blocks in sources[source]:
                for block in range(blocks):
                    target = grid.part(outs[output], filled[output][0], base + entry, place)
                    target[...] = grid.part(ref, blocks, row, block)[...]
                    place += 1
    if passed is not None:
        outs[-1][...] = sources[passed][0][0][...]
    for out, source in zip(outs, carry):
        if source is not None:
            out[out.shape[0] - grid.list_rows:, :] = list_at(source)


def pick(grid, plan, filled, lists, sources, carry=(), tables=(), passed=None, after=(), cost=COST):
    flat = [x for source in sources for x, _ in source]
    width = flat[0].shape[-1]
    carry = carry or (None,) * len(filled)
    shapes = [grid.shape(rows, blocks, width, 0 if source is None else 1)
              for (blocks, rows), source in zip(filled, carry)]
    if passed is not None:
        filled = [*filled, (0, 0)]
        shapes.append(jax.ShapeDtypeStruct(sources[passed][0][0].shape, flat[0].dtype))
    layout = tuple(tuple(blocks for _, blocks in source) for source in sources)
    table = (grid.list_rows, width)
    scratch = [pltpu.VMEM(table, jnp.int32)] * len(tables) + [pltpu.SMEM(table, jnp.int32)] * len(tables)
    scratch += [pltpu.SemaphoreType.DMA((len(tables),))] if tables else []
    return pl.pallas_call(
        functools.partial(pick_kernel, grid, plan, layout, carry, tables, len(lists), tuple(filled), passed),
        grid_spec=pltpu.PrefetchScalarGridSpec(
            num_scalar_prefetch=len(lists),
            grid=(1,),
            in_specs=[*map(resident, flat), *([ANYWHERE] * len(after))],
            out_specs=[*map(resident, shapes)],
            scratch_shapes=scratch,
        ),
        out_shape=shapes,
        compiler_params=PARAMS,
        cost_estimate=cost,
        name="pick_rows",
    )(*lists, *flat, *after)


def stage_kernel(grid, plan, layout, carried, slot_rows, slot_cols, slot_counts, turned, matrix, *refs):
    arrays, at = [], 0
    for blocks in layout:
        arrays.append([(refs[at + i], k, base) for i, (k, base) in enumerate(blocks)])
        at += len(blocks)
    earlier = refs[at:at + 3] if carried else ()
    own, up, down, total = refs[-4:]
    width = own.shape[-1]
    first_group = lax.axis_index("rows") == 0
    for old, new in zip(earlier, (own, up, down)):
        for slot in range(carried):
            for f in range(3):
                new[slot, f] = old[slot, f]
    z, y = grid.spot()
    for slot, (panel, sources) in enumerate(plan(z, y), start=carried):
        total[...] = jnp.zeros_like(total)
        for array, whole, present in sources:
            live = slot_counts[0, panel]
            if present is not True:
                live = jnp.where(present, live, 0)
            parts = arrays[array]

            def product(entry, whole=whole, parts=parts, panel=panel):
                pick = slot_cols[panel, entry] if whole else entry
                right = jnp.concatenate(
                    [grid.part(x, blocks, base + pick, block)[...] for x, blocks, base in parts for block in range(blocks)],
                    axis=1)
                return jnp.dot(matrix[panel, entry], right, preferred_element_type=jnp.float32)

            def add(left, value):
                result = jnp.dot(left, value, preferred_element_type=jnp.float32)
                for k in range(3):
                    total[k] += result[:, k * width:(k + 1) * width]

            def two(u, carry, product=product, panel=panel):
                first, second = 2 * u, 2 * u + 1
                left = jnp.concatenate(
                    [turned[slot_rows[panel, first]], turned[slot_rows[panel, second]]], axis=1)
                value = jnp.concatenate([product(first), product(second)], axis=0).astype(jnp.bfloat16)
                add(left, value)
                return carry

            lax.fori_loop(0, live // 2, two, 0)

            @pl.when(live % 2 == 1)
            def _(live=live, product=product, panel=panel):
                add(turned[slot_rows[panel, live - 1]], product(live - 1).astype(jnp.bfloat16))

        begin = jnp.where(first_group, 0, width)
        for f in range(3):
            k = jnp.where(first_group, (f + 2) % 3, f)
            own[slot, f] = total[k, pl.ds(pl.multiple_of(begin, width), width), :].astype(own.dtype)
            up[slot, f] = total[k, pl.ds(pl.multiple_of(begin + width, width), width), :].astype(up.dtype)
            down[slot, f] = total[k, 0:width, :].astype(down.dtype)


def stage(grid, plan, lists, turned, matrix, sources, earlier=(), after=()):
    width = turned.shape[1] // 3
    carried = earlier[0].shape[0] if earlier else 0
    slots = carried + len(plan(jnp.int32(0), jnp.int32(0)))
    flat = [x for source in sources for x, *_ in source]
    layout = tuple(tuple((blocks, base[0] if base else 0) for _, blocks, *base in source) for source in sources)
    out = jax.ShapeDtypeStruct((slots, 3, width, width), jnp.bfloat16)
    return pl.pallas_call(
        functools.partial(stage_kernel, grid, plan, layout, carried),
        grid_spec=pltpu.PrefetchScalarGridSpec(
            num_scalar_prefetch=3,
            grid=(1,),
            in_specs=[*map(resident, (turned, matrix, *flat, *earlier)), *([ANYWHERE] * len(after))],
            out_specs=[resident(out)] * 3,
            scratch_shapes=[pltpu.VMEM((3, 3 * width, width), jnp.float32)],
        ),
        out_shape=[out] * 3,
        compiler_params=PARAMS,
        cost_estimate=COST,
        name="stage_products",
    )(*lists, turned, matrix, *flat, *earlier, *after)


def assemble_kernel(grid, plans, *refs):
    out = refs[-1]
    rows = refs[0].shape[2]
    panels = grid.panels
    z, y = grid.spot()
    for index, group in enumerate(plans):
        own, lower, upper = refs[3 * index:3 * index + 3]
        slots = [slot for plan in group for slot in plan(z, y)]
        for slot, (panel, _) in enumerate(slots):
            for d in range(5):
                terms = []
                if 0 <= d - 1 < 3:
                    terms.append(own[slot, d - 1].astype(jnp.float32))
                if d < 3:
                    terms.append(lower[slot, d].astype(jnp.float32))
                if 0 <= d - 2 < 3:
                    terms.append(upper[slot, d - 2].astype(jnp.float32))
                out[pl.ds(d * panels + panel, rows, stride=5 * panels), :] = functools.reduce(jnp.add, terms)


def assemble(grid, plans, pieces):
    panels = grid.panels
    width = pieces[0][0].shape[-1]
    rows = width // 4
    flat = [x for piece in pieces for x in piece]
    result = pl.pallas_call(
        functools.partial(assemble_kernel, grid, plans),
        grid=(width // rows,),
        in_specs=[pl.BlockSpec((x.shape[0], 3, rows, width), lambda i: (0, 0, i, 0)) for x in flat],
        out_specs=pl.BlockSpec((rows * 5 * panels, width), lambda i: (i, 0)),
        out_shape=jax.ShapeDtypeStruct((width * 5 * panels, width), jnp.float32),
        compiler_params=PARAMS,
        cost_estimate=COST,
        name="assemble_coarse",
    )(*flat)
    return result.reshape(width, 5, panels, width).transpose(0, 2, 1, 3)


def per_device(fine_blocks, block_rows, block_cols, block_counts, prolong_blocks, prolong_mask):
    matrix = fine_blocks[0, 0]
    cols_list = block_cols[0, 0]
    lists = (block_rows[0, 0], cols_list, block_counts[0])
    groups = lax.axis_size("rows")
    grid = Grid(lax.axis_size("blk"), cols_list.shape[1], matrix.shape[2])
    cap, sides, columns = grid.cap, grid.sides, grid.columns
    every, inner = range(groups), range(1, groups - 1)

    def move(x, pairs, members=every):
        perm = [(a * groups + g, b * groups + g) for g in members for a, b in pairs]
        return lax.ppermute(x, ("blk", "rows"), perm) if perm else jnp.zeros_like(x)

    def move_both(pair, pairs):
        return (move(pair[0][0], pairs), 2), (move(pair[1][0], pairs, inner), 1)

    def move_across(arrays, lines=range(LINES)):
        return [((move(x, grid.across(shift, lines)), 3),) for x, shift in zip(arrays, sides)]

    def exchange(parts):
        lower = lax.ppermute(parts[1], "rows", [(g, g + 1) for g in range(groups - 1)])
        upper = lax.ppermute(parts[2], "rows", [(g + 1, g) for g in range(groups - 1)])
        return parts[0], lower, upper

    count = len(sides)
    mids = (1, 2)

    head, tail = pack(grid, prolong_mask.transpose(2, 0, 1), cols_list, prolong_blocks[0])
    own = ((head, 2), (tail, 1))
    half = move_both(own, grid.swaps([(0, 1), (2, 3)]))
    other = move_both(own, grid.swaps([(1, 2)]))
    side_lists = [move(cols_list, [(b, a) for a, b in grid.across(shift)]) for shift in sides]

    def own_requests(z, y):
        return [(index, grid.panel(z, y, 0), 0, index, 0) for index in range(count)]

    beside = move_across(pick(grid, own_requests, [(3, cap)] * count, side_lists, [own]))
    turned = turn(grid, head, tail)

    far_head = move(half[0][0], grid.swaps([(1, 2)]))

    def early_requests(z, y):
        return [(0, grid.panel(grid.lines(z)[1], y, 0), 0, 0, 0)]

    early, end_list = pick(grid, early_requests, [(2, cap), (0, 0)], [], [other[:1], half[:1]], (None, 1), (1,),
                           cost=COST)
    end_lists = [move(end_list, [(b, a) for a, b in grid.across(shift, mids)]) for shift in sides]
    tables = [(half[0],), *[((x, 0),) for x in end_lists]]
    end_heads = [move(early, grid.ends(0))]

    def half_requests(z, y):
        return [(index, grid.panel(grid.lines(z)[0], y, 0), 0, index, 0) for index in range(count)]

    half_picked = pick(grid, half_requests, [(3, cap)] * count, side_lists, [half], after=[x for ((x, _),) in beside], cost=COST)
    half_crossed = move_across(half_picked)

    def other_requests(z, y):
        return [(index, grid.panel(grid.lines(z)[1], y, 0), 0, index, 0) for index in range(count)]

    end_picked = pick(grid, other_requests, [(3, cap)] * count, [], [other, *tables[1:]],
                      tables=tuple(range(1, 1 + count)), after=[*half_picked, end_heads[0]], cost=COST)
    end_crossed = [((move(x, grid.ends(shift)), 3),) for x, shift in zip(end_picked, sides)]
    picked = pick(grid, other_requests, [(3, cap)] * count, side_lists, [other],
                  after=[*end_picked], cost=COST)
    other_crossed = move_across(picked, mids)
    far_tail = move(half[1][0], grid.swaps([(1, 2)]), inner)
    far = ((far_head, 2), (far_tail, 1))
    parts = stage(grid, grid.work_near, lists, turned, matrix, [own, half, *beside])

    def far_requests(z, y):
        return [(index, grid.panel(grid.lines(z)[2], y, 0), 0, index, 0) for index in range(columns)]

    far_picked = pick(grid, far_requests, [(2, cap)] * columns, [], [far[:1], *tables], tables=tuple(range(1, 2 + count)),
                      after=[parts[0]], cost=COST)
    far_heads = [move(x, grid.ends(shift)) for shift, x in enumerate(far_picked)]

    def last_requests(z, y):
        _, line_other, line_far = grid.lines(z)
        row = grid.panel(line_far, y, 0)
        return ([(index, row, 0, index, 0) for index in range(count)] +
                [(count, grid.panel(line_other, y, 0), 1, count, 0), (count, row, 2, count, cap)] +
                [(count + 1 + index, row, 2, count + 1 + index, 0) for index in range(count)])

    picked = pick(grid, last_requests, [(3, cap)] * count + [(1, 2 * cap)] + [(1, cap)] * count, side_lists,
                  [far, other[1:], far[1:], *tables], tables=tuple(range(3, 4 + count)), after=[*far_picked, end_heads[0], *[x for ((x, _),) in end_crossed], *[x for ((x, _),) in half_crossed]],
                  cost=COST)
    far_crossed = move_across(picked, mids)
    end_tail = move(picked[count], grid.ends(0), inner)
    far_tails = [move(x, grid.ends(shift), inner) for x, shift in zip(picked[count + 1:], sides)]
    sources = []
    for i in range(count):
        sources += [half_crossed[i], other_crossed[i], end_crossed[i]]
    parts = stage(grid, grid.work_middle, lists, turned, matrix, sources, parts, far_heads[:1])
    first = exchange(parts)

    sources = [other, ((end_heads[0], 2), (end_tail, 1, 0)), far, ((far_heads[0], 2), (end_tail, 1, cap))]
    for i in range(count):
        sources += [far_crossed[i], ((far_heads[1 + i], 2), (far_tails[i], 1))]
    last = exchange(stage(grid, grid.work_far, lists, turned, matrix, sources, (), first[1:2]))
    return assemble(grid, ((grid.work_near, grid.work_middle), (grid.work_far,)), [first, last])[None, None]


def solution(mesh):
    in_specs = (
        P("rows", "blk", None, None, None, None),
        P("rows", "blk", None, None),
        P("rows", "blk", None, None),
        P("rows", "blk", None),
        P("rows", "blk", None, None),
        P("rows", "blk", None),
    )
    out_specs = P("rows", "blk", None, None, None, None)
    return jax.shard_map(
        per_device, mesh=mesh, in_specs=in_specs, out_specs=out_specs, check_vma=False
    )
```

```python
import functools
import jax
import jax.numpy as jnp
from jax import lax
from jax.experimental import pallas as pl
from jax.experimental.pallas import tpu as pltpu
from jax.sharding import PartitionSpec as P

VMEM_LIMIT = 24 * 1024 * 1024
PACK_VMEM_LIMIT = 60 * 1024 * 1024
PARAMS = pltpu.CompilerParams(vmem_limit_bytes=VMEM_LIMIT)
COST = pl.CostEstimate(flops=1024, bytes_accessed=1024, transcendentals=0)
PICK_COST = pl.CostEstimate(flops=20000000000, bytes_accessed=1024, transcendentals=0)
ANYWHERE = pl.BlockSpec(memory_space=pl.ANY)


def resident(x):
    return pl.BlockSpec(x.shape, lambda i, *_, n=len(x.shape): (0,) * n)


LINES = 4


class Grid:
    def __init__(self, panels, cap, pores):
        self.panels, self.cap, self.pores = panels, cap, pores
        self.columns = panels // LINES
        self.sides = range(1, self.columns)
        self.list_rows = -(-panels // 16) * 16

    def spot(self):
        place = lax.axis_index("blk")
        return place // self.columns, place % self.columns

    def lines(self, z):
        upper = z >= 2
        return jnp.where(z % 2 == 1, z - 1, z + 1), jnp.where(upper, 1, 2), jnp.where(upper, 0, 3)

    def middle(self, z):
        return (z == 1) | (z == 2)

    def panel(self, line, y, shift):
        column = y - shift
        return line * self.columns + jnp.where(column < 0, column + self.columns, column)

    def swaps(self, lines):
        return [(h * self.columns + c, k * self.columns + c)
                for h, k in (*lines, *[(k, h) for h, k in lines]) for c in range(self.columns)]

    def across(self, shift, lines=range(LINES)):
        return [(h * self.columns + c, h * self.columns + (c + shift) % self.columns)
                for h in lines for c in range(self.columns)]

    def ends(self, shift):
        return [(h * self.columns + c, end * self.columns + (c + shift) % self.columns)
                for h, end in ((1, 0), (2, 3)) for c in range(self.columns)]

    def part(self, ref, blocks, row, block):
        start = (row * blocks + block) * self.pores
        if not isinstance(start, int):
            start = pl.multiple_of(start, self.pores)
        return ref.at[pl.ds(start, self.pores), :]

    def shape(self, rows, blocks, width, lists=0):
        return jax.ShapeDtypeStruct((rows * blocks * self.pores + lists * self.list_rows, width), jnp.bfloat16)


    def work_near(self, z, y):
        half, _, _ = self.lines(z)
        return ([(self.panel(z, y, 0), [(0, True, True)]), (self.panel(half, y, 0), [(1, True, True)])] +
                [(self.panel(z, y, shift), [(1 + shift, False, True)]) for shift in self.sides])

    def work_middle(self, z, y):
        half, other, _ = self.lines(z)
        middle = self.middle(z)
        end = jnp.logical_not(middle)
        work = []
        for i, shift in enumerate(self.sides):
            work += [(self.panel(half, y, shift), [(3 * i, False, True)]),
                     (self.panel(other, y, shift), [(3 * i + 1, False, middle), (3 * i + 2, False, end)])]
        return work

    def work_far(self, z, y):
        _, other, far = self.lines(z)
        middle = self.middle(z)
        end = jnp.logical_not(middle)
        return ([(self.panel(other, y, 0), [(0, True, middle), (1, False, end)]),
                 (self.panel(far, y, 0), [(2, True, middle), (3, False, end)])] +
                [(self.panel(far, y, shift), [(2 + 2 * shift, False, middle), (3 + 2 * shift, False, end)])
                 for shift in self.sides])


def pack_kernel(grid, mask_from, cols_from, prolong_from, head, tail, mask, cols, prolong, done):
    group, groups = lax.axis_index("rows"), lax.axis_size("rows")
    width = tail.shape[-1]
    rows = prolong.shape[0]
    step = rows // 4 if rows % 4 == 0 else rows
    copies = [pltpu.make_async_copy(mask_from, mask, done.at[0]), pltpu.make_async_copy(cols_from, cols, done.at[1])]
    for index in range(rows // step):
        some = pl.ds(index * step, step)
        copies.append(pltpu.make_async_copy(prolong_from.at[some], prolong.at[some], done.at[2 + index]))
    for copy in copies:
        copy.start()
    copies[0].wait()
    copies[1].wait()
    for i in range(rows):
        if i % step == 0:
            copies[2 + i // step].wait()
        blocks = []
        for e in range(3):
            candidate = group + e - 1
            keep = (mask[e, 0, i] == 1) & (candidate >= 0) & (candidate < groups)
            block = prolong[i, :, e * width:(e + 1) * width]
            blocks.append(block * jnp.where(keep, 1.0, 0.0).astype(block.dtype))
        grid.part(head, 2, i, 0)[...] = jnp.where(group == 0, blocks[1], blocks[0])
        grid.part(head, 2, i, 1)[...] = jnp.where(group == 0, blocks[2], blocks[1])
        grid.part(tail, 1, i, 0)[...] = jnp.where(group == 0, blocks[0], blocks[2])
    line = lax.broadcasted_iota(jnp.int32, (grid.list_rows, width), 0)
    column = lax.broadcasted_iota(jnp.int32, (grid.list_rows, width), 1)
    numbers = jnp.zeros((grid.list_rows, width), jnp.int32)
    for panel in range(grid.panels):
        for entry in range(grid.cap):
            numbers = jnp.where((line == panel) & (column == entry), cols[panel, entry], numbers)
    start = rows * 2 * grid.pores
    head[start:start + grid.list_rows, :] = numbers.astype(jnp.float32).astype(head.dtype)


def pack(grid, mask, cols, prolong):
    rows, _, width3 = prolong.shape
    outs = [grid.shape(rows, 2, width3 // 3, 1), grid.shape(rows, 1, width3 // 3)]
    return pl.pallas_call(
        functools.partial(pack_kernel, grid),
        grid=(1,),
        in_specs=[pl.BlockSpec(memory_space=pl.ANY)] * 3,
        out_specs=[*map(resident, outs)],
        scratch_shapes=[
            pltpu.SMEM(mask.shape, mask.dtype),
            pltpu.SMEM(cols.shape, cols.dtype),
            pltpu.VMEM(prolong.shape, prolong.dtype),
            pltpu.SemaphoreType.DMA((6,)),
        ],
        out_shape=outs,
        compiler_params=pltpu.CompilerParams(vmem_limit_bytes=PACK_VMEM_LIMIT),
        cost_estimate=COST,
        name="pack_rows",
    )(mask, cols, prolong)


def turn_kernel(grid, head, tail, turned):
    width = head.shape[-1]
    for i in range(turned.shape[0]):
        parts = (grid.part(head, 2, i, 0), grid.part(head, 2, i, 1), grid.part(tail, 1, i, 0))
        for k, part in enumerate(parts):
            turned[i, k * width:(k + 1) * width, :] = part[...].T


def turn(grid, head, tail):
    rows, width = tail.shape[0] // grid.pores, tail.shape[1]
    out = jax.ShapeDtypeStruct((rows, 3 * width, grid.pores), head.dtype)
    return pl.pallas_call(
        functools.partial(turn_kernel, grid),
        grid=(1,),
        in_specs=[resident(head), resident(tail)],
        out_specs=resident(out),
        out_shape=out,
        compiler_params=PARAMS,
        cost_estimate=COST,
        name="turn_rows",
    )(head, tail)


def pick_kernel(grid, plan, layout, carry, tables, lists, filled, passed, *refs):
    wanted = list(refs[:lists])
    sources, at = [], lists
    for blocks in layout:
        sources.append([(refs[at + i], k) for i, k in enumerate(blocks)])
        at += len(blocks)
    scratch = 2 * len(tables) + 1 if tables else 0
    outs = refs[len(refs) - len(filled) - scratch:len(refs) - scratch]
    z, y = grid.spot()

    def list_at(source):
        ref = sources[source][0][0]
        return ref[ref.shape[0] - grid.list_rows:, :]

    if tables:
        numbers, plain, done = refs[-scratch:-1 - len(tables)], refs[-1 - len(tables):-1], refs[-1]
        for table, source in enumerate(tables):
            numbers[table][...] = list_at(source).astype(jnp.float32).astype(jnp.int32)
            pltpu.make_async_copy(numbers[table], plain[table], done.at[table]).start()
        for table in range(len(tables)):
            pltpu.make_async_copy(numbers[table], plain[table], done.at[table]).wait()
        wanted += plain
    for index, list_row, source, output, base in plan(z, y):
        for entry in range(grid.cap):
            row = wanted[index][list_row, entry]
            place = 0
            for ref, blocks in sources[source]:
                for block in range(blocks):
                    target = grid.part(outs[output], filled[output][0], base + entry, place)
                    target[...] = grid.part(ref, blocks, row, block)[...]
                    place += 1
    if passed is not None:
        outs[-1][...] = sources[passed][0][0][...]
    for out, source in zip(outs, carry):
        if source is not None:
            out[out.shape[0] - grid.list_rows:, :] = list_at(source)


def pick(grid, plan, filled, lists, sources, carry=(), tables=(), passed=None, after=(), cost=COST):
    flat = [x for source in sources for x, _ in source]
    width = flat[0].shape[-1]
    carry = carry or (None,) * len(filled)
    shapes = [grid.shape(rows, blocks, width, 0 if source is None else 1)
              for (blocks, rows), source in zip(filled, carry)]
    if passed is not None:
        filled = [*filled, (0, 0)]
        shapes.append(jax.ShapeDtypeStruct(sources[passed][0][0].shape, flat[0].dtype))
    layout = tuple(tuple(blocks for _, blocks in source) for source in sources)
    table = (grid.list_rows, width)
    scratch = [pltpu.VMEM(table, jnp.int32)] * len(tables) + [pltpu.SMEM(table, jnp.int32)] * len(tables)
    scratch += [pltpu.SemaphoreType.DMA((len(tables),))] if tables else []
    return pl.pallas_call(
        functools.partial(pick_kernel, grid, plan, layout, carry, tables, len(lists), tuple(filled), passed),
        grid_spec=pltpu.PrefetchScalarGridSpec(
            num_scalar_prefetch=len(lists),
            grid=(1,),
            in_specs=[*map(resident, flat), *([ANYWHERE] * len(after))],
            out_specs=[*map(resident, shapes)],
            scratch_shapes=scratch,
        ),
        out_shape=shapes,
        compiler_params=PARAMS,
        cost_estimate=cost,
        name="pick_rows",
    )(*lists, *flat, *after)


def stage_kernel(grid, plan, layout, carried, slot_rows, slot_cols, slot_counts, turned, matrix, *refs):
    arrays, at = [], 0
    for blocks in layout:
        arrays.append([(refs[at + i], k, base) for i, (k, base) in enumerate(blocks)])
        at += len(blocks)
    earlier = refs[at:at + 3] if carried else ()
    own, up, down, total = refs[-4:]
    width = own.shape[-1]
    first_group = lax.axis_index("rows") == 0
    for old, new in zip(earlier, (own, up, down)):
        for slot in range(carried):
            for f in range(3):
                new[slot, f] = old[slot, f]
    z, y = grid.spot()
    for slot, (panel, sources) in enumerate(plan(z, y), start=carried):
        total[...] = jnp.zeros_like(total)
        for array, whole, present in sources:
            live = slot_counts[0, panel]
            if present is not True:
                live = jnp.where(present, live, 0)
            parts = arrays[array]

            def product(entry, whole=whole, parts=parts, panel=panel):
                pick = slot_cols[panel, entry] if whole else entry
                right = jnp.concatenate(
                    [grid.part(x, blocks, base + pick, block)[...] for x, blocks, base in parts for block in range(blocks)],
                    axis=1)
                return jnp.dot(matrix[panel, entry], right, preferred_element_type=jnp.float32)

            def add(left, value):
                result = jnp.dot(left, value, preferred_element_type=jnp.float32)
                for k in range(3):
                    total[k] += result[:, k * width:(k + 1) * width]

            def two(u, carry, product=product, panel=panel):
                first, second = 2 * u, 2 * u + 1
                left = jnp.concatenate(
                    [turned[slot_rows[panel, first]], turned[slot_rows[panel, second]]], axis=1)
                value = jnp.concatenate([product(first), product(second)], axis=0).astype(jnp.bfloat16)
                add(left, value)
                return carry

            lax.fori_loop(0, live // 2, two, 0)

            @pl.when(live % 2 == 1)
            def _(live=live, product=product, panel=panel):
                add(turned[slot_rows[panel, live - 1]], product(live - 1).astype(jnp.bfloat16))

        begin = jnp.where(first_group, 0, width)
        for f in range(3):
            k = jnp.where(first_group, (f + 2) % 3, f)
            own[slot, f] = total[k, pl.ds(pl.multiple_of(begin, width), width), :].astype(own.dtype)
            up[slot, f] = total[k, pl.ds(pl.multiple_of(begin + width, width), width), :].astype(up.dtype)
            down[slot, f] = total[k, 0:width, :].astype(down.dtype)


def stage(grid, plan, lists, turned, matrix, sources, earlier=(), after=()):
    width = turned.shape[1] // 3
    carried = earlier[0].shape[0] if earlier else 0
    slots = carried + len(plan(jnp.int32(0), jnp.int32(0)))
    flat = [x for source in sources for x, *_ in source]
    layout = tuple(tuple((blocks, base[0] if base else 0) for _, blocks, *base in source) for source in sources)
    out = jax.ShapeDtypeStruct((slots, 3, width, width), jnp.bfloat16)
    return pl.pallas_call(
        functools.partial(stage_kernel, grid, plan, layout, carried),
        grid_spec=pltpu.PrefetchScalarGridSpec(
            num_scalar_prefetch=3,
            grid=(1,),
            in_specs=[*map(resident, (turned, matrix, *flat, *earlier)), *([ANYWHERE] * len(after))],
            out_specs=[resident(out)] * 3,
            scratch_shapes=[pltpu.VMEM((3, 3 * width, width), jnp.float32)],
        ),
        out_shape=[out] * 3,
        compiler_params=PARAMS,
        cost_estimate=COST,
        name="stage_products",
    )(*lists, turned, matrix, *flat, *earlier, *after)


def assemble_kernel(grid, plans, *refs):
    out = refs[-1]
    rows = refs[0].shape[2]
    panels = grid.panels
    z, y = grid.spot()
    for index, group in enumerate(plans):
        own, lower, upper = refs[3 * index:3 * index + 3]
        slots = [slot for plan in group for slot in plan(z, y)]
        for slot, (panel, _) in enumerate(slots):
            for d in range(5):
                terms = []
                if 0 <= d - 1 < 3:
                    terms.append(own[slot, d - 1].astype(jnp.float32))
                if d < 3:
                    terms.append(lower[slot, d].astype(jnp.float32))
                if 0 <= d - 2 < 3:
                    terms.append(upper[slot, d - 2].astype(jnp.float32))
                out[pl.ds(d * panels + panel, rows, stride=5 * panels), :] = functools.reduce(jnp.add, terms)


def assemble(grid, plans, pieces):
    panels = grid.panels
    width = pieces[0][0].shape[-1]
    rows = width // 4
    flat = [x for piece in pieces for x in piece]
    result = pl.pallas_call(
        functools.partial(assemble_kernel, grid, plans),
        grid=(width // rows,),
        in_specs=[pl.BlockSpec((x.shape[0], 3, rows, width), lambda i: (0, 0, i, 0)) for x in flat],
        out_specs=pl.BlockSpec((rows * 5 * panels, width), lambda i: (i, 0)),
        out_shape=jax.ShapeDtypeStruct((width * 5 * panels, width), jnp.float32),
        compiler_params=PARAMS,
        cost_estimate=COST,
        name="assemble_coarse",
    )(*flat)
    return result.reshape(width, 5, panels, width).transpose(0, 2, 1, 3)


def per_device(fine_blocks, block_rows, block_cols, block_counts, prolong_blocks, prolong_mask):
    matrix = fine_blocks[0, 0]
    cols_list = block_cols[0, 0]
    lists = (block_rows[0, 0], cols_list, block_counts[0])
    groups = lax.axis_size("rows")
    grid = Grid(lax.axis_size("blk"), cols_list.shape[1], matrix.shape[2])
    cap, sides, columns = grid.cap, grid.sides, grid.columns
    every, inner = range(groups), range(1, groups - 1)

    def move(x, pairs, members=every):
        perm = [(a * groups + g, b * groups + g) for g in members for a, b in pairs]
        return lax.ppermute(x, ("blk", "rows"), perm) if perm else jnp.zeros_like(x)

    def move_both(pair, pairs):
        return (move(pair[0][0], pairs), 2), (move(pair[1][0], pairs, inner), 1)

    def move_across(arrays, lines=range(LINES)):
        return [((move(x, grid.across(shift, lines)), 3),) for x, shift in zip(arrays, sides)]

    def exchange(parts):
        lower = lax.ppermute(parts[1], "rows", [(g, g + 1) for g in range(groups - 1)])
        upper = lax.ppermute(parts[2], "rows", [(g + 1, g) for g in range(groups - 1)])
        return parts[0], lower, upper

    count = len(sides)
    mids = (1, 2)

    head, tail = pack(grid, prolong_mask.transpose(2, 0, 1), cols_list, prolong_blocks[0])
    own = ((head, 2), (tail, 1))
    half = move_both(own, grid.swaps([(0, 1), (2, 3)]))
    other = move_both(own, grid.swaps([(1, 2)]))
    side_lists = [move(cols_list, [(b, a) for a, b in grid.across(shift)]) for shift in sides]

    def own_requests(z, y):
        return [(index, grid.panel(z, y, 0), 0, index, 0) for index in range(count)]

    beside = move_across(pick(grid, own_requests, [(3, cap)] * count, side_lists, [own]))
    turned = turn(grid, head, tail)

    far_head = move(half[0][0], grid.swaps([(1, 2)]))

    def early_requests(z, y):
        return [(0, grid.panel(grid.lines(z)[1], y, 0), 0, 0, 0)]

    early, end_list = pick(grid, early_requests, [(2, cap), (0, 0)], [], [other[:1], half[:1]], (None, 1), (1,),
                           cost=PICK_COST)
    end_lists = [move(end_list, [(b, a) for a, b in grid.across(shift, mids)]) for shift in sides]
    tables = [(half[0],), *[((x, 0),) for x in end_lists]]
    end_heads = [move(early, grid.ends(0))]

    def half_requests(z, y):
        return [(index, grid.panel(grid.lines(z)[0], y, 0), 0, index, 0) for index in range(count)]

    half_picked = pick(grid, half_requests, [(3, cap)] * count, side_lists, [half], after=[x for ((x, _),) in beside], cost=COST)
    half_crossed = move_across(half_picked)

    def other_requests(z, y):
        return [(index, grid.panel(grid.lines(z)[1], y, 0), 0, index, 0) for index in range(count)]

    end_picked = pick(grid, other_requests, [(3, cap)] * count, [], [other, *tables[1:]],
                      tables=tuple(range(1, 1 + count)), after=[*half_picked, end_heads[0]], cost=COST)
    end_crossed = [((move(x, grid.ends(shift)), 3),) for x, shift in zip(end_picked, sides)]
    picked = pick(grid, other_requests, [(3, cap)] * count, side_lists, [other],
                  after=[*end_picked], cost=COST)
    other_crossed = move_across(picked, mids)
    far_tail = move(half[1][0], grid.swaps([(1, 2)]), inner)
    far = ((far_head, 2), (far_tail, 1))
    parts = stage(grid, grid.work_near, lists, turned, matrix, [own, half, *beside])

    def far_requests(z, y):
        return [(index, grid.panel(grid.lines(z)[2], y, 0), 0, index, 0) for index in range(columns)]

    far_picked = pick(grid, far_requests, [(2, cap)] * columns, [], [far[:1], *tables], tables=tuple(range(1, 2 + count)),
                      after=[parts[0]], cost=COST)
    far_heads = [move(x, grid.ends(shift)) for shift, x in enumerate(far_picked)]

    def last_requests(z, y):
        _, line_other, line_far = grid.lines(z)
        row = grid.panel(line_far, y, 0)
        return ([(index, row, 0, index, 0) for index in range(count)] +
                [(count, grid.panel(line_other, y, 0), 1, count, 0), (count, row, 2, count, cap)] +
                [(count + 1 + index, row, 2, count + 1 + index, 0) for index in range(count)])

    picked = pick(grid, last_requests, [(3, cap)] * count + [(1, 2 * cap)] + [(1, cap)] * count, side_lists,
                  [far, other[1:], far[1:], *tables], tables=tuple(range(3, 4 + count)), after=[*far_picked, far_heads[0], end_heads[0], *[x for ((x, _),) in end_crossed], *[x for ((x, _),) in half_crossed]],
                  cost=COST)
    far_crossed = move_across(picked, mids)
    end_tail = move(picked[count], grid.ends(0), inner)
    far_tails = [move(x, grid.ends(shift), inner) for x, shift in zip(picked[count + 1:], sides)]
    sources = []
    for i in range(count):
        sources += [half_crossed[i], other_crossed[i], end_crossed[i]]
    parts = stage(grid, grid.work_middle, lists, turned, matrix, sources, parts, ())

    sources = [other, ((end_heads[0], 2), (end_tail, 1, 0)), far, ((far_heads[0], 2), (end_tail, 1, cap))]
    for i in range(count):
        sources += [far_crossed[i], ((far_heads[1 + i], 2), (far_tails[i], 1))]
    parts = stage(grid, grid.work_far, lists, turned, matrix, sources, parts)
    return assemble(grid, ((grid.work_near, grid.work_middle, grid.work_far),), [exchange(parts)])[None, None]


def solution(mesh):
    in_specs = (
        P("rows", "blk", None, None, None, None),
        P("rows", "blk", None, None),
        P("rows", "blk", None, None),
        P("rows", "blk", None),
        P("rows", "blk", None, None),
        P("rows", "blk", None),
    )
    out_specs = P("rows", "blk", None, None, None, None)
    return jax.shard_map(
        per_device, mesh=mesh, in_specs=in_specs, out_specs=out_specs, check_vma=False
    )
```

```python
import functools
import jax
import jax.numpy as jnp
from jax import lax
from jax.experimental import pallas as pl
from jax.experimental.pallas import tpu as pltpu
from jax.sharding import PartitionSpec as P

VMEM_LIMIT = 24 * 1024 * 1024
PACK_VMEM_LIMIT = 60 * 1024 * 1024
PARAMS = pltpu.CompilerParams(vmem_limit_bytes=VMEM_LIMIT)
COST = pl.CostEstimate(flops=1024, bytes_accessed=1024, transcendentals=0)
PICK_COST = pl.CostEstimate(flops=20000000000, bytes_accessed=1024, transcendentals=0)
ANYWHERE = pl.BlockSpec(memory_space=pl.ANY)


def resident(x):
    return pl.BlockSpec(x.shape, lambda i, *_, n=len(x.shape): (0,) * n)


LINES = 4


class Grid:
    def __init__(self, panels, cap, pores):
        self.panels, self.cap, self.pores = panels, cap, pores
        self.columns = panels // LINES
        self.sides = range(1, self.columns)
        self.list_rows = -(-panels // 16) * 16

    def spot(self):
        place = lax.axis_index("blk")
        return place // self.columns, place % self.columns

    def lines(self, z):
        upper = z >= 2
        return jnp.where(z % 2 == 1, z - 1, z + 1), jnp.where(upper, 1, 2), jnp.where(upper, 0, 3)

    def middle(self, z):
        return (z == 1) | (z == 2)

    def panel(self, line, y, shift):
        column = y - shift
        return line * self.columns + jnp.where(column < 0, column + self.columns, column)

    def swaps(self, lines):
        return [(h * self.columns + c, k * self.columns + c)
                for h, k in (*lines, *[(k, h) for h, k in lines]) for c in range(self.columns)]

    def across(self, shift, lines=range(LINES)):
        return [(h * self.columns + c, h * self.columns + (c + shift) % self.columns)
                for h in lines for c in range(self.columns)]

    def ends(self, shift):
        return [(h * self.columns + c, end * self.columns + (c + shift) % self.columns)
                for h, end in ((1, 0), (2, 3)) for c in range(self.columns)]

    def part(self, ref, blocks, row, block):
        start = (row * blocks + block) * self.pores
        if not isinstance(start, int):
            start = pl.multiple_of(start, self.pores)
        return ref.at[pl.ds(start, self.pores), :]

    def shape(self, rows, blocks, width, lists=0):
        return jax.ShapeDtypeStruct((rows * blocks * self.pores + lists * self.list_rows, width), jnp.bfloat16)


    def work_near(self, z, y):
        half, _, _ = self.lines(z)
        return ([(self.panel(z, y, 0), [(0, True, True)]), (self.panel(half, y, 0), [(1, True, True)])] +
                [(self.panel(z, y, shift), [(1 + shift, False, True)]) for shift in self.sides])

    def work_middle(self, z, y):
        half, other, _ = self.lines(z)
        middle = self.middle(z)
        end = jnp.logical_not(middle)
        work = []
        for i, shift in enumerate(self.sides):
            work += [(self.panel(half, y, shift), [(3 * i, False, True)]),
                     (self.panel(other, y, shift), [(3 * i + 1, False, middle), (3 * i + 2, False, end)])]
        return work

    def work_far(self, z, y):
        _, other, far = self.lines(z)
        middle = self.middle(z)
        end = jnp.logical_not(middle)
        return ([(self.panel(other, y, 0), [(0, True, middle), (1, False, end)]),
                 (self.panel(far, y, 0), [(2, True, middle), (3, False, end)])] +
                [(self.panel(far, y, shift), [(2 + 2 * shift, False, middle), (3 + 2 * shift, False, end)])
                 for shift in self.sides])


def pack_kernel(grid, mask_from, cols_from, prolong_from, head, tail, mask, cols, prolong, done):
    group, groups = lax.axis_index("rows"), lax.axis_size("rows")
    width = tail.shape[-1]
    rows = prolong.shape[0]
    step = rows // 4 if rows % 4 == 0 else rows
    copies = [pltpu.make_async_copy(mask_from, mask, done.at[0]), pltpu.make_async_copy(cols_from, cols, done.at[1])]
    for index in range(rows // step):
        some = pl.ds(index * step, step)
        copies.append(pltpu.make_async_copy(prolong_from.at[some], prolong.at[some], done.at[2 + index]))
    for copy in copies:
        copy.start()
    copies[0].wait()
    copies[1].wait()
    for i in range(rows):
        if i % step == 0:
            copies[2 + i // step].wait()
        blocks = []
        for e in range(3):
            candidate = group + e - 1
            keep = (mask[e, 0, i] == 1) & (candidate >= 0) & (candidate < groups)
            block = prolong[i, :, e * width:(e + 1) * width]
            blocks.append(block * jnp.where(keep, 1.0, 0.0).astype(block.dtype))
        grid.part(head, 2, i, 0)[...] = jnp.where(group == 0, blocks[1], blocks[0])
        grid.part(head, 2, i, 1)[...] = jnp.where(group == 0, blocks[2], blocks[1])
        grid.part(tail, 1, i, 0)[...] = jnp.where(group == 0, blocks[0], blocks[2])
    line = lax.broadcasted_iota(jnp.int32, (grid.list_rows, width), 0)
    column = lax.broadcasted_iota(jnp.int32, (grid.list_rows, width), 1)
    numbers = jnp.zeros((grid.list_rows, width), jnp.int32)
    for panel in range(grid.panels):
        for entry in range(grid.cap):
            numbers = jnp.where((line == panel) & (column == entry), cols[panel, entry], numbers)
    start = rows * 2 * grid.pores
    head[start:start + grid.list_rows, :] = numbers.astype(jnp.float32).astype(head.dtype)


def pack(grid, mask, cols, prolong):
    rows, _, width3 = prolong.shape
    outs = [grid.shape(rows, 2, width3 // 3, 1), grid.shape(rows, 1, width3 // 3)]
    return pl.pallas_call(
        functools.partial(pack_kernel, grid),
        grid=(1,),
        in_specs=[pl.BlockSpec(memory_space=pl.ANY)] * 3,
        out_specs=[*map(resident, outs)],
        scratch_shapes=[
            pltpu.SMEM(mask.shape, mask.dtype),
            pltpu.SMEM(cols.shape, cols.dtype),
            pltpu.VMEM(prolong.shape, prolong.dtype),
            pltpu.SemaphoreType.DMA((6,)),
        ],
        out_shape=outs,
        compiler_params=pltpu.CompilerParams(vmem_limit_bytes=PACK_VMEM_LIMIT),
        cost_estimate=COST,
        name="pack_rows",
    )(mask, cols, prolong)


def turn_kernel(grid, head, tail, turned):
    width = head.shape[-1]
    for i in range(turned.shape[0]):
        parts = (grid.part(head, 2, i, 0), grid.part(head, 2, i, 1), grid.part(tail, 1, i, 0))
        for k, part in enumerate(parts):
            turned[i, k * width:(k + 1) * width, :] = part[...].T


def turn(grid, head, tail):
    rows, width = tail.shape[0] // grid.pores, tail.shape[1]
    out = jax.ShapeDtypeStruct((rows, 3 * width, grid.pores), head.dtype)
    return pl.pallas_call(
        functools.partial(turn_kernel, grid),
        grid=(1,),
        in_specs=[resident(head), resident(tail)],
        out_specs=resident(out),
        out_shape=out,
        compiler_params=PARAMS,
        cost_estimate=COST,
        name="turn_rows",
    )(head, tail)


def pick_kernel(grid, plan, layout, carry, tables, lists, filled, passed, *refs):
    wanted = list(refs[:lists])
    sources, at = [], lists
    for blocks in layout:
        sources.append([(refs[at + i], k) for i, k in enumerate(blocks)])
        at += len(blocks)
    scratch = 2 * len(tables) + 1 if tables else 0
    outs = refs[len(refs) - len(filled) - scratch:len(refs) - scratch]
    z, y = grid.spot()

    def list_at(source):
        ref = sources[source][0][0]
        return ref[ref.shape[0] - grid.list_rows:, :]

    if tables:
        numbers, plain, done = refs[-scratch:-1 - len(tables)], refs[-1 - len(tables):-1], refs[-1]
        for table, source in enumerate(tables):
            numbers[table][...] = list_at(source).astype(jnp.float32).astype(jnp.int32)
            pltpu.make_async_copy(numbers[table], plain[table], done.at[table]).start()
        for table in range(len(tables)):
            pltpu.make_async_copy(numbers[table], plain[table], done.at[table]).wait()
        wanted += plain
    for index, list_row, source, output, base in plan(z, y):
        for entry in range(grid.cap):
            row = wanted[index][list_row, entry]
            place = 0
            for ref, blocks in sources[source]:
                for block in range(blocks):
                    target = grid.part(outs[output], filled[output][0], base + entry, place)
                    target[...] = grid.part(ref, blocks, row, block)[...]
                    place += 1
    if passed is not None:
        outs[-1][...] = sources[passed][0][0][...]
    for out, source in zip(outs, carry):
        if source is not None:
            out[out.shape[0] - grid.list_rows:, :] = list_at(source)


def pick(grid, plan, filled, lists, sources, carry=(), tables=(), passed=None, after=(), cost=COST):
    flat = [x for source in sources for x, _ in source]
    width = flat[0].shape[-1]
    carry = carry or (None,) * len(filled)
    shapes = [grid.shape(rows, blocks, width, 0 if source is None else 1)
              for (blocks, rows), source in zip(filled, carry)]
    if passed is not None:
        filled = [*filled, (0, 0)]
        shapes.append(jax.ShapeDtypeStruct(sources[passed][0][0].shape, flat[0].dtype))
    layout = tuple(tuple(blocks for _, blocks in source) for source in sources)
    table = (grid.list_rows, width)
    scratch = [pltpu.VMEM(table, jnp.int32)] * len(tables) + [pltpu.SMEM(table, jnp.int32)] * len(tables)
    scratch += [pltpu.SemaphoreType.DMA((len(tables),))] if tables else []
    return pl.pallas_call(
        functools.partial(pick_kernel, grid, plan, layout, carry, tables, len(lists), tuple(filled), passed),
        grid_spec=pltpu.PrefetchScalarGridSpec(
            num_scalar_prefetch=len(lists),
            grid=(1,),
            in_specs=[*map(resident, flat), *([ANYWHERE] * len(after))],
            out_specs=[*map(resident, shapes)],
            scratch_shapes=scratch,
        ),
        out_shape=shapes,
        compiler_params=PARAMS,
        cost_estimate=cost,
        name="pick_rows",
    )(*lists, *flat, *after)


def stage_kernel(grid, plan, layout, carried, slot_rows, slot_cols, slot_counts, turned, matrix, *refs):
    arrays, at = [], 0
    for blocks in layout:
        arrays.append([(refs[at + i], k, base) for i, (k, base) in enumerate(blocks)])
        at += len(blocks)
    earlier = refs[at:at + 3] if carried else ()
    own, up, down, total = refs[-4:]
    width = own.shape[-1]
    first_group = lax.axis_index("rows") == 0
    for old, new in zip(earlier, (own, up, down)):
        for slot in range(carried):
            for f in range(3):
                new[slot, f] = old[slot, f]
    z, y = grid.spot()
    for slot, (panel, sources) in enumerate(plan(z, y), start=carried):
        total[...] = jnp.zeros_like(total)
        for array, whole, present in sources:
            live = slot_counts[0, panel]
            if present is not True:
                live = jnp.where(present, live, 0)
            parts = arrays[array]

            def product(entry, whole=whole, parts=parts, panel=panel):
                pick = slot_cols[panel, entry] if whole else entry
                right = jnp.concatenate(
                    [grid.part(x, blocks, base + pick, block)[...] for x, blocks, base in parts for block in range(blocks)],
                    axis=1)
                return jnp.dot(matrix[panel, entry], right, preferred_element_type=jnp.float32)

            def add(left, value):
                result = jnp.dot(left, value, preferred_element_type=jnp.float32)
                for k in range(3):
                    total[k] += result[:, k * width:(k + 1) * width]

            def two(u, carry, product=product, panel=panel):
                first, second = 2 * u, 2 * u + 1
                left = jnp.concatenate(
                    [turned[slot_rows[panel, first]], turned[slot_rows[panel, second]]], axis=1)
                value = jnp.concatenate([product(first), product(second)], axis=0).astype(jnp.bfloat16)
                add(left, value)
                return carry

            lax.fori_loop(0, live // 2, two, 0)

            @pl.when(live % 2 == 1)
            def _(live=live, product=product, panel=panel):
                add(turned[slot_rows[panel, live - 1]], product(live - 1).astype(jnp.bfloat16))

        begin = jnp.where(first_group, 0, width)
        for f in range(3):
            k = jnp.where(first_group, (f + 2) % 3, f)
            own[slot, f] = total[k, pl.ds(pl.multiple_of(begin, width), width), :].astype(own.dtype)
            up[slot, f] = total[k, pl.ds(pl.multiple_of(begin + width, width), width), :].astype(up.dtype)
            down[slot, f] = total[k, 0:width, :].astype(down.dtype)


def stage(grid, plan, lists, turned, matrix, sources, earlier=(), after=()):
    width = turned.shape[1] // 3
    carried = earlier[0].shape[0] if earlier else 0
    slots = carried + len(plan(jnp.int32(0), jnp.int32(0)))
    flat = [x for source in sources for x, *_ in source]
    layout = tuple(tuple((blocks, base[0] if base else 0) for _, blocks, *base in source) for source in sources)
    out = jax.ShapeDtypeStruct((slots, 3, width, width), jnp.bfloat16)
    return pl.pallas_call(
        functools.partial(stage_kernel, grid, plan, layout, carried),
        grid_spec=pltpu.PrefetchScalarGridSpec(
            num_scalar_prefetch=3,
            grid=(1,),
            in_specs=[*map(resident, (turned, matrix, *flat, *earlier)), *([ANYWHERE] * len(after))],
            out_specs=[resident(out)] * 3,
            scratch_shapes=[pltpu.VMEM((3, 3 * width, width), jnp.float32)],
        ),
        out_shape=[out] * 3,
        compiler_params=PARAMS,
        cost_estimate=COST,
        name="stage_products",
    )(*lists, turned, matrix, *flat, *earlier, *after)


def assemble_kernel(grid, plans, *refs):
    out = refs[-1]
    rows = refs[0].shape[2]
    panels = grid.panels
    z, y = grid.spot()
    for index, group in enumerate(plans):
        own, lower, upper = refs[3 * index:3 * index + 3]
        slots = [slot for plan in group for slot in plan(z, y)]
        for slot, (panel, _) in enumerate(slots):
            for d in range(5):
                terms = []
                if 0 <= d - 1 < 3:
                    terms.append(own[slot, d - 1].astype(jnp.float32))
                if d < 3:
                    terms.append(lower[slot, d].astype(jnp.float32))
                if 0 <= d - 2 < 3:
                    terms.append(upper[slot, d - 2].astype(jnp.float32))
                out[pl.ds(d * panels + panel, rows, stride=5 * panels), :] = functools.reduce(jnp.add, terms)


def assemble(grid, plans, pieces):
    panels = grid.panels
    width = pieces[0][0].shape[-1]
    rows = width // 4
    flat = [x for piece in pieces for x in piece]
    result = pl.pallas_call(
        functools.partial(assemble_kernel, grid, plans),
        grid=(width // rows,),
        in_specs=[pl.BlockSpec((x.shape[0], 3, rows, width), lambda i: (0, 0, i, 0)) for x in flat],
        out_specs=pl.BlockSpec((rows * 5 * panels, width), lambda i: (i, 0)),
        out_shape=jax.ShapeDtypeStruct((width * 5 * panels, width), jnp.float32),
        compiler_params=PARAMS,
        cost_estimate=COST,
        name="assemble_coarse",
    )(*flat)
    return result.reshape(width, 5, panels, width).transpose(0, 2, 1, 3)


def per_device(fine_blocks, block_rows, block_cols, block_counts, prolong_blocks, prolong_mask):
    matrix = fine_blocks[0, 0]
    cols_list = block_cols[0, 0]
    lists = (block_rows[0, 0], cols_list, block_counts[0])
    groups = lax.axis_size("rows")
    grid = Grid(lax.axis_size("blk"), cols_list.shape[1], matrix.shape[2])
    cap, sides, columns = grid.cap, grid.sides, grid.columns
    every, inner = range(groups), range(1, groups - 1)

    def move(x, pairs, members=every):
        perm = [(a * groups + g, b * groups + g) for g in members for a, b in pairs]
        return lax.ppermute(x, ("blk", "rows"), perm) if perm else jnp.zeros_like(x)

    def move_both(pair, pairs):
        return (move(pair[0][0], pairs), 2), (move(pair[1][0], pairs, inner), 1)

    def move_across(arrays, lines=range(LINES)):
        return [((move(x, grid.across(shift, lines)), 3),) for x, shift in zip(arrays, sides)]

    def exchange(parts):
        lower = lax.ppermute(parts[1], "rows", [(g, g + 1) for g in range(groups - 1)])
        upper = lax.ppermute(parts[2], "rows", [(g + 1, g) for g in range(groups - 1)])
        return parts[0], lower, upper

    count = len(sides)
    mids = (1, 2)

    head, tail = pack(grid, prolong_mask.transpose(2, 0, 1), cols_list, prolong_blocks[0])
    own = ((head, 2), (tail, 1))
    half = move_both(own, grid.swaps([(0, 1), (2, 3)]))
    other = move_both(own, grid.swaps([(1, 2)]))
    side_lists = [move(cols_list, [(b, a) for a, b in grid.across(shift)]) for shift in sides]

    def own_requests(z, y):
        return [(index, grid.panel(z, y, 0), 0, index, 0) for index in range(count)]

    beside = move_across(pick(grid, own_requests, [(3, cap)] * count, side_lists, [own]))
    turned = turn(grid, head, tail)

    far_head = move(half[0][0], grid.swaps([(1, 2)]))

    def early_requests(z, y):
        return [(0, grid.panel(grid.lines(z)[1], y, 0), 0, 0, 0)]

    early, end_list = pick(grid, early_requests, [(2, cap), (0, 0)], [], [other[:1], half[:1]], (None, 1), (1,),
                           cost=PICK_COST)
    end_lists = [move(end_list, [(b, a) for a, b in grid.across(shift, mids)]) for shift in sides]
    tables = [(half[0],), *[((x, 0),) for x in end_lists]]
    end_heads = [move(early, grid.ends(0))]

    def half_requests(z, y):
        return [(index, grid.panel(grid.lines(z)[0], y, 0), 0, index, 0) for index in range(count)]

    half_picked = pick(grid, half_requests, [(3, cap)] * count, side_lists, [half], after=[x for ((x, _),) in beside], cost=COST)
    half_crossed = move_across(half_picked)

    def other_requests(z, y):
        return [(index, grid.panel(grid.lines(z)[1], y, 0), 0, index, 0) for index in range(count)]

    end_picked = pick(grid, other_requests, [(3, cap)] * count, [], [other, *tables[1:]],
                      tables=tuple(range(1, 1 + count)), after=[*half_picked, end_heads[0]], cost=COST)
    end_crossed = [((move(x, grid.ends(shift)), 3),) for x, shift in zip(end_picked, sides)]
    picked = pick(grid, other_requests, [(3, cap)] * count, side_lists, [other],
                  after=[*end_picked], cost=COST)
    other_crossed = move_across(picked, mids)
    far_tail = move(half[1][0], grid.swaps([(1, 2)]), inner)
    far = ((far_head, 2), (far_tail, 1))
    parts = stage(grid, grid.work_near, lists, turned, matrix, [own, half, *beside])

    def far_requests(z, y):
        return [(index, grid.panel(grid.lines(z)[2], y, 0), 0, index, 0) for index in range(columns)]

    far_picked = pick(grid, far_requests, [(2, cap)] * columns, [], [far[:1], *tables], tables=tuple(range(1, 2 + count)),
                      after=[parts[0]], cost=COST)
    far_heads = [move(x, grid.ends(shift)) for shift, x in enumerate(far_picked)]

    def last_requests(z, y):
        _, line_other, line_far = grid.lines(z)
        row = grid.panel(line_far, y, 0)
        return ([(index, row, 0, index, 0) for index in range(count)] +
                [(count, grid.panel(line_other, y, 0), 1, count, 0), (count, row, 2, count, cap)] +
                [(count + 1 + index, row, 2, count + 1 + index, 0) for index in range(count)])

    picked = pick(grid, last_requests, [(3, cap)] * count + [(1, 2 * cap)] + [(1, cap)] * count, side_lists,
                  [far, other[1:], far[1:], *tables], tables=tuple(range(3, 4 + count)), after=[*far_picked, far_heads[0], end_heads[0], *[x for ((x, _),) in end_crossed], *[x for ((x, _),) in half_crossed]],
                  cost=COST)
    far_crossed = move_across(picked, mids)
    end_tail = move(picked[count], grid.ends(0), inner)
    far_tails = [move(x, grid.ends(shift), inner) for x, shift in zip(picked[count + 1:], sides)]
    sources = []
    for i in range(count):
        sources += [half_crossed[i], other_crossed[i], end_crossed[i]]
    parts = stage(grid, grid.work_middle, lists, turned, matrix, sources, parts, far_tails)
    first = exchange(parts)

    sources = [other, ((end_heads[0], 2), (end_tail, 1, 0)), far, ((far_heads[0], 2), (end_tail, 1, cap))]
    for i in range(count):
        sources += [far_crossed[i], ((far_heads[1 + i], 2), (far_tails[i], 1))]
    last = exchange(stage(grid, grid.work_far, lists, turned, matrix, sources, (), first[1:2]))
    return assemble(grid, ((grid.work_near, grid.work_middle), (grid.work_far,)), [first, last])[None, None]


def solution(mesh):
    in_specs = (
        P("rows", "blk", None, None, None, None),
        P("rows", "blk", None, None),
        P("rows", "blk", None, None),
        P("rows", "blk", None),
        P("rows", "blk", None, None),
        P("rows", "blk", None),
    )
    out_specs = P("rows", "blk", None, None, None, None)
    return jax.shard_map(
        per_device, mesh=mesh, in_specs=in_specs, out_specs=out_specs, check_vma=False
    )
```

```python
import functools
import jax
import jax.numpy as jnp
from jax import lax
from jax.experimental import pallas as pl
from jax.experimental.pallas import tpu as pltpu
from jax.sharding import PartitionSpec as P

VMEM_LIMIT = 24 * 1024 * 1024
PACK_VMEM_LIMIT = 60 * 1024 * 1024
PARAMS = pltpu.CompilerParams(vmem_limit_bytes=VMEM_LIMIT)
COST = pl.CostEstimate(flops=1024, bytes_accessed=1024, transcendentals=0)
ANYWHERE = pl.BlockSpec(memory_space=pl.ANY)


def resident(x):
    return pl.BlockSpec(x.shape, lambda i, *_, n=len(x.shape): (0,) * n)


LINES = 4


class Grid:
    def __init__(self, panels, cap, pores):
        self.panels, self.cap, self.pores = panels, cap, pores
        self.columns = panels // LINES
        self.sides = range(1, self.columns)
        self.list_rows = -(-panels // 16) * 16

    def spot(self):
        place = lax.axis_index("blk")
        return place // self.columns, place % self.columns

    def lines(self, z):
        upper = z >= 2
        return jnp.where(z % 2 == 1, z - 1, z + 1), jnp.where(upper, 1, 2), jnp.where(upper, 0, 3)

    def middle(self, z):
        return (z == 1) | (z == 2)

    def panel(self, line, y, shift):
        column = y - shift
        return line * self.columns + jnp.where(column < 0, column + self.columns, column)

    def swaps(self, lines):
        return [(h * self.columns + c, k * self.columns + c)
                for h, k in (*lines, *[(k, h) for h, k in lines]) for c in range(self.columns)]

    def across(self, shift, lines=range(LINES)):
        return [(h * self.columns + c, h * self.columns + (c + shift) % self.columns)
                for h in lines for c in range(self.columns)]

    def ends(self, shift):
        return [(h * self.columns + c, end * self.columns + (c + shift) % self.columns)
                for h, end in ((1, 0), (2, 3)) for c in range(self.columns)]

    def part(self, ref, blocks, row, block):
        start = (row * blocks + block) * self.pores
        if not isinstance(start, int):
            start = pl.multiple_of(start, self.pores)
        return ref.at[pl.ds(start, self.pores), :]

    def shape(self, rows, blocks, width, lists=0):
        return jax.ShapeDtypeStruct((rows * blocks * self.pores + lists * self.list_rows, width), jnp.bfloat16)


    def work_near(self, z, y):
        half, _, _ = self.lines(z)
        return ([(self.panel(z, y, 0), [(0, True, True)]), (self.panel(half, y, 0), [(1, True, True)])] +
                [(self.panel(z, y, shift), [(1 + shift, False, True)]) for shift in self.sides])

    def work_middle(self, z, y):
        half, other, _ = self.lines(z)
        middle = self.middle(z)
        end = jnp.logical_not(middle)
        work = []
        for i, shift in enumerate(self.sides):
            work += [(self.panel(half, y, shift), [(3 * i, False, True)]),
                     (self.panel(other, y, shift), [(3 * i + 1, False, middle), (3 * i + 2, False, end)])]
        return work

    def work_far(self, z, y):
        _, other, far = self.lines(z)
        middle = self.middle(z)
        end = jnp.logical_not(middle)
        return ([(self.panel(other, y, 0), [(0, True, middle), (1, False, end)]),
                 (self.panel(far, y, 0), [(2, True, middle), (3, False, end)])] +
                [(self.panel(far, y, shift), [(2 + 2 * shift, False, middle), (3 + 2 * shift, False, end)])
                 for shift in self.sides])


def pack_kernel(grid, mask_from, cols_from, prolong_from, head, tail, mask, cols, prolong, done):
    group, groups = lax.axis_index("rows"), lax.axis_size("rows")
    width = tail.shape[-1]
    rows = prolong.shape[0]
    step = rows // 4 if rows % 4 == 0 else rows
    copies = [pltpu.make_async_copy(mask_from, mask, done.at[0]), pltpu.make_async_copy(cols_from, cols, done.at[1])]
    for index in range(rows // step):
        some = pl.ds(index * step, step)
        copies.append(pltpu.make_async_copy(prolong_from.at[some], prolong.at[some], done.at[2 + index]))
    for copy in copies:
        copy.start()
    copies[0].wait()
    copies[1].wait()
    for i in range(rows):
        if i % step == 0:
            copies[2 + i // step].wait()
        blocks = []
        for e in range(3):
            candidate = group + e - 1
            keep = (mask[e, 0, i] == 1) & (candidate >= 0) & (candidate < groups)
            block = prolong[i, :, e * width:(e + 1) * width]
            blocks.append(block * jnp.where(keep, 1.0, 0.0).astype(block.dtype))
        grid.part(head, 2, i, 0)[...] = jnp.where(group == 0, blocks[1], blocks[0])
        grid.part(head, 2, i, 1)[...] = jnp.where(group == 0, blocks[2], blocks[1])
        grid.part(tail, 1, i, 0)[...] = jnp.where(group == 0, blocks[0], blocks[2])
    line = lax.broadcasted_iota(jnp.int32, (grid.list_rows, width), 0)
    column = lax.broadcasted_iota(jnp.int32, (grid.list_rows, width), 1)
    numbers = jnp.zeros((grid.list_rows, width), jnp.int32)
    for panel in range(grid.panels):
        for entry in range(grid.cap):
            numbers = jnp.where((line == panel) & (column == entry), cols[panel, entry], numbers)
    start = rows * 2 * grid.pores
    head[start:start + grid.list_rows, :] = numbers.astype(jnp.float32).astype(head.dtype)


def pack(grid, mask, cols, prolong):
    rows, _, width3 = prolong.shape
    outs = [grid.shape(rows, 2, width3 // 3, 1), grid.shape(rows, 1, width3 // 3)]
    return pl.pallas_call(
        functools.partial(pack_kernel, grid),
        grid=(1,),
        in_specs=[pl.BlockSpec(memory_space=pl.ANY)] * 3,
        out_specs=[*map(resident, outs)],
        scratch_shapes=[
            pltpu.SMEM(mask.shape, mask.dtype),
            pltpu.SMEM(cols.shape, cols.dtype),
            pltpu.VMEM(prolong.shape, prolong.dtype),
            pltpu.SemaphoreType.DMA((6,)),
        ],
        out_shape=outs,
        compiler_params=pltpu.CompilerParams(vmem_limit_bytes=PACK_VMEM_LIMIT),
        cost_estimate=COST,
        name="pack_rows",
    )(mask, cols, prolong)


def turn_kernel(grid, head, tail, turned):
    width = head.shape[-1]
    for i in range(turned.shape[0]):
        parts = (grid.part(head, 2, i, 0), grid.part(head, 2, i, 1), grid.part(tail, 1, i, 0))
        for k, part in enumerate(parts):
            turned[i, k * width:(k + 1) * width, :] = part[...].T


def turn(grid, head, tail):
    rows, width = tail.shape[0] // grid.pores, tail.shape[1]
    out = jax.ShapeDtypeStruct((rows, 3 * width, grid.pores), head.dtype)
    return pl.pallas_call(
        functools.partial(turn_kernel, grid),
        grid=(1,),
        in_specs=[resident(head), resident(tail)],
        out_specs=resident(out),
        out_shape=out,
        compiler_params=PARAMS,
        cost_estimate=COST,
        name="turn_rows",
    )(head, tail)


def pick_kernel(grid, plan, layout, carry, tables, lists, filled, passed, *refs):
    wanted = list(refs[:lists])
    sources, at = [], lists
    for blocks in layout:
        sources.append([(refs[at + i], k) for i, k in enumerate(blocks)])
        at += len(blocks)
    scratch = 2 * len(tables) + 1 if tables else 0
    outs = refs[len(refs) - len(filled) - scratch:len(refs) - scratch]
    z, y = grid.spot()

    def list_at(source):
        ref = sources[source][0][0]
        return ref[ref.shape[0] - grid.list_rows:, :]

    if tables:
        numbers, plain, done = refs[-scratch:-1 - len(tables)], refs[-1 - len(tables):-1], refs[-1]
        for table, source in enumerate(tables):
            numbers[table][...] = list_at(source).astype(jnp.float32).astype(jnp.int32)
            pltpu.make_async_copy(numbers[table], plain[table], done.at[table]).start()
        for table in range(len(tables)):
            pltpu.make_async_copy(numbers[table], plain[table], done.at[table]).wait()
        wanted += plain
    for index, list_row, source, output, base in plan(z, y):
        for entry in range(grid.cap):
            row = wanted[index][list_row, entry]
            place = 0
            for ref, blocks in sources[source]:
                for block in range(blocks):
                    target = grid.part(outs[output], filled[output][0], base + entry, place)
                    target[...] = grid.part(ref, blocks, row, block)[...]
                    place += 1
    if passed is not None:
        outs[-1][...] = sources[passed][0][0][...]
    for out, source in zip(outs, carry):
        if source is not None:
            out[out.shape[0] - grid.list_rows:, :] = list_at(source)


def pick(grid, plan, filled, lists, sources, carry=(), tables=(), passed=None, after=(), cost=COST):
    flat = [x for source in sources for x, _ in source]
    width = flat[0].shape[-1]
    carry = carry or (None,) * len(filled)
    shapes = [grid.shape(rows, blocks, width, 0 if source is None else 1)
              for (blocks, rows), source in zip(filled, carry)]
    if passed is not None:
        filled = [*filled, (0, 0)]
        shapes.append(jax.ShapeDtypeStruct(sources[passed][0][0].shape, flat[0].dtype))
    layout = tuple(tuple(blocks for _, blocks in source) for source in sources)
    table = (grid.list_rows, width)
    scratch = [pltpu.VMEM(table, jnp.int32)] * len(tables) + [pltpu.SMEM(table, jnp.int32)] * len(tables)
    scratch += [pltpu.SemaphoreType.DMA((len(tables),))] if tables else []
    return pl.pallas_call(
        functools.partial(pick_kernel, grid, plan, layout, carry, tables, len(lists), tuple(filled), passed),
        grid_spec=pltpu.PrefetchScalarGridSpec(
            num_scalar_prefetch=len(lists),
            grid=(1,),
            in_specs=[*map(resident, flat), *([ANYWHERE] * len(after))],
            out_specs=[*map(resident, shapes)],
            scratch_shapes=scratch,
        ),
        out_shape=shapes,
        compiler_params=PARAMS,
        cost_estimate=cost,
        name="pick_rows",
    )(*lists, *flat, *after)


def stage_kernel(grid, plan, layout, carried, slot_rows, slot_cols, slot_counts, turned, matrix, *refs):
    arrays, at = [], 0
    for blocks in layout:
        arrays.append([(refs[at + i], k, base) for i, (k, base) in enumerate(blocks)])
        at += len(blocks)
    earlier = refs[at:at + 3] if carried else ()
    own, up, down, total = refs[-4:]
    width = own.shape[-1]
    first_group = lax.axis_index("rows") == 0
    for old, new in zip(earlier, (own, up, down)):
        for slot in range(carried):
            for f in range(3):
                new[slot, f] = old[slot, f]
    z, y = grid.spot()
    for slot, (panel, sources) in enumerate(plan(z, y), start=carried):
        total[...] = jnp.zeros_like(total)
        for array, whole, present in sources:
            live = slot_counts[0, panel]
            if present is not True:
                live = jnp.where(present, live, 0)
            parts = arrays[array]

            def product(entry, whole=whole, parts=parts, panel=panel):
                pick = slot_cols[panel, entry] if whole else entry
                right = jnp.concatenate(
                    [grid.part(x, blocks, base + pick, block)[...] for x, blocks, base in parts for block in range(blocks)],
                    axis=1)
                return jnp.dot(matrix[panel, entry], right, preferred_element_type=jnp.float32)

            def add(left, value):
                result = jnp.dot(left, value, preferred_element_type=jnp.float32)
                for k in range(3):
                    total[k] += result[:, k * width:(k + 1) * width]

            def two(u, carry, product=product, panel=panel):
                first, second = 2 * u, 2 * u + 1
                left = jnp.concatenate(
                    [turned[slot_rows[panel, first]], turned[slot_rows[panel, second]]], axis=1)
                value = jnp.concatenate([product(first), product(second)], axis=0).astype(jnp.bfloat16)
                add(left, value)
                return carry

            lax.fori_loop(0, live // 2, two, 0)

            @pl.when(live % 2 == 1)
            def _(live=live, product=product, panel=panel):
                add(turned[slot_rows[panel, live - 1]], product(live - 1).astype(jnp.bfloat16))

        begin = jnp.where(first_group, 0, width)
        for f in range(3):
            k = jnp.where(first_group, (f + 2) % 3, f)
            own[slot, f] = total[k, pl.ds(pl.multiple_of(begin, width), width), :].astype(own.dtype)
            up[slot, f] = total[k, pl.ds(pl.multiple_of(begin + width, width), width), :].astype(up.dtype)
            down[slot, f] = total[k, 0:width, :].astype(down.dtype)


def stage(grid, plan, lists, turned, matrix, sources, earlier=(), after=()):
    width = turned.shape[1] // 3
    carried = earlier[0].shape[0] if earlier else 0
    slots = carried + len(plan(jnp.int32(0), jnp.int32(0)))
    flat = [x for source in sources for x, *_ in source]
    layout = tuple(tuple((blocks, base[0] if base else 0) for _, blocks, *base in source) for source in sources)
    out = jax.ShapeDtypeStruct((slots, 3, width, width), jnp.bfloat16)
    return pl.pallas_call(
        functools.partial(stage_kernel, grid, plan, layout, carried),
        grid_spec=pltpu.PrefetchScalarGridSpec(
            num_scalar_prefetch=3,
            grid=(1,),
            in_specs=[*map(resident, (turned, matrix, *flat, *earlier)), *([ANYWHERE] * len(after))],
            out_specs=[resident(out)] * 3,
            scratch_shapes=[pltpu.VMEM((3, 3 * width, width), jnp.float32)],
        ),
        out_shape=[out] * 3,
        compiler_params=PARAMS,
        cost_estimate=COST,
        name="stage_products",
    )(*lists, turned, matrix, *flat, *earlier, *after)


def assemble_kernel(grid, plans, *refs):
    out = refs[-1]
    rows = refs[0].shape[2]
    panels = grid.panels
    z, y = grid.spot()
    for index, group in enumerate(plans):
        own, lower, upper = refs[3 * index:3 * index + 3]
        slots = [slot for plan in group for slot in plan(z, y)]
        for slot, (panel, _) in enumerate(slots):
            for d in range(5):
                terms = []
                if 0 <= d - 1 < 3:
                    terms.append(own[slot, d - 1].astype(jnp.float32))
                if d < 3:
                    terms.append(lower[slot, d].astype(jnp.float32))
                if 0 <= d - 2 < 3:
                    terms.append(upper[slot, d - 2].astype(jnp.float32))
                out[pl.ds(d * panels + panel, rows, stride=5 * panels), :] = functools.reduce(jnp.add, terms)


def assemble(grid, plans, pieces):
    panels = grid.panels
    width = pieces[0][0].shape[-1]
    rows = width // 4
    flat = [x for piece in pieces for x in piece]
    result = pl.pallas_call(
        functools.partial(assemble_kernel, grid, plans),
        grid=(width // rows,),
        in_specs=[pl.BlockSpec((x.shape[0], 3, rows, width), lambda i: (0, 0, i, 0)) for x in flat],
        out_specs=pl.BlockSpec((rows * 5 * panels, width), lambda i: (i, 0)),
        out_shape=jax.ShapeDtypeStruct((width * 5 * panels, width), jnp.float32),
        compiler_params=PARAMS,
        cost_estimate=COST,
        name="assemble_coarse",
    )(*flat)
    return result.reshape(width, 5, panels, width).transpose(0, 2, 1, 3)


def per_device(fine_blocks, block_rows, block_cols, block_counts, prolong_blocks, prolong_mask):
    matrix = fine_blocks[0, 0]
    cols_list = block_cols[0, 0]
    lists = (block_rows[0, 0], cols_list, block_counts[0])
    groups = lax.axis_size("rows")
    grid = Grid(lax.axis_size("blk"), cols_list.shape[1], matrix.shape[2])
    cap, sides, columns = grid.cap, grid.sides, grid.columns
    every, inner = range(groups), range(1, groups - 1)

    def move(x, pairs, members=every):
        perm = [(a * groups + g, b * groups + g) for g in members for a, b in pairs]
        return lax.ppermute(x, ("blk", "rows"), perm) if perm else jnp.zeros_like(x)

    def move_both(pair, pairs):
        return (move(pair[0][0], pairs), 2), (move(pair[1][0], pairs, inner), 1)

    def move_across(arrays, lines=range(LINES)):
        return [((move(x, grid.across(shift, lines)), 3),) for x, shift in zip(arrays, sides)]

    def exchange(parts):
        lower = lax.ppermute(parts[1], "rows", [(g, g + 1) for g in range(groups - 1)])
        upper = lax.ppermute(parts[2], "rows", [(g + 1, g) for g in range(groups - 1)])
        return parts[0], lower, upper

    count = len(sides)
    mids = (1, 2)

    head, tail = pack(grid, prolong_mask.transpose(2, 0, 1), cols_list, prolong_blocks[0])
    own = ((head, 2), (tail, 1))
    half = move_both(own, grid.swaps([(0, 1), (2, 3)]))
    other = move_both(own, grid.swaps([(1, 2)]))
    side_lists = [move(cols_list, [(b, a) for a, b in grid.across(shift)]) for shift in sides]

    def own_requests(z, y):
        return [(index, grid.panel(z, y, 0), 0, index, 0) for index in range(count)]

    beside = move_across(pick(grid, own_requests, [(3, cap)] * count, side_lists, [own]))
    turned = turn(grid, head, tail)

    far_head = move(half[0][0], grid.swaps([(1, 2)]))

    def early_requests(z, y):
        return [(0, grid.panel(grid.lines(z)[1], y, 0), 0, 0, 0)]

    early, end_list = pick(grid, early_requests, [(2, cap), (0, 0)], [], [other[:1], half[:1]], (None, 1), (1,),
                           cost=COST)
    end_lists = [move(end_list, [(b, a) for a, b in grid.across(shift, mids)]) for shift in sides]
    tables = [(half[0],), *[((x, 0),) for x in end_lists]]
    end_heads = [move(early, grid.ends(0))]

    def half_requests(z, y):
        return [(index, grid.panel(grid.lines(z)[0], y, 0), 0, index, 0) for index in range(count)]

    half_picked = pick(grid, half_requests, [(3, cap)] * count, side_lists, [half], after=[x for ((x, _),) in beside], cost=COST)
    half_crossed = move_across(half_picked)

    def other_requests(z, y):
        return [(index, grid.panel(grid.lines(z)[1], y, 0), 0, index, 0) for index in range(count)]

    end_picked = pick(grid, other_requests, [(3, cap)] * count, [], [other, *tables[1:]],
                      tables=tuple(range(1, 1 + count)), after=[*half_picked, end_heads[0]], cost=COST)
    end_crossed = [((move(x, grid.ends(shift)), 3),) for x, shift in zip(end_picked, sides)]
    picked = pick(grid, other_requests, [(3, cap)] * count, side_lists, [other],
                  after=[*end_picked], cost=COST)
    other_crossed = move_across(picked, mids)
    far_tail = move(half[1][0], grid.swaps([(1, 2)]), inner)
    far = ((far_head, 2), (far_tail, 1))
    parts = stage(grid, grid.work_near, lists, turned, matrix, [own, half, *beside])

    def far_requests(z, y):
        return [(index, grid.panel(grid.lines(z)[2], y, 0), 0, index, 0) for index in range(columns)]

    far_picked = pick(grid, far_requests, [(2, cap)] * columns, [], [far[:1], *tables], tables=tuple(range(1, 2 + count)),
                      after=[parts[0], *picked], cost=COST)
    far_heads = [move(x, grid.ends(shift)) for shift, x in enumerate(far_picked)]

    def last_requests(z, y):
        _, line_other, line_far = grid.lines(z)
        row = grid.panel(line_far, y, 0)
        return ([(index, row, 0, index, 0) for index in range(count)] +
                [(count, grid.panel(line_other, y, 0), 1, count, 0), (count, row, 2, count, cap)] +
                [(count + 1 + index, row, 2, count + 1 + index, 0) for index in range(count)])

    picked = pick(grid, last_requests, [(3, cap)] * count + [(1, 2 * cap)] + [(1, cap)] * count, side_lists,
                  [far, other[1:], far[1:], *tables], tables=tuple(range(3, 4 + count)), after=[*far_picked, end_heads[0], *[x for ((x, _),) in end_crossed], *[x for ((x, _),) in half_crossed]],
                  cost=COST)
    far_crossed = move_across(picked, mids)
    end_tail = move(picked[count], grid.ends(0), inner)
    far_tails = [move(x, grid.ends(shift), inner) for x, shift in zip(picked[count + 1:], sides)]
    sources = []
    for i in range(count):
        sources += [half_crossed[i], other_crossed[i], end_crossed[i]]
    parts = stage(grid, grid.work_middle, lists, turned, matrix, sources, parts, [*far_heads[:1], *far_tails])
    first = exchange(parts)

    sources = [other, ((end_heads[0], 2), (end_tail, 1, 0)), far, ((far_heads[0], 2), (end_tail, 1, cap))]
    for i in range(count):
        sources += [far_crossed[i], ((far_heads[1 + i], 2), (far_tails[i], 1))]
    last = exchange(stage(grid, grid.work_far, lists, turned, matrix, sources, (), first[1:2]))
    return assemble(grid, ((grid.work_near, grid.work_middle), (grid.work_far,)), [first, last])[None, None]


def solution(mesh):
    in_specs = (
        P("rows", "blk", None, None, None, None),
        P("rows", "blk", None, None),
        P("rows", "blk", None, None),
        P("rows", "blk", None),
        P("rows", "blk", None, None),
        P("rows", "blk", None),
    )
    out_specs = P("rows", "blk", None, None, None, None)
    return jax.shard_map(
        per_device, mesh=mesh, in_specs=in_specs, out_specs=out_specs, check_vma=False
    )
```

```python
import functools
import jax
import jax.numpy as jnp
from jax import lax
from jax.experimental import pallas as pl
from jax.experimental.pallas import tpu as pltpu
from jax.sharding import PartitionSpec as P

VMEM_LIMIT = 24 * 1024 * 1024
PACK_VMEM_LIMIT = 60 * 1024 * 1024
PARAMS = pltpu.CompilerParams(vmem_limit_bytes=VMEM_LIMIT)
COST = pl.CostEstimate(flops=1024, bytes_accessed=1024, transcendentals=0)
ANYWHERE = pl.BlockSpec(memory_space=pl.ANY)


def resident(x):
    return pl.BlockSpec(x.shape, lambda i, *_, n=len(x.shape): (0,) * n)


LINES = 4


class Grid:
    def __init__(self, panels, cap, pores):
        self.panels, self.cap, self.pores = panels, cap, pores
        self.columns = panels // LINES
        self.sides = range(1, self.columns)
        self.list_rows = -(-panels // 16) * 16

    def spot(self):
        place = lax.axis_index("blk")
        return place // self.columns, place % self.columns

    def lines(self, z):
        upper = z >= 2
        return jnp.where(z % 2 == 1, z - 1, z + 1), jnp.where(upper, 1, 2), jnp.where(upper, 0, 3)

    def middle(self, z):
        return (z == 1) | (z == 2)

    def panel(self, line, y, shift):
        column = y - shift
        return line * self.columns + jnp.where(column < 0, column + self.columns, column)

    def swaps(self, lines):
        return [(h * self.columns + c, k * self.columns + c)
                for h, k in (*lines, *[(k, h) for h, k in lines]) for c in range(self.columns)]

    def across(self, shift, lines=range(LINES)):
        return [(h * self.columns + c, h * self.columns + (c + shift) % self.columns)
                for h in lines for c in range(self.columns)]

    def ends(self, shift):
        return [(h * self.columns + c, end * self.columns + (c + shift) % self.columns)
                for h, end in ((1, 0), (2, 3)) for c in range(self.columns)]

    def part(self, ref, blocks, row, block):
        start = (row * blocks + block) * self.pores
        if not isinstance(start, int):
            start = pl.multiple_of(start, self.pores)
        return ref.at[pl.ds(start, self.pores), :]

    def shape(self, rows, blocks, width, lists=0):
        return jax.ShapeDtypeStruct((rows * blocks * self.pores + lists * self.list_rows, width), jnp.bfloat16)


    def work_near(self, z, y):
        half, _, _ = self.lines(z)
        return ([(self.panel(z, y, 0), [(0, True, True)]), (self.panel(half, y, 0), [(1, True, True)])] +
                [(self.panel(z, y, shift), [(1 + shift, False, True)]) for shift in self.sides])

    def work_middle(self, z, y):
        half, other, _ = self.lines(z)
        middle = self.middle(z)
        end = jnp.logical_not(middle)
        work = []
        for i, shift in enumerate(self.sides):
            work += [(self.panel(half, y, shift), [(3 * i, False, True)]),
                     (self.panel(other, y, shift), [(3 * i + 1, False, middle), (3 * i + 2, False, end)])]
        return work

    def work_far(self, z, y):
        _, other, far = self.lines(z)
        middle = self.middle(z)
        end = jnp.logical_not(middle)
        return ([(self.panel(other, y, 0), [(0, True, middle), (1, False, end)]),
                 (self.panel(far, y, 0), [(2, True, middle), (3, False, end)])] +
                [(self.panel(far, y, shift), [(2 + 2 * shift, False, middle), (3 + 2 * shift, False, end)])
                 for shift in self.sides])


def pack_kernel(grid, mask_from, cols_from, prolong_from, head, tail, mask, cols, prolong, done):
    group, groups = lax.axis_index("rows"), lax.axis_size("rows")
    width = tail.shape[-1]
    rows = prolong.shape[0]
    step = rows // 4 if rows % 4 == 0 else rows
    copies = [pltpu.make_async_copy(mask_from, mask, done.at[0]), pltpu.make_async_copy(cols_from, cols, done.at[1])]
    for index in range(rows // step):
        some = pl.ds(index * step, step)
        copies.append(pltpu.make_async_copy(prolong_from.at[some], prolong.at[some], done.at[2 + index]))
    for copy in copies:
        copy.start()
    copies[0].wait()
    copies[1].wait()
    for i in range(rows):
        if i % step == 0:
            copies[2 + i // step].wait()
        blocks = []
        for e in range(3):
            candidate = group + e - 1
            keep = (mask[e, 0, i] == 1) & (candidate >= 0) & (candidate < groups)
            block = prolong[i, :, e * width:(e + 1) * width]
            blocks.append(block * jnp.where(keep, 1.0, 0.0).astype(block.dtype))
        grid.part(head, 2, i, 0)[...] = jnp.where(group == 0, blocks[1], blocks[0])
        grid.part(head, 2, i, 1)[...] = jnp.where(group == 0, blocks[2], blocks[1])
        grid.part(tail, 1, i, 0)[...] = jnp.where(group == 0, blocks[0], blocks[2])
    line = lax.broadcasted_iota(jnp.int32, (grid.list_rows, width), 0)
    column = lax.broadcasted_iota(jnp.int32, (grid.list_rows, width), 1)
    numbers = jnp.zeros((grid.list_rows, width), jnp.int32)
    for panel in range(grid.panels):
        for entry in range(grid.cap):
            numbers = jnp.where((line == panel) & (column == entry), cols[panel, entry], numbers)
    start = rows * 2 * grid.pores
    head[start:start + grid.list_rows, :] = numbers.astype(jnp.float32).astype(head.dtype)


def pack(grid, mask, cols, prolong):
    rows, _, width3 = prolong.shape
    outs = [grid.shape(rows, 2, width3 // 3, 1), grid.shape(rows, 1, width3 // 3)]
    return pl.pallas_call(
        functools.partial(pack_kernel, grid),
        grid=(1,),
        in_specs=[pl.BlockSpec(memory_space=pl.ANY)] * 3,
        out_specs=[*map(resident, outs)],
        scratch_shapes=[
            pltpu.SMEM(mask.shape, mask.dtype),
            pltpu.SMEM(cols.shape, cols.dtype),
            pltpu.VMEM(prolong.shape, prolong.dtype),
            pltpu.SemaphoreType.DMA((6,)),
        ],
        out_shape=outs,
        compiler_params=pltpu.CompilerParams(vmem_limit_bytes=PACK_VMEM_LIMIT),
        cost_estimate=COST,
        name="pack_rows",
    )(mask, cols, prolong)


def turn_kernel(grid, head, tail, turned):
    width = head.shape[-1]
    for i in range(turned.shape[0]):
        parts = (grid.part(head, 2, i, 0), grid.part(head, 2, i, 1), grid.part(tail, 1, i, 0))
        for k, part in enumerate(parts):
            turned[i, k * width:(k + 1) * width, :] = part[...].T


def turn(grid, head, tail):
    rows, width = tail.shape[0] // grid.pores, tail.shape[1]
    out = jax.ShapeDtypeStruct((rows, 3 * width, grid.pores), head.dtype)
    return pl.pallas_call(
        functools.partial(turn_kernel, grid),
        grid=(1,),
        in_specs=[resident(head), resident(tail)],
        out_specs=resident(out),
        out_shape=out,
        compiler_params=PARAMS,
        cost_estimate=COST,
        name="turn_rows",
    )(head, tail)


def pick_kernel(grid, plan, layout, carry, tables, lists, filled, passed, *refs):
    wanted = list(refs[:lists])
    sources, at = [], lists
    for blocks in layout:
        sources.append([(refs[at + i], k) for i, k in enumerate(blocks)])
        at += len(blocks)
    scratch = 2 * len(tables) + 1 if tables else 0
    outs = refs[len(refs) - len(filled) - scratch:len(refs) - scratch]
    z, y = grid.spot()

    def list_at(source):
        ref = sources[source][0][0]
        return ref[ref.shape[0] - grid.list_rows:, :]

    if tables:
        numbers, plain, done = refs[-scratch:-1 - len(tables)], refs[-1 - len(tables):-1], refs[-1]
        for table, source in enumerate(tables):
            numbers[table][...] = list_at(source).astype(jnp.float32).astype(jnp.int32)
            pltpu.make_async_copy(numbers[table], plain[table], done.at[table]).start()
        for table in range(len(tables)):
            pltpu.make_async_copy(numbers[table], plain[table], done.at[table]).wait()
        wanted += plain
    for index, list_row, source, output, base in plan(z, y):
        for entry in range(grid.cap):
            row = wanted[index][list_row, entry]
            place = 0
            for ref, blocks in sources[source]:
                for block in range(blocks):
                    target = grid.part(outs[output], filled[output][0], base + entry, place)
                    target[...] = grid.part(ref, blocks, row, block)[...]
                    place += 1
    if passed is not None:
        outs[-1][...] = sources[passed][0][0][...]
    for out, source in zip(outs, carry):
        if source is not None:
            out[out.shape[0] - grid.list_rows:, :] = list_at(source)


def pick(grid, plan, filled, lists, sources, carry=(), tables=(), passed=None, after=(), cost=COST):
    flat = [x for source in sources for x, _ in source]
    width = flat[0].shape[-1]
    carry = carry or (None,) * len(filled)
    shapes = [grid.shape(rows, blocks, width, 0 if source is None else 1)
              for (blocks, rows), source in zip(filled, carry)]
    if passed is not None:
        filled = [*filled, (0, 0)]
        shapes.append(jax.ShapeDtypeStruct(sources[passed][0][0].shape, flat[0].dtype))
    layout = tuple(tuple(blocks for _, blocks in source) for source in sources)
    table = (grid.list_rows, width)
    scratch = [pltpu.VMEM(table, jnp.int32)] * len(tables) + [pltpu.SMEM(table, jnp.int32)] * len(tables)
    scratch += [pltpu.SemaphoreType.DMA((len(tables),))] if tables else []
    return pl.pallas_call(
        functools.partial(pick_kernel, grid, plan, layout, carry, tables, len(lists), tuple(filled), passed),
        grid_spec=pltpu.PrefetchScalarGridSpec(
            num_scalar_prefetch=len(lists),
            grid=(1,),
            in_specs=[*map(resident, flat), *([ANYWHERE] * len(after))],
            out_specs=[*map(resident, shapes)],
            scratch_shapes=scratch,
        ),
        out_shape=shapes,
        compiler_params=PARAMS,
        cost_estimate=cost,
        name="pick_rows",
    )(*lists, *flat, *after)


def stage_kernel(grid, plan, layout, carried, slot_rows, slot_cols, slot_counts, turned, matrix, *refs):
    arrays, at = [], 0
    for blocks in layout:
        arrays.append([(refs[at + i], k, base) for i, (k, base) in enumerate(blocks)])
        at += len(blocks)
    earlier = refs[at:at + 3] if carried else ()
    own, up, down, total, values, lefts = refs[-6:]
    cap = matrix.shape[1]
    width = own.shape[-1]
    first_group = lax.axis_index("rows") == 0
    for old, new in zip(earlier, (own, up, down)):
        for slot in range(carried):
            for f in range(3):
                new[slot, f] = old[slot, f]
    z, y = grid.spot()
    for slot, (panel, sources) in enumerate(plan(z, y), start=carried):
        live = 0
        for _, _, present in sources:
            live = live + (slot_counts[0, panel] if present is True else jnp.where(present, slot_counts[0, panel], 0))
        for entry in range(cap):
            right = None
            for array, whole, present in sources:
                pick = slot_cols[panel, entry] if whole else entry
                part = jnp.concatenate(
                    [grid.part(x, blocks, base + pick, block)[...]
                     for x, blocks, base in arrays[array] for block in range(blocks)], axis=1)
                right = part if right is None else jnp.where(present, part, right)
            product = jnp.dot(matrix[panel, entry], right, preferred_element_type=jnp.float32)
            place = slice(entry * grid.pores, (entry + 1) * grid.pores)
            values[place, :] = jnp.where(entry < live, product, 0.0).astype(values.dtype)
            lefts[:, place] = turned[slot_rows[panel, entry]]
        result = jnp.dot(lefts[...], values[...], preferred_element_type=jnp.float32)
        for k in range(3):
            total[k] = result[:, k * width:(k + 1) * width]
        begin = jnp.where(first_group, 0, width)
        for f in range(3):
            k = jnp.where(first_group, (f + 2) % 3, f)
            own[slot, f] = total[k, pl.ds(pl.multiple_of(begin, width), width), :].astype(own.dtype)
            up[slot, f] = total[k, pl.ds(pl.multiple_of(begin + width, width), width), :].astype(up.dtype)
            down[slot, f] = total[k, 0:width, :].astype(down.dtype)


def stage(grid, plan, lists, turned, matrix, sources, earlier=(), after=()):
    width = turned.shape[1] // 3
    carried = earlier[0].shape[0] if earlier else 0
    slots = carried + len(plan(jnp.int32(0), jnp.int32(0)))
    flat = [x for source in sources for x, *_ in source]
    layout = tuple(tuple((blocks, base[0] if base else 0) for _, blocks, *base in source) for source in sources)
    out = jax.ShapeDtypeStruct((slots, 3, width, width), jnp.bfloat16)
    return pl.pallas_call(
        functools.partial(stage_kernel, grid, plan, layout, carried),
        grid_spec=pltpu.PrefetchScalarGridSpec(
            num_scalar_prefetch=3,
            grid=(1,),
            in_specs=[*map(resident, (turned, matrix, *flat, *earlier)), *([ANYWHERE] * len(after))],
            out_specs=[resident(out)] * 3,
            scratch_shapes=[
                pltpu.VMEM((3, 3 * width, width), jnp.float32),
                pltpu.VMEM((matrix.shape[1] * grid.pores, 3 * width), jnp.bfloat16),
                pltpu.VMEM((3 * width, matrix.shape[1] * grid.pores), jnp.bfloat16),
            ],
        ),
        out_shape=[out] * 3,
        compiler_params=PARAMS,
        cost_estimate=COST,
        name="stage_products",
    )(*lists, turned, matrix, *flat, *earlier, *after)


def assemble_kernel(grid, plans, *refs):
    out = refs[-1]
    rows = refs[0].shape[2]
    panels = grid.panels
    z, y = grid.spot()
    for index, group in enumerate(plans):
        own, lower, upper = refs[3 * index:3 * index + 3]
        slots = [slot for plan in group for slot in plan(z, y)]
        for slot, (panel, _) in enumerate(slots):
            for d in range(5):
                terms = []
                if 0 <= d - 1 < 3:
                    terms.append(own[slot, d - 1].astype(jnp.float32))
                if d < 3:
                    terms.append(lower[slot, d].astype(jnp.float32))
                if 0 <= d - 2 < 3:
                    terms.append(upper[slot, d - 2].astype(jnp.float32))
                out[pl.ds(d * panels + panel, rows, stride=5 * panels), :] = functools.reduce(jnp.add, terms)


def assemble(grid, plans, pieces):
    panels = grid.panels
    width = pieces[0][0].shape[-1]
    rows = width // 4
    flat = [x for piece in pieces for x in piece]
    result = pl.pallas_call(
        functools.partial(assemble_kernel, grid, plans),
        grid=(width // rows,),
        in_specs=[pl.BlockSpec((x.shape[0], 3, rows, width), lambda i: (0, 0, i, 0)) for x in flat],
        out_specs=pl.BlockSpec((rows * 5 * panels, width), lambda i: (i, 0)),
        out_shape=jax.ShapeDtypeStruct((width * 5 * panels, width), jnp.float32),
        compiler_params=PARAMS,
        cost_estimate=COST,
        name="assemble_coarse",
    )(*flat)
    return result.reshape(width, 5, panels, width).transpose(0, 2, 1, 3)


def per_device(fine_blocks, block_rows, block_cols, block_counts, prolong_blocks, prolong_mask):
    matrix = fine_blocks[0, 0]
    cols_list = block_cols[0, 0]
    lists = (block_rows[0, 0], cols_list, block_counts[0])
    groups = lax.axis_size("rows")
    grid = Grid(lax.axis_size("blk"), cols_list.shape[1], matrix.shape[2])
    cap, sides, columns = grid.cap, grid.sides, grid.columns
    every, inner = range(groups), range(1, groups - 1)

    def move(x, pairs, members=every):
        perm = [(a * groups + g, b * groups + g) for g in members for a, b in pairs]
        return lax.ppermute(x, ("blk", "rows"), perm) if perm else jnp.zeros_like(x)

    def move_both(pair, pairs):
        return (move(pair[0][0], pairs), 2), (move(pair[1][0], pairs, inner), 1)

    def move_across(arrays, lines=range(LINES)):
        return [((move(x, grid.across(shift, lines)), 3),) for x, shift in zip(arrays, sides)]

    def exchange(parts):
        lower = lax.ppermute(parts[1], "rows", [(g, g + 1) for g in range(groups - 1)])
        upper = lax.ppermute(parts[2], "rows", [(g + 1, g) for g in range(groups - 1)])
        return parts[0], lower, upper

    count = len(sides)
    mids = (1, 2)

    head, tail = pack(grid, prolong_mask.transpose(2, 0, 1), cols_list, prolong_blocks[0])
    own = ((head, 2), (tail, 1))
    half = move_both(own, grid.swaps([(0, 1), (2, 3)]))
    other = move_both(own, grid.swaps([(1, 2)]))
    side_lists = [move(cols_list, [(b, a) for a, b in grid.across(shift)]) for shift in sides]

    def own_requests(z, y):
        return [(index, grid.panel(z, y, 0), 0, index, 0) for index in range(count)]

    beside = move_across(pick(grid, own_requests, [(3, cap)] * count, side_lists, [own]))
    turned = turn(grid, head, tail)

    far_head = move(half[0][0], grid.swaps([(1, 2)]))

    def early_requests(z, y):
        return [(0, grid.panel(grid.lines(z)[1], y, 0), 0, 0, 0)]

    early, end_list = pick(grid, early_requests, [(2, cap), (0, 0)], [], [other[:1], half[:1]], (None, 1), (1,),
                           cost=COST)
    end_lists = [move(end_list, [(b, a) for a, b in grid.across(shift, mids)]) for shift in sides]
    tables = [(half[0],), *[((x, 0),) for x in end_lists]]
    end_heads = [move(early, grid.ends(0))]

    def half_requests(z, y):
        return [(index, grid.panel(grid.lines(z)[0], y, 0), 0, index, 0) for index in range(count)]

    half_picked = pick(grid, half_requests, [(3, cap)] * count, side_lists, [half], after=[x for ((x, _),) in beside], cost=COST)
    half_crossed = move_across(half_picked)

    def other_requests(z, y):
        return [(index, grid.panel(grid.lines(z)[1], y, 0), 0, index, 0) for index in range(count)]

    end_picked = pick(grid, other_requests, [(3, cap)] * count, [], [other, *tables[1:]],
                      tables=tuple(range(1, 1 + count)), after=[*half_picked, end_heads[0]], cost=COST)
    end_crossed = [((move(x, grid.ends(shift)), 3),) for x, shift in zip(end_picked, sides)]
    picked = pick(grid, other_requests, [(3, cap)] * count, side_lists, [other],
                  after=[*end_picked], cost=COST)
    other_crossed = move_across(picked, mids)
    far_tail = move(half[1][0], grid.swaps([(1, 2)]), inner)
    far = ((far_head, 2), (far_tail, 1))
    parts = stage(grid, grid.work_near, lists, turned, matrix, [own, half, *beside])

    def far_requests(z, y):
        return [(index, grid.panel(grid.lines(z)[2], y, 0), 0, index, 0) for index in range(columns)]

    far_picked = pick(grid, far_requests, [(2, cap)] * columns, [], [far[:1], *tables], tables=tuple(range(1, 2 + count)),
                      after=[parts[0], *picked], cost=COST)
    far_heads = [move(x, grid.ends(shift)) for shift, x in enumerate(far_picked)]

    def last_requests(z, y):
        _, line_other, line_far = grid.lines(z)
        row = grid.panel(line_far, y, 0)
        return ([(index, row, 0, index, 0) for index in range(count)] +
                [(count, grid.panel(line_other, y, 0), 1, count, 0), (count, row, 2, count, cap)] +
                [(count + 1 + index, row, 2, count + 1 + index, 0) for index in range(count)])

    picked = pick(grid, last_requests, [(3, cap)] * count + [(1, 2 * cap)] + [(1, cap)] * count, side_lists,
                  [far, other[1:], far[1:], *tables], tables=tuple(range(3, 4 + count)), after=[*far_picked, end_heads[0], *[x for ((x, _),) in end_crossed], *[x for ((x, _),) in half_crossed]],
                  cost=COST)
    far_crossed = move_across(picked, mids)
    end_tail = move(picked[count], grid.ends(0), inner)
    far_tails = [move(x, grid.ends(shift), inner) for x, shift in zip(picked[count + 1:], sides)]
    sources = []
    for i in range(count):
        sources += [half_crossed[i], other_crossed[i], end_crossed[i]]
    parts = stage(grid, grid.work_middle, lists, turned, matrix, sources, parts, [*far_heads[:1], *far_tails])
    first = exchange(parts)

    sources = [other, ((end_heads[0], 2), (end_tail, 1, 0)), far, ((far_heads[0], 2), (end_tail, 1, cap))]
    for i in range(count):
        sources += [far_crossed[i], ((far_heads[1 + i], 2), (far_tails[i], 1))]
    last = exchange(stage(grid, grid.work_far, lists, turned, matrix, sources, (), first[1:2]))
    return assemble(grid, ((grid.work_near, grid.work_middle), (grid.work_far,)), [first, last])[None, None]


def solution(mesh):
    in_specs = (
        P("rows", "blk", None, None, None, None),
        P("rows", "blk", None, None),
        P("rows", "blk", None, None),
        P("rows", "blk", None),
        P("rows", "blk", None, None),
        P("rows", "blk", None),
    )
    out_specs = P("rows", "blk", None, None, None, None)
    return jax.shard_map(
        per_device, mesh=mesh, in_specs=in_specs, out_specs=out_specs, check_vma=False
    )
```

```python
import functools
import jax
import jax.numpy as jnp
from jax import lax
from jax.experimental import pallas as pl
from jax.experimental.pallas import tpu as pltpu
from jax.sharding import PartitionSpec as P

VMEM_LIMIT = 24 * 1024 * 1024
PACK_VMEM_LIMIT = 60 * 1024 * 1024
PARAMS = pltpu.CompilerParams(vmem_limit_bytes=VMEM_LIMIT)
COST = pl.CostEstimate(flops=1024, bytes_accessed=1024, transcendentals=0)
ANYWHERE = pl.BlockSpec(memory_space=pl.ANY)


def resident(x):
    return pl.BlockSpec(x.shape, lambda i, *_, n=len(x.shape): (0,) * n)


LINES = 4


class Grid:
    def __init__(self, panels, cap, pores):
        self.panels, self.cap, self.pores = panels, cap, pores
        self.columns = panels // LINES
        self.sides = range(1, self.columns)
        self.list_rows = -(-panels // 16) * 16

    def spot(self):
        place = lax.axis_index("blk")
        return place // self.columns, place % self.columns

    def lines(self, z):
        upper = z >= 2
        return jnp.where(z % 2 == 1, z - 1, z + 1), jnp.where(upper, 1, 2), jnp.where(upper, 0, 3)

    def middle(self, z):
        return (z == 1) | (z == 2)

    def panel(self, line, y, shift):
        column = y - shift
        return line * self.columns + jnp.where(column < 0, column + self.columns, column)

    def swaps(self, lines):
        return [(h * self.columns + c, k * self.columns + c)
                for h, k in (*lines, *[(k, h) for h, k in lines]) for c in range(self.columns)]

    def across(self, shift, lines=range(LINES)):
        return [(h * self.columns + c, h * self.columns + (c + shift) % self.columns)
                for h in lines for c in range(self.columns)]

    def ends(self, shift):
        return [(h * self.columns + c, end * self.columns + (c + shift) % self.columns)
                for h, end in ((1, 0), (2, 3)) for c in range(self.columns)]

    def part(self, ref, blocks, row, block):
        start = (row * blocks + block) * self.pores
        if not isinstance(start, int):
            start = pl.multiple_of(start, self.pores)
        return ref.at[pl.ds(start, self.pores), :]

    def shape(self, rows, blocks, width, lists=0):
        return jax.ShapeDtypeStruct((rows * blocks * self.pores + lists * self.list_rows, width), jnp.bfloat16)


    def work_near(self, z, y):
        half, _, _ = self.lines(z)
        return ([(self.panel(z, y, 0), [(0, True, True)]), (self.panel(half, y, 0), [(1, True, True)])] +
                [(self.panel(z, y, shift), [(1 + shift, False, True)]) for shift in self.sides])

    def work_middle(self, z, y):
        half, other, _ = self.lines(z)
        middle = self.middle(z)
        end = jnp.logical_not(middle)
        work = []
        for i, shift in enumerate(self.sides):
            work += [(self.panel(half, y, shift), [(3 * i, False, True)]),
                     (self.panel(other, y, shift), [(3 * i + 1, False, middle), (3 * i + 2, False, end)])]
        return work

    def work_far(self, z, y):
        _, other, far = self.lines(z)
        middle = self.middle(z)
        end = jnp.logical_not(middle)
        return ([(self.panel(other, y, 0), [(0, True, middle), (1, False, end)]),
                 (self.panel(far, y, 0), [(2, True, middle), (3, False, end)])] +
                [(self.panel(far, y, shift), [(2 + 2 * shift, False, middle), (3 + 2 * shift, False, end)])
                 for shift in self.sides])


def pack_kernel(grid, mask_from, cols_from, prolong_from, head, tail, mask, cols, prolong, done):
    group, groups = lax.axis_index("rows"), lax.axis_size("rows")
    width = tail.shape[-1]
    rows = prolong.shape[0]
    step = rows // 4 if rows % 4 == 0 else rows
    copies = [pltpu.make_async_copy(mask_from, mask, done.at[0]), pltpu.make_async_copy(cols_from, cols, done.at[1])]
    for index in range(rows // step):
        some = pl.ds(index * step, step)
        copies.append(pltpu.make_async_copy(prolong_from.at[some], prolong.at[some], done.at[2 + index]))
    for copy in copies:
        copy.start()
    copies[0].wait()
    copies[1].wait()
    for i in range(rows):
        if i % step == 0:
            copies[2 + i // step].wait()
        blocks = []
        for e in range(3):
            candidate = group + e - 1
            keep = (mask[e, 0, i] == 1) & (candidate >= 0) & (candidate < groups)
            block = prolong[i, :, e * width:(e + 1) * width]
            blocks.append(block * jnp.where(keep, 1.0, 0.0).astype(block.dtype))
        grid.part(head, 2, i, 0)[...] = jnp.where(group == 0, blocks[1], blocks[0])
        grid.part(head, 2, i, 1)[...] = jnp.where(group == 0, blocks[2], blocks[1])
        grid.part(tail, 1, i, 0)[...] = jnp.where(group == 0, blocks[0], blocks[2])
    line = lax.broadcasted_iota(jnp.int32, (grid.list_rows, width), 0)
    column = lax.broadcasted_iota(jnp.int32, (grid.list_rows, width), 1)
    numbers = jnp.zeros((grid.list_rows, width), jnp.int32)
    for panel in range(grid.panels):
        for entry in range(grid.cap):
            numbers = jnp.where((line == panel) & (column == entry), cols[panel, entry], numbers)
    start = rows * 2 * grid.pores
    head[start:start + grid.list_rows, :] = numbers.astype(jnp.float32).astype(head.dtype)


def pack(grid, mask, cols, prolong):
    rows, _, width3 = prolong.shape
    outs = [grid.shape(rows, 2, width3 // 3, 1), grid.shape(rows, 1, width3 // 3)]
    return pl.pallas_call(
        functools.partial(pack_kernel, grid),
        grid=(1,),
        in_specs=[pl.BlockSpec(memory_space=pl.ANY)] * 3,
        out_specs=[*map(resident, outs)],
        scratch_shapes=[
            pltpu.SMEM(mask.shape, mask.dtype),
            pltpu.SMEM(cols.shape, cols.dtype),
            pltpu.VMEM(prolong.shape, prolong.dtype),
            pltpu.SemaphoreType.DMA((6,)),
        ],
        out_shape=outs,
        compiler_params=pltpu.CompilerParams(vmem_limit_bytes=PACK_VMEM_LIMIT),
        cost_estimate=COST,
        name="pack_rows",
    )(mask, cols, prolong)


def turn_kernel(grid, head, tail, turned):
    width = head.shape[-1]
    for i in range(turned.shape[0]):
        parts = (grid.part(head, 2, i, 0), grid.part(head, 2, i, 1), grid.part(tail, 1, i, 0))
        for k, part in enumerate(parts):
            turned[i, k * width:(k + 1) * width, :] = part[...].T


def turn(grid, head, tail):
    rows, width = tail.shape[0] // grid.pores, tail.shape[1]
    out = jax.ShapeDtypeStruct((rows, 3 * width, grid.pores), head.dtype)
    return pl.pallas_call(
        functools.partial(turn_kernel, grid),
        grid=(1,),
        in_specs=[resident(head), resident(tail)],
        out_specs=resident(out),
        out_shape=out,
        compiler_params=PARAMS,
        cost_estimate=COST,
        name="turn_rows",
    )(head, tail)


def pick_kernel(grid, plan, layout, carry, tables, lists, filled, passed, *refs):
    wanted = list(refs[:lists])
    sources, at = [], lists
    for blocks in layout:
        sources.append([(refs[at + i], k) for i, k in enumerate(blocks)])
        at += len(blocks)
    scratch = 2 * len(tables) + 1 if tables else 0
    outs = refs[len(refs) - len(filled) - scratch:len(refs) - scratch]
    z, y = grid.spot()

    def list_at(source):
        ref = sources[source][0][0]
        return ref[ref.shape[0] - grid.list_rows:, :]

    if tables:
        numbers, plain, done = refs[-scratch:-1 - len(tables)], refs[-1 - len(tables):-1], refs[-1]
        for table, source in enumerate(tables):
            numbers[table][...] = list_at(source).astype(jnp.float32).astype(jnp.int32)
            pltpu.make_async_copy(numbers[table], plain[table], done.at[table]).start()
        for table in range(len(tables)):
            pltpu.make_async_copy(numbers[table], plain[table], done.at[table]).wait()
        wanted += plain
    for index, list_row, source, output, base in plan(z, y):
        for entry in range(grid.cap):
            row = wanted[index][list_row, entry]
            place = 0
            for ref, blocks in sources[source]:
                for block in range(blocks):
                    target = grid.part(outs[output], filled[output][0], base + entry, place)
                    target[...] = grid.part(ref, blocks, row, block)[...]
                    place += 1
    if passed is not None:
        outs[-1][...] = sources[passed][0][0][...]
    for out, source in zip(outs, carry):
        if source is not None:
            out[out.shape[0] - grid.list_rows:, :] = list_at(source)


def pick(grid, plan, filled, lists, sources, carry=(), tables=(), passed=None, after=(), cost=COST):
    flat = [x for source in sources for x, _ in source]
    width = flat[0].shape[-1]
    carry = carry or (None,) * len(filled)
    shapes = [grid.shape(rows, blocks, width, 0 if source is None else 1)
              for (blocks, rows), source in zip(filled, carry)]
    if passed is not None:
        filled = [*filled, (0, 0)]
        shapes.append(jax.ShapeDtypeStruct(sources[passed][0][0].shape, flat[0].dtype))
    layout = tuple(tuple(blocks for _, blocks in source) for source in sources)
    table = (grid.list_rows, width)
    scratch = [pltpu.VMEM(table, jnp.int32)] * len(tables) + [pltpu.SMEM(table, jnp.int32)] * len(tables)
    scratch += [pltpu.SemaphoreType.DMA((len(tables),))] if tables else []
    return pl.pallas_call(
        functools.partial(pick_kernel, grid, plan, layout, carry, tables, len(lists), tuple(filled), passed),
        grid_spec=pltpu.PrefetchScalarGridSpec(
            num_scalar_prefetch=len(lists),
            grid=(1,),
            in_specs=[*map(resident, flat), *([ANYWHERE] * len(after))],
            out_specs=[*map(resident, shapes)],
            scratch_shapes=scratch,
        ),
        out_shape=shapes,
        compiler_params=PARAMS,
        cost_estimate=cost,
        name="pick_rows",
    )(*lists, *flat, *after)


def stage_kernel(grid, plan, layout, carried, slot_rows, slot_cols, slot_counts, turned, matrix, *refs):
    arrays, at = [], 0
    for blocks in layout:
        arrays.append([(refs[at + i], k, base) for i, (k, base) in enumerate(blocks)])
        at += len(blocks)
    earlier = refs[at:at + 3] if carried else ()
    own, up, down, total, values, lefts = refs[-6:]
    cap = matrix.shape[1]
    width = own.shape[-1]
    first_group = lax.axis_index("rows") == 0
    for old, new in zip(earlier, (own, up, down)):
        for slot in range(carried):
            for f in range(3):
                new[slot, f] = old[slot, f]
    z, y = grid.spot()
    for slot, (panel, sources) in enumerate(plan(z, y), start=carried):
        live = 0
        for _, _, present in sources:
            live = live + (slot_counts[0, panel] if present is True else jnp.where(present, slot_counts[0, panel], 0))
        for entry in range(cap):
            right = None
            for array, whole, present in sources:
                pick = slot_cols[panel, entry] if whole else entry
                part = jnp.concatenate(
                    [grid.part(x, blocks, base + pick, block)[...]
                     for x, blocks, base in arrays[array] for block in range(blocks)], axis=1)
                right = part if right is None else jnp.where(present, part, right)
            product = jnp.dot(matrix[panel, entry], right, preferred_element_type=jnp.float32)
            place = slice(entry * grid.pores, (entry + 1) * grid.pores)
            values[place, :] = jnp.where(entry < live, product, 0.0).astype(values.dtype)
            lefts[:, place] = turned[slot_rows[panel, entry]]
        result = jnp.dot(lefts[...], values[...], preferred_element_type=jnp.float32)
        for k in range(3):
            total[k] = result[:, k * width:(k + 1) * width]
        begin = jnp.where(first_group, 0, width)
        for f in range(3):
            k = jnp.where(first_group, (f + 2) % 3, f)
            own[slot, f] = total[k, pl.ds(pl.multiple_of(begin, width), width), :].astype(own.dtype)
            up[slot, f] = total[k, pl.ds(pl.multiple_of(begin + width, width), width), :].astype(up.dtype)
            down[slot, f] = total[k, 0:width, :].astype(down.dtype)


def stage(grid, plan, lists, turned, matrix, sources, earlier=(), after=()):
    width = turned.shape[1] // 3
    carried = earlier[0].shape[0] if earlier else 0
    slots = carried + len(plan(jnp.int32(0), jnp.int32(0)))
    flat = [x for source in sources for x, *_ in source]
    layout = tuple(tuple((blocks, base[0] if base else 0) for _, blocks, *base in source) for source in sources)
    out = jax.ShapeDtypeStruct((slots, 3, width, width), jnp.bfloat16)
    return pl.pallas_call(
        functools.partial(stage_kernel, grid, plan, layout, carried),
        grid_spec=pltpu.PrefetchScalarGridSpec(
            num_scalar_prefetch=3,
            grid=(1,),
            in_specs=[*map(resident, (turned, matrix, *flat, *earlier)), *([ANYWHERE] * len(after))],
            out_specs=[resident(out)] * 3,
            scratch_shapes=[
                pltpu.VMEM((3, 3 * width, width), jnp.float32),
                pltpu.VMEM((matrix.shape[1] * grid.pores, 3 * width), jnp.bfloat16),
                pltpu.VMEM((3 * width, matrix.shape[1] * grid.pores), jnp.bfloat16),
            ],
        ),
        out_shape=[out] * 3,
        compiler_params=PARAMS,
        cost_estimate=COST,
        name="stage_products",
    )(*lists, turned, matrix, *flat, *earlier, *after)


def assemble_kernel(grid, plans, *refs):
    out = refs[-1]
    rows = refs[0].shape[2]
    panels = grid.panels
    z, y = grid.spot()
    for index, group in enumerate(plans):
        own, lower, upper = refs[3 * index:3 * index + 3]
        slots = [slot for plan in group for slot in plan(z, y)]
        for slot, (panel, _) in enumerate(slots):
            for d in range(5):
                terms = []
                if 0 <= d - 1 < 3:
                    terms.append(own[slot, d - 1].astype(jnp.float32))
                if d < 3:
                    terms.append(lower[slot, d].astype(jnp.float32))
                if 0 <= d - 2 < 3:
                    terms.append(upper[slot, d - 2].astype(jnp.float32))
                out[pl.ds(d * panels + panel, rows, stride=5 * panels), :] = functools.reduce(jnp.add, terms)


def assemble(grid, plans, pieces):
    panels = grid.panels
    width = pieces[0][0].shape[-1]
    rows = width // 4
    flat = [x for piece in pieces for x in piece]
    result = pl.pallas_call(
        functools.partial(assemble_kernel, grid, plans),
        grid=(width // rows,),
        in_specs=[pl.BlockSpec((x.shape[0], 3, rows, width), lambda i: (0, 0, i, 0)) for x in flat],
        out_specs=pl.BlockSpec((rows * 5 * panels, width), lambda i: (i, 0)),
        out_shape=jax.ShapeDtypeStruct((width * 5 * panels, width), jnp.float32),
        compiler_params=PARAMS,
        cost_estimate=COST,
        name="assemble_coarse",
    )(*flat)
    return result.reshape(width, 5, panels, width).transpose(0, 2, 1, 3)


def per_device(fine_blocks, block_rows, block_cols, block_counts, prolong_blocks, prolong_mask):
    matrix = fine_blocks[0, 0]
    cols_list = block_cols[0, 0]
    lists = (block_rows[0, 0], cols_list, block_counts[0])
    groups = lax.axis_size("rows")
    grid = Grid(lax.axis_size("blk"), cols_list.shape[1], matrix.shape[2])
    cap, sides, columns = grid.cap, grid.sides, grid.columns
    every, inner = range(groups), range(1, groups - 1)

    def move(x, pairs, members=every):
        perm = [(a * groups + g, b * groups + g) for g in members for a, b in pairs]
        return lax.ppermute(x, ("blk", "rows"), perm) if perm else jnp.zeros_like(x)

    def move_both(pair, pairs):
        return (move(pair[0][0], pairs), 2), (move(pair[1][0], pairs, inner), 1)

    def move_across(arrays, lines=range(LINES)):
        return [((move(x, grid.across(shift, lines)), 3),) for x, shift in zip(arrays, sides)]

    def exchange(parts):
        lower = lax.ppermute(parts[1], "rows", [(g, g + 1) for g in range(groups - 1)])
        upper = lax.ppermute(parts[2], "rows", [(g + 1, g) for g in range(groups - 1)])
        return parts[0], lower, upper

    count = len(sides)
    mids = (1, 2)

    head, tail = pack(grid, prolong_mask.transpose(2, 0, 1), cols_list, prolong_blocks[0])
    own = ((head, 2), (tail, 1))
    half = move_both(own, grid.swaps([(0, 1), (2, 3)]))
    other = move_both(own, grid.swaps([(1, 2)]))
    side_lists = [move(cols_list, [(b, a) for a, b in grid.across(shift)]) for shift in sides]

    def own_requests(z, y):
        return [(index, grid.panel(z, y, 0), 0, index, 0) for index in range(count)]

    beside = move_across(pick(grid, own_requests, [(3, cap)] * count, side_lists, [own]))
    turned = turn(grid, head, tail)

    far_head = move(half[0][0], grid.swaps([(1, 2)]))

    def early_requests(z, y):
        return [(0, grid.panel(grid.lines(z)[1], y, 0), 0, 0, 0)]

    early, end_list = pick(grid, early_requests, [(2, cap), (0, 0)], [], [other[:1], half[:1]], (None, 1), (1,),
                           cost=COST)
    end_lists = [move(end_list, [(b, a) for a, b in grid.across(shift, mids)]) for shift in sides]
    tables = [(half[0],), *[((x, 0),) for x in end_lists]]
    end_heads = [move(early, grid.ends(0))]

    def half_requests(z, y):
        return [(index, grid.panel(grid.lines(z)[0], y, 0), 0, index, 0) for index in range(count)]

    half_picked = pick(grid, half_requests, [(3, cap)] * count, side_lists, [half], after=[x for ((x, _),) in beside], cost=COST)
    half_crossed = move_across(half_picked)

    def other_requests(z, y):
        return [(index, grid.panel(grid.lines(z)[1], y, 0), 0, index, 0) for index in range(count)]

    end_picked = pick(grid, other_requests, [(3, cap)] * count, [], [other, *tables[1:]],
                      tables=tuple(range(1, 1 + count)), after=[*half_picked, end_heads[0]], cost=COST)
    end_crossed = [((move(x, grid.ends(shift)), 3),) for x, shift in zip(end_picked, sides)]
    picked = pick(grid, other_requests, [(3, cap)] * count, side_lists, [other],
                  after=[*end_picked], cost=COST)
    other_crossed = move_across(picked, mids)
    far_tail = move(half[1][0], grid.swaps([(1, 2)]), inner)
    far = ((far_head, 2), (far_tail, 1))
    parts = stage(grid, grid.work_near, lists, turned, matrix, [own, half, *beside])

    def far_requests(z, y):
        return [(index, grid.panel(grid.lines(z)[2], y, 0), 0, index, 0) for index in range(columns)]

    far_picked = pick(grid, far_requests, [(2, cap)] * columns, [], [far[:1], *tables], tables=tuple(range(1, 2 + count)),
                      after=[parts[0], *picked], cost=COST)
    far_heads = [move(x, grid.ends(shift)) for shift, x in enumerate(far_picked)]

    def last_requests(z, y):
        _, line_other, line_far = grid.lines(z)
        row = grid.panel(line_far, y, 0)
        return ([(index, row, 0, index, 0) for index in range(count)] +
                [(count, grid.panel(line_other, y, 0), 1, count, 0), (count, row, 2, count, cap)] +
                [(count + 1 + index, row, 2, count + 1 + index, 0) for index in range(count)])

    picked = pick(grid, last_requests, [(3, cap)] * count + [(1, 2 * cap)] + [(1, cap)] * count, side_lists,
                  [far, other[1:], far[1:], *tables], tables=tuple(range(3, 4 + count)), after=[*far_picked, end_heads[0], *[x for ((x, _),) in end_crossed]],
                  cost=COST)
    far_crossed = move_across(picked, mids)
    end_tail = move(picked[count], grid.ends(0), inner)
    far_tails = [move(x, grid.ends(shift), inner) for x, shift in zip(picked[count + 1:], sides)]
    sources = []
    for i in range(count):
        sources += [half_crossed[i], other_crossed[i], end_crossed[i]]
    parts = stage(grid, grid.work_middle, lists, turned, matrix, sources, parts, [*far_heads[:1], *far_tails])
    first = exchange(parts)

    sources = [other, ((end_heads[0], 2), (end_tail, 1, 0)), far, ((far_heads[0], 2), (end_tail, 1, cap))]
    for i in range(count):
        sources += [far_crossed[i], ((far_heads[1 + i], 2), (far_tails[i], 1))]
    last = exchange(stage(grid, grid.work_far, lists, turned, matrix, sources, (), first[1:2]))
    return assemble(grid, ((grid.work_near, grid.work_middle), (grid.work_far,)), [first, last])[None, None]


def solution(mesh):
    in_specs = (
        P("rows", "blk", None, None, None, None),
        P("rows", "blk", None, None),
        P("rows", "blk", None, None),
        P("rows", "blk", None),
        P("rows", "blk", None, None),
        P("rows", "blk", None),
    )
    out_specs = P("rows", "blk", None, None, None, None)
    return jax.shard_map(
        per_device, mesh=mesh, in_specs=in_specs, out_specs=out_specs, check_vma=False
    )
```

```python
import functools
import jax
import jax.numpy as jnp
from jax import lax
from jax.experimental import pallas as pl
from jax.experimental.pallas import tpu as pltpu
from jax.sharding import PartitionSpec as P

VMEM_LIMIT = 24 * 1024 * 1024
PACK_VMEM_LIMIT = 60 * 1024 * 1024
PARAMS = pltpu.CompilerParams(vmem_limit_bytes=VMEM_LIMIT)
COST = pl.CostEstimate(flops=1024, bytes_accessed=1024, transcendentals=0)
ANYWHERE = pl.BlockSpec(memory_space=pl.ANY)


def resident(x):
    return pl.BlockSpec(x.shape, lambda i, *_, n=len(x.shape): (0,) * n)


LINES = 4


class Grid:
    def __init__(self, panels, cap, pores):
        self.panels, self.cap, self.pores = panels, cap, pores
        self.columns = panels // LINES
        self.sides = range(1, self.columns)
        self.list_rows = -(-panels // 16) * 16

    def spot(self):
        place = lax.axis_index("blk")
        return place // self.columns, place % self.columns

    def lines(self, z):
        upper = z >= 2
        return jnp.where(z % 2 == 1, z - 1, z + 1), jnp.where(upper, 1, 2), jnp.where(upper, 0, 3)

    def middle(self, z):
        return (z == 1) | (z == 2)

    def panel(self, line, y, shift):
        column = y - shift
        return line * self.columns + jnp.where(column < 0, column + self.columns, column)

    def swaps(self, lines):
        return [(h * self.columns + c, k * self.columns + c)
                for h, k in (*lines, *[(k, h) for h, k in lines]) for c in range(self.columns)]

    def across(self, shift, lines=range(LINES)):
        return [(h * self.columns + c, h * self.columns + (c + shift) % self.columns)
                for h in lines for c in range(self.columns)]

    def ends(self, shift):
        return [(h * self.columns + c, end * self.columns + (c + shift) % self.columns)
                for h, end in ((1, 0), (2, 3)) for c in range(self.columns)]

    def part(self, ref, blocks, row, block):
        start = (row * blocks + block) * self.pores
        if not isinstance(start, int):
            start = pl.multiple_of(start, self.pores)
        return ref.at[pl.ds(start, self.pores), :]

    def shape(self, rows, blocks, width, lists=0):
        return jax.ShapeDtypeStruct((rows * blocks * self.pores + lists * self.list_rows, width), jnp.bfloat16)


    def work_near(self, z, y):
        half, _, _ = self.lines(z)
        return ([(self.panel(z, y, 0), [(0, True, True)]), (self.panel(half, y, 0), [(1, True, True)])] +
                [(self.panel(z, y, shift), [(1 + shift, False, True)]) for shift in self.sides])

    def work_middle(self, z, y):
        half, other, _ = self.lines(z)
        middle = self.middle(z)
        end = jnp.logical_not(middle)
        work = []
        for i, shift in enumerate(self.sides):
            work += [(self.panel(half, y, shift), [(3 * i, False, True)]),
                     (self.panel(other, y, shift), [(3 * i + 1, False, middle), (3 * i + 2, False, end)])]
        return work

    def work_far(self, z, y):
        _, other, far = self.lines(z)
        middle = self.middle(z)
        end = jnp.logical_not(middle)
        return ([(self.panel(other, y, 0), [(0, True, middle), (1, False, end)]),
                 (self.panel(far, y, 0), [(2, True, middle), (3, False, end)])] +
                [(self.panel(far, y, shift), [(2 + 2 * shift, False, middle), (3 + 2 * shift, False, end)])
                 for shift in self.sides])


def pack_kernel(grid, mask_from, cols_from, prolong_from, head, tail, mask, cols, prolong, done):
    group, groups = lax.axis_index("rows"), lax.axis_size("rows")
    width = tail.shape[-1]
    rows = prolong.shape[0]
    step = rows // 4 if rows % 4 == 0 else rows
    copies = [pltpu.make_async_copy(mask_from, mask, done.at[0]), pltpu.make_async_copy(cols_from, cols, done.at[1])]
    for index in range(rows // step):
        some = pl.ds(index * step, step)
        copies.append(pltpu.make_async_copy(prolong_from.at[some], prolong.at[some], done.at[2 + index]))
    for copy in copies:
        copy.start()
    copies[0].wait()
    copies[1].wait()
    for i in range(rows):
        if i % step == 0:
            copies[2 + i // step].wait()
        blocks = []
        for e in range(3):
            candidate = group + e - 1
            keep = (mask[e, 0, i] == 1) & (candidate >= 0) & (candidate < groups)
            block = prolong[i, :, e * width:(e + 1) * width]
            blocks.append(block * jnp.where(keep, 1.0, 0.0).astype(block.dtype))
        grid.part(head, 2, i, 0)[...] = jnp.where(group == 0, blocks[1], blocks[0])
        grid.part(head, 2, i, 1)[...] = jnp.where(group == 0, blocks[2], blocks[1])
        grid.part(tail, 1, i, 0)[...] = jnp.where(group == 0, blocks[0], blocks[2])
    line = lax.broadcasted_iota(jnp.int32, (grid.list_rows, width), 0)
    column = lax.broadcasted_iota(jnp.int32, (grid.list_rows, width), 1)
    numbers = jnp.zeros((grid.list_rows, width), jnp.int32)
    for panel in range(grid.panels):
        for entry in range(grid.cap):
            numbers = jnp.where((line == panel) & (column == entry), cols[panel, entry], numbers)
    start = rows * 2 * grid.pores
    head[start:start + grid.list_rows, :] = numbers.astype(jnp.float32).astype(head.dtype)


def pack(grid, mask, cols, prolong):
    rows, _, width3 = prolong.shape
    outs = [grid.shape(rows, 2, width3 // 3, 1), grid.shape(rows, 1, width3 // 3)]
    return pl.pallas_call(
        functools.partial(pack_kernel, grid),
        grid=(1,),
        in_specs=[pl.BlockSpec(memory_space=pl.ANY)] * 3,
        out_specs=[*map(resident, outs)],
        scratch_shapes=[
            pltpu.SMEM(mask.shape, mask.dtype),
            pltpu.SMEM(cols.shape, cols.dtype),
            pltpu.VMEM(prolong.shape, prolong.dtype),
            pltpu.SemaphoreType.DMA((6,)),
        ],
        out_shape=outs,
        compiler_params=pltpu.CompilerParams(vmem_limit_bytes=PACK_VMEM_LIMIT),
        cost_estimate=COST,
        name="pack_rows",
    )(mask, cols, prolong)


def turn_kernel(grid, head, tail, turned):
    width = head.shape[-1]
    for i in range(turned.shape[0]):
        parts = (grid.part(head, 2, i, 0), grid.part(head, 2, i, 1), grid.part(tail, 1, i, 0))
        for k, part in enumerate(parts):
            turned[i, k * width:(k + 1) * width, :] = part[...].T


def turn(grid, head, tail):
    rows, width = tail.shape[0] // grid.pores, tail.shape[1]
    out = jax.ShapeDtypeStruct((rows, 3 * width, grid.pores), head.dtype)
    return pl.pallas_call(
        functools.partial(turn_kernel, grid),
        grid=(1,),
        in_specs=[resident(head), resident(tail)],
        out_specs=resident(out),
        out_shape=out,
        compiler_params=PARAMS,
        cost_estimate=COST,
        name="turn_rows",
    )(head, tail)


def pick_kernel(grid, plan, layout, carry, tables, lists, filled, passed, *refs):
    wanted = list(refs[:lists])
    sources, at = [], lists
    for blocks in layout:
        sources.append([(refs[at + i], k) for i, k in enumerate(blocks)])
        at += len(blocks)
    scratch = 2 * len(tables) + 1 if tables else 0
    outs = refs[len(refs) - len(filled) - scratch:len(refs) - scratch]
    z, y = grid.spot()

    def list_at(source):
        ref = sources[source][0][0]
        return ref[ref.shape[0] - grid.list_rows:, :]

    if tables:
        numbers, plain, done = refs[-scratch:-1 - len(tables)], refs[-1 - len(tables):-1], refs[-1]
        for table, source in enumerate(tables):
            numbers[table][...] = list_at(source).astype(jnp.float32).astype(jnp.int32)
            pltpu.make_async_copy(numbers[table], plain[table], done.at[table]).start()
        for table in range(len(tables)):
            pltpu.make_async_copy(numbers[table], plain[table], done.at[table]).wait()
        wanted += plain
    for index, list_row, source, output, base in plan(z, y):
        for entry in range(grid.cap):
            row = wanted[index][list_row, entry]
            place = 0
            for ref, blocks in sources[source]:
                for block in range(blocks):
                    target = grid.part(outs[output], filled[output][0], base + entry, place)
                    target[...] = grid.part(ref, blocks, row, block)[...]
                    place += 1
    if passed is not None:
        outs[-1][...] = sources[passed][0][0][...]
    for out, source in zip(outs, carry):
        if source is not None:
            out[out.shape[0] - grid.list_rows:, :] = list_at(source)


def pick(grid, plan, filled, lists, sources, carry=(), tables=(), passed=None, after=(), cost=COST):
    flat = [x for source in sources for x, _ in source]
    width = flat[0].shape[-1]
    carry = carry or (None,) * len(filled)
    shapes = [grid.shape(rows, blocks, width, 0 if source is None else 1)
              for (blocks, rows), source in zip(filled, carry)]
    if passed is not None:
        filled = [*filled, (0, 0)]
        shapes.append(jax.ShapeDtypeStruct(sources[passed][0][0].shape, flat[0].dtype))
    layout = tuple(tuple(blocks for _, blocks in source) for source in sources)
    table = (grid.list_rows, width)
    scratch = [pltpu.VMEM(table, jnp.int32)] * len(tables) + [pltpu.SMEM(table, jnp.int32)] * len(tables)
    scratch += [pltpu.SemaphoreType.DMA((len(tables),))] if tables else []
    return pl.pallas_call(
        functools.partial(pick_kernel, grid, plan, layout, carry, tables, len(lists), tuple(filled), passed),
        grid_spec=pltpu.PrefetchScalarGridSpec(
            num_scalar_prefetch=len(lists),
            grid=(1,),
            in_specs=[*map(resident, flat), *([ANYWHERE] * len(after))],
            out_specs=[*map(resident, shapes)],
            scratch_shapes=scratch,
        ),
        out_shape=shapes,
        compiler_params=PARAMS,
        cost_estimate=cost,
        name="pick_rows",
    )(*lists, *flat, *after)


def stage_kernel(grid, plan, layout, carried, slot_rows, slot_cols, slot_counts, turned, matrix, *refs):
    arrays, at = [], 0
    for blocks in layout:
        arrays.append([(refs[at + i], k, base) for i, (k, base) in enumerate(blocks)])
        at += len(blocks)
    earlier = refs[at:at + 3] if carried else ()
    own, up, down, total, values, lefts = refs[-6:]
    cap = matrix.shape[1]
    width = own.shape[-1]
    first_group = lax.axis_index("rows") == 0
    for old, new in zip(earlier, (own, up, down)):
        for slot in range(carried):
            for f in range(3):
                new[slot, f] = old[slot, f]
    z, y = grid.spot()
    for slot, (panel, sources) in enumerate(plan(z, y), start=carried):
        live = 0
        for _, _, present in sources:
            live = live + (slot_counts[0, panel] if present is True else jnp.where(present, slot_counts[0, panel], 0))
        for entry in range(cap):
            right = None
            for array, whole, present in sources:
                pick = slot_cols[panel, entry] if whole else entry
                part = jnp.concatenate(
                    [grid.part(x, blocks, base + pick, block)[...]
                     for x, blocks, base in arrays[array] for block in range(blocks)], axis=1)
                right = part if right is None else jnp.where(present, part, right)
            product = jnp.dot(matrix[panel, entry], right, preferred_element_type=jnp.float32)
            place = slice(entry * grid.pores, (entry + 1) * grid.pores)
            values[place, :] = jnp.where(entry < live, product, 0.0).astype(values.dtype)
            lefts[:, place] = turned[slot_rows[panel, entry]]
        result = jnp.dot(lefts[...], values[...], preferred_element_type=jnp.float32)
        for k in range(3):
            total[k] = result[:, k * width:(k + 1) * width]
        begin = jnp.where(first_group, 0, width)
        for f in range(3):
            k = jnp.where(first_group, (f + 2) % 3, f)
            own[slot, f] = total[k, pl.ds(pl.multiple_of(begin, width), width), :].astype(own.dtype)
            up[slot, f] = total[k, pl.ds(pl.multiple_of(begin + width, width), width), :].astype(up.dtype)
            down[slot, f] = total[k, 0:width, :].astype(down.dtype)


def stage(grid, plan, lists, turned, matrix, sources, earlier=(), after=()):
    width = turned.shape[1] // 3
    carried = earlier[0].shape[0] if earlier else 0
    slots = carried + len(plan(jnp.int32(0), jnp.int32(0)))
    flat = [x for source in sources for x, *_ in source]
    layout = tuple(tuple((blocks, base[0] if base else 0) for _, blocks, *base in source) for source in sources)
    out = jax.ShapeDtypeStruct((slots, 3, width, width), jnp.bfloat16)
    return pl.pallas_call(
        functools.partial(stage_kernel, grid, plan, layout, carried),
        grid_spec=pltpu.PrefetchScalarGridSpec(
            num_scalar_prefetch=3,
            grid=(1,),
            in_specs=[*map(resident, (turned, matrix, *flat, *earlier)), *([ANYWHERE] * len(after))],
            out_specs=[resident(out)] * 3,
            scratch_shapes=[
                pltpu.VMEM((3, 3 * width, width), jnp.float32),
                pltpu.VMEM((matrix.shape[1] * grid.pores, 3 * width), jnp.bfloat16),
                pltpu.VMEM((3 * width, matrix.shape[1] * grid.pores), jnp.bfloat16),
            ],
        ),
        out_shape=[out] * 3,
        compiler_params=PARAMS,
        cost_estimate=COST,
        name="stage_products",
    )(*lists, turned, matrix, *flat, *earlier, *after)


def assemble_kernel(grid, plans, *refs):
    out = refs[-1]
    rows = refs[0].shape[2]
    panels = grid.panels
    z, y = grid.spot()
    for index, group in enumerate(plans):
        own, lower, upper = refs[3 * index:3 * index + 3]
        slots = [slot for plan in group for slot in plan(z, y)]
        for slot, (panel, _) in enumerate(slots):
            for d in range(5):
                terms = []
                if 0 <= d - 1 < 3:
                    terms.append(own[slot, d - 1].astype(jnp.float32))
                if d < 3:
                    terms.append(lower[slot, d].astype(jnp.float32))
                if 0 <= d - 2 < 3:
                    terms.append(upper[slot, d - 2].astype(jnp.float32))
                out[pl.ds(d * panels + panel, rows, stride=5 * panels), :] = functools.reduce(jnp.add, terms)


def assemble(grid, plans, pieces):
    panels = grid.panels
    width = pieces[0][0].shape[-1]
    rows = width // 8
    flat = [x for piece in pieces for x in piece]
    result = pl.pallas_call(
        functools.partial(assemble_kernel, grid, plans),
        grid=(width // rows,),
        in_specs=[pl.BlockSpec((x.shape[0], 3, rows, width), lambda i: (0, 0, i, 0)) for x in flat],
        out_specs=pl.BlockSpec((rows * 5 * panels, width), lambda i: (i, 0)),
        out_shape=jax.ShapeDtypeStruct((width * 5 * panels, width), jnp.float32),
        compiler_params=PARAMS,
        cost_estimate=COST,
        name="assemble_coarse",
    )(*flat)
    return result.reshape(width, 5, panels, width).transpose(0, 2, 1, 3)


def per_device(fine_blocks, block_rows, block_cols, block_counts, prolong_blocks, prolong_mask):
    matrix = fine_blocks[0, 0]
    cols_list = block_cols[0, 0]
    lists = (block_rows[0, 0], cols_list, block_counts[0])
    groups = lax.axis_size("rows")
    grid = Grid(lax.axis_size("blk"), cols_list.shape[1], matrix.shape[2])
    cap, sides, columns = grid.cap, grid.sides, grid.columns
    every, inner = range(groups), range(1, groups - 1)

    def move(x, pairs, members=every):
        perm = [(a * groups + g, b * groups + g) for g in members for a, b in pairs]
        return lax.ppermute(x, ("blk", "rows"), perm) if perm else jnp.zeros_like(x)

    def move_both(pair, pairs):
        return (move(pair[0][0], pairs), 2), (move(pair[1][0], pairs, inner), 1)

    def move_across(arrays, lines=range(LINES)):
        return [((move(x, grid.across(shift, lines)), 3),) for x, shift in zip(arrays, sides)]

    def exchange(parts):
        lower = lax.ppermute(parts[1], "rows", [(g, g + 1) for g in range(groups - 1)])
        upper = lax.ppermute(parts[2], "rows", [(g + 1, g) for g in range(groups - 1)])
        return parts[0], lower, upper

    count = len(sides)
    mids = (1, 2)

    head, tail = pack(grid, prolong_mask.transpose(2, 0, 1), cols_list, prolong_blocks[0])
    own = ((head, 2), (tail, 1))
    half = move_both(own, grid.swaps([(0, 1), (2, 3)]))
    other = move_both(own, grid.swaps([(1, 2)]))
    side_lists = [move(cols_list, [(b, a) for a, b in grid.across(shift)]) for shift in sides]

    def own_requests(z, y):
        return [(index, grid.panel(z, y, 0), 0, index, 0) for index in range(count)]

    beside = move_across(pick(grid, own_requests, [(3, cap)] * count, side_lists, [own]))
    turned = turn(grid, head, tail)

    far_head = move(half[0][0], grid.swaps([(1, 2)]))

    def early_requests(z, y):
        return [(0, grid.panel(grid.lines(z)[1], y, 0), 0, 0, 0)]

    early, end_list = pick(grid, early_requests, [(2, cap), (0, 0)], [], [other[:1], half[:1]], (None, 1), (1,),
                           cost=COST)
    end_lists = [move(end_list, [(b, a) for a, b in grid.across(shift, mids)]) for shift in sides]
    tables = [(half[0],), *[((x, 0),) for x in end_lists]]
    end_heads = [move(early, grid.ends(0))]

    def half_requests(z, y):
        return [(index, grid.panel(grid.lines(z)[0], y, 0), 0, index, 0) for index in range(count)]

    half_picked = pick(grid, half_requests, [(3, cap)] * count, side_lists, [half], after=[x for ((x, _),) in beside], cost=COST)
    half_crossed = move_across(half_picked)

    def other_requests(z, y):
        return [(index, grid.panel(grid.lines(z)[1], y, 0), 0, index, 0) for index in range(count)]

    end_picked = pick(grid, other_requests, [(3, cap)] * count, [], [other, *tables[1:]],
                      tables=tuple(range(1, 1 + count)), after=[*half_picked, end_heads[0]], cost=COST)
    end_crossed = [((move(x, grid.ends(shift)), 3),) for x, shift in zip(end_picked, sides)]
    picked = pick(grid, other_requests, [(3, cap)] * count, side_lists, [other],
                  after=[*end_picked], cost=COST)
    other_crossed = move_across(picked, mids)
    far_tail = move(half[1][0], grid.swaps([(1, 2)]), inner)
    far = ((far_head, 2), (far_tail, 1))
    parts = stage(grid, grid.work_near, lists, turned, matrix, [own, half, *beside])

    def far_requests(z, y):
        return [(index, grid.panel(grid.lines(z)[2], y, 0), 0, index, 0) for index in range(columns)]

    far_picked = pick(grid, far_requests, [(2, cap)] * columns, [], [far[:1], *tables], tables=tuple(range(1, 2 + count)),
                      after=[parts[0], *picked], cost=COST)
    far_heads = [move(x, grid.ends(shift)) for shift, x in enumerate(far_picked)]

    def last_requests(z, y):
        _, line_other, line_far = grid.lines(z)
        row = grid.panel(line_far, y, 0)
        return ([(index, row, 0, index, 0) for index in range(count)] +
                [(count, grid.panel(line_other, y, 0), 1, count, 0), (count, row, 2, count, cap)] +
                [(count + 1 + index, row, 2, count + 1 + index, 0) for index in range(count)])

    picked = pick(grid, last_requests, [(3, cap)] * count + [(1, 2 * cap)] + [(1, cap)] * count, side_lists,
                  [far, other[1:], far[1:], *tables], tables=tuple(range(3, 4 + count)), after=[*far_picked, end_heads[0], *[x for ((x, _),) in end_crossed], *[x for ((x, _),) in half_crossed]],
                  cost=COST)
    far_crossed = move_across(picked, mids)
    end_tail = move(picked[count], grid.ends(0), inner)
    far_tails = [move(x, grid.ends(shift), inner) for x, shift in zip(picked[count + 1:], sides)]
    sources = []
    for i in range(count):
        sources += [half_crossed[i], other_crossed[i], end_crossed[i]]
    parts = stage(grid, grid.work_middle, lists, turned, matrix, sources, parts, [*far_heads[:1], *far_tails])
    first = exchange(parts)

    sources = [other, ((end_heads[0], 2), (end_tail, 1, 0)), far, ((far_heads[0], 2), (end_tail, 1, cap))]
    for i in range(count):
        sources += [far_crossed[i], ((far_heads[1 + i], 2), (far_tails[i], 1))]
    last = exchange(stage(grid, grid.work_far, lists, turned, matrix, sources, (), first[1:2]))
    return assemble(grid, ((grid.work_near, grid.work_middle), (grid.work_far,)), [first, last])[None, None]


def solution(mesh):
    in_specs = (
        P("rows", "blk", None, None, None, None),
        P("rows", "blk", None, None),
        P("rows", "blk", None, None),
        P("rows", "blk", None),
        P("rows", "blk", None, None),
        P("rows", "blk", None),
    )
    out_specs = P("rows", "blk", None, None, None, None)
    return jax.shard_map(
        per_device, mesh=mesh, in_specs=in_specs, out_specs=out_specs, check_vma=False
    )
```
